32 devices in a mesh: groups: 2 (over y), lon: 4 (over z), lat: 2 (over x), chan: 2 (over core).
Axes of the slice: x: 2, y: 2, z: 4, core: 2. Of those that a mesh axis runs over, the one named last changes fastest.
Arguments:
- state: bfloat16 [32, 720, 256], P(('groups', 'lat'), 'lon', 'chan'), parts along dimension 0, may hold values from -6 to 6
- sup_rows: int32 [16, 5], P('lat'), may hold values from 0 to 15, as said below
- sup_count: int32 [16], P('lat'), may hold values from 2 to 5
- lon_reach: int32 [16], P('lat'), may hold values from 1 to 8
- psi: float32 [16, 5, 4, 17], P('lat'), may hold values from -1 to 1
- weights: bfloat16 [2, 4, 256, 256], replicated, may hold values from -0.1875 to 0.1875
Outputs:
- fields: bfloat16 [32, 720, 256], P(('groups', 'lat'), 'lon', 'chan'), parts along dimension 0
The draws below stay inside these ranges and needn't reach their ends.
There are 2 independent parts, one for each index of `groups`. The reference program is written for one: setup_inputs(seed, part) draws one part's arguments, and reference() takes and returns one part's arrays. A program takes and returns all parts, laid end to end along the dimension named above; an argument that names none is the same for every part. Nothing has to cross between parts.
Inputs may be any that keep to these rules, and one draw needn't show every extreme that they name: sup_rows[i, s] lies within 2 rows of i.
All inputs are finite; a program needn't handle non-finite values.
Results may differ from the reference program's by a relative error of at most 0.0059.
Values may be sent and summed in bfloat16 or wider, within the bound.
No kernel may reach another device: no remote copies, remote signals or barrier semaphores. Data moves between devices by JAX's collectives and lax.ppermute only.
A program may use at most 64 MiB of HBM per device.

```python
import jax
import jax.numpy as jnp
from jax import lax

CH = 256
K = 4
LAYERS = 2
SPAN = 2
SUP = 5
RMAX = 8
LAT_DEV = 8
OFFS = 17
NLAT = 16
NLON = 720


def polar_rows():
    index = jnp.arange(NLAT, dtype=jnp.int32)
    edge = max(1, NLAT // 16)
    return (index < edge) | (index >= NLAT - edge)


def draw_sup_rows(key, part):
    key = jax.random.fold_in(key, 11)
    index = jnp.arange(NLAT, dtype=jnp.int32)
    shifts = jax.random.randint(key, (NLAT, SUP), -SPAN, SPAN + 1, dtype=jnp.int32)
    return jnp.clip(index[:, None] + shifts, 0, NLAT - 1).astype(jnp.int32)


def draw_sup_count(key, part):
    key = jax.random.fold_in(key, 12)
    index = jnp.arange(NLAT, dtype=jnp.int32)
    counts = jax.random.randint(key, (NLAT,), 2, SUP + 1, dtype=jnp.int32)
    counts = jnp.where(polar_rows(), SUP, counts)
    return jnp.where(index == NLAT // 2, 2, counts).astype(jnp.int32)


def draw_lon_reach(key, part):
    key = jax.random.fold_in(key, 13)
    index = jnp.arange(NLAT, dtype=jnp.int32)
    reach = jax.random.randint(key, (NLAT,), 1, RMAX + 1, dtype=jnp.int32)
    reach = jnp.where(polar_rows(), RMAX, reach)
    return jnp.where(index == NLAT // 2, 1, reach).astype(jnp.int32)


def levels(own_key, shape, cuts, smallest, high):
    def one(dim, blocks):
        draws = jax.random.uniform(jax.random.fold_in(jax.random.fold_in(own_key, 6), dim), (blocks,), jnp.float32, smallest / len(cuts), high / len(cuts))
        return jnp.repeat(jnp.exp(draws), shape[dim] // blocks).reshape((-1,) + (1,) * (len(shape) - dim - 1))

    factor_of = one(*cuts[0])
    for cut in cuts[1:]:
        factor_of = factor_of * one(*cut)
    return factor_of


def bell_draw(stream_key, shape, spread, most, cuts=(), held_as=jnp.bfloat16):
    loudness = levels(stream_key, shape, cuts, -0.22, 0.18) if cuts else 1.0
    values = jax.random.normal(stream_key, shape, jnp.float32) * spread * loudness
    return jnp.minimum(jnp.maximum(values, -most), most).astype(held_as)


def setup_inputs(seed: int = 0, part: int = 0) -> dict:
    keys = jax.random.split(jax.random.key(seed), 7)
    own_keys = jax.random.split(jax.random.fold_in(keys[6], part), 7)
    state = bell_draw(own_keys[0], (NLAT, NLON, CH), 1.0, 6.0, ((0, 2), (1, 4), (2, 2)))
    sup_rows = draw_sup_rows(jax.random.fold_in(keys[6], 71), part)
    sup_count = draw_sup_count(jax.random.fold_in(keys[6], 71), part)
    lon_reach = draw_lon_reach(jax.random.fold_in(keys[6], 71), part)
    psi = bell_draw(keys[4], (NLAT, SUP, K, OFFS), (SUP * OFFS // 2) ** -0.5, 1.0, ((0, 2),), jnp.float32)
    weights = bell_draw(keys[5], (LAYERS, K, CH, CH), (K * CH) ** -0.5, 0.1875)
    return {"state": state, "sup_rows": sup_rows, "sup_count": sup_count, "lon_reach": lon_reach, "psi": psi, "weights": weights}


def band_matrix(rows_tab, counts, reach, psi, row0, total_rows):
    lat_rows, slots, basis_count, offsets = psi.shape
    half_reach = offsets // 2
    slot_live = jnp.arange(slots, dtype=jnp.int32)[None, :] < counts[:, None]
    off_live = jnp.abs(jnp.arange(offsets, dtype=jnp.int32) - half_reach)[None, :] <= reach[:, None]
    target = row0 - SPAN + jnp.arange(total_rows, dtype=jnp.int32)
    onehot = ((rows_tab[:, :, None] == target[None, None, :]) & slot_live[:, :, None]).astype(jnp.float32)
    masked = psi * off_live[:, None, None, :].astype(jnp.float32)
    band_full = jnp.einsum('isr,isko->kiro', onehot, masked, precision=lax.Precision.HIGHEST)
    return band_full.astype(jnp.bfloat16).reshape(basis_count * lat_rows, total_rows * offsets)


def reference(state, sup_rows, sup_count, lon_reach, psi, weights):
    block_count = NLAT // LAT_DEV
    total_rows = LAT_DEV + 2 * SPAN
    starts = jnp.arange(block_count, dtype=jnp.int32) * LAT_DEV

    def block_band(row0):
        return band_matrix(lax.dynamic_slice_in_dim(sup_rows, row0, LAT_DEV, 0),
                           lax.dynamic_slice_in_dim(sup_count, row0, LAT_DEV, 0),
                           lax.dynamic_slice_in_dim(lon_reach, row0, LAT_DEV, 0),
                           lax.dynamic_slice_in_dim(psi, row0, LAT_DEV, 0), row0, total_rows)

    bands = lax.map(block_band, starts)
    fields = state
    for layer in range(LAYERS):
        padded = jnp.pad(fields, ((SPAN, SPAN), (0, 0), (0, 0)))
        wrapped = jnp.concatenate([padded[:, NLON - RMAX:], padded, padded[:, :RMAX]], axis=1)
        layer_weights = weights[layer].astype(jnp.float32)

        def one_block(item):
            band_block, row0 = item
            window = lax.dynamic_slice_in_dim(wrapped, row0, total_rows, 0)
            unfolded = jnp.stack([window[:, offset:offset + NLON, :] for offset in range(2 * RMAX + 1)], axis=1)
            unfolded = unfolded.reshape(total_rows * (2 * RMAX + 1), NLON * CH)
            features = jnp.dot(band_block, unfolded, preferred_element_type=jnp.float32).astype(jnp.bfloat16)
            features = features.reshape(K, LAT_DEV, NLON, CH).astype(jnp.float32)
            mixed = jnp.einsum('kijc,kcd->ijd', features, layer_weights)
            previous = lax.dynamic_slice_in_dim(fields, row0, LAT_DEV, 0)
            return (previous.astype(jnp.float32) + jax.nn.gelu(mixed)).astype(jnp.bfloat16)

        fields = lax.map(one_block, (bands, starts)).reshape(NLAT, NLON, CH)
    return fields
```

```python
import functools

import jax
import jax.numpy as jnp
from jax import lax
from jax.experimental import pallas as pl
from jax.experimental.pallas import tpu as pltpu
from jax.sharding import PartitionSpec as P

LAYERS = 2
SPAN = 2
HALO = LAYERS * SPAN
BLOCK = 16
GROUP = 4
VMEM_LIMIT = 48 * 1024 * 1024
MIXED = jnp.bfloat16


def vmem():
    return pl.BlockSpec(memory_space=pltpu.VMEM)


def smem():
    return pl.BlockSpec(memory_space=pltpu.SMEM)


def toeplitz(rows_tab, basis):
    count, lanes = rows_tab.shape
    moved = jnp.concatenate(
        [rows_tab if jj == 0 else pltpu.roll(rows_tab, jj, 1) for jj in range(BLOCK)], axis=0
    ).astype(MIXED)
    total = count * BLOCK
    out_row = lax.broadcasted_iota(jnp.int32, (total, total), 0)
    in_row = lax.broadcasted_iota(jnp.int32, (total, total), 1)
    source = (out_row % BLOCK) * count + out_row // BLOCK
    order = (in_row == source).astype(jnp.float32).astype(MIXED)
    return jnp.dot(order, moved, preferred_element_type=jnp.float32).astype(MIXED)


def prep_kernel(sides, state_ref, sup_ref, count_ref, reach_ref, psi_ref, tables_ref, *rest):
    sends, (slots, rows_scr) = rest[:sides], rest[sides:]
    lat_rows, cols, _ = state_ref.shape
    _, sup, basis, offsets = psi_ref.shape
    reach_max = offsets // 2
    lanes = tables_ref.shape[2]
    window = 2 * BLOCK
    lat = lax.axis_index("lat")
    slots[...] = jnp.zeros_like(slots)
    for i in range(lat_rows):
        for s in range(sup):
            rel = jnp.clip(sup_ref[i, s] - (lat * lat_rows + i) + SPAN, 0, 2 * SPAN)
            live = jnp.where(s < count_ref[i], 1.0, 0.0)
            slots[i, rel, :, 0:offsets] += psi_ref[i, s] * live
    lane = lax.broadcasted_iota(jnp.int32, (basis, lanes), 1)
    bands = []
    for i in range(lat_rows):
        band = slots[i, 0]
        for rel in range(1, 2 * SPAN + 1):
            band = band + pltpu.roll(slots[i, rel], rel * window, 1)
        off = lane % window - reach_max
        bands.append(jnp.where(jnp.abs(off) <= reach_ref[i], band, 0.0))
    for g in range(lat_rows // GROUP):
        for m in range(GROUP):
            band = bands[g * GROUP + m]
            rows_scr[m * basis : (m + 1) * basis, :] = (
                band if m == 0 else pltpu.roll(band, m * window, 1)
            )
        tables_ref[g] = toeplitz(rows_scr[...], basis)

    def edge_rows(first):
        return [
            bands[first] if m == 0 else pltpu.roll(bands[first + m], m * window, 1)
            for m in range(SPAN)
        ]

    head, tail = edge_rows(0), edge_rows(lat_rows - SPAN)
    for n, send in enumerate(sends):
        if sides == 1:
            take_tail = lat == 0
            base = jnp.where(take_tail, lat_rows - HALO, 0)
            picked = [jnp.where(take_tail, t, h) for h, t in zip(head, tail)]
        else:
            base = lat_rows - HALO if n == 0 else 0
            picked = tail if n == 0 else head
        for m in range(SPAN):
            rows_scr[m * basis : (m + 1) * basis, :] = picked[m]
        half = lanes // 2
        for t in range(HALO):
            extra = jnp.concatenate(
                [
                    rows_scr[2 * t : 2 * t + 1, 0:half],
                    rows_scr[2 * t : 2 * t + 1, half:],
                    rows_scr[2 * t + 1 : 2 * t + 2, 0:half],
                    rows_scr[2 * t + 1 : 2 * t + 2, half:],
                ],
                axis=0,
            )
            send[t, 0:cols, :] = state_ref[base + t]
            send[t, cols : cols + 4, :] = extra.astype(send.dtype)


def edges_kernel(sides, own_ref, other_ref, *rest):
    own_halos, other_halos = rest[:sides], rest[sides : 2 * sides]
    left_ref, right_ref = rest[2 * sides :]
    lat_rows, cols, width = own_ref.shape
    chan = lax.axis_index("chan")
    wide = left_ref.shape[1]
    start = (cols - wide) // BLOCK * BLOCK
    skip = cols - wide - start
    for side, first in ((0, own_ref), (1, other_ref)):
        lane = pl.ds(pl.multiple_of((chan if side == 0 else 1 - chan) * width, width), width)
        halos = own_halos if side == 0 else other_halos
        pieces = [(first, lat_rows)] + [(h, HALO) for h in halos]
        row = 0
        for ref, count in pieces:
            for t in range(count):
                left_ref[row, :, lane] = ref[t, 0:wide, :]
                last = ref[t, start:cols, :].astype(jnp.float32)
                right_ref[row, :, lane] = last[skip:, :].astype(right_ref.dtype)
                row += 1


def gelu(x):
    return 0.5 * x * (1.0 + jnp.tanh(0.7978845608028654 * (x + 0.044715 * (x * x * x))))


def main_kernel(sides, own_ref, other_ref, *rest):
    own_halos, other_halos = rest[:sides], rest[sides : 2 * sides]
    (left_ref, right_ref, tables_ref, weights_ref, out_ref) = rest[2 * sides : 2 * sides + 5]
    fields, feats, fields2 = rest[2 * sides + 5 :]
    lat_rows, cols, width = own_ref.shape
    basis, chans = weights_ref.shape[1], weights_ref.shape[2]
    chan = lax.axis_index("chan")
    lat = lax.axis_index("lat")
    wide = left_ref.shape[1]
    window = 2 * BLOCK
    lon_total = fields.shape[1]
    blocks1 = lon_total // BLOCK - 1
    blocks2 = -(-cols // BLOCK)
    groups = lat_rows // GROUP
    own_lane = pl.ds(pl.multiple_of(chan * width, width), width)
    other_lane = pl.ds(pl.multiple_of((1 - chan) * width, width), width)

    if sides == 1:
        top = lat > 0
        halo_base = [jnp.where(top, 0, lat_rows + HALO)]
        empty_base = [jnp.where(top, lat_rows + HALO, 0)]
        win_base = [jnp.where(top, 0, lat_rows + HALO - SPAN)]
        out_base = [jnp.where(top, 0, lat_rows + SPAN)]
        empty_out = [jnp.where(top, lat_rows + SPAN, 0)]
    else:
        halo_base = [0, lat_rows + HALO]
        win_base = [0, lat_rows + HALO - SPAN]
        out_base = [0, lat_rows + SPAN]
        empty_base, empty_out = [], []

    whole = cols // BLOCK * BLOCK
    rest_cols = lon_total - wide - whole
    for base in empty_base:
        for t in range(HALO):
            fields[base + t] = jnp.zeros(fields.shape[1:], fields.dtype)

    def place(own, other, dest, row):
        tails = []
        for ref, lane in ((own, own_lane), (other, other_lane)):
            fields[dest, wide : wide + whole, lane] = ref[0:whole, :]
        for ref, lane in ((own, own_lane), (other, other_lane)):
            tail = jnp.concatenate(
                [
                    ref[whole:cols, :].astype(jnp.float32),
                    right_ref[row, :, lane].astype(jnp.float32),
                    jnp.zeros((rest_cols - (cols - whole) - wide, width), jnp.float32),
                ],
                axis=0,
            )
            fields[dest, wide + whole : lon_total, lane] = tail.astype(fields.dtype)
        fields[dest, 0:wide, :] = left_ref[row]

    row = 0
    for t in range(lat_rows):
        place(own_ref.at[t], other_ref.at[t], HALO + t, row)
        row += 1
    for n in range(sides):
        for t in range(HALO):
            place(own_halos[n].at[t], other_halos[n].at[t], halo_base[n] + t, row)
            row += 1

    halo_tables = []
    for n in range(sides):
        flat = [own_halos[n][t, cols : cols + 4, :].astype(jnp.float32) for t in range(HALO)]
        rows_tab = jnp.concatenate(
            [
                jnp.concatenate([x[2 * q : 2 * q + 1, :], x[2 * q + 1 : 2 * q + 2, :]], axis=1)
                for x in flat
                for q in range(2)
            ],
            axis=0,
        )
        halo_tables.append(toeplitz(rows_tab, basis))

    def spread(result, first, out_rows, at):
        result = result.astype(MIXED)
        for m in range(out_rows):
            for k in range(basis):
                begin = (m * basis + k) * BLOCK
                feats[first + m, pl.ds(at, BLOCK), k * chans : (k + 1) * chans] = result[
                    begin : begin + BLOCK, :
                ]

    def conv(source, table, base, in_rows, first, out_rows, at):
        taken = source[pl.ds(base, in_rows), pl.ds(at, window), :]
        taken = taken.reshape(in_rows * window, chans)
        spread(
            jnp.dot(table, taken, preferred_element_type=jnp.float32), first, out_rows, at
        )

    def layer1(jb, carry):
        at = pl.multiple_of(jb * BLOCK, BLOCK)
        for g in range(groups):
            conv(
                fields,
                tables_ref[g],
                HALO - SPAN + g * GROUP,
                GROUP + 2 * SPAN,
                g * GROUP,
                GROUP,
                at,
            )
        for n in range(sides):
            count = 3 * SPAN
            conv(
                fields,
                halo_tables[n][:, : count * window],
                win_base[n],
                count,
                lat_rows + n * SPAN,
                SPAN,
                at,
            )
        return carry

    lax.fori_loop(0, blocks1, layer1, 0)

    for base in empty_out:
        for t in range(SPAN):
            fields2[base + t] = jnp.zeros(fields2.shape[1:], fields2.dtype)
    shift = wide // 2
    lon1 = blocks1 * BLOCK

    def mix1(source, dest, i):
        mixed = jnp.dot(
            feats[i],
            weights_ref[0].reshape(basis * chans, chans),
            preferred_element_type=jnp.float32,
        )
        before = fields[source].astype(jnp.float32)[shift : shift + lon1, :]
        fields2[dest] = (before + gelu(mixed)).astype(fields2.dtype)

    def mix1_own(i, carry):
        mix1(HALO + i, SPAN + i, i)
        return carry

    lax.fori_loop(0, lat_rows, mix1_own, 0)
    for n in range(sides):
        for m in range(SPAN):
            source = out_base[n] + SPAN + m
            mix1(source, out_base[n] + m, lat_rows + n * SPAN + m)

    def layer2(jb, carry):
        at = pl.multiple_of(jb * BLOCK, BLOCK)
        for g in range(groups):
            conv(fields2, tables_ref[g], g * GROUP, GROUP + 2 * SPAN, g * GROUP, GROUP, at)
        return carry

    lax.fori_loop(0, blocks2, layer2, 0)
    lon2 = blocks2 * BLOCK

    def mix2(i, carry):
        mixed = jnp.dot(
            feats[i, 0:lon2, :],
            weights_ref[1, :, :, own_lane].reshape(basis * chans, width),
            preferred_element_type=jnp.float32,
        )
        before = fields2[SPAN + i, :, own_lane].astype(jnp.float32)[shift : shift + lon2, :]
        out_ref[i] = (before + gelu(mixed))[0:cols, :].astype(out_ref.dtype)
        return carry

    lax.fori_loop(0, lat_rows, mix2, 0)


def per_device(state, sup_rows, sup_count, lon_reach, psi, weights):
    lat_rows, cols, width = state.shape
    _, _, basis, offsets = psi.shape
    chans = weights.shape[2]
    lats, lons = lax.axis_size("lat"), lax.axis_size("lon")
    sides = 1 if lats == 2 else 2
    groups = lat_rows // GROUP
    in_rows = GROUP + 2 * SPAN
    window = 2 * BLOCK
    lanes = in_rows * window
    wide = LAYERS * (offsets // 2)
    ext = lat_rows + sides * HALO
    lon_total = (-(-(cols + wide) // BLOCK) + 1) * BLOCK
    swap = [(0, 1), (1, 0)]
    params = pltpu.CompilerParams(vmem_limit_bytes=VMEM_LIMIT)

    other = lax.ppermute(state, "chan", swap)

    send_type = jax.ShapeDtypeStruct((HALO, cols + 4, width), state.dtype)
    tables, *sends = pl.pallas_call(
        functools.partial(prep_kernel, sides),
        out_shape=[jax.ShapeDtypeStruct((groups, GROUP * basis * BLOCK, lanes), MIXED)]
        + [send_type] * sides,
        in_specs=[vmem(), smem(), smem(), smem(), vmem()],
        out_specs=[vmem()] * (1 + sides),
        scratch_shapes=[
            pltpu.VMEM((lat_rows, 2 * SPAN + 1, basis, lanes), jnp.float32),
            pltpu.VMEM((GROUP * basis, lanes), jnp.float32),
        ],
        compiler_params=params,
        name="prep",
    )(state, sup_rows, sup_count, lon_reach, psi)

    if sides == 1:
        own_halos = [lax.ppermute(sends[0], "lat", swap)]
    else:
        own_halos = [
            lax.ppermute(sends[0], "lat", [(i, i + 1) for i in range(lats - 1)]),
            lax.ppermute(sends[1], "lat", [(i + 1, i) for i in range(lats - 1)]),
        ]
    other_halos = [lax.ppermute(h, "chan", swap) for h in own_halos]

    edge_type = jax.ShapeDtypeStruct((ext, wide, chans), state.dtype)
    head, tail = pl.pallas_call(
        functools.partial(edges_kernel, sides),
        out_shape=[edge_type] * 2,
        in_specs=[vmem()] * (2 + 2 * sides),
        out_specs=[vmem()] * 2,
        compiler_params=params,
        name="edges",
    )(state, other, *own_halos, *other_halos)
    right = lax.ppermute(head, "lon", [((i + 1) % lons, i) for i in range(lons)])
    left = lax.ppermute(tail, "lon", [(i, (i + 1) % lons) for i in range(lons)])

    return pl.pallas_call(
        functools.partial(main_kernel, sides),
        out_shape=jax.ShapeDtypeStruct(state.shape, state.dtype),
        in_specs=[vmem()] * (6 + 2 * sides),
        out_specs=vmem(),
        scratch_shapes=[
            pltpu.VMEM((lat_rows + 2 * HALO, lon_total, chans), state.dtype),
            pltpu.VMEM((lat_rows + sides * SPAN, lon_total - BLOCK, basis * chans), MIXED),
            pltpu.VMEM((lat_rows + 2 * SPAN, lon_total - BLOCK, chans), state.dtype),
        ],
        compiler_params=params,
        name="layers",
    )(state, other, *own_halos, *other_halos, left, right, tables, weights)


def solution(mesh):
    return jax.shard_map(
        per_device,
        mesh=mesh,
        in_specs=(
            P(("groups", "lat"), "lon", "chan"),
            P("lat", None),
            P("lat"),
            P("lat"),
            P("lat", None, None, None),
            P(),
        ),
        out_specs=P(("groups", "lat"), "lon", "chan"),
        check_vma=False,
    )
```

```python
import functools

import jax
import jax.numpy as jnp
from jax import lax
from jax.experimental import pallas as pl
from jax.experimental.pallas import tpu as pltpu
from jax.sharding import PartitionSpec as P

LAYERS = 2
SPAN = 2
HALO = LAYERS * SPAN
BLOCK = 16
WINDOW = 2 * BLOCK
GROUP = 4
WIDE = BLOCK
VMEM_LIMIT = 48 * 1024 * 1024
BF16 = jnp.bfloat16
F32 = jnp.float32


def vmem():
    return pl.BlockSpec(memory_space=pltpu.VMEM)


def smem():
    return pl.BlockSpec(memory_space=pltpu.SMEM)


def toeplitz(rows_tab):
    count, _ = rows_tab.shape
    moved = jnp.concatenate(
        [rows_tab if jj == 0 else pltpu.roll(rows_tab, jj, 1) for jj in range(BLOCK)], axis=0
    ).astype(BF16)
    total = count * BLOCK
    out_row = lax.broadcasted_iota(jnp.int32, (total, total), 0)
    in_row = lax.broadcasted_iota(jnp.int32, (total, total), 1)
    source = (out_row % BLOCK) * count + out_row // BLOCK
    order = (in_row == source).astype(F32).astype(BF16)
    return jnp.dot(order, moved, preferred_element_type=F32).astype(BF16)


def prep_kernel(
    sides, sup_ref, count_ref, reach_ref, psi_ref, tables_ref, bands_ref, slots, rows_scr
):
    lat_rows, sup, basis, offsets = psi_ref.shape
    reach_max = offsets // 2
    lanes = tables_ref.shape[2]
    lat = lax.axis_index("lat")
    slots[...] = jnp.zeros_like(slots)
    for i in range(lat_rows):
        for s in range(sup):
            rel = jnp.clip(sup_ref[i, s] - (lat * lat_rows + i) + SPAN, 0, 2 * SPAN)
            live = jnp.where(s < count_ref[i], 1.0, 0.0)
            slots[i, rel, :, 0:offsets] += psi_ref[i, s] * live
    lane = lax.broadcasted_iota(jnp.int32, (basis, lanes), 1)
    bands = []
    for i in range(lat_rows):
        band = slots[i, 0]
        for rel in range(1, 2 * SPAN + 1):
            band = band + pltpu.roll(slots[i, rel], rel * WINDOW, 1)
        off = lane % WINDOW - reach_max
        bands.append(jnp.where(jnp.abs(off) <= reach_ref[i], band, 0.0))
    for g in range(lat_rows // GROUP):
        for m in range(GROUP):
            band = bands[g * GROUP + m]
            rows_scr[m * basis : (m + 1) * basis, :] = (
                band if m == 0 else pltpu.roll(band, m * WINDOW, 1)
            )
        tables_ref[g] = toeplitz(rows_scr[...])

    def edge_rows(first):
        return [
            bands[first] if m == 0 else pltpu.roll(bands[first + m], m * WINDOW, 1)
            for m in range(SPAN)
        ]

    head, tail = edge_rows(0), edge_rows(lat_rows - SPAN)
    rows_scr[...] = jnp.zeros_like(rows_scr)
    for n in range(sides):
        if sides == 1:
            picked = [jnp.where(lat == 0, t, h) for h, t in zip(head, tail)]
        else:
            picked = tail if n == 0 else head
        for m in range(SPAN):
            rows_scr[m * basis : (m + 1) * basis, :] = picked[m]
        bands_ref[n] = rows_scr[...].astype(BF16)


def edges_kernel(sides, half, own_ref, other_ref, bands_ref, fields_ref, lon_ref, *rest):
    lat_refs, corner_refs, (wide_scr,) = rest[:sides], rest[sides : 2 * sides], rest[2 * sides :]
    cols, lat_rows, width = own_ref.shape
    lon_total = fields_ref.shape[1]
    part = half + WIDE
    chan = lax.axis_index("chan")
    lat = lax.axis_index("lat")

    def build(core):
        start = 0 if core == 0 else half - WIDE
        count = min(cols - start, part)
        edge = 0 if core == 0 else count - WIDE
        at = WIDE if core == 0 else 0
        for c, ref in ((core, own_ref), (1 - core, other_ref)):
            lane = slice(c * width, (c + 1) * width)
            wide_scr[c, 0 : count * lat_rows, :] = (
                ref[start : start + count].astype(F32).reshape(count * lat_rows, width)
            )
            if count < part:
                wide_scr[c, count * lat_rows :, :] = jnp.zeros(
                    ((part - count) * lat_rows, width), F32
                )
            for r in range(lat_rows):
                fields_ref[r, at : at + part, lane] = wide_scr[
                    c, pl.ds(r, part, stride=lat_rows), :
                ].astype(BF16)
                lon_ref[r, :, lane] = wide_scr[
                    c, pl.ds(edge * lat_rows + r, WIDE, stride=lat_rows), :
                ].astype(BF16)
        empty = slice(0, WIDE) if core == 0 else slice(part, lon_total)
        fields_ref[:, empty, :] = jnp.zeros((lat_rows, WIDE, 2 * width), BF16)

    @pl.when(chan == 0)
    def _():
        build(0)

    @pl.when(chan == 1)
    def _():
        build(1)

    at = pl.multiple_of((1 - chan) * WIDE, WIDE)
    for n in range(sides):
        if sides == 1:
            base = jnp.where(lat == 0, lat_rows - HALO, 0)
        else:
            base = lat_rows - HALO if n == 0 else 0
        for t in range(HALO):
            lat_refs[n][t] = fields_ref[base + t, pl.ds(at, part), :]
            corner_refs[n][t] = lon_ref[base + t]
        corner_refs[n][HALO] = bands_ref[n]


def gelu(x):
    return 0.5 * x * (1.0 + jnp.tanh(0.7978845608028654 * (x + 0.044715 * (x * x * x))))


def layers_kernel(sides, half, cols, own_ref, lon_ref, *rest):
    lat_refs, corner_refs = rest[:sides], rest[sides : 2 * sides]
    tables_ref, weights_ref, keep_ref, send_ref = rest[2 * sides : 2 * sides + 4]
    fields, feats, fields2, turned = rest[2 * sides + 4 :]
    lat_rows, lon_total, chans = own_ref.shape
    basis = weights_ref.shape[1]
    width = chans // 2
    chan = lax.axis_index("chan")
    lat = lax.axis_index("lat")
    blocks1 = lon_total // BLOCK - 1
    blocks2 = half // BLOCK
    groups = lat_rows // GROUP
    part = half + WIDE
    count1 = cols - half + WIDE
    whole1 = count1 // BLOCK * BLOCK

    if sides == 1:
        top = lat > 0
        halo_base = [jnp.where(top, 0, lat_rows + HALO)]
        empty_base = [jnp.where(top, lat_rows + HALO, 0)]
        win_base = [jnp.where(top, 0, lat_rows + HALO - SPAN)]
        out_base = [jnp.where(top, 0, lat_rows + SPAN)]
        empty_out = [jnp.where(top, lat_rows + SPAN, 0)]
    else:
        halo_base = [0, lat_rows + HALO]
        win_base = [0, lat_rows + HALO - SPAN]
        out_base = [0, lat_rows + SPAN]
        empty_base, empty_out = [], []

    for base in empty_base:
        for t in range(HALO):
            fields[base + t] = jnp.zeros((lon_total, chans), BF16)
    fields[HALO : HALO + lat_rows] = own_ref[...]
    halo_at = pl.multiple_of((1 - chan) * WIDE, WIDE)
    for n in range(sides):
        for t in range(HALO):
            fields[halo_base[n] + t, pl.ds(halo_at, part), :] = lat_refs[n][t]

    @pl.when(chan == 0)
    def _():
        for r in range(lat_rows):
            fields[HALO + r, 0:WIDE, :] = lon_ref[r]
        for n in range(sides):
            for t in range(HALO):
                fields[halo_base[n] + t, 0:WIDE, :] = corner_refs[n][t]

    @pl.when(chan == 1)
    def _():
        def tail(dest, side):
            before = fields[dest, whole1 : whole1 + BLOCK, :].astype(F32)[0 : count1 - whole1, :]
            empty = jnp.zeros((lon_total - count1 - WIDE, chans), F32)
            fields[dest, whole1:lon_total, :] = jnp.concatenate(
                [before, side.astype(F32), empty], axis=0
            ).astype(BF16)

        for r in range(lat_rows):
            tail(HALO + r, lon_ref[r])
        for n in range(sides):
            for t in range(HALO):
                tail(halo_base[n] + t, corner_refs[n][t])

    halo_tables = [
        toeplitz(corner_refs[n][HALO].astype(F32)[0 : SPAN * basis, :]) for n in range(sides)
    ]

    def conv(source, table, base, in_rows, first, out_rows, at):
        taken = source[pl.ds(base, in_rows), at : at + WINDOW, :]
        taken = taken.reshape(in_rows * WINDOW, chans)
        result = jnp.dot(table, taken, preferred_element_type=F32).astype(BF16)
        for m in range(out_rows):
            for k in range(basis):
                begin = (m * basis + k) * BLOCK
                feats[first + m, at : at + BLOCK, k * chans : (k + 1) * chans] = result[
                    begin : begin + BLOCK, :
                ]

    for jb in range(blocks1):
        at = jb * BLOCK
        for g in range(groups):
            base = HALO - SPAN + g * GROUP
            conv(fields, tables_ref[g], base, GROUP + 2 * SPAN, g * GROUP, GROUP, at)
        for n in range(sides):
            rows = 3 * SPAN
            table = halo_tables[n][:, : rows * WINDOW]
            conv(fields, table, win_base[n], rows, lat_rows + n * SPAN, SPAN, at)

    for base in empty_out:
        for t in range(SPAN):
            fields2[base + t] = jnp.zeros(fields2.shape[1:], BF16)
    shift = BLOCK // 2
    lon1 = blocks1 * BLOCK

    def mix(layer, rows, lons, source, first):
        taken = feats[rows, 0:lons, :]
        mixed = jnp.dot(
            taken,
            weights_ref[layer].reshape(basis * chans, chans),
            preferred_element_type=F32,
        )
        before = source[first].astype(F32)[shift : shift + lons, :]
        return before + gelu(mixed)

    for i in range(lat_rows):
        fields2[SPAN + i] = mix(0, i, lon1, fields, HALO + i).astype(BF16)
    for n in range(sides):
        for m in range(SPAN):
            dest = out_base[n] + m
            row = lat_rows + n * SPAN + m
            fields2[dest] = mix(0, row, lon1, fields, dest + SPAN).astype(BF16)

    for jb in range(blocks2):
        for g in range(groups):
            base = g * GROUP
            conv(fields2, tables_ref[g], base, GROUP + 2 * SPAN, base, GROUP, jb * BLOCK)
    for i in range(lat_rows):
        done = mix(1, i, half, fields2, SPAN + i)
        for c in range(2):
            turned[c, pl.ds(i, half, stride=lat_rows), :] = done[:, c * width : (c + 1) * width]
    keep_ref[...] = turned[chan].reshape(half, lat_rows, width).astype(BF16)
    send_ref[...] = turned[1 - chan].reshape(half, lat_rows, width).astype(BF16)


def join_kernel(keep_ref, got_ref, out_ref):
    half = keep_ref.shape[0]
    rest = out_ref.shape[0] - half
    chan = lax.axis_index("chan")

    @pl.when(chan == 0)
    def _():
        out_ref[0:half] = keep_ref[...]
        out_ref[half:] = got_ref[0:rest]

    @pl.when(chan == 1)
    def _():
        out_ref[0:half] = got_ref[...]
        out_ref[half:] = keep_ref[0:rest]


def per_device(state, sup_rows, sup_count, lon_reach, psi, weights):
    lat_rows, cols, width = state.shape
    basis = psi.shape[2]
    chans = weights.shape[2]
    lats, lons = lax.axis_size("lat"), lax.axis_size("lon")
    sides = 1 if lats == 2 else 2
    groups = lat_rows // GROUP
    lanes = (GROUP + 2 * SPAN) * WINDOW
    half = -(-cols // (2 * BLOCK)) * BLOCK
    part = half + WIDE
    lon_total = half + 2 * WIDE
    swap = [(0, 1), (1, 0)]
    params = pltpu.CompilerParams(vmem_limit_bytes=VMEM_LIMIT)

    def shape(*dims):
        return jax.ShapeDtypeStruct(dims, BF16)

    def to_lat(step):
        if lats == 2:
            return [(a, 1 - a) for a in range(lats)]
        return [(a, a + step) for a in range(lats) if 0 <= a + step < lats]

    forth = [((z, 1), ((z + 1) % lons, 0)) for z in range(lons)]
    back = [((z, 0), ((z - 1) % lons, 1)) for z in range(lons)]
    to_lon = forth + back

    own = jnp.transpose(state, (1, 0, 2))
    other = lax.ppermute(own, "chan", swap)

    tables, bands = pl.pallas_call(
        functools.partial(prep_kernel, sides),
        out_shape=[
            shape(groups, GROUP * basis * BLOCK, lanes),
            shape(sides, GROUP * basis, lanes),
        ],
        in_specs=[smem(), smem(), smem(), vmem()],
        out_specs=[vmem()] * 2,
        scratch_shapes=[
            pltpu.VMEM((lat_rows, 2 * SPAN + 1, basis, lanes), F32),
            pltpu.VMEM((GROUP * basis, lanes), F32),
        ],
        compiler_params=params,
        name="prep",
    )(sup_rows, sup_count, lon_reach, psi)

    fields, lon_edge, *sends = pl.pallas_call(
        functools.partial(edges_kernel, sides, half),
        out_shape=[shape(lat_rows, lon_total, chans), shape(lat_rows, WIDE, chans)]
        + [shape(HALO, part, chans)] * sides
        + [shape(HALO + 1, WIDE, chans)] * sides,
        in_specs=[vmem()] * 3,
        out_specs=[vmem()] * (2 + 2 * sides),
        scratch_shapes=[pltpu.VMEM((2, part * lat_rows, width), F32)],
        compiler_params=params,
        name="edges",
    )(own, other, bands)

    steps = [1, -1][:sides]
    lat_halos = [lax.ppermute(sends[n], "lat", to_lat(steps[n])) for n in range(sides)]
    lon_halo = lax.ppermute(
        lon_edge, ("lon", "chan"), [(z * 2 + c, y * 2 + d) for (z, c), (y, d) in to_lon]
    )
    corners = [
        lax.ppermute(
            sends[sides + n],
            ("lon", "lat", "chan"),
            [
                ((z * lats + a) * 2 + c, (y * lats + b) * 2 + d)
                for a, b in to_lat(steps[n])
                for (z, c), (y, d) in to_lon
            ],
        )
        for n in range(sides)
    ]

    keep, send = pl.pallas_call(
        functools.partial(layers_kernel, sides, half, cols),
        out_shape=[shape(half, lat_rows, width)] * 2,
        in_specs=[vmem()] * (4 + 2 * sides),
        out_specs=[vmem()] * 2,
        scratch_shapes=[
            pltpu.VMEM((lat_rows + 2 * HALO, lon_total, chans), BF16),
            pltpu.VMEM((lat_rows + sides * SPAN, lon_total - BLOCK, basis * chans), BF16),
            pltpu.VMEM((lat_rows + 2 * SPAN, lon_total - BLOCK, chans), BF16),
            pltpu.VMEM((2, half * lat_rows, width), F32),
        ],
        compiler_params=params,
        name="layers",
    )(fields, lon_halo, *lat_halos, *corners, tables, weights)

    got = lax.ppermute(send, "chan", swap)
    out = pl.pallas_call(
        join_kernel,
        out_shape=shape(cols, lat_rows, width),
        in_specs=[vmem()] * 2,
        out_specs=vmem(),
        compiler_params=params,
        name="join",
    )(keep, got)
    return jnp.transpose(out, (1, 0, 2))


def solution(mesh):
    return jax.shard_map(
        per_device,
        mesh=mesh,
        in_specs=(
            P(("groups", "lat"), "lon", "chan"),
            P("lat", None),
            P("lat"),
            P("lat"),
            P("lat", None, None, None),
            P(),
        ),
        out_specs=P(("groups", "lat"), "lon", "chan"),
        check_vma=False,
    )
```

```python
import functools

import jax
import jax.numpy as jnp
from jax import lax
from jax.experimental import pallas as pl
from jax.experimental.pallas import tpu as pltpu
from jax.sharding import PartitionSpec as P

LAYERS = 2
SPAN = 2
HALO = LAYERS * SPAN
BLOCK = 16
WINDOW = 2 * BLOCK
GROUP = 4
PAIR = 2
WIDE = BLOCK
SHIFT = BLOCK // 2
VMEM_LIMIT = 48 * 1024 * 1024
BF16 = jnp.bfloat16
F32 = jnp.float32


def vmem():
    return pl.BlockSpec(memory_space=pltpu.VMEM)


def hbm():
    return pl.BlockSpec(memory_space=pltpu.HBM)


def toeplitz(rows_tab):
    count, _ = rows_tab.shape
    moved = jnp.concatenate(
        [rows_tab if jj == 0 else pltpu.roll(rows_tab, jj, 1) for jj in range(BLOCK)], axis=0
    ).astype(BF16)
    total = count * BLOCK
    out_row = lax.broadcasted_iota(jnp.int32, (total, total), 0)
    in_row = lax.broadcasted_iota(jnp.int32, (total, total), 1)
    source = (out_row % BLOCK) * count + out_row // BLOCK
    order = (in_row == source).astype(F32).astype(BF16)
    return jnp.dot(order, moved, preferred_element_type=F32).astype(BF16)


def turn(ref, wide_scr, start, count, total):
    _, lat_rows, width = ref.shape
    wide_scr[0 : count * lat_rows, :] = (
        ref[start : start + count].astype(F32).reshape(count * lat_rows, width)
    )
    if count < total:
        wide_scr[count * lat_rows : total * lat_rows, :] = jnp.zeros(
            ((total - count) * lat_rows, width), F32
        )


def core_part(core, cols, half):
    start = 0 if core == 0 else half - WIDE
    return start, min(cols - start, half + WIDE)


def prep_kernel(
    sides,
    half,
    state_hbm,
    sup_hbm,
    count_hbm,
    reach_hbm,
    psi_hbm,
    part_ref,
    edge_ref,
    rows_ref,
    bands_ref,
    state_ref,
    sup_ref,
    count_ref,
    reach_ref,
    psi_ref,
    slots,
    pairs_scr,
    wide_scr,
    sems,
):
    copies = [
        pltpu.make_async_copy(source, dest, sems.at[n])
        for n, (source, dest) in enumerate(
            [
                (psi_hbm, psi_ref),
                (sup_hbm, sup_ref),
                (count_hbm, count_ref),
                (reach_hbm, reach_ref),
                (state_hbm, state_ref),
            ]
        )
    ]
    for copy in copies:
        copy.start()
    cols, lat_rows, width = state_ref.shape
    _, sup, basis, offsets = psi_ref.shape
    reach_max = offsets // 2
    lanes = rows_ref.shape[2]
    part = part_ref.shape[1]
    lat = lax.axis_index("lat")
    chan = lax.axis_index("chan")
    slots[...] = jnp.zeros_like(slots)
    for copy in copies[:4]:
        copy.wait()
    for i in range(lat_rows):
        for s in range(sup):
            rel = jnp.clip(sup_ref[i, s] - (lat * lat_rows + i) + SPAN, 0, 2 * SPAN)
            live = jnp.where(s < count_ref[i], 1.0, 0.0)
            slots[i, rel, :, 0:offsets] += psi_ref[i, s] * live
    lane = lax.broadcasted_iota(jnp.int32, (basis, lanes), 1)
    off = lane % WINDOW - reach_max
    for i in range(lat_rows):
        band = slots[i, 0]
        for rel in range(1, 2 * SPAN + 1):
            band = band + pltpu.roll(slots[i, rel], rel * WINDOW, 1)
        band = jnp.where(jnp.abs(off) <= reach_ref[i], band, 0.0)
        m = i % PAIR
        pairs_scr[i // PAIR, m * basis : (m + 1) * basis, :] = (
            band if m == 0 else pltpu.roll(band, m * WINDOW, 1)
        )
    pairs = lat_rows // PAIR

    def group(g):
        first, second = pairs_scr[2 * g], pairs_scr[2 * g + 1]
        return jnp.concatenate([first, pltpu.roll(second, PAIR * WINDOW, 1)], axis=0)

    if sides == 1:
        rows_ref[0] = group(lat).astype(BF16)
        rows_ref[1] = group(1 - lat).astype(BF16)
        mid, near = pairs_scr[2 - lat], pairs_scr[(pairs - 1) * (1 - lat)]
        rows_ref[2] = jnp.concatenate([mid, near], axis=0).astype(BF16)
        edge_pairs = [near]
    else:
        for g in range(lat_rows // GROUP):
            rows_ref[g] = group(g).astype(BF16)
        edge_pairs = [pairs_scr[pairs - 1], pairs_scr[0]]
    for n in range(sides):
        bands_ref[n] = jnp.concatenate(
            [edge_pairs[n], jnp.zeros_like(edge_pairs[n])], axis=0
        ).astype(BF16)

    copies[4].wait()

    def build(core):
        start, count = core_part(core, cols, half)
        edge = 0 if core == 0 else count - WIDE
        turn(state_ref, wide_scr, start, count, part)
        for r in range(lat_rows):
            part_ref[r] = wide_scr[pl.ds(r, part, stride=lat_rows), :].astype(BF16)
            edge_ref[r] = wide_scr[pl.ds(edge * lat_rows + r, WIDE, stride=lat_rows), :].astype(
                BF16
            )

    @pl.when(chan == 0)
    def _():
        build(0)

    @pl.when(chan == 1)
    def _():
        build(1)


def edges_kernel(
    sides, half, part_ref, edge_ref, other_ref, bands_ref, fields_ref, lon_ref, *rest
):
    lat_refs, corner_refs, (wide_scr,) = rest[:sides], rest[sides : 2 * sides], rest[2 * sides :]
    cols, lat_rows, width = other_ref.shape
    lon_total = fields_ref.shape[1]
    part = part_ref.shape[1]
    chan = lax.axis_index("chan")
    lat = lax.axis_index("lat")

    def build(core):
        start, count = core_part(core, cols, half)
        edge = 0 if core == 0 else count - WIDE
        at = WIDE if core == 0 else 0
        own = slice(core * width, (core + 1) * width)
        lane = slice((1 - core) * width, (2 - core) * width)
        turn(other_ref, wide_scr, start, count, part)
        for r in range(lat_rows):
            fields_ref[r, at : at + part, own] = part_ref[r]
            lon_ref[r, :, own] = edge_ref[r]
            fields_ref[r, at : at + part, lane] = wide_scr[
                pl.ds(r, part, stride=lat_rows), :
            ].astype(BF16)
            lon_ref[r, :, lane] = wide_scr[
                pl.ds(edge * lat_rows + r, WIDE, stride=lat_rows), :
            ].astype(BF16)
        empty = slice(0, WIDE) if core == 0 else slice(part, lon_total)
        fields_ref[:, empty, :] = jnp.zeros((lat_rows, WIDE, 2 * width), BF16)

    @pl.when(chan == 0)
    def _():
        build(0)

    @pl.when(chan == 1)
    def _():
        build(1)

    at = pl.multiple_of((1 - chan) * WIDE, WIDE)
    for n in range(sides):
        if sides == 1:
            base = jnp.where(lat == 0, lat_rows - HALO, 0)
        else:
            base = lat_rows - HALO if n == 0 else 0
        for t in range(HALO):
            lat_refs[n][t] = fields_ref[base + t, pl.ds(at, part), :]
            corner_refs[n][t] = lon_ref[base + t]
        corner_refs[n][HALO] = bands_ref[n]


def tables_kernel(rows_ref, tables_ref):
    for g in range(rows_ref.shape[0]):
        tables_ref[g] = toeplitz(rows_ref[g].astype(F32))


def gelu(x):
    return 0.5 * x * (1.0 + jnp.tanh(0.7978845608028654 * (x + 0.044715 * (x * x * x))))


def add_lon_halo(cols, half, rows, halos):
    chan = lax.axis_index("chan")
    _, count = core_part(1, cols, half)
    whole = count // BLOCK * BLOCK

    @pl.when(chan == 0)
    def _():
        for row, halo in zip(rows, halos):
            row[0:WIDE, :] = halo[...]

    @pl.when(chan == 1)
    def _():
        for row, halo in zip(rows, halos):
            lon_total, chans = row.shape
            before = row[whole : whole + BLOCK, :].astype(F32)[0 : count - whole, :]
            empty = jnp.zeros((lon_total - count - WIDE, chans), F32)
            row[whole:lon_total, :] = jnp.concatenate(
                [before, halo[...].astype(F32), empty], axis=0
            ).astype(BF16)


def conv(source, table, base, in_rows, feats, first, out_rows, at):
    chans = source.shape[2]
    basis = table.shape[0] // (out_rows * BLOCK)
    taken = source[pl.ds(base, in_rows), at : at + WINDOW, :]
    taken = taken.reshape(in_rows * WINDOW, chans)
    result = jnp.dot(table, taken, preferred_element_type=F32).astype(BF16)
    for m in range(out_rows):
        for k in range(basis):
            begin = (m * basis + k) * BLOCK
            feats[first + m, at : at + BLOCK, k * chans : (k + 1) * chans] = result[
                begin : begin + BLOCK, :
            ]


def mix(weights_ref, layer, feats, row, lons, before):
    _, basis, chans, _ = weights_ref.shape
    mixed = jnp.dot(
        feats[row, 0:lons, :],
        weights_ref[layer].reshape(basis * chans, chans),
        preferred_element_type=F32,
    )
    return before[...].astype(F32)[SHIFT : SHIFT + lons, :] + gelu(mixed)


def place(turned, done, row, lat_rows):
    half, chans = done.shape
    width = chans // 2
    for c in range(2):
        turned[c, pl.ds(row, half, stride=lat_rows), :] = done[:, c * width : (c + 1) * width]


def hand_out(turned, keep_ref, send_ref):
    chan = lax.axis_index("chan")
    keep_ref[...] = turned[chan].reshape(keep_ref.shape).astype(BF16)
    send_ref[...] = turned[1 - chan].reshape(send_ref.shape).astype(BF16)


def far_kernel(
    half,
    cols,
    own_ref,
    lon_ref,
    tables_ref,
    weights_hbm,
    ext_ref,
    next_ref,
    weights_ref,
    keep_ref,
    send_ref,
    fields,
    feats,
    turned,
    sem,
):
    fetch = pltpu.make_async_copy(weights_hbm, weights_ref, sem)
    fetch.start()
    lat_rows, lon_total, chans = own_ref.shape
    lat = lax.axis_index("lat")
    lon1 = lon_total - BLOCK
    turned[...] = jnp.zeros_like(turned)

    for t in range(SPAN):
        fields[t] = jnp.zeros((lon_total, chans), BF16)
        fields[SPAN + lat_rows + t] = jnp.zeros((lon_total, chans), BF16)
    fields[SPAN : SPAN + lat_rows] = own_ref[...]
    add_lon_halo(
        cols,
        half,
        [fields.at[SPAN + r] for r in range(lat_rows)],
        [lon_ref.at[r] for r in range(lat_rows)],
    )
    ext_ref[...] = fields[SPAN : SPAN + lat_rows]

    far = GROUP * lat
    mid = GROUP - PAIR * lat
    rows6 = PAIR + 2 * SPAN
    for jb in range(lon1 // BLOCK):
        at = jb * BLOCK
        conv(fields, tables_ref[0], far, GROUP + 2 * SPAN, feats, 0, GROUP, at)
        table = tables_ref[2, 0 : tables_ref.shape[1] // 2, 0 : rows6 * WINDOW]
        conv(fields, table, mid, rows6, feats, GROUP, PAIR, at)
    fetch.wait()
    for t in range(SPAN):
        next_ref[(GROUP + SPAN) * lat + t] = jnp.zeros((lon1, chans), BF16)
    for t in range(GROUP):
        next_ref[SPAN + t] = mix(
            weights_ref, 0, feats, t, lon1, fields.at[SPAN + far + t]
        ).astype(BF16)
    for t in range(PAIR):
        next_ref[(GROUP + SPAN) * (1 - lat) + t] = mix(
            weights_ref, 0, feats, GROUP + t, lon1, fields.at[SPAN + mid + t]
        ).astype(BF16)
    for jb in range(half // BLOCK):
        conv(next_ref, tables_ref[0], 0, GROUP + 2 * SPAN, feats, 0, GROUP, jb * BLOCK)
    for t in range(GROUP):
        done = mix(weights_ref, 1, feats, t, half, next_ref.at[SPAN + t])
        place(turned, done, far + t, lat_rows)
    hand_out(turned, keep_ref, send_ref)


def near_kernel(
    half,
    cols,
    ext_ref,
    next_ref,
    lat_ref,
    corner_ref,
    tables_ref,
    weights_ref,
    keep_ref,
    send_ref,
    fields,
    near,
    feats,
    turned,
):
    lat_rows, lon_total, chans = ext_ref.shape
    basis = weights_ref.shape[1]
    part = lat_ref.shape[1]
    lat = lax.axis_index("lat")
    chan = lax.axis_index("chan")
    lon1 = lon_total - BLOCK
    rows6 = PAIR + 2 * SPAN
    turned[...] = jnp.zeros_like(turned)

    halo = HALO * (1 - lat)
    own = HALO * lat
    at = pl.multiple_of((1 - chan) * WIDE, WIDE)
    for t in range(HALO):
        fields[own + t] = ext_ref[HALO * (1 - lat) + t]
        fields[halo + t] = jnp.zeros((lon_total, chans), BF16)
        fields[halo + t, pl.ds(at, part), :] = lat_ref[t]
    add_lon_halo(
        cols,
        half,
        [fields.at[halo + t] for t in range(HALO)],
        [corner_ref.at[t] for t in range(HALO)],
    )
    halo_table = toeplitz(corner_ref[HALO].astype(F32)[0 : PAIR * basis, :])
    last_table = tables_ref[2, tables_ref.shape[1] // 2 :, 0 : rows6 * WINDOW]
    last = SPAN * lat
    beyond = SPAN * (1 - lat)
    for jb in range(lon1 // BLOCK):
        conv(fields, last_table, last, rows6, feats, 0, PAIR, jb * BLOCK)
        table = halo_table[:, 0 : rows6 * WINDOW]
        conv(fields, table, beyond, rows6, feats, PAIR, PAIR, jb * BLOCK)
    for t in range(GROUP):
        near[GROUP * lat + t] = next_ref[GROUP * (1 - lat) + t]
    for t in range(PAIR):
        near[GROUP * (1 - lat) + SPAN * lat + t] = mix(
            weights_ref, 0, feats, t, lon1, fields.at[SPAN + last + t]
        ).astype(BF16)
        near[(GROUP + SPAN) * (1 - lat) + t] = mix(
            weights_ref, 0, feats, PAIR + t, lon1, fields.at[SPAN + beyond + t]
        ).astype(BF16)
    for jb in range(half // BLOCK):
        conv(near, tables_ref[1], 0, GROUP + 2 * SPAN, feats, 0, GROUP, jb * BLOCK)
    for t in range(GROUP):
        done = mix(weights_ref, 1, feats, t, half, near.at[SPAN + t])
        place(turned, done, GROUP * (1 - lat) + t, lat_rows)
    hand_out(turned, keep_ref, send_ref)


def all_kernel(half, cols, own_ref, lon_ref, *rest):
    lat_refs, corner_refs = rest[:2], rest[2:4]
    tables_ref, weights_ref, keep_ref, send_ref, fields, feats, after, turned = rest[4:]
    lat_rows, lon_total, chans = own_ref.shape
    basis = weights_ref.shape[1]
    part = half + WIDE
    chan = lax.axis_index("chan")
    groups = lat_rows // GROUP
    lon1 = lon_total - BLOCK
    halo_base = [0, lat_rows + HALO]
    win_base = [0, lat_rows + HALO - SPAN]
    out_base = [0, lat_rows + SPAN]
    rows6 = PAIR + 2 * SPAN

    fields[HALO : HALO + lat_rows] = own_ref[...]
    at = pl.multiple_of((1 - chan) * WIDE, WIDE)
    rows = [fields.at[HALO + r] for r in range(lat_rows)]
    halos = [lon_ref.at[r] for r in range(lat_rows)]
    for n in range(2):
        for t in range(HALO):
            fields[halo_base[n] + t] = jnp.zeros((lon_total, chans), BF16)
            fields[halo_base[n] + t, pl.ds(at, part), :] = lat_refs[n][t]
            rows.append(fields.at[halo_base[n] + t])
            halos.append(corner_refs[n].at[t])
    add_lon_halo(cols, half, rows, halos)
    halo_tables = [
        toeplitz(corner_refs[n][HALO].astype(F32)[0 : PAIR * basis, :])[:, 0 : rows6 * WINDOW]
        for n in range(2)
    ]
    for jb in range(lon1 // BLOCK):
        at = jb * BLOCK
        for g in range(groups):
            base = HALO - SPAN + g * GROUP
            conv(
                fields, tables_ref[g], base, GROUP + 2 * SPAN, feats, g * GROUP, GROUP, at
            )
        for n in range(2):
            first = lat_rows + n * PAIR
            conv(fields, halo_tables[n], win_base[n], rows6, feats, first, PAIR, at)
    for i in range(lat_rows):
        after[SPAN + i] = mix(weights_ref, 0, feats, i, lon1, fields.at[HALO + i]).astype(BF16)
    for n in range(2):
        for m in range(PAIR):
            dest = out_base[n] + m
            after[dest] = mix(
                weights_ref, 0, feats, lat_rows + n * PAIR + m, lon1, fields.at[dest + SPAN]
            ).astype(BF16)
    for jb in range(half // BLOCK):
        for g in range(groups):
            base = g * GROUP
            conv(
                after, tables_ref[g], base, GROUP + 2 * SPAN, feats, base, GROUP, jb * BLOCK
            )
    for i in range(lat_rows):
        done = mix(weights_ref, 1, feats, i, half, after.at[SPAN + i])
        place(turned, done, i, lat_rows)
    hand_out(turned, keep_ref, send_ref)


def join_kernel(pieces, *refs):
    keep_refs, got_refs, (out_ref,) = refs[:pieces], refs[pieces : 2 * pieces], refs[2 * pieces :]
    half = keep_refs[0].shape[0]
    rest = out_ref.shape[0] - half
    chan = lax.axis_index("chan")

    def total(parts, count):
        value = parts[0][0:count].astype(F32)
        for other in parts[1:]:
            value = value + other[0:count].astype(F32)
        return value.astype(BF16)

    @pl.when(chan == 0)
    def _():
        out_ref[0:half] = total(keep_refs, half)
        out_ref[half:] = total(got_refs, rest)

    @pl.when(chan == 1)
    def _():
        out_ref[0:half] = total(got_refs, half)
        out_ref[half:] = total(keep_refs, rest)


def per_device(state, sup_rows, sup_count, lon_reach, psi, weights):
    lat_rows, cols, width = state.shape
    _, sup, basis, _ = psi.shape
    chans = weights.shape[2]
    lats, lons = lax.axis_size("lat"), lax.axis_size("lon")
    sides = 1 if lats == 2 else 2
    groups = lat_rows // GROUP
    lanes = (GROUP + 2 * SPAN) * WINDOW
    half = -(-cols // (2 * BLOCK)) * BLOCK
    part = half + WIDE
    lon_total = half + 2 * WIDE
    lon1 = lon_total - BLOCK
    tabs = groups + 1 if sides == 1 else groups
    swap = [(0, 1), (1, 0)]
    params = pltpu.CompilerParams(vmem_limit_bytes=VMEM_LIMIT)

    def shape(*dims):
        return jax.ShapeDtypeStruct(dims, BF16)

    def to_lat(step):
        if lats == 2:
            return [(a, 1 - a) for a in range(lats)]
        return [(a, a + step) for a in range(lats) if 0 <= a + step < lats]

    forth = [((z, 1), ((z + 1) % lons, 0)) for z in range(lons)]
    back = [((z, 0), ((z - 1) % lons, 1)) for z in range(lons)]
    to_lon = forth + back

    own = jnp.transpose(state, (1, 0, 2))
    other = lax.ppermute(own, "chan", swap)

    part_own, edge_own, rows, bands = pl.pallas_call(
        functools.partial(prep_kernel, sides, half),
        out_shape=[
            shape(lat_rows, part, width),
            shape(lat_rows, WIDE, width),
            shape(tabs, GROUP * basis, lanes),
            shape(sides, GROUP * basis, lanes),
        ],
        in_specs=[hbm()] * 5,
        out_specs=[vmem()] * 4,
        scratch_shapes=[
            pltpu.VMEM((cols, lat_rows, width), BF16),
            pltpu.SMEM((lat_rows, sup), jnp.int32),
            pltpu.SMEM((lat_rows,), jnp.int32),
            pltpu.SMEM((lat_rows,), jnp.int32),
            pltpu.VMEM(psi.shape, F32),
            pltpu.VMEM((lat_rows, 2 * SPAN + 1, basis, lanes), F32),
            pltpu.VMEM((lat_rows // PAIR, PAIR * basis, lanes), F32),
            pltpu.VMEM((part * lat_rows, width), F32),
            pltpu.SemaphoreType.DMA((5,)),
        ],
        compiler_params=params,
        name="prep",
    )(own, sup_rows, sup_count, lon_reach, psi)

    fields, lon_edge, *sends = pl.pallas_call(
        functools.partial(edges_kernel, sides, half),
        out_shape=[shape(lat_rows, lon_total, chans), shape(lat_rows, WIDE, chans)]
        + [shape(HALO, part, chans)] * sides
        + [shape(HALO + 1, WIDE, chans)] * sides,
        in_specs=[vmem()] * 4,
        out_specs=[vmem()] * (2 + 2 * sides),
        scratch_shapes=[pltpu.VMEM((part * lat_rows, width), F32)],
        compiler_params=params,
        name="edges",
    )(part_own, edge_own, other, bands)

    steps = [1, -1][:sides]
    corners = [
        lax.ppermute(
            sends[sides + n],
            ("lon", "lat", "chan"),
            [
                ((z * lats + a) * 2 + c, (y * lats + b) * 2 + d)
                for a, b in to_lat(steps[n])
                for (z, c), (y, d) in to_lon
            ],
        )
        for n in range(sides)
    ]
    lon_halo = lax.ppermute(
        lon_edge, ("lon", "chan"), [(z * 2 + c, y * 2 + d) for (z, c), (y, d) in to_lon]
    )
    lat_halos = [lax.ppermute(sends[n], "lat", to_lat(steps[n])) for n in range(sides)]

    tables = pl.pallas_call(
        tables_kernel,
        out_shape=shape(tabs, GROUP * basis * BLOCK, lanes),
        in_specs=[vmem()],
        out_specs=vmem(),
        compiler_params=params,
        name="tables",
    )(rows)

    def cost(conv_rows, mix_rows):
        flops = 2 * lon1 * chans * basis * (conv_rows * lanes + mix_rows * chans)
        return pl.CostEstimate(flops=flops, bytes_accessed=weights.size * 2, transcendentals=0)

    piece = shape(half, lat_rows, width)
    turned = pltpu.VMEM((2, half * lat_rows, width), F32)
    if sides == 1:
        ext, after, weights_in, keep, send = pl.pallas_call(
            functools.partial(far_kernel, half, cols),
            out_shape=[
                shape(lat_rows, lon_total, chans),
                shape(lat_rows, lon1, chans),
                shape(*weights.shape),
                piece,
                piece,
            ],
            in_specs=[vmem()] * 3 + [hbm()],
            out_specs=[vmem()] * 5,
            scratch_shapes=[
                pltpu.VMEM((lat_rows + 2 * SPAN, lon_total, chans), BF16),
                pltpu.VMEM((GROUP + PAIR, lon1, basis * chans), BF16),
                turned,
                pltpu.SemaphoreType.DMA,
            ],
            compiler_params=params,
            cost_estimate=cost(10, 10),
            name="far_rows",
        )(fields, lon_halo, tables, weights)
        keeps, gots = [keep], [lax.ppermute(send, "chan", swap)]
        keep, send = pl.pallas_call(
            functools.partial(near_kernel, half, cols),
            out_shape=[piece] * 2,
            in_specs=[vmem()] * 6,
            out_specs=[vmem()] * 2,
            scratch_shapes=[
                pltpu.VMEM((2 * HALO, lon_total, chans), BF16),
                pltpu.VMEM((GROUP + 2 * SPAN, lon1, chans), BF16),
                pltpu.VMEM((GROUP, lon1, basis * chans), BF16),
                turned,
            ],
            compiler_params=params,
            cost_estimate=cost(8, 8),
            name="near_rows",
        )(ext, after, lat_halos[0], corners[0], tables, weights_in)
    else:
        keeps, gots = [], []
        keep, send = pl.pallas_call(
            functools.partial(all_kernel, half, cols),
            out_shape=[piece] * 2,
            in_specs=[vmem()] * (4 + 2 * sides),
            out_specs=[vmem()] * 2,
            scratch_shapes=[
                pltpu.VMEM((lat_rows + 2 * HALO, lon_total, chans), BF16),
                pltpu.VMEM((lat_rows + 2 * PAIR, lon1, basis * chans), BF16),
                pltpu.VMEM((lat_rows + 2 * SPAN, lon1, chans), BF16),
                turned,
            ],
            compiler_params=params,
            cost_estimate=cost(20, 20),
            name="all_rows",
        )(fields, lon_halo, *lat_halos, *corners, tables, weights)
    keeps.append(keep)
    gots.append(lax.ppermute(send, "chan", swap))

    out = pl.pallas_call(
        functools.partial(join_kernel, len(keeps)),
        out_shape=shape(cols, lat_rows, width),
        in_specs=[vmem()] * (2 * len(keeps)),
        out_specs=vmem(),
        compiler_params=params,
        name="join",
    )(*keeps, *gots)
    return jnp.transpose(out, (1, 0, 2))


def solution(mesh):
    return jax.shard_map(
        per_device,
        mesh=mesh,
        in_specs=(
            P(("groups", "lat"), "lon", "chan"),
            P("lat", None),
            P("lat"),
            P("lat"),
            P("lat", None, None, None),
            P(),
        ),
        out_specs=P(("groups", "lat"), "lon", "chan"),
        check_vma=False,
    )
```

```python
import functools

import jax
import jax.numpy as jnp
from jax import lax
from jax.experimental import pallas as pl
from jax.experimental.pallas import tpu as pltpu
from jax.sharding import PartitionSpec as P

LAYERS = 2
SPAN = 2
HALO = LAYERS * SPAN
BLOCK = 16
WINDOW = 2 * BLOCK
GROUP = 4
PAIR = 2
WIDE = BLOCK
SHIFT = BLOCK // 2
VMEM_LIMIT = 48 * 1024 * 1024
BF16 = jnp.bfloat16
F32 = jnp.float32


def vmem():
    return pl.BlockSpec(memory_space=pltpu.VMEM)


def hbm():
    return pl.BlockSpec(memory_space=pltpu.HBM)


def in_hbm(x):
    return pltpu.with_memory_space_constraint(x, pltpu.HBM)


def toeplitz(rows_tab):
    count, _ = rows_tab.shape
    moved = jnp.concatenate(
        [rows_tab if jj == 0 else pltpu.roll(rows_tab, jj, 1) for jj in range(BLOCK)], axis=0
    ).astype(BF16)
    total = count * BLOCK
    out_row = lax.broadcasted_iota(jnp.int32, (total, total), 0)
    in_row = lax.broadcasted_iota(jnp.int32, (total, total), 1)
    source = (out_row % BLOCK) * count + out_row // BLOCK
    order = (in_row == source).astype(F32).astype(BF16)
    return jnp.dot(order, moved, preferred_element_type=F32).astype(BF16)


def own_kernel(sides, half, state_hbm, part_ref, edge_ref, *rest):
    lat_refs, (state_ref, wide_scr, sem) = rest[:sides], rest[sides:]
    fetch = pltpu.make_async_copy(state_hbm, state_ref, sem)
    fetch.start()
    cols, lat_rows, width = state_ref.shape
    part = part_ref.shape[1]
    lat = lax.axis_index("lat")
    chan = lax.axis_index("chan")
    padded = wide_scr.shape[0] // lat_rows
    wide_scr[cols * lat_rows :, :] = jnp.zeros(((padded - cols) * lat_rows, width), F32)
    fetch.wait()
    wide_scr[0 : cols * lat_rows, :] = state_ref[...].astype(F32).reshape(cols * lat_rows, width)
    for n in range(sides):
        if sides == 1:
            base = jnp.where(lat == 0, lat_rows - HALO, 0)
        else:
            base = lat_rows - HALO if n == 0 else 0
        for t in range(HALO):
            lat_refs[n][t] = wide_scr[pl.ds(base + t, cols, stride=lat_rows), :].astype(BF16)
    start = (half - WIDE) * lat_rows * chan
    edge = (cols - WIDE) * lat_rows * chan
    for r in range(lat_rows):
        part_ref[r] = wide_scr[pl.ds(start + r, part, stride=lat_rows), :].astype(BF16)
        edge_ref[r] = wide_scr[pl.ds(edge + r, WIDE, stride=lat_rows), :].astype(BF16)


def edges_kernel(half, part_ref, edge_ref, other_ref, fields_ref, lon_ref, wide_scr):
    cols, lat_rows, width = other_ref.shape
    lon_total = fields_ref.shape[1]
    part = part_ref.shape[1]
    chan = lax.axis_index("chan")
    padded = wide_scr.shape[0] // lat_rows
    wide_scr[cols * lat_rows :, :] = jnp.zeros(((padded - cols) * lat_rows, width), F32)

    def build(core):
        start = 0 if core == 0 else half - WIDE
        edge = 0 if core == 0 else cols - WIDE
        stop = start + part if core == 0 else cols
        at = WIDE if core == 0 else 0
        own = slice(core * width, (core + 1) * width)
        lane = slice((1 - core) * width, (2 - core) * width)
        wide_scr[start * lat_rows : stop * lat_rows, :] = (
            other_ref[start:stop].astype(F32).reshape((stop - start) * lat_rows, width)
        )
        for r in range(lat_rows):
            lon_ref[r, :, own] = edge_ref[r]
            lon_ref[r, :, lane] = wide_scr[
                pl.ds(edge * lat_rows + r, WIDE, stride=lat_rows), :
            ].astype(BF16)
            fields_ref[r, at : at + part, own] = part_ref[r]
            fields_ref[r, at : at + part, lane] = wide_scr[
                pl.ds(start * lat_rows + r, part, stride=lat_rows), :
            ].astype(BF16)
        empty = slice(0, WIDE) if core == 0 else slice(part, lon_total)
        fields_ref[:, empty, :] = jnp.zeros((lat_rows, WIDE, 2 * width), BF16)

    @pl.when(chan == 0)
    def _():
        build(0)

    @pl.when(chan == 1)
    def _():
        build(1)


def bands_kernel(
    sides, sup_hbm, count_hbm, reach_hbm, psi_hbm, lon_ref, rows_ref, *rest
):
    corner_refs = rest[:sides]
    sup_ref, count_ref, reach_ref, psi_ref, slots, pairs_scr, sems = rest[sides:]
    copies = [
        pltpu.make_async_copy(source, dest, sems.at[n])
        for n, (source, dest) in enumerate(
            [
                (psi_hbm, psi_ref),
                (sup_hbm, sup_ref),
                (count_hbm, count_ref),
                (reach_hbm, reach_ref),
            ]
        )
    ]
    for copy in copies:
        copy.start()
    lat_rows, sup, basis, offsets = psi_ref.shape
    reach_max = offsets // 2
    lanes = rows_ref.shape[2]
    lat = lax.axis_index("lat")
    slots[...] = jnp.zeros_like(slots)
    for n in range(sides):
        if sides == 1:
            base = jnp.where(lat == 0, lat_rows - HALO, 0)
        else:
            base = lat_rows - HALO if n == 0 else 0
        for t in range(HALO):
            corner_refs[n][t] = lon_ref[base + t]
    for copy in copies:
        copy.wait()
    for i in range(lat_rows):
        for s in range(sup):
            rel = jnp.clip(sup_ref[i, s] - (lat * lat_rows + i) + SPAN, 0, 2 * SPAN)
            live = jnp.where(s < count_ref[i], 1.0, 0.0)
            slots[i, rel, :, 0:offsets] += psi_ref[i, s] * live
    lane = lax.broadcasted_iota(jnp.int32, (basis, lanes), 1)
    off = lane % WINDOW - reach_max
    for i in range(lat_rows):
        band = slots[i, 0]
        for rel in range(1, 2 * SPAN + 1):
            band = band + pltpu.roll(slots[i, rel], rel * WINDOW, 1)
        band = jnp.where(jnp.abs(off) <= reach_ref[i], band, 0.0)
        m = i % PAIR
        pairs_scr[i // PAIR, m * basis : (m + 1) * basis, :] = (
            band if m == 0 else pltpu.roll(band, m * WINDOW, 1)
        )
    pairs = lat_rows // PAIR

    def group(g):
        first, second = pairs_scr[2 * g], pairs_scr[2 * g + 1]
        return jnp.concatenate([first, pltpu.roll(second, PAIR * WINDOW, 1)], axis=0)

    if sides == 1:
        rows_ref[0] = group(lat).astype(BF16)
        rows_ref[1] = group(1 - lat).astype(BF16)
        mid, near = pairs_scr[2 - lat], pairs_scr[(pairs - 1) * (1 - lat)]
        rows_ref[2] = jnp.concatenate([mid, near], axis=0).astype(BF16)
        edge_pairs = [near]
    else:
        for g in range(lat_rows // GROUP):
            rows_ref[g] = group(g).astype(BF16)
        edge_pairs = [pairs_scr[pairs - 1], pairs_scr[0]]
    for n in range(sides):
        corner_refs[n][HALO] = jnp.concatenate(
            [edge_pairs[n], jnp.zeros_like(edge_pairs[n])], axis=0
        ).astype(BF16)


def tables_kernel(rows_ref, tables_ref):
    for g in range(rows_ref.shape[0]):
        tables_ref[g] = toeplitz(rows_ref[g].astype(F32))


def gelu(x):
    return 0.5 * x * (1.0 + jnp.tanh(0.7978845608028654 * (x + 0.044715 * (x * x * x))))


def add_lat_halo(cols, half, rows, own_halos, other_halos):
    chan = lax.axis_index("chan")

    def fill(core):
        start = 0 if core == 0 else half - WIDE
        stop = half + WIDE if core == 0 else cols
        at = WIDE if core == 0 else 0
        for row, own, other in zip(rows, own_halos, other_halos):
            width = own.shape[1]
            for c, halo in ((core, own), (1 - core, other)):
                row[at : at + stop - start, c * width : (c + 1) * width] = halo[start:stop, :]

    @pl.when(chan == 0)
    def _():
        fill(0)

    @pl.when(chan == 1)
    def _():
        fill(1)


def add_lon_halo(cols, half, rows, halos):
    chan = lax.axis_index("chan")
    count = cols - half + WIDE
    whole = count // BLOCK * BLOCK

    @pl.when(chan == 0)
    def _():
        for row, halo in zip(rows, halos):
            row[0:WIDE, :] = halo[...]

    @pl.when(chan == 1)
    def _():
        for row, halo in zip(rows, halos):
            lon_total, chans = row.shape
            before = row[whole : whole + BLOCK, :].astype(F32)[0 : count - whole, :]
            empty = jnp.zeros((lon_total - count - WIDE, chans), F32)
            row[whole:lon_total, :] = jnp.concatenate(
                [before, halo[...].astype(F32), empty], axis=0
            ).astype(BF16)


def conv(source, table, base, in_rows, feats, first, out_rows, at):
    chans = source.shape[2]
    basis = table.shape[0] // (out_rows * BLOCK)
    taken = source[pl.ds(base, in_rows), at : at + WINDOW, :]
    taken = taken.reshape(in_rows * WINDOW, chans)
    result = jnp.dot(table, taken, preferred_element_type=F32).astype(BF16)
    for m in range(out_rows):
        for k in range(basis):
            begin = (m * basis + k) * BLOCK
            feats[first + m, at : at + BLOCK, k * chans : (k + 1) * chans] = result[
                begin : begin + BLOCK, :
            ]


def mix(weights_ref, layer, feats, row, lons, before):
    _, basis, chans, _ = weights_ref.shape
    mixed = jnp.dot(
        feats[row, 0:lons, :],
        weights_ref[layer].reshape(basis * chans, chans),
        preferred_element_type=F32,
    )
    return before[...].astype(F32)[SHIFT : SHIFT + lons, :] + gelu(mixed)


def place(turned, done, row, lat_rows):
    half, chans = done.shape
    width = chans // 2
    for c in range(2):
        turned[c, pl.ds(row, half, stride=lat_rows), :] = done[:, c * width : (c + 1) * width]


def hand_out(turned, keep_ref, send_ref):
    chan = lax.axis_index("chan")
    keep_ref[...] = turned[chan].reshape(keep_ref.shape).astype(BF16)
    send_ref[...] = turned[1 - chan].reshape(send_ref.shape).astype(BF16)


def far_kernel(
    half,
    cols,
    own_ref,
    lon_ref,
    tables_ref,
    weights_hbm,
    ext_ref,
    next_ref,
    weights_ref,
    keep_ref,
    send_ref,
    fields,
    feats,
    turned,
    sem,
):
    fetch = pltpu.make_async_copy(weights_hbm, weights_ref, sem)
    fetch.start()
    lat_rows, lon_total, chans = own_ref.shape
    lat = lax.axis_index("lat")
    lon1 = lon_total - BLOCK
    turned[...] = jnp.zeros_like(turned)

    for t in range(SPAN):
        fields[t] = jnp.zeros((lon_total, chans), BF16)
        fields[SPAN + lat_rows + t] = jnp.zeros((lon_total, chans), BF16)
    fields[SPAN : SPAN + lat_rows] = own_ref[...]
    add_lon_halo(
        cols,
        half,
        [fields.at[SPAN + r] for r in range(lat_rows)],
        [lon_ref.at[r] for r in range(lat_rows)],
    )
    ext_ref[...] = fields[SPAN : SPAN + lat_rows]

    far = GROUP * lat
    mid = GROUP - PAIR * lat
    rows6 = PAIR + 2 * SPAN
    for jb in range(lon1 // BLOCK):
        at = jb * BLOCK
        conv(fields, tables_ref[0], far, GROUP + 2 * SPAN, feats, 0, GROUP, at)
        table = tables_ref[2, 0 : tables_ref.shape[1] // 2, 0 : rows6 * WINDOW]
        conv(fields, table, mid, rows6, feats, GROUP, PAIR, at)
    fetch.wait()
    for t in range(SPAN):
        next_ref[(GROUP + SPAN) * lat + t] = jnp.zeros((lon1, chans), BF16)
    for t in range(GROUP):
        next_ref[SPAN + t] = mix(
            weights_ref, 0, feats, t, lon1, fields.at[SPAN + far + t]
        ).astype(BF16)
    for t in range(PAIR):
        next_ref[(GROUP + SPAN) * (1 - lat) + t] = mix(
            weights_ref, 0, feats, GROUP + t, lon1, fields.at[SPAN + mid + t]
        ).astype(BF16)
    for jb in range(half // BLOCK):
        conv(next_ref, tables_ref[0], 0, GROUP + 2 * SPAN, feats, 0, GROUP, jb * BLOCK)
    for t in range(GROUP):
        done = mix(weights_ref, 1, feats, t, half, next_ref.at[SPAN + t])
        place(turned, done, far + t, lat_rows)
    hand_out(turned, keep_ref, send_ref)


def near_kernel(
    half,
    cols,
    ext_ref,
    next_ref,
    lat_ref,
    lat_other_ref,
    corner_ref,
    tables_ref,
    weights_ref,
    keep_ref,
    send_ref,
    fields,
    near,
    feats,
    turned,
):
    lat_rows, lon_total, chans = ext_ref.shape
    basis = weights_ref.shape[1]
    lat = lax.axis_index("lat")
    lon1 = lon_total - BLOCK
    rows6 = PAIR + 2 * SPAN
    turned[...] = jnp.zeros_like(turned)

    halo = HALO * (1 - lat)
    own = HALO * lat
    for t in range(HALO):
        fields[own + t] = ext_ref[HALO * (1 - lat) + t]
    add_lat_halo(
        cols,
        half,
        [fields.at[halo + t] for t in range(HALO)],
        [lat_ref.at[t] for t in range(HALO)],
        [lat_other_ref.at[t] for t in range(HALO)],
    )
    add_lon_halo(
        cols,
        half,
        [fields.at[halo + t] for t in range(HALO)],
        [corner_ref.at[t] for t in range(HALO)],
    )
    halo_table = toeplitz(corner_ref[HALO].astype(F32)[0 : PAIR * basis, :])
    last_table = tables_ref[2, tables_ref.shape[1] // 2 :, 0 : rows6 * WINDOW]
    last = SPAN * lat
    beyond = SPAN * (1 - lat)
    for jb in range(lon1 // BLOCK):
        conv(fields, last_table, last, rows6, feats, 0, PAIR, jb * BLOCK)
        table = halo_table[:, 0 : rows6 * WINDOW]
        conv(fields, table, beyond, rows6, feats, PAIR, PAIR, jb * BLOCK)
    for t in range(GROUP):
        near[GROUP * lat + t] = next_ref[GROUP * (1 - lat) + t]
    for t in range(PAIR):
        near[GROUP * (1 - lat) + SPAN * lat + t] = mix(
            weights_ref, 0, feats, t, lon1, fields.at[SPAN + last + t]
        ).astype(BF16)
        near[(GROUP + SPAN) * (1 - lat) + t] = mix(
            weights_ref, 0, feats, PAIR + t, lon1, fields.at[SPAN + beyond + t]
        ).astype(BF16)
    for jb in range(half // BLOCK):
        conv(near, tables_ref[1], 0, GROUP + 2 * SPAN, feats, 0, GROUP, jb * BLOCK)
    for t in range(GROUP):
        done = mix(weights_ref, 1, feats, t, half, near.at[SPAN + t])
        place(turned, done, GROUP * (1 - lat) + t, lat_rows)
    hand_out(turned, keep_ref, send_ref)


def all_kernel(half, cols, own_ref, lon_ref, *rest):
    lat_refs, other_refs, corner_refs = rest[:2], rest[2:4], rest[4:6]
    tables_ref, weights_ref, keep_ref, send_ref, fields, feats, after, turned = rest[6:]
    lat_rows, lon_total, chans = own_ref.shape
    basis = weights_ref.shape[1]
    groups = lat_rows // GROUP
    lon1 = lon_total - BLOCK
    halo_base = [0, lat_rows + HALO]
    win_base = [0, lat_rows + HALO - SPAN]
    out_base = [0, lat_rows + SPAN]
    rows6 = PAIR + 2 * SPAN

    fields[HALO : HALO + lat_rows] = own_ref[...]
    rows = [fields.at[HALO + r] for r in range(lat_rows)]
    halos = [lon_ref.at[r] for r in range(lat_rows)]
    for n in range(2):
        halo_rows = [fields.at[halo_base[n] + t] for t in range(HALO)]
        add_lat_halo(
            cols,
            half,
            halo_rows,
            [lat_refs[n].at[t] for t in range(HALO)],
            [other_refs[n].at[t] for t in range(HALO)],
        )
        rows += halo_rows
        halos += [corner_refs[n].at[t] for t in range(HALO)]
    add_lon_halo(cols, half, rows, halos)
    halo_tables = [
        toeplitz(corner_refs[n][HALO].astype(F32)[0 : PAIR * basis, :])[:, 0 : rows6 * WINDOW]
        for n in range(2)
    ]
    for jb in range(lon1 // BLOCK):
        at = jb * BLOCK
        for g in range(groups):
            base = HALO - SPAN + g * GROUP
            conv(
                fields, tables_ref[g], base, GROUP + 2 * SPAN, feats, g * GROUP, GROUP, at
            )
        for n in range(2):
            first = lat_rows + n * PAIR
            conv(fields, halo_tables[n], win_base[n], rows6, feats, first, PAIR, at)
    for i in range(lat_rows):
        after[SPAN + i] = mix(weights_ref, 0, feats, i, lon1, fields.at[HALO + i]).astype(BF16)
    for n in range(2):
        for m in range(PAIR):
            dest = out_base[n] + m
            after[dest] = mix(
                weights_ref, 0, feats, lat_rows + n * PAIR + m, lon1, fields.at[dest + SPAN]
            ).astype(BF16)
    for jb in range(half // BLOCK):
        for g in range(groups):
            base = g * GROUP
            conv(
                after, tables_ref[g], base, GROUP + 2 * SPAN, feats, base, GROUP, jb * BLOCK
            )
    for i in range(lat_rows):
        done = mix(weights_ref, 1, feats, i, half, after.at[SPAN + i])
        place(turned, done, i, lat_rows)
    hand_out(turned, keep_ref, send_ref)


def join_kernel(pieces, *refs):
    keep_refs, got_refs, (out_ref,) = refs[:pieces], refs[pieces : 2 * pieces], refs[2 * pieces :]
    half = keep_refs[0].shape[0]
    rest = out_ref.shape[0] - half
    chan = lax.axis_index("chan")

    def total(parts, count):
        value = parts[0][0:count].astype(F32)
        for other in parts[1:]:
            value = value + other[0:count].astype(F32)
        return value.astype(BF16)

    @pl.when(chan == 0)
    def _():
        out_ref[0:half] = total(keep_refs, half)
        out_ref[half:] = total(got_refs, rest)

    @pl.when(chan == 1)
    def _():
        out_ref[0:half] = total(got_refs, half)
        out_ref[half:] = total(keep_refs, rest)


def per_device(state, sup_rows, sup_count, lon_reach, psi, weights):
    lat_rows, cols, width = state.shape
    _, sup, basis, _ = psi.shape
    chans = weights.shape[2]
    lats, lons = lax.axis_size("lat"), lax.axis_size("lon")
    sides = 1 if lats == 2 else 2
    groups = lat_rows // GROUP
    lanes = (GROUP + 2 * SPAN) * WINDOW
    half = -(-cols // (2 * BLOCK)) * BLOCK
    part = half + WIDE
    lon_total = half + 2 * WIDE
    lon1 = lon_total - BLOCK
    tabs = groups + 1 if sides == 1 else groups
    swap = [(0, 1), (1, 0)]
    params = pltpu.CompilerParams(vmem_limit_bytes=VMEM_LIMIT)

    def shape(*dims):
        return jax.ShapeDtypeStruct(dims, BF16)

    def to_lat(step):
        if lats == 2:
            return [(a, 1 - a) for a in range(lats)]
        return [(a, a + step) for a in range(lats) if 0 <= a + step < lats]

    forth = [((z, 1), ((z + 1) % lons, 0)) for z in range(lons)]
    back = [((z, 0), ((z - 1) % lons, 1)) for z in range(lons)]
    to_lon = forth + back

    own = jnp.transpose(state, (1, 0, 2))
    other = lax.ppermute(own, "chan", swap)

    wide = pltpu.VMEM(((half + part) // BLOCK * BLOCK * lat_rows, width), F32)
    part_own, edge_own, *lat_edges = pl.pallas_call(
        functools.partial(own_kernel, sides, half),
        out_shape=[shape(lat_rows, part, width), shape(lat_rows, WIDE, width)]
        + [shape(HALO, cols, width)] * sides,
        in_specs=[hbm()],
        out_specs=[vmem()] * (2 + sides),
        scratch_shapes=[
            pltpu.VMEM((cols, lat_rows, width), BF16),
            wide,
            pltpu.SemaphoreType.DMA,
        ],
        compiler_params=params,
        name="own",
    )(in_hbm(own))

    steps = [1, -1][:sides]
    lat_halos = [lax.ppermute(lat_edges[n], "lat", to_lat(steps[n])) for n in range(sides)]
    lat_others = [lax.ppermute(h, "chan", swap) for h in lat_halos]

    fields, lon_edge = pl.pallas_call(
        functools.partial(edges_kernel, half),
        out_shape=[shape(lat_rows, lon_total, chans), shape(lat_rows, WIDE, chans)],
        in_specs=[vmem()] * 3,
        out_specs=[vmem()] * 2,
        scratch_shapes=[wide],
        compiler_params=params,
        name="edges",
    )(part_own, edge_own, other)
    lon_halo = lax.ppermute(
        lon_edge, ("lon", "chan"), [(z * 2 + c, y * 2 + d) for (z, c), (y, d) in to_lon]
    )

    rows, *corner_edges = pl.pallas_call(
        functools.partial(bands_kernel, sides),
        out_shape=[shape(tabs, GROUP * basis, lanes)] + [shape(HALO + 1, WIDE, chans)] * sides,
        in_specs=[hbm()] * 4 + [vmem()],
        out_specs=[vmem()] * (1 + sides),
        scratch_shapes=[
            pltpu.SMEM((lat_rows, sup), jnp.int32),
            pltpu.SMEM((lat_rows,), jnp.int32),
            pltpu.SMEM((lat_rows,), jnp.int32),
            pltpu.VMEM(psi.shape, F32),
            pltpu.VMEM((lat_rows, 2 * SPAN + 1, basis, lanes), F32),
            pltpu.VMEM((lat_rows // PAIR, PAIR * basis, lanes), F32),
            pltpu.SemaphoreType.DMA((4,)),
        ],
        compiler_params=params,
        name="bands",
    )(in_hbm(sup_rows), in_hbm(sup_count), in_hbm(lon_reach), in_hbm(psi), lon_edge)
    corners = [
        lax.ppermute(
            corner_edges[n],
            ("lon", "lat", "chan"),
            [
                ((z * lats + a) * 2 + c, (y * lats + b) * 2 + d)
                for a, b in to_lat(steps[n])
                for (z, c), (y, d) in to_lon
            ],
        )
        for n in range(sides)
    ]

    tables = pl.pallas_call(
        tables_kernel,
        out_shape=shape(tabs, GROUP * basis * BLOCK, lanes),
        in_specs=[vmem()],
        out_specs=vmem(),
        compiler_params=params,
        name="tables",
    )(rows)

    def cost(conv_rows, mix_rows):
        flops = 2 * lon1 * chans * basis * (conv_rows * lanes + mix_rows * chans)
        return pl.CostEstimate(flops=flops, bytes_accessed=weights.size * 2, transcendentals=0)

    piece = shape(half, lat_rows, width)
    turned = pltpu.VMEM((2, half * lat_rows, width), F32)
    if sides == 1:
        ext, after, weights_in, keep, send = pl.pallas_call(
            functools.partial(far_kernel, half, cols),
            out_shape=[
                shape(lat_rows, lon_total, chans),
                shape(lat_rows, lon1, chans),
                shape(*weights.shape),
                piece,
                piece,
            ],
            in_specs=[vmem()] * 3 + [hbm()],
            out_specs=[vmem()] * 5,
            scratch_shapes=[
                pltpu.VMEM((lat_rows + 2 * SPAN, lon_total, chans), BF16),
                pltpu.VMEM((GROUP + PAIR, lon1, basis * chans), BF16),
                turned,
                pltpu.SemaphoreType.DMA,
            ],
            compiler_params=params,
            cost_estimate=cost(10, 10),
            name="far_rows",
        )(fields, lon_halo, tables, in_hbm(weights))
        keeps, gots = [keep], [lax.ppermute(send, "chan", swap)]
        keep, send = pl.pallas_call(
            functools.partial(near_kernel, half, cols),
            out_shape=[piece] * 2,
            in_specs=[vmem()] * 7,
            out_specs=[vmem()] * 2,
            scratch_shapes=[
                pltpu.VMEM((2 * HALO, lon_total, chans), BF16),
                pltpu.VMEM((GROUP + 2 * SPAN, lon1, chans), BF16),
                pltpu.VMEM((GROUP, lon1, basis * chans), BF16),
                turned,
            ],
            compiler_params=params,
            cost_estimate=cost(8, 8),
            name="near_rows",
        )(ext, after, lat_halos[0], lat_others[0], corners[0], tables, weights_in)
    else:
        keeps, gots = [], []
        keep, send = pl.pallas_call(
            functools.partial(all_kernel, half, cols),
            out_shape=[piece] * 2,
            in_specs=[vmem()] * (4 + 3 * sides),
            out_specs=[vmem()] * 2,
            scratch_shapes=[
                pltpu.VMEM((lat_rows + 2 * HALO, lon_total, chans), BF16),
                pltpu.VMEM((lat_rows + 2 * PAIR, lon1, basis * chans), BF16),
                pltpu.VMEM((lat_rows + 2 * SPAN, lon1, chans), BF16),
                turned,
            ],
            compiler_params=params,
            cost_estimate=cost(20, 20),
            name="all_rows",
        )(fields, lon_halo, *lat_halos, *lat_others, *corners, tables, weights)
    keeps.append(keep)
    gots.append(lax.ppermute(send, "chan", swap))

    out = pl.pallas_call(
        functools.partial(join_kernel, len(keeps)),
        out_shape=shape(cols, lat_rows, width),
        in_specs=[vmem()] * (2 * len(keeps)),
        out_specs=vmem(),
        compiler_params=params,
        name="join",
    )(*keeps, *gots)
    return jnp.transpose(out, (1, 0, 2))


def solution(mesh):
    return jax.shard_map(
        per_device,
        mesh=mesh,
        in_specs=(
            P(("groups", "lat"), "lon", "chan"),
            P("lat", None),
            P("lat"),
            P("lat"),
            P("lat", None, None, None),
            P(),
        ),
        out_specs=P(("groups", "lat"), "lon", "chan"),
        check_vma=False,
    )
```

```python
import functools

import jax
import jax.numpy as jnp
from jax import lax
from jax.experimental import pallas as pl
from jax.experimental.pallas import tpu as pltpu
from jax.sharding import PartitionSpec as P

LAYERS = 2
SPAN = 2
HALO = LAYERS * SPAN
BLOCK = 16
WINDOW = 2 * BLOCK
GROUP = 4
PAIR = 2
WIDE = BLOCK
SHIFT = BLOCK // 2
VMEM_LIMIT = 48 * 1024 * 1024
BF16 = jnp.bfloat16
F32 = jnp.float32


def vmem():
    return pl.BlockSpec(memory_space=pltpu.VMEM)


def smem():
    return pl.BlockSpec(memory_space=pltpu.SMEM)


def hbm():
    return pl.BlockSpec(memory_space=pltpu.HBM)


def in_hbm(x):
    return pltpu.with_memory_space_constraint(x, pltpu.HBM)


def toeplitz(rows_tab):
    count, _ = rows_tab.shape
    moved = jnp.concatenate(
        [rows_tab if jj == 0 else pltpu.roll(rows_tab, jj, 1) for jj in range(BLOCK)], axis=0
    ).astype(BF16)
    total = count * BLOCK
    out_row = lax.broadcasted_iota(jnp.int32, (total, total), 0)
    in_row = lax.broadcasted_iota(jnp.int32, (total, total), 1)
    source = (out_row % BLOCK) * count + out_row // BLOCK
    order = (in_row == source).astype(F32).astype(BF16)
    return jnp.dot(order, moved, preferred_element_type=F32).astype(BF16)


def own_kernel(sides, half, state_hbm, *rest):
    sources, (part_ref, edge_ref), rest = rest[:5], rest[5:7], rest[7:]
    lat_refs, dests, (state_ref, wide_scr, sems) = rest[:sides], rest[sides : sides + 5], rest[sides + 5 :]
    fetch = pltpu.make_async_copy(state_hbm, state_ref, sems.at[5])
    fetch.start()
    others = [
        pltpu.make_async_copy(source, dest, sems.at[n])
        for n, (source, dest) in enumerate(zip(sources, dests))
    ]
    for copy in others:
        copy.start()
    cols, lat_rows, width = state_ref.shape
    part = part_ref.shape[1]
    lat = lax.axis_index("lat")
    chan = lax.axis_index("chan")
    padded = wide_scr.shape[0] // lat_rows
    wide_scr[cols * lat_rows :, :] = jnp.zeros(((padded - cols) * lat_rows, width), F32)
    fetch.wait()
    wide_scr[0 : cols * lat_rows, :] = state_ref[...].astype(F32).reshape(cols * lat_rows, width)
    for n in range(sides):
        if sides == 1:
            base = jnp.where(lat == 0, lat_rows - HALO, 0)
        else:
            base = lat_rows - HALO if n == 0 else 0
        for t in range(HALO):
            lat_refs[n][t] = wide_scr[pl.ds(base + t, cols, stride=lat_rows), :].astype(BF16)
    start = (half - WIDE) * lat_rows * chan
    edge = (cols - WIDE) * lat_rows * chan
    for r in range(lat_rows):
        part_ref[r] = wide_scr[pl.ds(start + r, part, stride=lat_rows), :].astype(BF16)
        edge_ref[r] = wide_scr[pl.ds(edge + r, WIDE, stride=lat_rows), :].astype(BF16)
    for copy in others:
        copy.wait()


def edges_kernel(half, part_ref, edge_ref, other_ref, fields_ref, lon_ref, wide_scr):
    cols, lat_rows, width = other_ref.shape
    lon_total = fields_ref.shape[1]
    part = part_ref.shape[1]
    chan = lax.axis_index("chan")
    padded = wide_scr.shape[0] // lat_rows
    wide_scr[cols * lat_rows :, :] = jnp.zeros(((padded - cols) * lat_rows, width), F32)

    def build(core):
        start = 0 if core == 0 else half - WIDE
        edge = 0 if core == 0 else cols - WIDE
        stop = start + part if core == 0 else cols
        at = WIDE if core == 0 else 0
        own = slice(core * width, (core + 1) * width)
        lane = slice((1 - core) * width, (2 - core) * width)
        wide_scr[start * lat_rows : stop * lat_rows, :] = (
            other_ref[start:stop].astype(F32).reshape((stop - start) * lat_rows, width)
        )
        for r in range(lat_rows):
            lon_ref[r, :, own] = edge_ref[r]
            lon_ref[r, :, lane] = wide_scr[
                pl.ds(edge * lat_rows + r, WIDE, stride=lat_rows), :
            ].astype(BF16)
            fields_ref[r, at : at + part, own] = part_ref[r]
            fields_ref[r, at : at + part, lane] = wide_scr[
                pl.ds(start * lat_rows + r, part, stride=lat_rows), :
            ].astype(BF16)
        empty = slice(0, WIDE) if core == 0 else slice(part, lon_total)
        fields_ref[:, empty, :] = jnp.zeros((lat_rows, WIDE, 2 * width), BF16)

    @pl.when(chan == 0)
    def _():
        build(0)

    @pl.when(chan == 1)
    def _():
        build(1)


def bands_kernel(
    sides, sup_ref, count_ref, reach_ref, psi_ref, lon_ref, rows_ref, *rest
):
    corner_refs, (slots, pairs_scr) = rest[:sides], rest[sides:]
    lat_rows, sup, basis, offsets = psi_ref.shape
    reach_max = offsets // 2
    lanes = rows_ref.shape[2]
    lat = lax.axis_index("lat")
    slots[...] = jnp.zeros_like(slots)
    for n in range(sides):
        if sides == 1:
            base = jnp.where(lat == 0, lat_rows - HALO, 0)
        else:
            base = lat_rows - HALO if n == 0 else 0
        for t in range(HALO):
            corner_refs[n][t] = lon_ref[base + t]
    for i in range(lat_rows):
        for s in range(sup):
            rel = jnp.clip(sup_ref[i, s] - (lat * lat_rows + i) + SPAN, 0, 2 * SPAN)
            live = jnp.where(s < count_ref[i], 1.0, 0.0)
            slots[i, rel, :, 0:offsets] += psi_ref[i, s] * live
    lane = lax.broadcasted_iota(jnp.int32, (basis, lanes), 1)
    off = lane % WINDOW - reach_max
    for i in range(lat_rows):
        band = slots[i, 0]
        for rel in range(1, 2 * SPAN + 1):
            band = band + pltpu.roll(slots[i, rel], rel * WINDOW, 1)
        band = jnp.where(jnp.abs(off) <= reach_ref[i], band, 0.0)
        m = i % PAIR
        pairs_scr[i // PAIR, m * basis : (m + 1) * basis, :] = (
            band if m == 0 else pltpu.roll(band, m * WINDOW, 1)
        )
    pairs = lat_rows // PAIR

    def group(g):
        first, second = pairs_scr[2 * g], pairs_scr[2 * g + 1]
        return jnp.concatenate([first, pltpu.roll(second, PAIR * WINDOW, 1)], axis=0)

    if sides == 1:
        rows_ref[0] = group(lat).astype(BF16)
        rows_ref[1] = group(1 - lat).astype(BF16)
        mid, near = pairs_scr[2 - lat], pairs_scr[(pairs - 1) * (1 - lat)]
        rows_ref[2] = jnp.concatenate([mid, near], axis=0).astype(BF16)
        edge_pairs = [near]
    else:
        for g in range(lat_rows // GROUP):
            rows_ref[g] = group(g).astype(BF16)
        edge_pairs = [pairs_scr[pairs - 1], pairs_scr[0]]
    for n in range(sides):
        corner_refs[n][HALO] = jnp.concatenate(
            [edge_pairs[n], jnp.zeros_like(edge_pairs[n])], axis=0
        ).astype(BF16)


def tables_kernel(rows_ref, tables_ref):
    for g in range(rows_ref.shape[0]):
        tables_ref[g] = toeplitz(rows_ref[g].astype(F32))


def gelu(x):
    return 0.5 * x * (1.0 + jnp.tanh(0.7978845608028654 * (x + 0.044715 * (x * x * x))))


def add_lat_halo(cols, half, rows, own_halos, other_halos):
    chan = lax.axis_index("chan")

    def fill(core):
        start = 0 if core == 0 else half - WIDE
        stop = half + WIDE if core == 0 else cols
        at = WIDE if core == 0 else 0
        for row, own, other in zip(rows, own_halos, other_halos):
            width = own.shape[1]
            for c, halo in ((core, own), (1 - core, other)):
                row[at : at + stop - start, c * width : (c + 1) * width] = halo[start:stop, :]

    @pl.when(chan == 0)
    def _():
        fill(0)

    @pl.when(chan == 1)
    def _():
        fill(1)


def add_lon_halo(cols, half, rows, halos):
    chan = lax.axis_index("chan")
    count = cols - half + WIDE
    whole = count // BLOCK * BLOCK

    @pl.when(chan == 0)
    def _():
        for row, halo in zip(rows, halos):
            row[0:WIDE, :] = halo[...]

    @pl.when(chan == 1)
    def _():
        for row, halo in zip(rows, halos):
            lon_total, chans = row.shape
            before = row[whole : whole + BLOCK, :].astype(F32)[0 : count - whole, :]
            empty = jnp.zeros((lon_total - count - WIDE, chans), F32)
            row[whole:lon_total, :] = jnp.concatenate(
                [before, halo[...].astype(F32), empty], axis=0
            ).astype(BF16)


def conv(source, table, base, in_rows, feats, first, out_rows, at):
    chans = source.shape[2]
    basis = table.shape[0] // (out_rows * BLOCK)
    taken = source[pl.ds(base, in_rows), at : at + WINDOW, :]
    taken = taken.reshape(in_rows * WINDOW, chans)
    result = jnp.dot(table, taken, preferred_element_type=F32).astype(BF16)
    for m in range(out_rows):
        for k in range(basis):
            begin = (m * basis + k) * BLOCK
            feats[first + m, at : at + BLOCK, k * chans : (k + 1) * chans] = result[
                begin : begin + BLOCK, :
            ]


def mix(weights_ref, layer, feats, row, lons, before):
    _, basis, chans, _ = weights_ref.shape
    mixed = jnp.dot(
        feats[row, 0:lons, :],
        weights_ref[layer].reshape(basis * chans, chans),
        preferred_element_type=F32,
    )
    return before[...].astype(F32)[SHIFT : SHIFT + lons, :] + gelu(mixed)


def place(turned, done, row, lat_rows):
    half, chans = done.shape
    width = chans // 2
    for c in range(2):
        turned[c, pl.ds(row, half, stride=lat_rows), :] = done[:, c * width : (c + 1) * width]


def hand_out(turned, keep_ref, send_ref, far_keep_ref=None, far_send_ref=None):
    chan = lax.axis_index("chan")
    keep = turned[chan].reshape(keep_ref.shape)
    send = turned[1 - chan].reshape(send_ref.shape)
    if far_keep_ref is not None:
        keep = keep + far_keep_ref[...].astype(F32)
        send = send + far_send_ref[...].astype(F32)
    keep_ref[...] = keep.astype(BF16)
    send_ref[...] = send.astype(BF16)


def far1_kernel(
    half,
    cols,
    own_ref,
    lon_ref,
    tables_ref,
    weights_ref,
    ext_ref,
    next_ref,
    fields,
    feats,
):
    lat_rows, lon_total, chans = own_ref.shape
    lat = lax.axis_index("lat")
    lon1 = lon_total - BLOCK

    for t in range(SPAN):
        fields[t] = jnp.zeros((lon_total, chans), BF16)
        fields[SPAN + lat_rows + t] = jnp.zeros((lon_total, chans), BF16)
    fields[SPAN : SPAN + lat_rows] = own_ref[...]
    add_lon_halo(
        cols,
        half,
        [fields.at[SPAN + r] for r in range(lat_rows)],
        [lon_ref.at[r] for r in range(lat_rows)],
    )
    ext_ref[...] = fields[SPAN : SPAN + lat_rows]

    far = GROUP * lat
    mid = GROUP - PAIR * lat
    rows6 = PAIR + 2 * SPAN
    for jb in range(lon1 // BLOCK):
        at = jb * BLOCK
        conv(fields, tables_ref[0], far, GROUP + 2 * SPAN, feats, 0, GROUP, at)
        table = tables_ref[2, 0 : tables_ref.shape[1] // 2, 0 : rows6 * WINDOW]
        conv(fields, table, mid, rows6, feats, GROUP, PAIR, at)
    for t in range(SPAN):
        next_ref[(GROUP + SPAN) * lat + t] = jnp.zeros((lon1, chans), BF16)
    for t in range(GROUP):
        next_ref[SPAN + t] = mix(
            weights_ref, 0, feats, t, lon1, fields.at[SPAN + far + t]
        ).astype(BF16)
    for t in range(PAIR):
        next_ref[(GROUP + SPAN) * (1 - lat) + t] = mix(
            weights_ref, 0, feats, GROUP + t, lon1, fields.at[SPAN + mid + t]
        ).astype(BF16)


def far2_kernel(half, next_ref, tables_ref, weights_ref, keep_ref, send_ref, feats, turned):
    lat_rows = next_ref.shape[0]
    lat = lax.axis_index("lat")
    turned[...] = jnp.zeros_like(turned)
    for jb in range(half // BLOCK):
        conv(next_ref, tables_ref[0], 0, GROUP + 2 * SPAN, feats, 0, GROUP, jb * BLOCK)
    for t in range(GROUP):
        done = mix(weights_ref, 1, feats, t, half, next_ref.at[SPAN + t])
        place(turned, done, GROUP * lat + t, lat_rows)
    hand_out(turned, keep_ref, send_ref)


def relay_kernel(halo_ref, _, out_ref):
    out_ref[...] = halo_ref[...]


def near_kernel(
    half,
    cols,
    ext_ref,
    next_ref,
    lat_ref,
    lat_other_ref,
    corner_ref,
    tables_ref,
    weights_ref,
    far_keep_ref,
    far_send_ref,
    keep_ref,
    send_ref,
    fields,
    near,
    feats,
    turned,
):
    lat_rows, lon_total, chans = ext_ref.shape
    basis = weights_ref.shape[1]
    lat = lax.axis_index("lat")
    lon1 = lon_total - BLOCK
    rows6 = PAIR + 2 * SPAN
    turned[...] = jnp.zeros_like(turned)

    halo = HALO * (1 - lat)
    own = HALO * lat
    for t in range(HALO):
        fields[own + t] = ext_ref[HALO * (1 - lat) + t]
    add_lat_halo(
        cols,
        half,
        [fields.at[halo + t] for t in range(HALO)],
        [lat_ref.at[t] for t in range(HALO)],
        [lat_other_ref.at[t] for t in range(HALO)],
    )
    add_lon_halo(
        cols,
        half,
        [fields.at[halo + t] for t in range(HALO)],
        [corner_ref.at[t] for t in range(HALO)],
    )
    halo_table = toeplitz(corner_ref[HALO].astype(F32)[0 : PAIR * basis, :])
    last_table = tables_ref[2, tables_ref.shape[1] // 2 :, 0 : rows6 * WINDOW]
    last = SPAN * lat
    beyond = SPAN * (1 - lat)
    for jb in range(lon1 // BLOCK):
        conv(fields, last_table, last, rows6, feats, 0, PAIR, jb * BLOCK)
        table = halo_table[:, 0 : rows6 * WINDOW]
        conv(fields, table, beyond, rows6, feats, PAIR, PAIR, jb * BLOCK)
    for t in range(GROUP):
        near[GROUP * lat + t] = next_ref[GROUP * (1 - lat) + t]
    for t in range(PAIR):
        near[GROUP * (1 - lat) + SPAN * lat + t] = mix(
            weights_ref, 0, feats, t, lon1, fields.at[SPAN + last + t]
        ).astype(BF16)
        near[(GROUP + SPAN) * (1 - lat) + t] = mix(
            weights_ref, 0, feats, PAIR + t, lon1, fields.at[SPAN + beyond + t]
        ).astype(BF16)
    for jb in range(half // BLOCK):
        conv(near, tables_ref[1], 0, GROUP + 2 * SPAN, feats, 0, GROUP, jb * BLOCK)
    for t in range(GROUP):
        done = mix(weights_ref, 1, feats, t, half, near.at[SPAN + t])
        place(turned, done, GROUP * (1 - lat) + t, lat_rows)
    hand_out(turned, keep_ref, send_ref, far_keep_ref, far_send_ref)


def all_kernel(half, cols, own_ref, lon_ref, *rest):
    lat_refs, other_refs, corner_refs = rest[:2], rest[2:4], rest[4:6]
    tables_ref, weights_ref, keep_ref, send_ref, fields, feats, after, turned = rest[6:]
    lat_rows, lon_total, chans = own_ref.shape
    basis = weights_ref.shape[1]
    groups = lat_rows // GROUP
    lon1 = lon_total - BLOCK
    halo_base = [0, lat_rows + HALO]
    win_base = [0, lat_rows + HALO - SPAN]
    out_base = [0, lat_rows + SPAN]
    rows6 = PAIR + 2 * SPAN

    fields[HALO : HALO + lat_rows] = own_ref[...]
    rows = [fields.at[HALO + r] for r in range(lat_rows)]
    halos = [lon_ref.at[r] for r in range(lat_rows)]
    for n in range(2):
        halo_rows = [fields.at[halo_base[n] + t] for t in range(HALO)]
        add_lat_halo(
            cols,
            half,
            halo_rows,
            [lat_refs[n].at[t] for t in range(HALO)],
            [other_refs[n].at[t] for t in range(HALO)],
        )
        rows += halo_rows
        halos += [corner_refs[n].at[t] for t in range(HALO)]
    add_lon_halo(cols, half, rows, halos)
    halo_tables = [
        toeplitz(corner_refs[n][HALO].astype(F32)[0 : PAIR * basis, :])[:, 0 : rows6 * WINDOW]
        for n in range(2)
    ]
    for jb in range(lon1 // BLOCK):
        at = jb * BLOCK
        for g in range(groups):
            base = HALO - SPAN + g * GROUP
            conv(
                fields, tables_ref[g], base, GROUP + 2 * SPAN, feats, g * GROUP, GROUP, at
            )
        for n in range(2):
            first = lat_rows + n * PAIR
            conv(fields, halo_tables[n], win_base[n], rows6, feats, first, PAIR, at)
    for i in range(lat_rows):
        after[SPAN + i] = mix(weights_ref, 0, feats, i, lon1, fields.at[HALO + i]).astype(BF16)
    for n in range(2):
        for m in range(PAIR):
            dest = out_base[n] + m
            after[dest] = mix(
                weights_ref, 0, feats, lat_rows + n * PAIR + m, lon1, fields.at[dest + SPAN]
            ).astype(BF16)
    for jb in range(half // BLOCK):
        for g in range(groups):
            base = g * GROUP
            conv(
                after, tables_ref[g], base, GROUP + 2 * SPAN, feats, base, GROUP, jb * BLOCK
            )
    for i in range(lat_rows):
        done = mix(weights_ref, 1, feats, i, half, after.at[SPAN + i])
        place(turned, done, i, lat_rows)
    hand_out(turned, keep_ref, send_ref)


def join_kernel(keep_ref, got_ref, out_hbm, sems):
    half = keep_ref.shape[0]
    rest = out_hbm.shape[0] - half
    chan = lax.axis_index("chan")

    def copy(first, second):
        copies = [
            pltpu.make_async_copy(first, out_hbm.at[0:half], sems.at[0]),
            pltpu.make_async_copy(second.at[0:rest], out_hbm.at[half : half + rest], sems.at[1]),
        ]
        for c in copies:
            c.start()
        for c in copies:
            c.wait()

    @pl.when(chan == 0)
    def _():
        copy(keep_ref, got_ref)

    @pl.when(chan == 1)
    def _():
        copy(got_ref, keep_ref)


def per_device(state, sup_rows, sup_count, lon_reach, psi, weights):
    lat_rows, cols, width = state.shape
    basis = psi.shape[2]
    chans = weights.shape[2]
    lats, lons = lax.axis_size("lat"), lax.axis_size("lon")
    sides = 1 if lats == 2 else 2
    groups = lat_rows // GROUP
    lanes = (GROUP + 2 * SPAN) * WINDOW
    half = -(-cols // (2 * BLOCK)) * BLOCK
    part = half + WIDE
    lon_total = half + 2 * WIDE
    lon1 = lon_total - BLOCK
    tabs = groups + 1 if sides == 1 else groups
    swap = [(0, 1), (1, 0)]
    params = pltpu.CompilerParams(vmem_limit_bytes=VMEM_LIMIT)

    def shape(*dims):
        return jax.ShapeDtypeStruct(dims, BF16)

    def to_lat(step):
        if lats == 2:
            return [(a, 1 - a) for a in range(lats)]
        return [(a, a + step) for a in range(lats) if 0 <= a + step < lats]

    forth = [((z, 1), ((z + 1) % lons, 0)) for z in range(lons)]
    back = [((z, 0), ((z - 1) % lons, 1)) for z in range(lons)]
    to_lon = forth + back

    own = jnp.transpose(state, (1, 0, 2))
    other = lax.ppermute(own, "chan", swap)

    wide = pltpu.VMEM(((half + part) // BLOCK * BLOCK * lat_rows, width), F32)
    later = [sup_rows, sup_count, lon_reach, psi, weights]
    part_own, edge_own, *rest = pl.pallas_call(
        functools.partial(own_kernel, sides, half),
        out_shape=[shape(lat_rows, part, width), shape(lat_rows, WIDE, width)]
        + [shape(HALO, cols, width)] * sides
        + [jax.ShapeDtypeStruct(x.shape, x.dtype) for x in later],
        in_specs=[hbm()] * 6,
        out_specs=[vmem()] * (7 + sides),
        scratch_shapes=[
            pltpu.VMEM((cols, lat_rows, width), BF16),
            wide,
            pltpu.SemaphoreType.DMA((6,)),
        ],
        compiler_params=params,
        name="own",
    )(*[in_hbm(x) for x in [own] + later])
    lat_edges, later = rest[:sides], rest[sides:]

    steps = [1, -1][:sides]
    lat_halos = [lax.ppermute(lat_edges[n], "lat", to_lat(steps[n])) for n in range(sides)]

    fields, lon_edge = pl.pallas_call(
        functools.partial(edges_kernel, half),
        out_shape=[shape(lat_rows, lon_total, chans), shape(lat_rows, WIDE, chans)],
        in_specs=[vmem()] * 3,
        out_specs=[vmem()] * 2,
        scratch_shapes=[wide],
        compiler_params=params,
        name="edges",
    )(part_own, edge_own, other)
    lon_halo = lax.ppermute(
        lon_edge, ("lon", "chan"), [(z * 2 + c, y * 2 + d) for (z, c), (y, d) in to_lon]
    )

    rows, *corner_edges = pl.pallas_call(
        functools.partial(bands_kernel, sides),
        out_shape=[shape(tabs, GROUP * basis, lanes)] + [shape(HALO + 1, WIDE, chans)] * sides,
        in_specs=[smem()] * 3 + [vmem()] * 2,
        out_specs=[vmem()] * (1 + sides),
        scratch_shapes=[
            pltpu.VMEM((lat_rows, 2 * SPAN + 1, basis, lanes), F32),
            pltpu.VMEM((lat_rows // PAIR, PAIR * basis, lanes), F32),
        ],
        compiler_params=params,
        name="bands",
    )(*later[:4], lon_edge)
    corners = [
        lax.ppermute(
            corner_edges[n],
            ("lon", "lat", "chan"),
            [
                ((z * lats + a) * 2 + c, (y * lats + b) * 2 + d)
                for a, b in to_lat(steps[n])
                for (z, c), (y, d) in to_lon
            ],
        )
        for n in range(sides)
    ]

    tables = pl.pallas_call(
        tables_kernel,
        out_shape=shape(tabs, GROUP * basis * BLOCK, lanes),
        in_specs=[vmem()],
        out_specs=vmem(),
        compiler_params=params,
        name="tables",
    )(rows)

    def cost(conv_rows, mix_rows):
        flops = 2 * lon1 * chans * basis * (conv_rows * lanes + mix_rows * chans)
        return pl.CostEstimate(flops=flops, bytes_accessed=0, transcendentals=0)

    weights_in = later[4]
    piece = shape(half, lat_rows, width)
    turned = pltpu.VMEM((2, half * lat_rows, width), F32)
    if sides == 1:
        ext, after = pl.pallas_call(
            functools.partial(far1_kernel, half, cols),
            out_shape=[shape(lat_rows, lon_total, chans), shape(lat_rows, lon1, chans)],
            in_specs=[vmem()] * 4,
            out_specs=[vmem()] * 2,
            scratch_shapes=[
                pltpu.VMEM((lat_rows + 2 * SPAN, lon_total, chans), BF16),
                pltpu.VMEM((GROUP + PAIR, lon1, basis * chans), BF16),
            ],
            compiler_params=params,
            cost_estimate=cost(6, 6),
            name="far_rows_1",
        )(fields, lon_halo, tables, weights_in)
        relayed = pl.pallas_call(
            relay_kernel,
            out_shape=shape(*lat_halos[0].shape),
            in_specs=[vmem()] * 2,
            out_specs=vmem(),
            compiler_params=params,
            name="relay",
        )(lat_halos[0], after)
        lat_other = lax.ppermute(relayed, "chan", swap)
        far_keep, far_send = pl.pallas_call(
            functools.partial(far2_kernel, half),
            out_shape=[piece] * 2,
            in_specs=[vmem()] * 3,
            out_specs=[vmem()] * 2,
            scratch_shapes=[pltpu.VMEM((GROUP, half, basis * chans), BF16), turned],
            compiler_params=params,
            cost_estimate=cost(4, 4),
            name="far_rows_2",
        )(after, tables, weights_in)
        keep, send = pl.pallas_call(
            functools.partial(near_kernel, half, cols),
            out_shape=[piece] * 2,
            in_specs=[vmem()] * 9,
            out_specs=[vmem()] * 2,
            scratch_shapes=[
                pltpu.VMEM((2 * HALO, lon_total, chans), BF16),
                pltpu.VMEM((GROUP + 2 * SPAN, lon1, chans), BF16),
                pltpu.VMEM((GROUP, lon1, basis * chans), BF16),
                turned,
            ],
            compiler_params=params,
            cost_estimate=cost(8, 8),
            name="near_rows",
        )(
            ext,
            after,
            lat_halos[0],
            lat_other,
            corners[0],
            tables,
            weights_in,
            far_keep,
            far_send,
        )
    else:
        lat_others = [lax.ppermute(h, "chan", swap) for h in lat_halos]
        keep, send = pl.pallas_call(
            functools.partial(all_kernel, half, cols),
            out_shape=[piece] * 2,
            in_specs=[vmem()] * (4 + 3 * sides),
            out_specs=[vmem()] * 2,
            scratch_shapes=[
                pltpu.VMEM((lat_rows + 2 * HALO, lon_total, chans), BF16),
                pltpu.VMEM((lat_rows + 2 * PAIR, lon1, basis * chans), BF16),
                pltpu.VMEM((lat_rows + 2 * SPAN, lon1, chans), BF16),
                turned,
            ],
            compiler_params=params,
            cost_estimate=cost(20, 20),
            name="all_rows",
        )(fields, lon_halo, *lat_halos, *lat_others, *corners, tables, weights_in)
    got = lax.ppermute(send, "chan", swap)

    out = pl.pallas_call(
        join_kernel,
        out_shape=shape(cols, lat_rows, width),
        in_specs=[vmem()] * 2,
        out_specs=hbm(),
        scratch_shapes=[pltpu.SemaphoreType.DMA((2,))],
        compiler_params=params,
        name="join",
    )(keep, got)
    return jnp.transpose(out, (1, 0, 2))


def solution(mesh):
    return jax.shard_map(
        per_device,
        mesh=mesh,
        in_specs=(
            P(("groups", "lat"), "lon", "chan"),
            P("lat", None),
            P("lat"),
            P("lat"),
            P("lat", None, None, None),
            P(),
        ),
        out_specs=P(("groups", "lat"), "lon", "chan"),
        check_vma=False,
    )
```

```python
import functools

import jax
import jax.numpy as jnp
from jax import lax
from jax.experimental import pallas as pl
from jax.experimental.pallas import tpu as pltpu
from jax.sharding import PartitionSpec as P

LAYERS = 2
SPAN = 2
HALO = LAYERS * SPAN
BLOCK = 16
WINDOW = 2 * BLOCK
GROUP = 4
PAIR = 2
WIDE = BLOCK
SHIFT = BLOCK // 2
VMEM_LIMIT = 48 * 1024 * 1024
BF16 = jnp.bfloat16
F32 = jnp.float32


def vmem():
    return pl.BlockSpec(memory_space=pltpu.VMEM)


def smem():
    return pl.BlockSpec(memory_space=pltpu.SMEM)


def hbm():
    return pl.BlockSpec(memory_space=pltpu.HBM)


def in_hbm(x):
    return pltpu.with_memory_space_constraint(x, pltpu.HBM)


def toeplitz(rows_tab):
    count, _ = rows_tab.shape
    moved = jnp.concatenate(
        [rows_tab if jj == 0 else pltpu.roll(rows_tab, jj, 1) for jj in range(BLOCK)], axis=0
    ).astype(BF16)
    total = count * BLOCK
    out_row = lax.broadcasted_iota(jnp.int32, (total, total), 0)
    in_row = lax.broadcasted_iota(jnp.int32, (total, total), 1)
    source = (out_row % BLOCK) * count + out_row // BLOCK
    order = (in_row == source).astype(F32).astype(BF16)
    return jnp.dot(order, moved, preferred_element_type=F32).astype(BF16)


def neighbour_rows(sides, lat_rows):
    if sides == 1:
        return [(1 - lax.axis_index("lat")) * (lat_rows - HALO)]
    return [lat_rows - HALO, 0]


def band_row(refs, slots, i):
    sup_ref, count_ref, reach_ref, psi_ref = refs
    lat_rows, sup, basis, offsets = psi_ref.shape
    lanes = slots.shape[2]
    row = lax.axis_index("lat") * lat_rows + i
    slots[...] = jnp.zeros_like(slots)
    for s in range(sup):
        rel = jnp.clip(sup_ref[i, s] - row + SPAN, 0, 2 * SPAN)
        live = jnp.where(s < count_ref[i], 1.0, 0.0)
        slots[rel, :, 0:offsets] += psi_ref[i, s] * live
    band = slots[0]
    for rel in range(1, 2 * SPAN + 1):
        band = band + pltpu.roll(slots[rel], rel * WINDOW, 1)
    off = lax.broadcasted_iota(jnp.int32, (basis, lanes), 1) % WINDOW - offsets // 2
    return jnp.where(jnp.abs(off) <= reach_ref[i], band, 0.0)


def own_kernel(sides, half, *refs):
    sources, refs = refs[:5], refs[5:]
    dests, refs = refs[:5], refs[5:]
    same_refs, cross_refs, refs = refs[:sides], refs[sides : 2 * sides], refs[2 * sides :]
    smems, (slots, pair_scr, wide_scr, sems) = refs[:3], refs[3:]
    copies = [
        pltpu.make_async_copy(source, dest, sems.at[n])
        for n, (source, dest) in enumerate(
            list(zip(sources[:3], smems)) + list(zip(sources, dests))
        )
    ]
    for copy in copies:
        copy.start()
    psi_ref, state_ref = dests[3:]
    cols, lat_rows, width = state_ref.shape
    basis = psi_ref.shape[2]
    part = cross_refs[0].shape[1]
    lanes = pair_scr.shape[1]
    chan = lax.axis_index("chan")
    padded = wide_scr.shape[0] // lat_rows
    wide_scr[cols * lat_rows :, :] = jnp.zeros(((padded - cols) * lat_rows, width), F32)
    for copy in copies[:7]:
        copy.wait()
    firsts = neighbour_rows(sides, lat_rows)
    for n, first in enumerate(firsts):
        if sides == 1:
            first = (1 - lax.axis_index("lat")) * (lat_rows - PAIR)
        else:
            first = (lat_rows - PAIR, 0)[n]
        for m in range(PAIR):
            band = band_row((*smems, psi_ref), slots.at[n * PAIR + m], first + m)
            pair_scr[m * basis : (m + 1) * basis, :] = (
                band if m == 0 else pltpu.roll(band, m * WINDOW, 1)
            )
        per = PAIR * basis // HALO
        for t in range(HALO):
            extra = [
                pair_scr[per * t + q : per * t + q + 1, x : x + width]
                for q in range(per)
                for x in range(0, lanes, width)
            ]
            same_refs[n][t, part:, :] = jnp.concatenate(extra, axis=0).astype(BF16)
    copies[7].wait()
    wide_scr[0 : cols * lat_rows, :] = state_ref[...].astype(F32).reshape(cols * lat_rows, width)
    step = (half - WIDE) * lat_rows
    for n, first in enumerate(firsts):
        for t in range(HALO):
            for dest, core in ((same_refs[n], chan), (cross_refs[n], 1 - chan)):
                dest[t, 0:part, :] = wide_scr[
                    pl.ds(step * core + first + t, part, stride=lat_rows), :
                ].astype(BF16)


def edges_kernel(sides, half, own_ref, other_ref, fields_ref, lon_ref, *rest):
    corner_refs, (wide_scr,) = rest[:sides], rest[sides:]
    cols, lat_rows, width = other_ref.shape
    lon_total = fields_ref.shape[1]
    part = half + WIDE
    chan = lax.axis_index("chan")
    padded = wide_scr.shape[1] // lat_rows
    wide_scr[:, cols * lat_rows :, :] = jnp.zeros((2, (padded - cols) * lat_rows, width), F32)

    def build(core):
        start = 0 if core == 0 else half - WIDE
        edge = 0 if core == 0 else cols - WIDE
        stop = start + part if core == 0 else cols
        at = WIDE if core == 0 else 0
        for c, ref in ((core, own_ref), (1 - core, other_ref)):
            lane = slice(c * width, (c + 1) * width)
            wide_scr[c, start * lat_rows : stop * lat_rows, :] = (
                ref[start:stop].astype(F32).reshape((stop - start) * lat_rows, width)
            )
            for r in range(lat_rows):
                lon_ref[r, :, lane] = wide_scr[
                    c, pl.ds(edge * lat_rows + r, WIDE, stride=lat_rows), :
                ].astype(BF16)
                fields_ref[r, at : at + part, lane] = wide_scr[
                    c, pl.ds(start * lat_rows + r, part, stride=lat_rows), :
                ].astype(BF16)
        empty = slice(0, WIDE) if core == 0 else slice(part, lon_total)
        fields_ref[:, empty, :] = jnp.zeros((lat_rows, WIDE, 2 * width), BF16)

    @pl.when(chan == 0)
    def _():
        build(0)

    @pl.when(chan == 1)
    def _():
        build(1)

    for n, first in enumerate(neighbour_rows(sides, lat_rows)):
        for t in range(HALO):
            corner_refs[n][t] = lon_ref[first + t]


def bands_kernel(
    sides,
    sup_ref,
    count_ref,
    reach_ref,
    psi_ref,
    weights_hbm,
    rows_ref,
    weights_ref,
    slots,
    pairs_scr,
    sem,
):
    fetch = pltpu.make_async_copy(weights_hbm, weights_ref, sem)
    fetch.start()
    lat_rows, _, basis, _ = psi_ref.shape
    lat = lax.axis_index("lat")
    for i in range(lat_rows):
        band = band_row((sup_ref, count_ref, reach_ref, psi_ref), slots.at[i], i)
        m = i % PAIR
        pairs_scr[i // PAIR, m * basis : (m + 1) * basis, :] = (
            band if m == 0 else pltpu.roll(band, m * WINDOW, 1)
        )
    pairs = lat_rows // PAIR

    def group(g):
        first, second = pairs_scr[2 * g], pairs_scr[2 * g + 1]
        return jnp.concatenate([first, pltpu.roll(second, PAIR * WINDOW, 1)], axis=0)

    if sides == 1:
        rows_ref[0] = group(lat).astype(BF16)
        rows_ref[1] = group(1 - lat).astype(BF16)
        mid, near = pairs_scr[2 - lat], pairs_scr[(pairs - 1) * (1 - lat)]
        rows_ref[2] = jnp.concatenate([mid, near], axis=0).astype(BF16)
    else:
        for g in range(lat_rows // GROUP):
            rows_ref[g] = group(g).astype(BF16)
    fetch.wait()


def tables_kernel(rows_ref, tables_ref):
    for g in range(rows_ref.shape[0]):
        tables_ref[g] = toeplitz(rows_ref[g].astype(F32))


def gelu(x):
    return 0.5 * x * (1.0 + jnp.tanh(0.7978845608028654 * (x + 0.044715 * (x * x * x))))


def add_lat_halo(rows, same, cross):
    chan = lax.axis_index("chan")
    _, part, width = cross.shape
    at = pl.ds(pl.multiple_of((1 - chan) * WIDE, WIDE), part)
    own = pl.ds(pl.multiple_of(chan * width, width), width)
    other = pl.ds(pl.multiple_of((1 - chan) * width, width), width)
    for t, row in enumerate(rows):
        row[at, own] = same[t, 0:part, :]
        row[at, other] = cross[t]


def halo_table(same, basis):
    count, total, width = same.shape
    per = PAIR * basis // count
    first = total - per * (GROUP + 2 * SPAN) * WINDOW // width
    lanes = (total - first) // per
    rows = []
    for t in range(count):
        flat = same[t, first:total, :].astype(F32)
        for q in range(per):
            parts = [flat[q * lanes + x : q * lanes + x + 1, :] for x in range(lanes)]
            rows.append(jnp.concatenate(parts, axis=1))
    return toeplitz(jnp.concatenate(rows, axis=0))


def add_lon_halo(cols, half, rows, halos):
    chan = lax.axis_index("chan")
    count = cols - half + WIDE
    whole = count // BLOCK * BLOCK

    @pl.when(chan == 0)
    def _():
        for row, halo in zip(rows, halos):
            row[0:WIDE, :] = halo[...]

    @pl.when(chan == 1)
    def _():
        for row, halo in zip(rows, halos):
            lon_total, chans = row.shape
            before = row[whole : whole + BLOCK, :].astype(F32)[0 : count - whole, :]
            empty = jnp.zeros((lon_total - count - WIDE, chans), F32)
            row[whole:lon_total, :] = jnp.concatenate(
                [before, halo[...].astype(F32), empty], axis=0
            ).astype(BF16)


def conv(source, table, base, in_rows, feats, first, out_rows, at):
    chans = source.shape[2]
    basis = table.shape[0] // (out_rows * BLOCK)
    taken = source[pl.ds(base, in_rows), at : at + WINDOW, :]
    taken = taken.reshape(in_rows * WINDOW, chans)
    result = jnp.dot(table, taken, preferred_element_type=F32).astype(BF16)
    for m in range(out_rows):
        for k in range(basis):
            begin = (m * basis + k) * BLOCK
            feats[first + m, at : at + BLOCK, k * chans : (k + 1) * chans] = result[
                begin : begin + BLOCK, :
            ]


def mix(weights_ref, layer, feats, row, lons, before):
    _, basis, chans, _ = weights_ref.shape
    mixed = jnp.dot(
        feats[row, 0:lons, :],
        weights_ref[layer].reshape(basis * chans, chans),
        preferred_element_type=F32,
    )
    return before[...].astype(F32)[SHIFT : SHIFT + lons, :] + gelu(mixed)


def place(turned, done, row, lat_rows):
    half, chans = done.shape
    width = chans // 2
    for c in range(2):
        turned[c, pl.ds(row, half, stride=lat_rows), :] = done[:, c * width : (c + 1) * width]


def hand_out(turned, keep_ref, send_ref, far_keep_ref=None, far_send_ref=None):
    chan = lax.axis_index("chan")
    keep = turned[chan].reshape(keep_ref.shape)
    send = turned[1 - chan].reshape(send_ref.shape)
    if far_keep_ref is not None:
        keep = keep + far_keep_ref[...].astype(F32)
        send = send + far_send_ref[...].astype(F32)
    keep_ref[...] = keep.astype(BF16)
    send_ref[...] = send.astype(BF16)


def far1_kernel(
    half,
    cols,
    own_ref,
    lon_ref,
    tables_ref,
    weights_ref,
    ext_ref,
    next_ref,
    fields,
    feats,
):
    lat_rows, lon_total, chans = own_ref.shape
    lat = lax.axis_index("lat")
    lon1 = lon_total - BLOCK

    for t in range(SPAN):
        fields[t] = jnp.zeros((lon_total, chans), BF16)
        fields[SPAN + lat_rows + t] = jnp.zeros((lon_total, chans), BF16)
    fields[SPAN : SPAN + lat_rows] = own_ref[...]
    add_lon_halo(
        cols,
        half,
        [fields.at[SPAN + r] for r in range(lat_rows)],
        [lon_ref.at[r] for r in range(lat_rows)],
    )
    ext_ref[...] = fields[SPAN : SPAN + lat_rows]

    far = GROUP * lat
    mid = GROUP - PAIR * lat
    rows6 = PAIR + 2 * SPAN
    for jb in range(lon1 // BLOCK):
        at = jb * BLOCK
        conv(fields, tables_ref[0], far, GROUP + 2 * SPAN, feats, 0, GROUP, at)
        table = tables_ref[2, 0 : tables_ref.shape[1] // 2, 0 : rows6 * WINDOW]
        conv(fields, table, mid, rows6, feats, GROUP, PAIR, at)
    for t in range(SPAN):
        next_ref[(GROUP + SPAN) * lat + t] = jnp.zeros((lon1, chans), BF16)
    for t in range(GROUP):
        next_ref[SPAN + t] = mix(
            weights_ref, 0, feats, t, lon1, fields.at[SPAN + far + t]
        ).astype(BF16)
    for t in range(PAIR):
        next_ref[(GROUP + SPAN) * (1 - lat) + t] = mix(
            weights_ref, 0, feats, GROUP + t, lon1, fields.at[SPAN + mid + t]
        ).astype(BF16)


def far2_kernel(half, next_ref, tables_ref, weights_ref, keep_ref, send_ref, feats, turned):
    lat_rows = next_ref.shape[0]
    lat = lax.axis_index("lat")
    turned[...] = jnp.zeros_like(turned)
    for jb in range(half // BLOCK):
        conv(next_ref, tables_ref[0], 0, GROUP + 2 * SPAN, feats, 0, GROUP, jb * BLOCK)
    for t in range(GROUP):
        done = mix(weights_ref, 1, feats, t, half, next_ref.at[SPAN + t])
        place(turned, done, GROUP * lat + t, lat_rows)
    hand_out(turned, keep_ref, send_ref)


def near_kernel(
    half,
    cols,
    ext_ref,
    next_ref,
    same_ref,
    cross_ref,
    corner_ref,
    tables_ref,
    weights_ref,
    far_keep_ref,
    far_send_ref,
    keep_ref,
    send_ref,
    fields,
    near,
    feats,
    turned,
):
    lat_rows, lon_total, chans = ext_ref.shape
    basis = weights_ref.shape[1]
    lat = lax.axis_index("lat")
    lon1 = lon_total - BLOCK
    rows6 = PAIR + 2 * SPAN
    turned[...] = jnp.zeros_like(turned)

    halo = HALO * (1 - lat)
    own = HALO * lat
    for t in range(HALO):
        fields[own + t] = ext_ref[HALO * (1 - lat) + t]
    add_lat_halo([fields.at[halo + t] for t in range(HALO)], same_ref, cross_ref)
    add_lon_halo(
        cols,
        half,
        [fields.at[halo + t] for t in range(HALO)],
        [corner_ref.at[t] for t in range(HALO)],
    )
    beyond_table = halo_table(same_ref, basis)[:, 0 : rows6 * WINDOW]
    last_table = tables_ref[2, tables_ref.shape[1] // 2 :, 0 : rows6 * WINDOW]
    last = SPAN * lat
    beyond = SPAN * (1 - lat)
    for jb in range(lon1 // BLOCK):
        conv(fields, last_table, last, rows6, feats, 0, PAIR, jb * BLOCK)
        conv(fields, beyond_table, beyond, rows6, feats, PAIR, PAIR, jb * BLOCK)
    for t in range(GROUP):
        near[GROUP * lat + t] = next_ref[GROUP * (1 - lat) + t]
    for t in range(PAIR):
        near[GROUP * (1 - lat) + SPAN * lat + t] = mix(
            weights_ref, 0, feats, t, lon1, fields.at[SPAN + last + t]
        ).astype(BF16)
        near[(GROUP + SPAN) * (1 - lat) + t] = mix(
            weights_ref, 0, feats, PAIR + t, lon1, fields.at[SPAN + beyond + t]
        ).astype(BF16)
    for jb in range(half // BLOCK):
        conv(near, tables_ref[1], 0, GROUP + 2 * SPAN, feats, 0, GROUP, jb * BLOCK)
    for t in range(GROUP):
        done = mix(weights_ref, 1, feats, t, half, near.at[SPAN + t])
        place(turned, done, GROUP * (1 - lat) + t, lat_rows)
    hand_out(turned, keep_ref, send_ref, far_keep_ref, far_send_ref)


def all_kernel(half, cols, own_ref, lon_ref, *rest):
    same_refs, cross_refs, corner_refs = rest[:2], rest[2:4], rest[4:6]
    tables_ref, weights_ref, keep_ref, send_ref, fields, feats, after, turned = rest[6:]
    lat_rows, lon_total, chans = own_ref.shape
    basis = weights_ref.shape[1]
    groups = lat_rows // GROUP
    lon1 = lon_total - BLOCK
    halo_base = [0, lat_rows + HALO]
    win_base = [0, lat_rows + HALO - SPAN]
    out_base = [0, lat_rows + SPAN]
    rows6 = PAIR + 2 * SPAN

    fields[HALO : HALO + lat_rows] = own_ref[...]
    rows = [fields.at[HALO + r] for r in range(lat_rows)]
    halos = [lon_ref.at[r] for r in range(lat_rows)]
    for n in range(2):
        halo_rows = [fields.at[halo_base[n] + t] for t in range(HALO)]
        add_lat_halo(halo_rows, same_refs[n], cross_refs[n])
        rows += halo_rows
        halos += [corner_refs[n].at[t] for t in range(HALO)]
    add_lon_halo(cols, half, rows, halos)
    halo_tables = [halo_table(same_refs[n], basis)[:, 0 : rows6 * WINDOW] for n in range(2)]
    for jb in range(lon1 // BLOCK):
        at = jb * BLOCK
        for g in range(groups):
            base = HALO - SPAN + g * GROUP
            conv(
                fields, tables_ref[g], base, GROUP + 2 * SPAN, feats, g * GROUP, GROUP, at
            )
        for n in range(2):
            first = lat_rows + n * PAIR
            conv(fields, halo_tables[n], win_base[n], rows6, feats, first, PAIR, at)
    for i in range(lat_rows):
        after[SPAN + i] = mix(weights_ref, 0, feats, i, lon1, fields.at[HALO + i]).astype(BF16)
    for n in range(2):
        for m in range(PAIR):
            dest = out_base[n] + m
            after[dest] = mix(
                weights_ref, 0, feats, lat_rows + n * PAIR + m, lon1, fields.at[dest + SPAN]
            ).astype(BF16)
    for jb in range(half // BLOCK):
        for g in range(groups):
            base = g * GROUP
            conv(
                after, tables_ref[g], base, GROUP + 2 * SPAN, feats, base, GROUP, jb * BLOCK
            )
    for i in range(lat_rows):
        done = mix(weights_ref, 1, feats, i, half, after.at[SPAN + i])
        place(turned, done, i, lat_rows)
    hand_out(turned, keep_ref, send_ref)


def join_kernel(keep_ref, got_ref, out_hbm, sems):
    half = keep_ref.shape[0]
    rest = out_hbm.shape[0] - half
    chan = lax.axis_index("chan")

    def copy(first, second):
        copies = [
            pltpu.make_async_copy(first, out_hbm.at[0:half], sems.at[0]),
            pltpu.make_async_copy(second.at[0:rest], out_hbm.at[half : half + rest], sems.at[1]),
        ]
        for c in copies:
            c.start()
        for c in copies:
            c.wait()

    @pl.when(chan == 0)
    def _():
        copy(keep_ref, got_ref)

    @pl.when(chan == 1)
    def _():
        copy(got_ref, keep_ref)


def per_device(state, sup_rows, sup_count, lon_reach, psi, weights):
    lat_rows, cols, width = state.shape
    basis = psi.shape[2]
    chans = weights.shape[2]
    lats, lons = lax.axis_size("lat"), lax.axis_size("lon")
    sides = 1 if lats == 2 else 2
    groups = lat_rows // GROUP
    lanes = (GROUP + 2 * SPAN) * WINDOW
    half = -(-cols // (2 * BLOCK)) * BLOCK
    part = half + WIDE
    lon_total = half + 2 * WIDE
    lon1 = lon_total - BLOCK
    tabs = groups + 1 if sides == 1 else groups
    swap = [(0, 1), (1, 0)]
    params = pltpu.CompilerParams(vmem_limit_bytes=VMEM_LIMIT)

    def shape(*dims):
        return jax.ShapeDtypeStruct(dims, BF16)

    def to_lat(step):
        if lats == 2:
            return [(a, 1 - a) for a in range(lats)]
        return [(a, a + step) for a in range(lats) if 0 <= a + step < lats]

    forth = [((z, 1), ((z + 1) % lons, 0)) for z in range(lons)]
    back = [((z, 0), ((z - 1) % lons, 1)) for z in range(lons)]
    to_lon = forth + back

    own = jnp.transpose(state, (1, 0, 2))
    other = lax.ppermute(own, "chan", swap)

    def to_cross(step):
        return [(a * 2 + c, b * 2 + 1 - c) for a, b in to_lat(step) for c in range(2)]

    def scratch(*dims):
        return pltpu.VMEM(dims, F32)

    slots = (2 * SPAN + 1, basis, lanes)
    padded = (half + part) * lat_rows
    extra = PAIR * basis * lanes // (HALO * width)
    inputs = [sup_rows, sup_count, lon_reach, psi, own]
    sent = pl.pallas_call(
        functools.partial(own_kernel, sides, half),
        out_shape=[jax.ShapeDtypeStruct(x.shape, x.dtype) for x in inputs]
        + [shape(HALO, part + extra, width)] * sides
        + [shape(HALO, part, width)] * sides,
        in_specs=[hbm()] * 5,
        out_specs=[vmem()] * (5 + 2 * sides),
        scratch_shapes=[pltpu.SMEM(x.shape, x.dtype) for x in inputs[:3]]
        + [
            scratch(sides * PAIR, *slots),
            scratch(PAIR * basis, lanes),
            scratch(padded, width),
            pltpu.SemaphoreType.DMA((8,)),
        ],
        compiler_params=params,
        name="own",
    )(*[in_hbm(x) for x in inputs])
    inputs, sames, crosses = sent[:5], sent[5 : 5 + sides], sent[5 + sides :]
    steps = [1, -1][:sides]
    sames = [lax.ppermute(x, "lat", to_lat(step)) for x, step in zip(sames, steps)]
    crosses = [
        lax.ppermute(x, ("lat", "chan"), to_cross(step)) for x, step in zip(crosses, steps)
    ]

    fields, lon_edge, *corners = pl.pallas_call(
        functools.partial(edges_kernel, sides, half),
        out_shape=[shape(lat_rows, lon_total, chans), shape(lat_rows, WIDE, chans)]
        + [shape(HALO, WIDE, chans)] * sides,
        in_specs=[vmem()] * 2,
        out_specs=[vmem()] * (2 + sides),
        scratch_shapes=[scratch(2, padded, width)],
        compiler_params=params,
        name="edges",
    )(inputs[4], other)
    lon_halo = lax.ppermute(
        lon_edge, ("lon", "chan"), [(z * 2 + c, y * 2 + d) for (z, c), (y, d) in to_lon]
    )
    corners = [
        lax.ppermute(
            x,
            ("lon", "lat", "chan"),
            [
                ((z * lats + a) * 2 + c, (y * lats + b) * 2 + d)
                for a, b in to_lat(step)
                for (z, c), (y, d) in to_lon
            ],
        )
        for x, step in zip(corners, steps)
    ]

    rows, weights_in = pl.pallas_call(
        functools.partial(bands_kernel, sides),
        out_shape=[shape(tabs, GROUP * basis, lanes), shape(*weights.shape)],
        in_specs=[smem()] * 3 + [vmem(), hbm()],
        out_specs=[vmem()] * 2,
        scratch_shapes=[
            scratch(lat_rows, *slots),
            scratch(lat_rows // PAIR, PAIR * basis, lanes),
            pltpu.SemaphoreType.DMA,
        ],
        compiler_params=params,
        name="bands",
    )(*inputs[:4], in_hbm(weights))

    tables = pl.pallas_call(
        tables_kernel,
        out_shape=shape(tabs, GROUP * basis * BLOCK, lanes),
        in_specs=[vmem()],
        out_specs=vmem(),
        compiler_params=params,
        name="tables",
    )(rows)

    def cost(conv_rows, mix_rows):
        flops = 2 * lon1 * chans * basis * (conv_rows * lanes + mix_rows * chans)
        return pl.CostEstimate(flops=flops, bytes_accessed=0, transcendentals=0)

    piece = shape(half, lat_rows, width)
    turned = pltpu.VMEM((2, half * lat_rows, width), F32)
    if sides == 1:
        ext, after = pl.pallas_call(
            functools.partial(far1_kernel, half, cols),
            out_shape=[shape(lat_rows, lon_total, chans), shape(lat_rows, lon1, chans)],
            in_specs=[vmem()] * 4,
            out_specs=[vmem()] * 2,
            scratch_shapes=[
                pltpu.VMEM((lat_rows + 2 * SPAN, lon_total, chans), BF16),
                pltpu.VMEM((GROUP + PAIR, lon1, basis * chans), BF16),
            ],
            compiler_params=params,
            cost_estimate=cost(6, 6),
            name="far_rows_1",
        )(fields, lon_halo, tables, weights_in)
        far_keep, far_send = pl.pallas_call(
            functools.partial(far2_kernel, half),
            out_shape=[piece] * 2,
            in_specs=[vmem()] * 3,
            out_specs=[vmem()] * 2,
            scratch_shapes=[pltpu.VMEM((GROUP, half, basis * chans), BF16), turned],
            compiler_params=params,
            cost_estimate=cost(4, 4),
            name="far_rows_2",
        )(after, tables, weights_in)
        keep, send = pl.pallas_call(
            functools.partial(near_kernel, half, cols),
            out_shape=[piece] * 2,
            in_specs=[vmem()] * 9,
            out_specs=[vmem()] * 2,
            scratch_shapes=[
                pltpu.VMEM((2 * HALO, lon_total, chans), BF16),
                pltpu.VMEM((GROUP + 2 * SPAN, lon1, chans), BF16),
                pltpu.VMEM((GROUP, lon1, basis * chans), BF16),
                turned,
            ],
            compiler_params=params,
            cost_estimate=cost(8, 8),
            name="near_rows",
        )(
            ext,
            after,
            sames[0],
            crosses[0],
            corners[0],
            tables,
            weights_in,
            far_keep,
            far_send,
        )
    else:
        keep, send = pl.pallas_call(
            functools.partial(all_kernel, half, cols),
            out_shape=[piece] * 2,
            in_specs=[vmem()] * (4 + 3 * sides),
            out_specs=[vmem()] * 2,
            scratch_shapes=[
                pltpu.VMEM((lat_rows + 2 * HALO, lon_total, chans), BF16),
                pltpu.VMEM((lat_rows + 2 * PAIR, lon1, basis * chans), BF16),
                pltpu.VMEM((lat_rows + 2 * SPAN, lon1, chans), BF16),
                turned,
            ],
            compiler_params=params,
            cost_estimate=cost(20, 20),
            name="all_rows",
        )(fields, lon_halo, *sames, *crosses, *corners, tables, weights_in)
    got = lax.ppermute(send, "chan", swap)

    out = pl.pallas_call(
        join_kernel,
        out_shape=shape(cols, lat_rows, width),
        in_specs=[vmem()] * 2,
        out_specs=hbm(),
        scratch_shapes=[pltpu.SemaphoreType.DMA((2,))],
        compiler_params=params,
        name="join",
    )(keep, got)
    return jnp.transpose(out, (1, 0, 2))


def solution(mesh):
    return jax.shard_map(
        per_device,
        mesh=mesh,
        in_specs=(
            P(("groups", "lat"), "lon", "chan"),
            P("lat", None),
            P("lat"),
            P("lat"),
            P("lat", None, None, None),
            P(),
        ),
        out_specs=P(("groups", "lat"), "lon", "chan"),
        check_vma=False,
    )
```

```python
import functools

import jax
import jax.numpy as jnp
from jax import lax
from jax.experimental import pallas as pl
from jax.experimental.pallas import tpu as pltpu
from jax.sharding import PartitionSpec as P

LAYERS = 2
SPAN = 2
HALO = LAYERS * SPAN
BLOCK = 16
WINDOW = 2 * BLOCK
GROUP = 4
PAIR = 2
WIDE = BLOCK
SHIFT = BLOCK // 2
VMEM_LIMIT = 48 * 1024 * 1024
BF16 = jnp.bfloat16
F32 = jnp.float32


def vmem():
    return pl.BlockSpec(memory_space=pltpu.VMEM)


def smem():
    return pl.BlockSpec(memory_space=pltpu.SMEM)


def hbm():
    return pl.BlockSpec(memory_space=pltpu.HBM)


def in_hbm(x):
    return pltpu.with_memory_space_constraint(x, pltpu.HBM)


def toeplitz(rows_tab):
    count, _ = rows_tab.shape
    moved = jnp.concatenate(
        [rows_tab if jj == 0 else pltpu.roll(rows_tab, jj, 1) for jj in range(BLOCK)], axis=0
    ).astype(BF16)
    total = count * BLOCK
    out_row = lax.broadcasted_iota(jnp.int32, (total, total), 0)
    in_row = lax.broadcasted_iota(jnp.int32, (total, total), 1)
    source = (out_row % BLOCK) * count + out_row // BLOCK
    order = (in_row == source).astype(F32).astype(BF16)
    return jnp.dot(order, moved, preferred_element_type=F32).astype(BF16)


def neighbour_rows(sides, lat_rows):
    if sides == 1:
        return [(1 - lax.axis_index("lat")) * (lat_rows - HALO)]
    return [lat_rows - HALO, 0]


def band_rows(refs, slots, rows):
    sup_ref, count_ref, reach_ref, psi_ref = refs
    lat_rows, sup, basis, offsets = psi_ref.shape
    lanes = slots.shape[3]
    slots[...] = jnp.zeros_like(slots)
    for n, i in enumerate(rows):
        row = lax.axis_index("lat") * lat_rows + i
        values = [psi_ref[i, s] for s in range(sup)]
        places = [jnp.where(s < count_ref[i], sup_ref[i, s] - row, -lat_rows) for s in range(sup)]
        for rel in range(2 * SPAN + 1):
            total = jnp.zeros((basis, offsets), F32)
            for value, at in zip(values, places):
                total = total + jnp.where(at == rel - SPAN, value, 0.0)
            slots[n, rel, :, 0:offsets] = total
    off = lax.broadcasted_iota(jnp.int32, (basis, lanes), 1) % WINDOW - offsets // 2
    bands = []
    for n, i in enumerate(rows):
        band = slots[n, 0]
        for rel in range(1, 2 * SPAN + 1):
            band = band + pltpu.roll(slots[n, rel], rel * WINDOW, 1)
        bands.append(jnp.where(jnp.abs(off) <= reach_ref[i], band, 0.0))
    return bands


def put_pair(scr, bands):
    for m, band in enumerate(bands):
        basis = band.shape[0]
        scr[m * basis : (m + 1) * basis, :] = (
            band if m == 0 else pltpu.roll(band, m * WINDOW, 1)
        )


def own_kernel(sides, half, *refs):
    sources, refs = refs[:5], refs[5:]
    dests, refs = refs[:5], refs[5:]
    same_refs, cross_refs, refs = refs[:sides], refs[sides : 2 * sides], refs[2 * sides :]
    smems, (slots, pair_scr, wide_scr, sems) = refs[:3], refs[3:]
    copies = [
        pltpu.make_async_copy(source, dest, sems.at[n])
        for n, (source, dest) in enumerate(
            list(zip(sources[:3], smems)) + list(zip(sources, dests))
        )
    ]
    for copy in copies:
        copy.start()
    psi_ref, state_ref = dests[3:]
    cols, lat_rows, width = state_ref.shape
    basis = psi_ref.shape[2]
    part = cross_refs[0].shape[1]
    lanes = pair_scr.shape[1]
    chan = lax.axis_index("chan")
    padded = wide_scr.shape[0] // lat_rows
    wide_scr[cols * lat_rows :, :] = jnp.zeros(((padded - cols) * lat_rows, width), F32)
    for copy in copies[:7]:
        copy.wait()
    firsts = neighbour_rows(sides, lat_rows)
    if sides == 1:
        edges = [(1 - lax.axis_index("lat")) * (lat_rows - PAIR)]
    else:
        edges = [lat_rows - PAIR, 0]
    rows = [first + m for first in edges for m in range(PAIR)]
    bands = band_rows((*smems, psi_ref), slots, rows)
    for n in range(sides):
        put_pair(pair_scr, bands[n * PAIR : (n + 1) * PAIR])
        per = PAIR * basis // HALO
        for t in range(HALO):
            extra = [
                pair_scr[per * t + q : per * t + q + 1, x : x + width]
                for q in range(per)
                for x in range(0, lanes, width)
            ]
            same_refs[n][t, part:, :] = jnp.concatenate(extra, axis=0).astype(BF16)
    copies[7].wait()
    wide_scr[0 : cols * lat_rows, :] = state_ref[...].astype(F32).reshape(cols * lat_rows, width)
    step = (half - WIDE) * lat_rows
    for n, first in enumerate(firsts):
        for t in range(HALO):
            for dest, core in ((same_refs[n], chan), (cross_refs[n], 1 - chan)):
                dest[t, 0:part, :] = wide_scr[
                    pl.ds(step * core + first + t, part, stride=lat_rows), :
                ].astype(BF16)


def edges_kernel(sides, half, own_ref, other_ref, fields_ref, lon_ref, *rest):
    corner_refs, (wide_scr,) = rest[:sides], rest[sides:]
    cols, lat_rows, width = other_ref.shape
    lon_total = fields_ref.shape[1]
    part = half + WIDE
    chan = lax.axis_index("chan")
    padded = wide_scr.shape[1] // lat_rows
    wide_scr[:, cols * lat_rows :, :] = jnp.zeros((2, (padded - cols) * lat_rows, width), F32)

    def build(core):
        start = 0 if core == 0 else half - WIDE
        edge = 0 if core == 0 else cols - WIDE
        stop = start + part if core == 0 else cols
        at = WIDE if core == 0 else 0
        for c, ref in ((core, own_ref), (1 - core, other_ref)):
            lane = slice(c * width, (c + 1) * width)
            wide_scr[c, start * lat_rows : stop * lat_rows, :] = (
                ref[start:stop].astype(F32).reshape((stop - start) * lat_rows, width)
            )
            for r in range(lat_rows):
                lon_ref[r, :, lane] = wide_scr[
                    c, pl.ds(edge * lat_rows + r, WIDE, stride=lat_rows), :
                ].astype(BF16)
                fields_ref[r, at : at + part, lane] = wide_scr[
                    c, pl.ds(start * lat_rows + r, part, stride=lat_rows), :
                ].astype(BF16)
        empty = slice(0, WIDE) if core == 0 else slice(part, lon_total)
        fields_ref[:, empty, :] = jnp.zeros((lat_rows, WIDE, 2 * width), BF16)

    @pl.when(chan == 0)
    def _():
        build(0)

    @pl.when(chan == 1)
    def _():
        build(1)

    for n, first in enumerate(neighbour_rows(sides, lat_rows)):
        for t in range(HALO):
            corner_refs[n][t] = lon_ref[first + t]


def tables_kernel(
    sides,
    sup_ref,
    count_ref,
    reach_ref,
    psi_ref,
    weights_hbm,
    tables_ref,
    weights_ref,
    slots,
    pairs_scr,
    sem,
):
    fetch = pltpu.make_async_copy(weights_hbm, weights_ref, sem)
    fetch.start()
    lat_rows = psi_ref.shape[0]
    lat = lax.axis_index("lat")
    bands = band_rows((sup_ref, count_ref, reach_ref, psi_ref), slots, range(lat_rows))
    pairs = lat_rows // PAIR
    for p in range(pairs):
        put_pair(pairs_scr.at[p], bands[p * PAIR : (p + 1) * PAIR])

    def group(g):
        first, second = pairs_scr[2 * g], pairs_scr[2 * g + 1]
        return jnp.concatenate([first, pltpu.roll(second, PAIR * WINDOW, 1)], axis=0)

    if sides == 1:
        tables_ref[0] = toeplitz(group(lat))
        tables_ref[1] = toeplitz(group(1 - lat))
        mid, near = pairs_scr[2 - lat], pairs_scr[(pairs - 1) * (1 - lat)]
        tables_ref[2] = toeplitz(jnp.concatenate([mid, near], axis=0))
    else:
        for g in range(lat_rows // GROUP):
            tables_ref[g] = toeplitz(group(g))
    fetch.wait()


def gelu(x):
    return 0.5 * x * (1.0 + jnp.tanh(0.7978845608028654 * (x + 0.044715 * (x * x * x))))


def add_lat_halo(rows, same, cross):
    chan = lax.axis_index("chan")
    _, part, width = cross.shape
    at = pl.ds(pl.multiple_of((1 - chan) * WIDE, WIDE), part)
    own = pl.ds(pl.multiple_of(chan * width, width), width)
    other = pl.ds(pl.multiple_of((1 - chan) * width, width), width)
    for t, row in enumerate(rows):
        row[at, own] = same[t, 0:part, :]
        row[at, other] = cross[t]


def halo_table(same, basis):
    count, total, width = same.shape
    per = PAIR * basis // count
    first = total - per * (GROUP + 2 * SPAN) * WINDOW // width
    lanes = (total - first) // per
    rows = []
    for t in range(count):
        flat = same[t, first:total, :].astype(F32)
        for q in range(per):
            parts = [flat[q * lanes + x : q * lanes + x + 1, :] for x in range(lanes)]
            rows.append(jnp.concatenate(parts, axis=1))
    return toeplitz(jnp.concatenate(rows, axis=0))


def add_lon_halo(cols, half, rows, halos):
    chan = lax.axis_index("chan")
    count = cols - half + WIDE
    whole = count // BLOCK * BLOCK

    @pl.when(chan == 0)
    def _():
        for row, halo in zip(rows, halos):
            row[0:WIDE, :] = halo[...]

    @pl.when(chan == 1)
    def _():
        for row, halo in zip(rows, halos):
            lon_total, chans = row.shape
            before = row[whole : whole + BLOCK, :].astype(F32)[0 : count - whole, :]
            empty = jnp.zeros((lon_total - count - WIDE, chans), F32)
            row[whole:lon_total, :] = jnp.concatenate(
                [before, halo[...].astype(F32), empty], axis=0
            ).astype(BF16)


def conv(source, table, base, in_rows, feats, first, out_rows, at):
    chans = source.shape[2]
    basis = table.shape[0] // (out_rows * BLOCK)
    taken = source[pl.ds(base, in_rows), at : at + WINDOW, :]
    taken = taken.reshape(in_rows * WINDOW, chans)
    result = jnp.dot(table, taken, preferred_element_type=F32).astype(BF16)
    for m in range(out_rows):
        for k in range(basis):
            begin = (m * basis + k) * BLOCK
            feats[first + m, at : at + BLOCK, k * chans : (k + 1) * chans] = result[
                begin : begin + BLOCK, :
            ]


def mix(weights_ref, layer, feats, row, lons, before):
    _, basis, chans, _ = weights_ref.shape
    mixed = jnp.dot(
        feats[row, 0:lons, :],
        weights_ref[layer].reshape(basis * chans, chans),
        preferred_element_type=F32,
    )
    return before[...].astype(F32)[SHIFT : SHIFT + lons, :] + gelu(mixed)


def place(turned, done, row, lat_rows):
    half, chans = done.shape
    width = chans // 2
    for c in range(2):
        turned[c, pl.ds(row, half, stride=lat_rows), :] = done[:, c * width : (c + 1) * width]


def hand_out(turned, keep_ref, send_ref, far_keep_ref=None, far_send_ref=None):
    chan = lax.axis_index("chan")
    keep = turned[chan].reshape(keep_ref.shape)
    send = turned[1 - chan].reshape(send_ref.shape)
    if far_keep_ref is not None:
        keep = keep + far_keep_ref[...].astype(F32)
        send = send + far_send_ref[...].astype(F32)
    keep_ref[...] = keep.astype(BF16)
    send_ref[...] = send.astype(BF16)


def far1_kernel(
    half,
    cols,
    own_ref,
    lon_ref,
    tables_ref,
    weights_ref,
    ext_ref,
    next_ref,
    fields,
    feats,
):
    lat_rows, lon_total, chans = own_ref.shape
    lat = lax.axis_index("lat")
    lon1 = lon_total - BLOCK

    for t in range(SPAN):
        fields[t] = jnp.zeros((lon_total, chans), BF16)
        fields[SPAN + lat_rows + t] = jnp.zeros((lon_total, chans), BF16)
    fields[SPAN : SPAN + lat_rows] = own_ref[...]
    add_lon_halo(
        cols,
        half,
        [fields.at[SPAN + r] for r in range(lat_rows)],
        [lon_ref.at[r] for r in range(lat_rows)],
    )
    ext_ref[...] = fields[SPAN : SPAN + lat_rows]

    far = GROUP * lat
    mid = GROUP - PAIR * lat
    rows6 = PAIR + 2 * SPAN
    for jb in range(lon1 // BLOCK):
        at = jb * BLOCK
        conv(fields, tables_ref[0], far, GROUP + 2 * SPAN, feats, 0, GROUP, at)
        table = tables_ref[2, 0 : tables_ref.shape[1] // 2, 0 : rows6 * WINDOW]
        conv(fields, table, mid, rows6, feats, GROUP, PAIR, at)
    for t in range(SPAN):
        next_ref[(GROUP + SPAN) * lat + t] = jnp.zeros((lon1, chans), BF16)
    for t in range(GROUP):
        next_ref[SPAN + t] = mix(
            weights_ref, 0, feats, t, lon1, fields.at[SPAN + far + t]
        ).astype(BF16)
    for t in range(PAIR):
        next_ref[(GROUP + SPAN) * (1 - lat) + t] = mix(
            weights_ref, 0, feats, GROUP + t, lon1, fields.at[SPAN + mid + t]
        ).astype(BF16)


def far2_kernel(half, next_ref, tables_ref, weights_ref, keep_ref, send_ref, feats, turned):
    lat_rows = next_ref.shape[0]
    lat = lax.axis_index("lat")
    turned[...] = jnp.zeros_like(turned)
    for jb in range(half // BLOCK):
        conv(next_ref, tables_ref[0], 0, GROUP + 2 * SPAN, feats, 0, GROUP, jb * BLOCK)
    for t in range(GROUP):
        done = mix(weights_ref, 1, feats, t, half, next_ref.at[SPAN + t])
        place(turned, done, GROUP * lat + t, lat_rows)
    hand_out(turned, keep_ref, send_ref)


def near_kernel(
    half,
    cols,
    ext_ref,
    next_ref,
    same_ref,
    cross_ref,
    corner_ref,
    tables_ref,
    weights_ref,
    far_keep_ref,
    far_send_ref,
    keep_ref,
    send_ref,
    fields,
    near,
    feats,
    turned,
):
    lat_rows, lon_total, chans = ext_ref.shape
    basis = weights_ref.shape[1]
    lat = lax.axis_index("lat")
    lon1 = lon_total - BLOCK
    rows6 = PAIR + 2 * SPAN
    turned[...] = jnp.zeros_like(turned)

    halo = HALO * (1 - lat)
    own = HALO * lat
    for t in range(HALO):
        fields[own + t] = ext_ref[HALO * (1 - lat) + t]
    add_lat_halo([fields.at[halo + t] for t in range(HALO)], same_ref, cross_ref)
    add_lon_halo(
        cols,
        half,
        [fields.at[halo + t] for t in range(HALO)],
        [corner_ref.at[t] for t in range(HALO)],
    )
    beyond_table = halo_table(same_ref, basis)[:, 0 : rows6 * WINDOW]
    last_table = tables_ref[2, tables_ref.shape[1] // 2 :, 0 : rows6 * WINDOW]
    last = SPAN * lat
    beyond = SPAN * (1 - lat)
    for jb in range(lon1 // BLOCK):
        conv(fields, last_table, last, rows6, feats, 0, PAIR, jb * BLOCK)
        conv(fields, beyond_table, beyond, rows6, feats, PAIR, PAIR, jb * BLOCK)
    for t in range(GROUP):
        near[GROUP * lat + t] = next_ref[GROUP * (1 - lat) + t]
    for t in range(PAIR):
        near[GROUP * (1 - lat) + SPAN * lat + t] = mix(
            weights_ref, 0, feats, t, lon1, fields.at[SPAN + last + t]
        ).astype(BF16)
        near[(GROUP + SPAN) * (1 - lat) + t] = mix(
            weights_ref, 0, feats, PAIR + t, lon1, fields.at[SPAN + beyond + t]
        ).astype(BF16)
    for jb in range(half // BLOCK):
        conv(near, tables_ref[1], 0, GROUP + 2 * SPAN, feats, 0, GROUP, jb * BLOCK)
    for t in range(GROUP):
        done = mix(weights_ref, 1, feats, t, half, near.at[SPAN + t])
        place(turned, done, GROUP * (1 - lat) + t, lat_rows)
    hand_out(turned, keep_ref, send_ref, far_keep_ref, far_send_ref)


def all_kernel(half, cols, own_ref, lon_ref, *rest):
    same_refs, cross_refs, corner_refs = rest[:2], rest[2:4], rest[4:6]
    tables_ref, weights_ref, keep_ref, send_ref, fields, feats, after, turned = rest[6:]
    lat_rows, lon_total, chans = own_ref.shape
    basis = weights_ref.shape[1]
    groups = lat_rows // GROUP
    lon1 = lon_total - BLOCK
    halo_base = [0, lat_rows + HALO]
    win_base = [0, lat_rows + HALO - SPAN]
    out_base = [0, lat_rows + SPAN]
    rows6 = PAIR + 2 * SPAN

    fields[HALO : HALO + lat_rows] = own_ref[...]
    rows = [fields.at[HALO + r] for r in range(lat_rows)]
    halos = [lon_ref.at[r] for r in range(lat_rows)]
    for n in range(2):
        halo_rows = [fields.at[halo_base[n] + t] for t in range(HALO)]
        add_lat_halo(halo_rows, same_refs[n], cross_refs[n])
        rows += halo_rows
        halos += [corner_refs[n].at[t] for t in range(HALO)]
    add_lon_halo(cols, half, rows, halos)
    halo_tables = [halo_table(same_refs[n], basis)[:, 0 : rows6 * WINDOW] for n in range(2)]
    for jb in range(lon1 // BLOCK):
        at = jb * BLOCK
        for g in range(groups):
            base = HALO - SPAN + g * GROUP
            conv(
                fields, tables_ref[g], base, GROUP + 2 * SPAN, feats, g * GROUP, GROUP, at
            )
        for n in range(2):
            first = lat_rows + n * PAIR
            conv(fields, halo_tables[n], win_base[n], rows6, feats, first, PAIR, at)
    for i in range(lat_rows):
        after[SPAN + i] = mix(weights_ref, 0, feats, i, lon1, fields.at[HALO + i]).astype(BF16)
    for n in range(2):
        for m in range(PAIR):
            dest = out_base[n] + m
            after[dest] = mix(
                weights_ref, 0, feats, lat_rows + n * PAIR + m, lon1, fields.at[dest + SPAN]
            ).astype(BF16)
    for jb in range(half // BLOCK):
        for g in range(groups):
            base = g * GROUP
            conv(
                after, tables_ref[g], base, GROUP + 2 * SPAN, feats, base, GROUP, jb * BLOCK
            )
    for i in range(lat_rows):
        done = mix(weights_ref, 1, feats, i, half, after.at[SPAN + i])
        place(turned, done, i, lat_rows)
    hand_out(turned, keep_ref, send_ref)


def join_kernel(keep_ref, got_ref, out_hbm, sems):
    half = keep_ref.shape[0]
    rest = out_hbm.shape[0] - half
    chan = lax.axis_index("chan")

    def copy(first, second):
        copies = [
            pltpu.make_async_copy(first, out_hbm.at[0:half], sems.at[0]),
            pltpu.make_async_copy(second.at[0:rest], out_hbm.at[half : half + rest], sems.at[1]),
        ]
        for c in copies:
            c.start()
        for c in copies:
            c.wait()

    @pl.when(chan == 0)
    def _():
        copy(keep_ref, got_ref)

    @pl.when(chan == 1)
    def _():
        copy(got_ref, keep_ref)


def per_device(state, sup_rows, sup_count, lon_reach, psi, weights):
    lat_rows, cols, width = state.shape
    basis = psi.shape[2]
    chans = weights.shape[2]
    lats, lons = lax.axis_size("lat"), lax.axis_size("lon")
    sides = 1 if lats == 2 else 2
    groups = lat_rows // GROUP
    lanes = (GROUP + 2 * SPAN) * WINDOW
    half = -(-cols // (2 * BLOCK)) * BLOCK
    part = half + WIDE
    lon_total = half + 2 * WIDE
    lon1 = lon_total - BLOCK
    tabs = groups + 1 if sides == 1 else groups
    swap = [(0, 1), (1, 0)]
    params = pltpu.CompilerParams(vmem_limit_bytes=VMEM_LIMIT)

    def shape(*dims):
        return jax.ShapeDtypeStruct(dims, BF16)

    def to_lat(step):
        if lats == 2:
            return [(a, 1 - a) for a in range(lats)]
        return [(a, a + step) for a in range(lats) if 0 <= a + step < lats]

    forth = [((z, 1), ((z + 1) % lons, 0)) for z in range(lons)]
    back = [((z, 0), ((z - 1) % lons, 1)) for z in range(lons)]
    to_lon = forth + back

    own = jnp.transpose(state, (1, 0, 2))
    other = lax.ppermute(own, "chan", swap)

    def to_cross(step):
        return [(a * 2 + c, b * 2 + 1 - c) for a, b in to_lat(step) for c in range(2)]

    def scratch(*dims):
        return pltpu.VMEM(dims, F32)

    slots = (2 * SPAN + 1, basis, lanes)
    padded = (half + part) * lat_rows
    extra = PAIR * basis * lanes // (HALO * width)
    inputs = [sup_rows, sup_count, lon_reach, psi, own]
    sent = pl.pallas_call(
        functools.partial(own_kernel, sides, half),
        out_shape=[jax.ShapeDtypeStruct(x.shape, x.dtype) for x in inputs]
        + [shape(HALO, part + extra, width)] * sides
        + [shape(HALO, part, width)] * sides,
        in_specs=[hbm()] * 5,
        out_specs=[vmem()] * (5 + 2 * sides),
        scratch_shapes=[pltpu.SMEM(x.shape, x.dtype) for x in inputs[:3]]
        + [
            scratch(sides * PAIR, *slots),
            scratch(PAIR * basis, lanes),
            scratch(padded, width),
            pltpu.SemaphoreType.DMA((8,)),
        ],
        compiler_params=params,
        name="own",
    )(*[in_hbm(x) for x in inputs])
    inputs, sames, crosses = sent[:5], sent[5 : 5 + sides], sent[5 + sides :]
    steps = [1, -1][:sides]
    sames = [lax.ppermute(x, "lat", to_lat(step)) for x, step in zip(sames, steps)]
    crosses = [
        lax.ppermute(x, ("lat", "chan"), to_cross(step)) for x, step in zip(crosses, steps)
    ]

    fields, lon_edge, *corners = pl.pallas_call(
        functools.partial(edges_kernel, sides, half),
        out_shape=[shape(lat_rows, lon_total, chans), shape(lat_rows, WIDE, chans)]
        + [shape(HALO, WIDE, chans)] * sides,
        in_specs=[vmem()] * 2,
        out_specs=[vmem()] * (2 + sides),
        scratch_shapes=[scratch(2, padded, width)],
        compiler_params=params,
        name="edges",
    )(inputs[4], other)
    lon_halo = lax.ppermute(
        lon_edge, ("lon", "chan"), [(z * 2 + c, y * 2 + d) for (z, c), (y, d) in to_lon]
    )
    corners = [
        lax.ppermute(
            x,
            ("lon", "lat", "chan"),
            [
                ((z * lats + a) * 2 + c, (y * lats + b) * 2 + d)
                for a, b in to_lat(step)
                for (z, c), (y, d) in to_lon
            ],
        )
        for x, step in zip(corners, steps)
    ]

    tables, weights_in = pl.pallas_call(
        functools.partial(tables_kernel, sides),
        out_shape=[shape(tabs, GROUP * basis * BLOCK, lanes), shape(*weights.shape)],
        in_specs=[smem()] * 3 + [vmem(), hbm()],
        out_specs=[vmem()] * 2,
        scratch_shapes=[
            scratch(lat_rows, *slots),
            scratch(lat_rows // PAIR, PAIR * basis, lanes),
            pltpu.SemaphoreType.DMA,
        ],
        compiler_params=params,
        name="tables",
    )(*inputs[:4], in_hbm(weights))

    piece = shape(half, lat_rows, width)
    turned = pltpu.VMEM((2, half * lat_rows, width), F32)
    if sides == 1:
        ext, after = pl.pallas_call(
            functools.partial(far1_kernel, half, cols),
            out_shape=[shape(lat_rows, lon_total, chans), shape(lat_rows, lon1, chans)],
            in_specs=[vmem()] * 4,
            out_specs=[vmem()] * 2,
            scratch_shapes=[
                pltpu.VMEM((lat_rows + 2 * SPAN, lon_total, chans), BF16),
                pltpu.VMEM((GROUP + PAIR, lon1, basis * chans), BF16),
            ],
            compiler_params=params,
            name="far_rows_1",
        )(fields, lon_halo, tables, weights_in)
        far_keep, far_send = pl.pallas_call(
            functools.partial(far2_kernel, half),
            out_shape=[piece] * 2,
            in_specs=[vmem()] * 3,
            out_specs=[vmem()] * 2,
            scratch_shapes=[pltpu.VMEM((GROUP, half, basis * chans), BF16), turned],
            compiler_params=params,
            name="far_rows_2",
        )(after, tables, weights_in)
        keep, send = pl.pallas_call(
            functools.partial(near_kernel, half, cols),
            out_shape=[piece] * 2,
            in_specs=[vmem()] * 9,
            out_specs=[vmem()] * 2,
            scratch_shapes=[
                pltpu.VMEM((2 * HALO, lon_total, chans), BF16),
                pltpu.VMEM((GROUP + 2 * SPAN, lon1, chans), BF16),
                pltpu.VMEM((GROUP, lon1, basis * chans), BF16),
                turned,
            ],
            compiler_params=params,
            name="near_rows",
        )(
            ext,
            after,
            sames[0],
            crosses[0],
            corners[0],
            tables,
            weights_in,
            far_keep,
            far_send,
        )
    else:
        keep, send = pl.pallas_call(
            functools.partial(all_kernel, half, cols),
            out_shape=[piece] * 2,
            in_specs=[vmem()] * (4 + 3 * sides),
            out_specs=[vmem()] * 2,
            scratch_shapes=[
                pltpu.VMEM((lat_rows + 2 * HALO, lon_total, chans), BF16),
                pltpu.VMEM((lat_rows + 2 * PAIR, lon1, basis * chans), BF16),
                pltpu.VMEM((lat_rows + 2 * SPAN, lon1, chans), BF16),
                turned,
            ],
            compiler_params=params,
            name="all_rows",
        )(fields, lon_halo, *sames, *crosses, *corners, tables, weights_in)
    got = lax.ppermute(send, "chan", swap)

    out = pl.pallas_call(
        join_kernel,
        out_shape=shape(cols, lat_rows, width),
        in_specs=[vmem()] * 2,
        out_specs=hbm(),
        scratch_shapes=[pltpu.SemaphoreType.DMA((2,))],
        compiler_params=params,
        name="join",
    )(keep, got)
    return jnp.transpose(out, (1, 0, 2))


def solution(mesh):
    return jax.shard_map(
        per_device,
        mesh=mesh,
        in_specs=(
            P(("groups", "lat"), "lon", "chan"),
            P("lat", None),
            P("lat"),
            P("lat"),
            P("lat", None, None, None),
            P(),
        ),
        out_specs=P(("groups", "lat"), "lon", "chan"),
        check_vma=False,
    )
```

```python
import functools

import jax
import jax.numpy as jnp
from jax import lax
from jax.experimental import pallas as pl
from jax.experimental.pallas import tpu as pltpu
from jax.sharding import PartitionSpec as P

LAYERS = 2
SPAN = 2
HALO = LAYERS * SPAN
BLOCK = 16
WINDOW = 2 * BLOCK
GROUP = 4
PAIR = 2
WIDE = BLOCK
SHIFT = BLOCK // 2
VMEM_LIMIT = 48 * 1024 * 1024
BF16 = jnp.bfloat16
F32 = jnp.float32


def vmem():
    return pl.BlockSpec(memory_space=pltpu.VMEM)


def smem():
    return pl.BlockSpec(memory_space=pltpu.SMEM)


def hbm():
    return pl.BlockSpec(memory_space=pltpu.HBM)


def in_hbm(x):
    return pltpu.with_memory_space_constraint(x, pltpu.HBM)


def by_row(count):
    total = count * BLOCK
    out_row = lax.broadcasted_iota(jnp.int32, (total, total), 0)
    in_row = lax.broadcasted_iota(jnp.int32, (total, total), 1)
    source = (out_row % BLOCK) * count + out_row // BLOCK
    return (in_row == source).astype(F32).astype(BF16)


def toeplitz(rows_tab, order):
    moved = jnp.concatenate(
        [rows_tab if jj == 0 else pltpu.roll(rows_tab, jj, 1) for jj in range(BLOCK)], axis=0
    ).astype(BF16)
    return jnp.dot(order, moved, preferred_element_type=F32).astype(BF16)


def band_rows(refs, slots, rows):
    sup_ref, count_ref, reach_ref, psi_ref = refs
    lat_rows, sup, basis, offsets = psi_ref.shape
    lanes = slots.shape[3]
    slots[...] = jnp.zeros_like(slots)
    for n, i in enumerate(rows):
        row = lax.axis_index("lat") * lat_rows + i
        values = [psi_ref[i, s] for s in range(sup)]
        places = [jnp.where(s < count_ref[i], sup_ref[i, s] - row, -lat_rows) for s in range(sup)]
        for rel in range(2 * SPAN + 1):
            total = jnp.zeros((basis, offsets), F32)
            for value, at in zip(values, places):
                total = total + jnp.where(at == rel - SPAN, value, 0.0)
            slots[n, rel, :, 0:offsets] = total
    off = lax.broadcasted_iota(jnp.int32, (basis, lanes), 1) % WINDOW - offsets // 2
    bands = []
    for n, i in enumerate(rows):
        band = slots[n, 0]
        for rel in range(1, 2 * SPAN + 1):
            band = band + pltpu.roll(slots[n, rel], rel * WINDOW, 1)
        bands.append(jnp.where(jnp.abs(off) <= reach_ref[i], band, 0.0))
    return bands


def put_pair(scr, bands):
    for m, band in enumerate(bands):
        basis = band.shape[0]
        scr[m * basis : (m + 1) * basis, :] = (
            band if m == 0 else pltpu.roll(band, m * WINDOW, 1)
        )


def tables_kernel(sides, *refs):
    sources, refs = refs[:6], refs[6:]
    (state_ref, weights_ref, tables_ref, edges_ref, order_ref), refs = refs[:5], refs[5:]
    smems, (psi_ref, slots, pairs_scr, sems) = refs[:3], refs[3:]
    copies = [
        pltpu.make_async_copy(source, dest, sems.at[n])
        for n, (source, dest) in enumerate(
            zip(sources, (*smems, psi_ref, state_ref, weights_ref))
        )
    ]
    for copy in copies:
        copy.start()
    lat_rows, _, basis, _ = psi_ref.shape
    lat = lax.axis_index("lat")
    order = by_row(GROUP * basis)
    order_ref[...] = by_row(PAIR * basis)
    for copy in copies[:4]:
        copy.wait()
    bands = band_rows((*smems, psi_ref), slots, range(lat_rows))
    pairs = lat_rows // PAIR
    for p in range(pairs):
        put_pair(pairs_scr.at[p], bands[p * PAIR : (p + 1) * PAIR])

    def group(g):
        first, second = pairs_scr[2 * g], pairs_scr[2 * g + 1]
        return jnp.concatenate([first, pltpu.roll(second, PAIR * WINDOW, 1)], axis=0)

    if sides == 1:
        tables_ref[0] = toeplitz(group(lat), order)
        tables_ref[1] = toeplitz(group(1 - lat), order)
        mid, near = pairs_scr[2 - lat], pairs_scr[(pairs - 1) * (1 - lat)]
        tables_ref[2] = toeplitz(jnp.concatenate([mid, near], axis=0), order)
        edges = [near]
    else:
        for g in range(lat_rows // GROUP):
            tables_ref[g] = toeplitz(group(g), order)
        edges = [pairs_scr[pairs - 1], pairs_scr[0]]
    for n in range(sides):
        edges_ref[n] = jnp.concatenate([edges[n], jnp.zeros_like(edges[n])], axis=0).astype(BF16)
    for copy in copies[4:]:
        copy.wait()


def edges_kernel(sides, half, own_ref, other_ref, bands_ref, fields_ref, lon_ref, *rest):
    lat_refs, corner_refs, (wide_scr,) = rest[:sides], rest[sides : 2 * sides], rest[2 * sides :]
    cols, lat_rows, width = other_ref.shape
    lon_total = fields_ref.shape[1]
    part = half + WIDE
    chan = lax.axis_index("chan")
    padded = wide_scr.shape[1] // lat_rows
    wide_scr[:, cols * lat_rows :, :] = jnp.zeros((2, (padded - cols) * lat_rows, width), F32)

    def build(core):
        start = 0 if core == 0 else half - WIDE
        edge = 0 if core == 0 else cols - WIDE
        stop = start + part if core == 0 else cols
        at = WIDE if core == 0 else 0
        for c, ref in ((core, own_ref), (1 - core, other_ref)):
            lane = slice(c * width, (c + 1) * width)
            wide_scr[c, start * lat_rows : stop * lat_rows, :] = (
                ref[start:stop].astype(F32).reshape((stop - start) * lat_rows, width)
            )
            for r in range(lat_rows):
                lon_ref[r, :, lane] = wide_scr[
                    c, pl.ds(edge * lat_rows + r, WIDE, stride=lat_rows), :
                ].astype(BF16)
                fields_ref[r, at : at + part, lane] = wide_scr[
                    c, pl.ds(start * lat_rows + r, part, stride=lat_rows), :
                ].astype(BF16)
        empty = slice(0, WIDE) if core == 0 else slice(part, lon_total)
        fields_ref[:, empty, :] = jnp.zeros((lat_rows, WIDE, 2 * width), BF16)

    @pl.when(chan == 0)
    def _():
        build(0)

    @pl.when(chan == 1)
    def _():
        build(1)

    at = pl.multiple_of((1 - chan) * WIDE, WIDE)
    if sides == 1:
        firsts = [(1 - lax.axis_index("lat")) * (lat_rows - HALO)]
    else:
        firsts = [lat_rows - HALO, 0]
    for n, first in enumerate(firsts):
        per = lat_refs[n].shape[1] - part
        for t in range(HALO):
            lat_refs[n][t, 0:part, :] = fields_ref[first + t, pl.ds(at, part), :]
            lat_refs[n][t, part:, :] = bands_ref[n, per * t : per * (t + 1), :]
            corner_refs[n][t] = lon_ref[first + t]


def gelu(x):
    return 0.5 * x * (1.0 + jnp.tanh(0.7978845608028654 * (x + 0.044715 * (x * x * x))))


def add_lat_halo(rows, lat_ref, part):
    at = pl.ds(pl.multiple_of((1 - lax.axis_index("chan")) * WIDE, WIDE), part)
    for t, row in enumerate(rows):
        row[at, :] = lat_ref[t, 0:part, :]


def halo_table(lat_ref, part, order):
    rows = [lat_ref[t, part:, :].astype(F32) for t in range(lat_ref.shape[0])]
    return toeplitz(jnp.concatenate(rows, axis=0), order)


def add_lon_halo(cols, half, rows, halos):
    chan = lax.axis_index("chan")
    count = cols - half + WIDE
    whole = count // BLOCK * BLOCK

    @pl.when(chan == 0)
    def _():
        for row, halo in zip(rows, halos):
            row[0:WIDE, :] = halo[...]

    @pl.when(chan == 1)
    def _():
        for row, halo in zip(rows, halos):
            lon_total, chans = row.shape
            before = row[whole : whole + BLOCK, :].astype(F32)[0 : count - whole, :]
            empty = jnp.zeros((lon_total - count - WIDE, chans), F32)
            row[whole:lon_total, :] = jnp.concatenate(
                [before, halo[...].astype(F32), empty], axis=0
            ).astype(BF16)


def conv(source, table, base, in_rows, feats, first, out_rows, at):
    chans = source.shape[2]
    basis = table.shape[0] // (out_rows * BLOCK)
    taken = source[pl.ds(base, in_rows), at : at + WINDOW, :]
    taken = taken.reshape(in_rows * WINDOW, chans)
    result = jnp.dot(table, taken, preferred_element_type=F32).astype(BF16)
    for m in range(out_rows):
        for k in range(basis):
            begin = (m * basis + k) * BLOCK
            feats[first + m, at : at + BLOCK, k * chans : (k + 1) * chans] = result[
                begin : begin + BLOCK, :
            ]


def mix(weights_ref, layer, feats, row, lons, befores):
    _, basis, chans, _ = weights_ref.shape
    count = len(befores)
    mixed = jnp.dot(
        feats[row : row + count, 0:lons, :].reshape(count * lons, basis * chans),
        weights_ref[layer].reshape(basis * chans, chans),
        preferred_element_type=F32,
    )
    return [
        before[...].astype(F32)[SHIFT : SHIFT + lons, :] + gelu(mixed[n * lons : (n + 1) * lons])
        for n, before in enumerate(befores)
    ]


def place(turned, done, row, lat_rows):
    half, chans = done.shape
    width = chans // 2
    for c in range(2):
        turned[c, pl.ds(row, half, stride=lat_rows), :] = done[:, c * width : (c + 1) * width]


def hand_out(turned, keep_ref, send_ref, far_keep_ref=None, far_send_ref=None):
    chan = lax.axis_index("chan")
    keep = turned[chan].reshape(keep_ref.shape)
    send = turned[1 - chan].reshape(send_ref.shape)
    if far_keep_ref is not None:
        keep = keep + far_keep_ref[...].astype(F32)
        send = send + far_send_ref[...].astype(F32)
    keep_ref[...] = keep.astype(BF16)
    send_ref[...] = send.astype(BF16)


def far1_kernel(
    half,
    cols,
    own_ref,
    lon_ref,
    tables_ref,
    weights_ref,
    ext_ref,
    next_ref,
    fields,
    feats,
):
    lat_rows, lon_total, chans = own_ref.shape
    lat = lax.axis_index("lat")
    lon1 = lon_total - BLOCK

    for t in range(SPAN):
        fields[t] = jnp.zeros((lon_total, chans), BF16)
        fields[SPAN + lat_rows + t] = jnp.zeros((lon_total, chans), BF16)
    fields[SPAN : SPAN + lat_rows] = own_ref[...]
    add_lon_halo(
        cols,
        half,
        [fields.at[SPAN + r] for r in range(lat_rows)],
        [lon_ref.at[r] for r in range(lat_rows)],
    )
    ext_ref[...] = fields[SPAN : SPAN + lat_rows]

    far = GROUP * lat
    mid = GROUP - PAIR * lat
    rows6 = PAIR + 2 * SPAN
    for jb in range(lon1 // BLOCK):
        at = jb * BLOCK
        conv(fields, tables_ref[0], far, GROUP + 2 * SPAN, feats, 0, GROUP, at)
        table = tables_ref[2, 0 : tables_ref.shape[1] // 2, 0 : rows6 * WINDOW]
        conv(fields, table, mid, rows6, feats, GROUP, PAIR, at)
    for t in range(SPAN):
        next_ref[(GROUP + SPAN) * lat + t] = jnp.zeros((lon1, chans), BF16)
    dests = [SPAN + t for t in range(GROUP)]
    dests += [(GROUP + SPAN) * (1 - lat) + t for t in range(PAIR)]
    befores = [SPAN + far + t for t in range(GROUP)] + [SPAN + mid + t for t in range(PAIR)]
    for t in range(0, GROUP + PAIR, PAIR):
        done = mix(weights_ref, 0, feats, t, lon1, [fields.at[r] for r in befores[t : t + PAIR]])
        for dest, value in zip(dests[t : t + PAIR], done):
            next_ref[dest] = value.astype(BF16)


def far2_kernel(half, next_ref, tables_ref, weights_ref, keep_ref, send_ref, feats, turned):
    lat_rows = next_ref.shape[0]
    lat = lax.axis_index("lat")
    turned[...] = jnp.zeros_like(turned)
    for jb in range(half // BLOCK):
        conv(next_ref, tables_ref[0], 0, GROUP + 2 * SPAN, feats, 0, GROUP, jb * BLOCK)
    for t in range(0, GROUP, PAIR):
        befores = [next_ref.at[SPAN + t + m] for m in range(PAIR)]
        for m, done in enumerate(mix(weights_ref, 1, feats, t, half, befores)):
            place(turned, done, GROUP * lat + t + m, lat_rows)
    hand_out(turned, keep_ref, send_ref)


def near_kernel(
    half,
    cols,
    ext_ref,
    next_ref,
    lat_ref,
    corner_ref,
    tables_ref,
    weights_ref,
    order_ref,
    far_keep_ref,
    far_send_ref,
    keep_ref,
    send_ref,
    fields,
    near,
    feats,
    turned,
):
    lat_rows, lon_total, chans = ext_ref.shape
    lat = lax.axis_index("lat")
    lon1 = lon_total - BLOCK
    rows6 = PAIR + 2 * SPAN
    turned[...] = jnp.zeros_like(turned)

    halo = HALO * (1 - lat)
    own = HALO * lat
    for t in range(HALO):
        fields[own + t] = ext_ref[HALO * (1 - lat) + t]
    part = half + WIDE
    add_lat_halo([fields.at[halo + t] for t in range(HALO)], lat_ref, part)
    add_lon_halo(
        cols,
        half,
        [fields.at[halo + t] for t in range(HALO)],
        [corner_ref.at[t] for t in range(HALO)],
    )
    beyond_table = halo_table(lat_ref, part, order_ref[...])[:, 0 : rows6 * WINDOW]
    last_table = tables_ref[2, tables_ref.shape[1] // 2 :, 0 : rows6 * WINDOW]
    last = SPAN * lat
    beyond = SPAN * (1 - lat)
    for jb in range(lon1 // BLOCK):
        conv(fields, last_table, last, rows6, feats, 0, PAIR, jb * BLOCK)
        conv(fields, beyond_table, beyond, rows6, feats, PAIR, PAIR, jb * BLOCK)
    for t in range(GROUP):
        near[GROUP * lat + t] = next_ref[GROUP * (1 - lat) + t]
    for t, source, dest in (
        (0, last, GROUP * (1 - lat) + SPAN * lat),
        (PAIR, beyond, (GROUP + SPAN) * (1 - lat)),
    ):
        befores = [fields.at[SPAN + source + m] for m in range(PAIR)]
        for m, done in enumerate(mix(weights_ref, 0, feats, t, lon1, befores)):
            near[dest + m] = done.astype(BF16)
    for jb in range(half // BLOCK):
        conv(near, tables_ref[1], 0, GROUP + 2 * SPAN, feats, 0, GROUP, jb * BLOCK)
    for t in range(0, GROUP, PAIR):
        befores = [near.at[SPAN + t + m] for m in range(PAIR)]
        for m, done in enumerate(mix(weights_ref, 1, feats, t, half, befores)):
            place(turned, done, GROUP * (1 - lat) + t + m, lat_rows)
    hand_out(turned, keep_ref, send_ref, far_keep_ref, far_send_ref)


def all_kernel(half, cols, own_ref, lon_ref, *rest):
    lat_refs, corner_refs = rest[:2], rest[2:4]
    tables_ref, weights_ref, order_ref, keep_ref, send_ref, fields, feats, after, turned = rest[4:]
    lat_rows, lon_total, chans = own_ref.shape
    groups = lat_rows // GROUP
    lon1 = lon_total - BLOCK
    halo_base = [0, lat_rows + HALO]
    win_base = [0, lat_rows + HALO - SPAN]
    out_base = [0, lat_rows + SPAN]
    rows6 = PAIR + 2 * SPAN

    fields[HALO : HALO + lat_rows] = own_ref[...]
    rows = [fields.at[HALO + r] for r in range(lat_rows)]
    halos = [lon_ref.at[r] for r in range(lat_rows)]
    for n in range(2):
        halo_rows = [fields.at[halo_base[n] + t] for t in range(HALO)]
        add_lat_halo(halo_rows, lat_refs[n], half + WIDE)
        rows += halo_rows
        halos += [corner_refs[n].at[t] for t in range(HALO)]
    add_lon_halo(cols, half, rows, halos)
    halo_tables = [
        halo_table(lat_refs[n], half + WIDE, order_ref[...])[:, 0 : rows6 * WINDOW]
        for n in range(2)
    ]
    for jb in range(lon1 // BLOCK):
        at = jb * BLOCK
        for g in range(groups):
            base = HALO - SPAN + g * GROUP
            conv(
                fields, tables_ref[g], base, GROUP + 2 * SPAN, feats, g * GROUP, GROUP, at
            )
        for n in range(2):
            first = lat_rows + n * PAIR
            conv(fields, halo_tables[n], win_base[n], rows6, feats, first, PAIR, at)
    dests = [SPAN + i for i in range(lat_rows)]
    dests += [out_base[n] + m for n in range(2) for m in range(PAIR)]
    for i in range(0, len(dests), PAIR):
        befores = [fields.at[dest + SPAN] for dest in dests[i : i + PAIR]]
        done = mix(weights_ref, 0, feats, i, lon1, befores)
        for dest, value in zip(dests[i : i + PAIR], done):
            after[dest] = value.astype(BF16)
    for jb in range(half // BLOCK):
        for g in range(groups):
            base = g * GROUP
            conv(
                after, tables_ref[g], base, GROUP + 2 * SPAN, feats, base, GROUP, jb * BLOCK
            )
    for i in range(0, lat_rows, PAIR):
        befores = [after.at[SPAN + i + m] for m in range(PAIR)]
        for m, done in enumerate(mix(weights_ref, 1, feats, i, half, befores)):
            place(turned, done, i + m, lat_rows)
    hand_out(turned, keep_ref, send_ref)


def join_kernel(keep_ref, got_ref, out_hbm, sems):
    half = keep_ref.shape[0]
    rest = out_hbm.shape[0] - half
    chan = lax.axis_index("chan")

    def copy(first, second):
        copies = [
            pltpu.make_async_copy(first, out_hbm.at[0:half], sems.at[0]),
            pltpu.make_async_copy(second.at[0:rest], out_hbm.at[half : half + rest], sems.at[1]),
        ]
        for c in copies:
            c.start()
        for c in copies:
            c.wait()

    @pl.when(chan == 0)
    def _():
        copy(keep_ref, got_ref)

    @pl.when(chan == 1)
    def _():
        copy(got_ref, keep_ref)


def per_device(state, sup_rows, sup_count, lon_reach, psi, weights):
    lat_rows, cols, width = state.shape
    basis = psi.shape[2]
    chans = weights.shape[2]
    lats, lons = lax.axis_size("lat"), lax.axis_size("lon")
    sides = 1 if lats == 2 else 2
    groups = lat_rows // GROUP
    lanes = (GROUP + 2 * SPAN) * WINDOW
    half = -(-cols // (2 * BLOCK)) * BLOCK
    part = half + WIDE
    lon_total = half + 2 * WIDE
    lon1 = lon_total - BLOCK
    tabs = groups + 1 if sides == 1 else groups
    swap = [(0, 1), (1, 0)]
    params = pltpu.CompilerParams(vmem_limit_bytes=VMEM_LIMIT)

    def shape(*dims):
        return jax.ShapeDtypeStruct(dims, BF16)

    def to_lat(step):
        if lats == 2:
            return [(a, 1 - a) for a in range(lats)]
        return [(a, a + step) for a in range(lats) if 0 <= a + step < lats]

    forth = [((z, 1), ((z + 1) % lons, 0)) for z in range(lons)]
    back = [((z, 0), ((z - 1) % lons, 1)) for z in range(lons)]
    to_lon = forth + back

    own = jnp.transpose(state, (1, 0, 2))
    other = lax.ppermute(own, "chan", swap)

    def scratch(*dims):
        return pltpu.VMEM(dims, F32)

    inputs = [sup_rows, sup_count, lon_reach, psi, own, weights]
    state_in, weights_in, tables, bands, order = pl.pallas_call(
        functools.partial(tables_kernel, sides),
        out_shape=[
            shape(*own.shape),
            shape(*weights.shape),
            shape(tabs, GROUP * basis * BLOCK, lanes),
            shape(sides, GROUP * basis, lanes),
            shape(PAIR * basis * BLOCK, PAIR * basis * BLOCK),
        ],
        in_specs=[hbm()] * 6,
        out_specs=[vmem()] * 5,
        scratch_shapes=[pltpu.SMEM(x.shape, x.dtype) for x in inputs[:3]]
        + [
            scratch(*psi.shape),
            scratch(lat_rows, 2 * SPAN + 1, basis, lanes),
            scratch(lat_rows // PAIR, PAIR * basis, lanes),
            pltpu.SemaphoreType.DMA((6,)),
        ],
        compiler_params=params,
        name="tables",
    )(*[in_hbm(x) for x in inputs])

    extra = PAIR * basis // HALO
    fields, lon_edge, *sends = pl.pallas_call(
        functools.partial(edges_kernel, sides, half),
        out_shape=[shape(lat_rows, lon_total, chans), shape(lat_rows, WIDE, chans)]
        + [shape(HALO, part + extra, chans)] * sides
        + [shape(HALO, WIDE, chans)] * sides,
        in_specs=[vmem()] * 3,
        out_specs=[vmem()] * (2 + 2 * sides),
        scratch_shapes=[scratch(2, (half + part) * lat_rows, width)],
        compiler_params=params,
        name="edges",
    )(state_in, other, bands)

    steps = [1, -1][:sides]
    lat_halos = [lax.ppermute(x, "lat", to_lat(step)) for x, step in zip(sends, steps)]
    lon_halo = lax.ppermute(
        lon_edge, ("lon", "chan"), [(z * 2 + c, y * 2 + d) for (z, c), (y, d) in to_lon]
    )
    corners = [
        lax.ppermute(
            x,
            ("lon", "lat", "chan"),
            [
                ((z * lats + a) * 2 + c, (y * lats + b) * 2 + d)
                for a, b in to_lat(step)
                for (z, c), (y, d) in to_lon
            ],
        )
        for x, step in zip(sends[sides:], steps)
    ]

    piece = shape(half, lat_rows, width)
    turned = pltpu.VMEM((2, half * lat_rows, width), F32)
    if sides == 1:
        ext, after = pl.pallas_call(
            functools.partial(far1_kernel, half, cols),
            out_shape=[shape(lat_rows, lon_total, chans), shape(lat_rows, lon1, chans)],
            in_specs=[vmem()] * 4,
            out_specs=[vmem()] * 2,
            scratch_shapes=[
                pltpu.VMEM((lat_rows + 2 * SPAN, lon_total, chans), BF16),
                pltpu.VMEM((GROUP + PAIR, lon1, basis * chans), BF16),
            ],
            compiler_params=params,
            name="far_rows_1",
        )(fields, lon_halo, tables, weights_in)
        far_keep, far_send = pl.pallas_call(
            functools.partial(far2_kernel, half),
            out_shape=[piece] * 2,
            in_specs=[vmem()] * 3,
            out_specs=[vmem()] * 2,
            scratch_shapes=[pltpu.VMEM((GROUP, half, basis * chans), BF16), turned],
            compiler_params=params,
            name="far_rows_2",
        )(after, tables, weights_in)
        keep, send = pl.pallas_call(
            functools.partial(near_kernel, half, cols),
            out_shape=[piece] * 2,
            in_specs=[vmem()] * 9,
            out_specs=[vmem()] * 2,
            scratch_shapes=[
                pltpu.VMEM((2 * HALO, lon_total, chans), BF16),
                pltpu.VMEM((GROUP + 2 * SPAN, lon1, chans), BF16),
                pltpu.VMEM((GROUP, lon1, basis * chans), BF16),
                turned,
            ],
            compiler_params=params,
            name="near_rows",
        )(
            ext,
            after,
            lat_halos[0],
            corners[0],
            tables,
            weights_in,
            order,
            far_keep,
            far_send,
        )
    else:
        keep, send = pl.pallas_call(
            functools.partial(all_kernel, half, cols),
            out_shape=[piece] * 2,
            in_specs=[vmem()] * (5 + 2 * sides),
            out_specs=[vmem()] * 2,
            scratch_shapes=[
                pltpu.VMEM((lat_rows + 2 * HALO, lon_total, chans), BF16),
                pltpu.VMEM((lat_rows + 2 * PAIR, lon1, basis * chans), BF16),
                pltpu.VMEM((lat_rows + 2 * SPAN, lon1, chans), BF16),
                turned,
            ],
            compiler_params=params,
            name="all_rows",
        )(fields, lon_halo, *lat_halos, *corners, tables, weights_in, order)
    got = lax.ppermute(send, "chan", swap)

    out = pl.pallas_call(
        join_kernel,
        out_shape=shape(cols, lat_rows, width),
        in_specs=[vmem()] * 2,
        out_specs=hbm(),
        scratch_shapes=[pltpu.SemaphoreType.DMA((2,))],
        compiler_params=params,
        name="join",
    )(keep, got)
    return jnp.transpose(out, (1, 0, 2))


def solution(mesh):
    return jax.shard_map(
        per_device,
        mesh=mesh,
        in_specs=(
            P(("groups", "lat"), "lon", "chan"),
            P("lat", None),
            P("lat"),
            P("lat"),
            P("lat", None, None, None),
            P(),
        ),
        out_specs=P(("groups", "lat"), "lon", "chan"),
        check_vma=False,
    )
```

```python
import functools

import jax
import jax.numpy as jnp
from jax import lax
from jax.experimental import pallas as pl
from jax.experimental.pallas import tpu as pltpu
from jax.sharding import PartitionSpec as P

LAYERS = 2
SPAN = 2
HALO = LAYERS * SPAN
BLOCK = 16
WINDOW = 2 * BLOCK
GROUP = 4
PAIR = 2
WIDE = BLOCK
SHIFT = BLOCK // 2
VMEM_LIMIT = 48 * 1024 * 1024
BF16 = jnp.bfloat16
F32 = jnp.float32


def vmem():
    return pl.BlockSpec(memory_space=pltpu.VMEM)


def smem():
    return pl.BlockSpec(memory_space=pltpu.SMEM)


def hbm():
    return pl.BlockSpec(memory_space=pltpu.HBM)


def in_hbm(x):
    return pltpu.with_memory_space_constraint(x, pltpu.HBM)


def by_row(count):
    total = count * BLOCK
    out_row = lax.broadcasted_iota(jnp.int32, (total, total), 0)
    in_row = lax.broadcasted_iota(jnp.int32, (total, total), 1)
    source = (out_row % BLOCK) * count + out_row // BLOCK
    return (in_row == source).astype(F32).astype(BF16)


def toeplitz(rows_tab, order):
    moved = jnp.concatenate(
        [rows_tab if jj == 0 else pltpu.roll(rows_tab, jj, 1) for jj in range(BLOCK)], axis=0
    ).astype(BF16)
    return jnp.dot(order, moved, preferred_element_type=F32).astype(BF16)


def band_rows(refs, slots, rows):
    sup_ref, count_ref, reach_ref, psi_ref = refs
    lat_rows, sup, basis, offsets = psi_ref.shape
    lanes = slots.shape[3]
    slots[...] = jnp.zeros_like(slots)
    for n, i in enumerate(rows):
        row = lax.axis_index("lat") * lat_rows + i
        values = [psi_ref[i, s] for s in range(sup)]
        places = [jnp.where(s < count_ref[i], sup_ref[i, s] - row, -lat_rows) for s in range(sup)]
        for rel in range(2 * SPAN + 1):
            total = jnp.zeros((basis, offsets), F32)
            for value, at in zip(values, places):
                total = total + jnp.where(at == rel - SPAN, value, 0.0)
            slots[n, rel, :, 0:offsets] = total
    off = lax.broadcasted_iota(jnp.int32, (basis, lanes), 1) % WINDOW - offsets // 2
    bands = []
    for n, i in enumerate(rows):
        band = slots[n, 0]
        for rel in range(1, 2 * SPAN + 1):
            band = band + pltpu.roll(slots[n, rel], rel * WINDOW, 1)
        bands.append(jnp.where(jnp.abs(off) <= reach_ref[i], band, 0.0))
    return bands


def put_pair(scr, bands):
    for m, band in enumerate(bands):
        basis = band.shape[0]
        scr[m * basis : (m + 1) * basis, :] = (
            band if m == 0 else pltpu.roll(band, m * WINDOW, 1)
        )


def turn(ref, lon_from, lon_to, wide_scr):
    _, lat_rows, width = ref.shape
    wide_scr[lon_from * lat_rows : lon_to * lat_rows, :] = (
        ref[lon_from:lon_to].astype(F32).reshape((lon_to - lon_from) * lat_rows, width)
    )


def turned_row(wide_scr, lat_rows, row, start, count):
    return wide_scr[pl.ds(start * lat_rows + row, count, stride=lat_rows), :].astype(BF16)


def own_kernel(half, state_hbm, part_ref, edge_ref, state_ref, wide_scr, sem):
    fetch = pltpu.make_async_copy(state_hbm, state_ref, sem)
    fetch.start()
    cols, lat_rows, width = state_ref.shape
    part = part_ref.shape[1]
    chan = lax.axis_index("chan")
    wide_scr[cols * lat_rows :, :] = jnp.zeros(
        (wide_scr.shape[0] - cols * lat_rows, width), F32
    )
    fetch.wait()
    turn(state_ref, 0, cols, wide_scr)
    for r in range(lat_rows):
        part_ref[r] = turned_row(wide_scr, lat_rows, r, (half - WIDE) * chan, part)
        edge_ref[r] = turned_row(wide_scr, lat_rows, r, (cols - WIDE) * chan, WIDE)


def edges_kernel(
    sides, half, part_ref, edge_ref, other_ref, fields_ref, lon_ref, *rest
):
    lat_refs, (wide_scr,) = rest[:sides], rest[sides:]
    cols, lat_rows, width = other_ref.shape
    lon_total = fields_ref.shape[1]
    part = part_ref.shape[1]
    chan = lax.axis_index("chan")
    wide_scr[cols * lat_rows :, :] = jnp.zeros(
        (wide_scr.shape[0] - cols * lat_rows, width), F32
    )

    def build(core):
        start = 0 if core == 0 else half - WIDE
        edge = 0 if core == 0 else cols - WIDE
        stop = start + part if core == 0 else cols
        at = WIDE if core == 0 else 0
        own = slice(core * width, (core + 1) * width)
        lane = slice((1 - core) * width, (2 - core) * width)
        turn(other_ref, start, stop, wide_scr)
        for r in range(lat_rows):
            lon_ref[r, :, own] = edge_ref[r]
            lon_ref[r, :, lane] = turned_row(wide_scr, lat_rows, r, edge, WIDE)
            fields_ref[r, at : at + part, own] = part_ref[r]
            fields_ref[r, at : at + part, lane] = turned_row(wide_scr, lat_rows, r, start, part)
        empty = slice(0, WIDE) if core == 0 else slice(part, lon_total)
        fields_ref[:, empty, :] = jnp.zeros((lat_rows, WIDE, 2 * width), BF16)

    @pl.when(chan == 0)
    def _():
        build(0)

    @pl.when(chan == 1)
    def _():
        build(1)

    at = pl.multiple_of((1 - chan) * WIDE, WIDE)
    for n, first in enumerate(needed_rows(sides, lat_rows)):
        for t in range(HALO):
            lat_refs[n][t] = fields_ref[first + t, pl.ds(at, part), :]


def needed_rows(sides, lat_rows):
    if sides == 1:
        return [(1 - lax.axis_index("lat")) * (lat_rows - HALO)]
    return [lat_rows - HALO, 0]


def tables_kernel(sides, sup_hbm, count_hbm, reach_hbm, psi_hbm, weights_hbm, _, *refs):
    (weights_ref, tables_ref, edges_ref, order_ref), refs = refs[:4], refs[4:]
    smems, (psi_ref, slots, pairs_scr, sems) = refs[:3], refs[3:]
    sources = (sup_hbm, count_hbm, reach_hbm, psi_hbm, weights_hbm)
    copies = [
        pltpu.make_async_copy(source, dest, sems.at[n])
        for n, (source, dest) in enumerate(zip(sources, (*smems, psi_ref, weights_ref)))
    ]
    for copy in copies:
        copy.start()
    lat_rows, _, basis, _ = psi_ref.shape
    lat = lax.axis_index("lat")
    order = by_row(GROUP * basis)
    order_ref[...] = by_row(PAIR * basis)
    for copy in copies[:4]:
        copy.wait()
    bands = band_rows((*smems, psi_ref), slots, range(lat_rows))
    pairs = lat_rows // PAIR
    for p in range(pairs):
        put_pair(pairs_scr.at[p], bands[p * PAIR : (p + 1) * PAIR])

    def group(g):
        first, second = pairs_scr[2 * g], pairs_scr[2 * g + 1]
        return jnp.concatenate([first, pltpu.roll(second, PAIR * WINDOW, 1)], axis=0)

    if sides == 1:
        tables_ref[0] = toeplitz(group(lat), order)
        tables_ref[1] = toeplitz(group(1 - lat), order)
        mid, near = pairs_scr[2 - lat], pairs_scr[(pairs - 1) * (1 - lat)]
        tables_ref[2] = toeplitz(jnp.concatenate([mid, near], axis=0), order)
        edges = [near]
    else:
        for g in range(lat_rows // GROUP):
            tables_ref[g] = toeplitz(group(g), order)
        edges = [pairs_scr[pairs - 1], pairs_scr[0]]
    for n in range(sides):
        edges_ref[n] = jnp.concatenate([edges[n], jnp.zeros_like(edges[n])], axis=0).astype(BF16)
    copies[4].wait()


def corners_kernel(sides, lon_ref, bands_ref, *corner_refs):
    for n, first in enumerate(needed_rows(sides, lon_ref.shape[0])):
        for t in range(HALO):
            corner_refs[n][t] = lon_ref[first + t]
        corner_refs[n][HALO] = bands_ref[n]


def gelu(x):
    return 0.5 * x * (1.0 + jnp.tanh(0.7978845608028654 * (x + 0.044715 * (x * x * x))))


def add_lat_halo(rows, lat_ref):
    at = pl.ds(pl.multiple_of((1 - lax.axis_index("chan")) * WIDE, WIDE), lat_ref.shape[1])
    for t, row in enumerate(rows):
        row[at, :] = lat_ref[t]


def halo_table(corner_ref, order):
    count = order.shape[0] // BLOCK
    return toeplitz(corner_ref[HALO].astype(F32)[0:count, :], order)


def add_lon_halo(cols, half, rows, halos):
    chan = lax.axis_index("chan")
    count = cols - half + WIDE
    whole = count // BLOCK * BLOCK

    @pl.when(chan == 0)
    def _():
        for row, halo in zip(rows, halos):
            row[0:WIDE, :] = halo[...]

    @pl.when(chan == 1)
    def _():
        for row, halo in zip(rows, halos):
            lon_total, chans = row.shape
            before = row[whole : whole + BLOCK, :].astype(F32)[0 : count - whole, :]
            empty = jnp.zeros((lon_total - count - WIDE, chans), F32)
            row[whole:lon_total, :] = jnp.concatenate(
                [before, halo[...].astype(F32), empty], axis=0
            ).astype(BF16)


def conv(source, table, base, in_rows, feats, first, out_rows, at):
    chans = source.shape[2]
    basis = table.shape[0] // (out_rows * BLOCK)
    taken = source[pl.ds(base, in_rows), at : at + WINDOW, :]
    taken = taken.reshape(in_rows * WINDOW, chans)
    result = jnp.dot(table, taken, preferred_element_type=F32).astype(BF16)
    for m in range(out_rows):
        for k in range(basis):
            begin = (m * basis + k) * BLOCK
            feats[first + m, at : at + BLOCK, k * chans : (k + 1) * chans] = result[
                begin : begin + BLOCK, :
            ]


def mix(weights_ref, layer, feats, row, lons, befores):
    _, basis, chans, _ = weights_ref.shape
    count = len(befores)
    mixed = jnp.dot(
        feats[row : row + count, 0:lons, :].reshape(count * lons, basis * chans),
        weights_ref[layer].reshape(basis * chans, chans),
        preferred_element_type=F32,
    )
    return [
        before[...].astype(F32)[SHIFT : SHIFT + lons, :] + gelu(mixed[n * lons : (n + 1) * lons])
        for n, before in enumerate(befores)
    ]


def place(turned, done, row, lat_rows):
    half, chans = done.shape
    width = chans // 2
    for c in range(2):
        turned[c, pl.ds(row, half, stride=lat_rows), :] = done[:, c * width : (c + 1) * width]


def hand_out(turned, keep_ref, send_ref, far_keep_ref=None, far_send_ref=None):
    chan = lax.axis_index("chan")
    keep = turned[chan].reshape(keep_ref.shape)
    send = turned[1 - chan].reshape(send_ref.shape)
    if far_keep_ref is not None:
        keep = keep + far_keep_ref[...].astype(F32)
        send = send + far_send_ref[...].astype(F32)
    keep_ref[...] = keep.astype(BF16)
    send_ref[...] = send.astype(BF16)


def far1_kernel(
    half,
    cols,
    own_ref,
    lon_ref,
    tables_ref,
    weights_ref,
    ext_ref,
    next_ref,
    fields,
    feats,
):
    lat_rows, lon_total, chans = own_ref.shape
    lat = lax.axis_index("lat")
    lon1 = lon_total - BLOCK

    for t in range(SPAN):
        fields[t] = jnp.zeros((lon_total, chans), BF16)
        fields[SPAN + lat_rows + t] = jnp.zeros((lon_total, chans), BF16)
    fields[SPAN : SPAN + lat_rows] = own_ref[...]
    add_lon_halo(
        cols,
        half,
        [fields.at[SPAN + r] for r in range(lat_rows)],
        [lon_ref.at[r] for r in range(lat_rows)],
    )
    ext_ref[...] = fields[SPAN : SPAN + lat_rows]

    far = GROUP * lat
    mid = GROUP - PAIR * lat
    rows6 = PAIR + 2 * SPAN
    for jb in range(lon1 // BLOCK):
        at = jb * BLOCK
        conv(fields, tables_ref[0], far, GROUP + 2 * SPAN, feats, 0, GROUP, at)
        table = tables_ref[2, 0 : tables_ref.shape[1] // 2, 0 : rows6 * WINDOW]
        conv(fields, table, mid, rows6, feats, GROUP, PAIR, at)
    for t in range(SPAN):
        next_ref[(GROUP + SPAN) * lat + t] = jnp.zeros((lon1, chans), BF16)
    dests = [SPAN + t for t in range(GROUP)]
    dests += [(GROUP + SPAN) * (1 - lat) + t for t in range(PAIR)]
    befores = [SPAN + far + t for t in range(GROUP)] + [SPAN + mid + t for t in range(PAIR)]
    for t in range(0, GROUP + PAIR, PAIR):
        done = mix(weights_ref, 0, feats, t, lon1, [fields.at[r] for r in befores[t : t + PAIR]])
        for dest, value in zip(dests[t : t + PAIR], done):
            next_ref[dest] = value.astype(BF16)


def far2_kernel(half, next_ref, tables_ref, weights_ref, keep_ref, send_ref, feats, turned):
    lat_rows = next_ref.shape[0]
    lat = lax.axis_index("lat")
    turned[...] = jnp.zeros_like(turned)
    for jb in range(half // BLOCK):
        conv(next_ref, tables_ref[0], 0, GROUP + 2 * SPAN, feats, 0, GROUP, jb * BLOCK)
    for t in range(0, GROUP, PAIR):
        befores = [next_ref.at[SPAN + t + m] for m in range(PAIR)]
        for m, done in enumerate(mix(weights_ref, 1, feats, t, half, befores)):
            place(turned, done, GROUP * lat + t + m, lat_rows)
    hand_out(turned, keep_ref, send_ref)


def near_kernel(
    half,
    cols,
    ext_ref,
    next_ref,
    lat_ref,
    corner_ref,
    tables_ref,
    weights_ref,
    order_ref,
    far_keep_ref,
    far_send_ref,
    keep_ref,
    send_ref,
    fields,
    near,
    feats,
    turned,
):
    lat_rows, lon_total, chans = ext_ref.shape
    lat = lax.axis_index("lat")
    lon1 = lon_total - BLOCK
    rows6 = PAIR + 2 * SPAN
    turned[...] = jnp.zeros_like(turned)

    halo = HALO * (1 - lat)
    own = HALO * lat
    for t in range(HALO):
        fields[own + t] = ext_ref[HALO * (1 - lat) + t]
    add_lat_halo([fields.at[halo + t] for t in range(HALO)], lat_ref)
    add_lon_halo(
        cols,
        half,
        [fields.at[halo + t] for t in range(HALO)],
        [corner_ref.at[t] for t in range(HALO)],
    )
    beyond_table = halo_table(corner_ref, order_ref[...])[:, 0 : rows6 * WINDOW]
    last_table = tables_ref[2, tables_ref.shape[1] // 2 :, 0 : rows6 * WINDOW]
    last = SPAN * lat
    beyond = SPAN * (1 - lat)
    for jb in range(lon1 // BLOCK):
        conv(fields, last_table, last, rows6, feats, 0, PAIR, jb * BLOCK)
        conv(fields, beyond_table, beyond, rows6, feats, PAIR, PAIR, jb * BLOCK)
    for t in range(GROUP):
        near[GROUP * lat + t] = next_ref[GROUP * (1 - lat) + t]
    for t, source, dest in (
        (0, last, GROUP * (1 - lat) + SPAN * lat),
        (PAIR, beyond, (GROUP + SPAN) * (1 - lat)),
    ):
        befores = [fields.at[SPAN + source + m] for m in range(PAIR)]
        for m, done in enumerate(mix(weights_ref, 0, feats, t, lon1, befores)):
            near[dest + m] = done.astype(BF16)
    for jb in range(half // BLOCK):
        conv(near, tables_ref[1], 0, GROUP + 2 * SPAN, feats, 0, GROUP, jb * BLOCK)
    for t in range(0, GROUP, PAIR):
        befores = [near.at[SPAN + t + m] for m in range(PAIR)]
        for m, done in enumerate(mix(weights_ref, 1, feats, t, half, befores)):
            place(turned, done, GROUP * (1 - lat) + t + m, lat_rows)
    hand_out(turned, keep_ref, send_ref, far_keep_ref, far_send_ref)


def all_kernel(half, cols, own_ref, lon_ref, *rest):
    lat_refs, corner_refs = rest[:2], rest[2:4]
    tables_ref, weights_ref, order_ref, keep_ref, send_ref, fields, feats, after, turned = rest[4:]
    lat_rows, lon_total, chans = own_ref.shape
    groups = lat_rows // GROUP
    lon1 = lon_total - BLOCK
    halo_base = [0, lat_rows + HALO]
    win_base = [0, lat_rows + HALO - SPAN]
    out_base = [0, lat_rows + SPAN]
    rows6 = PAIR + 2 * SPAN

    fields[HALO : HALO + lat_rows] = own_ref[...]
    rows = [fields.at[HALO + r] for r in range(lat_rows)]
    halos = [lon_ref.at[r] for r in range(lat_rows)]
    for n in range(2):
        halo_rows = [fields.at[halo_base[n] + t] for t in range(HALO)]
        add_lat_halo(halo_rows, lat_refs[n])
        rows += halo_rows
        halos += [corner_refs[n].at[t] for t in range(HALO)]
    add_lon_halo(cols, half, rows, halos)
    halo_tables = [
        halo_table(corner_refs[n], order_ref[...])[:, 0 : rows6 * WINDOW] for n in range(2)
    ]
    for jb in range(lon1 // BLOCK):
        at = jb * BLOCK
        for g in range(groups):
            base = HALO - SPAN + g * GROUP
            conv(
                fields, tables_ref[g], base, GROUP + 2 * SPAN, feats, g * GROUP, GROUP, at
            )
        for n in range(2):
            first = lat_rows + n * PAIR
            conv(fields, halo_tables[n], win_base[n], rows6, feats, first, PAIR, at)
    dests = [SPAN + i for i in range(lat_rows)]
    dests += [out_base[n] + m for n in range(2) for m in range(PAIR)]
    for i in range(0, len(dests), PAIR):
        befores = [fields.at[dest + SPAN] for dest in dests[i : i + PAIR]]
        done = mix(weights_ref, 0, feats, i, lon1, befores)
        for dest, value in zip(dests[i : i + PAIR], done):
            after[dest] = value.astype(BF16)
    for jb in range(half // BLOCK):
        for g in range(groups):
            base = g * GROUP
            conv(
                after, tables_ref[g], base, GROUP + 2 * SPAN, feats, base, GROUP, jb * BLOCK
            )
    for i in range(0, lat_rows, PAIR):
        befores = [after.at[SPAN + i + m] for m in range(PAIR)]
        for m, done in enumerate(mix(weights_ref, 1, feats, i, half, befores)):
            place(turned, done, i + m, lat_rows)
    hand_out(turned, keep_ref, send_ref)


def join_kernel(keep_ref, got_ref, out_hbm, sems):
    half = keep_ref.shape[0]
    rest = out_hbm.shape[0] - half
    chan = lax.axis_index("chan")

    def copy(first, second):
        copies = [
            pltpu.make_async_copy(first, out_hbm.at[0:half], sems.at[0]),
            pltpu.make_async_copy(second.at[0:rest], out_hbm.at[half : half + rest], sems.at[1]),
        ]
        for c in copies:
            c.start()
        for c in copies:
            c.wait()

    @pl.when(chan == 0)
    def _():
        copy(keep_ref, got_ref)

    @pl.when(chan == 1)
    def _():
        copy(got_ref, keep_ref)


def per_device(state, sup_rows, sup_count, lon_reach, psi, weights):
    lat_rows, cols, width = state.shape
    basis = psi.shape[2]
    chans = weights.shape[2]
    lats, lons = lax.axis_size("lat"), lax.axis_size("lon")
    sides = 1 if lats == 2 else 2
    groups = lat_rows // GROUP
    lanes = (GROUP + 2 * SPAN) * WINDOW
    half = -(-cols // (2 * BLOCK)) * BLOCK
    part = half + WIDE
    lon_total = half + 2 * WIDE
    lon1 = lon_total - BLOCK
    tabs = groups + 1 if sides == 1 else groups
    swap = [(0, 1), (1, 0)]
    params = pltpu.CompilerParams(vmem_limit_bytes=VMEM_LIMIT)

    def shape(*dims):
        return jax.ShapeDtypeStruct(dims, BF16)

    def to_lat(step):
        if lats == 2:
            return [(a, 1 - a) for a in range(lats)]
        return [(a, a + step) for a in range(lats) if 0 <= a + step < lats]

    forth = [((z, 1), ((z + 1) % lons, 0)) for z in range(lons)]
    back = [((z, 0), ((z - 1) % lons, 1)) for z in range(lons)]
    to_lon = forth + back

    own = jnp.transpose(state, (1, 0, 2))
    other = lax.ppermute(own, "chan", swap)

    def scratch(*dims):
        return pltpu.VMEM(dims, F32)

    wide = scratch((half + part) * lat_rows, width)
    part_own, edge_own = pl.pallas_call(
        functools.partial(own_kernel, half),
        out_shape=[shape(lat_rows, part, width), shape(lat_rows, WIDE, width)],
        in_specs=[hbm()],
        out_specs=[vmem()] * 2,
        scratch_shapes=[pltpu.VMEM(own.shape, BF16), wide, pltpu.SemaphoreType.DMA],
        compiler_params=params,
        name="own",
    )(in_hbm(own))

    fields, lon_edge, *lat_edges = pl.pallas_call(
        functools.partial(edges_kernel, sides, half),
        out_shape=[shape(lat_rows, lon_total, chans), shape(lat_rows, WIDE, chans)]
        + [shape(HALO, part, chans)] * sides,
        in_specs=[vmem()] * 3,
        out_specs=[vmem()] * (2 + sides),
        scratch_shapes=[wide],
        compiler_params=params,
        name="edges",
    )(part_own, edge_own, other)

    steps = [1, -1][:sides]
    lat_halos = [lax.ppermute(x, "lat", to_lat(step)) for x, step in zip(lat_edges, steps)]
    lon_halo = lax.ppermute(
        lon_edge, ("lon", "chan"), [(z * 2 + c, y * 2 + d) for (z, c), (y, d) in to_lon]
    )

    inputs = [sup_rows, sup_count, lon_reach, psi, weights]
    weights_in, tables, bands, order = pl.pallas_call(
        functools.partial(tables_kernel, sides),
        out_shape=[
            shape(*weights.shape),
            shape(tabs, GROUP * basis * BLOCK, lanes),
            shape(sides, GROUP * basis, lanes),
            shape(PAIR * basis * BLOCK, PAIR * basis * BLOCK),
        ],
        in_specs=[hbm()] * 5 + [vmem()],
        out_specs=[vmem()] * 4,
        scratch_shapes=[pltpu.SMEM(x.shape, x.dtype) for x in inputs[:3]]
        + [
            scratch(*psi.shape),
            scratch(lat_rows, 2 * SPAN + 1, basis, lanes),
            scratch(lat_rows // PAIR, PAIR * basis, lanes),
            pltpu.SemaphoreType.DMA((5,)),
        ],
        compiler_params=params,
        name="tables",
    )(*[in_hbm(x) for x in inputs], lon_edge)

    corners = pl.pallas_call(
        functools.partial(corners_kernel, sides),
        out_shape=[shape(HALO + 1, WIDE, chans)] * sides,
        in_specs=[vmem()] * 2,
        out_specs=[vmem()] * sides,
        compiler_params=params,
        name="corners",
    )(lon_halo, bands)
    corners = [lax.ppermute(x, "lat", to_lat(step)) for x, step in zip(corners, steps)]

    piece = shape(half, lat_rows, width)
    turned = pltpu.VMEM((2, half * lat_rows, width), F32)
    if sides == 1:
        ext, after = pl.pallas_call(
            functools.partial(far1_kernel, half, cols),
            out_shape=[shape(lat_rows, lon_total, chans), shape(lat_rows, lon1, chans)],
            in_specs=[vmem()] * 4,
            out_specs=[vmem()] * 2,
            scratch_shapes=[
                pltpu.VMEM((lat_rows + 2 * SPAN, lon_total, chans), BF16),
                pltpu.VMEM((GROUP + PAIR, lon1, basis * chans), BF16),
            ],
            compiler_params=params,
            name="far_rows_1",
        )(fields, lon_halo, tables, weights_in)
        far_keep, far_send = pl.pallas_call(
            functools.partial(far2_kernel, half),
            out_shape=[piece] * 2,
            in_specs=[vmem()] * 3,
            out_specs=[vmem()] * 2,
            scratch_shapes=[pltpu.VMEM((GROUP, half, basis * chans), BF16), turned],
            compiler_params=params,
            name="far_rows_2",
        )(after, tables, weights_in)
        keep, send = pl.pallas_call(
            functools.partial(near_kernel, half, cols),
            out_shape=[piece] * 2,
            in_specs=[vmem()] * 9,
            out_specs=[vmem()] * 2,
            scratch_shapes=[
                pltpu.VMEM((2 * HALO, lon_total, chans), BF16),
                pltpu.VMEM((GROUP + 2 * SPAN, lon1, chans), BF16),
                pltpu.VMEM((GROUP, lon1, basis * chans), BF16),
                turned,
            ],
            compiler_params=params,
            name="near_rows",
        )(
            ext,
            after,
            lat_halos[0],
            corners[0],
            tables,
            weights_in,
            order,
            far_keep,
            far_send,
        )
    else:
        keep, send = pl.pallas_call(
            functools.partial(all_kernel, half, cols),
            out_shape=[piece] * 2,
            in_specs=[vmem()] * (5 + 2 * sides),
            out_specs=[vmem()] * 2,
            scratch_shapes=[
                pltpu.VMEM((lat_rows + 2 * HALO, lon_total, chans), BF16),
                pltpu.VMEM((lat_rows + 2 * PAIR, lon1, basis * chans), BF16),
                pltpu.VMEM((lat_rows + 2 * SPAN, lon1, chans), BF16),
                turned,
            ],
            compiler_params=params,
            name="all_rows",
        )(fields, lon_halo, *lat_halos, *corners, tables, weights_in, order)
    got = lax.ppermute(send, "chan", swap)

    out = pl.pallas_call(
        join_kernel,
        out_shape=shape(cols, lat_rows, width),
        in_specs=[vmem()] * 2,
        out_specs=hbm(),
        scratch_shapes=[pltpu.SemaphoreType.DMA((2,))],
        compiler_params=params,
        name="join",
    )(keep, got)
    return jnp.transpose(out, (1, 0, 2))


def solution(mesh):
    return jax.shard_map(
        per_device,
        mesh=mesh,
        in_specs=(
            P(("groups", "lat"), "lon", "chan"),
            P("lat", None),
            P("lat"),
            P("lat"),
            P("lat", None, None, None),
            P(),
        ),
        out_specs=P(("groups", "lat"), "lon", "chan"),
        check_vma=False,
    )
```

```python
import functools

import jax
import jax.numpy as jnp
from jax import lax
from jax.experimental import pallas as pl
from jax.experimental.pallas import tpu as pltpu
from jax.sharding import PartitionSpec as P

LAYERS = 2
SPAN = 2
HALO = LAYERS * SPAN
BLOCK = 16
WINDOW = 2 * BLOCK
GROUP = 4
PAIR = 2
WIDE = BLOCK
SHIFT = BLOCK // 2
VMEM_LIMIT = 48 * 1024 * 1024
BF16 = jnp.bfloat16
F32 = jnp.float32


def vmem():
    return pl.BlockSpec(memory_space=pltpu.VMEM)


def smem():
    return pl.BlockSpec(memory_space=pltpu.SMEM)


def hbm():
    return pl.BlockSpec(memory_space=pltpu.HBM)


def in_hbm(x):
    return pltpu.with_memory_space_constraint(x, pltpu.HBM)


def by_row(count):
    total = count * BLOCK
    out_row = lax.broadcasted_iota(jnp.int32, (total, total), 0)
    in_row = lax.broadcasted_iota(jnp.int32, (total, total), 1)
    source = (out_row % BLOCK) * count + out_row // BLOCK
    return (in_row == source).astype(F32).astype(BF16)


def toeplitz(rows_tab, order):
    moved = jnp.concatenate(
        [rows_tab if jj == 0 else pltpu.roll(rows_tab, jj, 1) for jj in range(BLOCK)], axis=0
    ).astype(BF16)
    return jnp.dot(order, moved, preferred_element_type=F32).astype(BF16)


def band_rows(refs, slots, rows):
    sup_ref, count_ref, reach_ref, psi_ref = refs
    lat_rows, sup, basis, offsets = psi_ref.shape
    lanes = slots.shape[3]
    slots[...] = jnp.zeros_like(slots)
    for n, i in enumerate(rows):
        row = lax.axis_index("lat") * lat_rows + i
        values = [psi_ref[i, s] for s in range(sup)]
        places = [jnp.where(s < count_ref[i], sup_ref[i, s] - row, -lat_rows) for s in range(sup)]
        for rel in range(2 * SPAN + 1):
            total = jnp.zeros((basis, offsets), F32)
            for value, at in zip(values, places):
                total = total + jnp.where(at == rel - SPAN, value, 0.0)
            slots[n, rel, :, 0:offsets] = total
    off = lax.broadcasted_iota(jnp.int32, (basis, lanes), 1) % WINDOW - offsets // 2
    bands = []
    for n, i in enumerate(rows):
        band = slots[n, 0]
        for rel in range(1, 2 * SPAN + 1):
            band = band + pltpu.roll(slots[n, rel], rel * WINDOW, 1)
        bands.append(jnp.where(jnp.abs(off) <= reach_ref[i], band, 0.0))
    return bands


def put_pair(scr, bands):
    for m, band in enumerate(bands):
        basis = band.shape[0]
        scr[m * basis : (m + 1) * basis, :] = (
            band if m == 0 else pltpu.roll(band, m * WINDOW, 1)
        )


def turn(ref, lon_from, lon_to, wide_scr):
    _, lat_rows, width = ref.shape
    wide_scr[lon_from * lat_rows : lon_to * lat_rows, :] = (
        ref[lon_from:lon_to].astype(F32).reshape((lon_to - lon_from) * lat_rows, width)
    )


def turned_row(wide_scr, lat_rows, row, start, count):
    return wide_scr[pl.ds(start * lat_rows + row, count, stride=lat_rows), :].astype(BF16)


def own_kernel(sides, half, *refs):
    sources, (part_ref, edge_ref, bands_ref), refs = refs[:5], refs[5:8], refs[8:]
    smems, (psi_ref, state_ref, slots, pair_scr, wide_scr, sems) = refs[:3], refs[3:]
    copies = [
        pltpu.make_async_copy(source, dest, sems.at[n])
        for n, (source, dest) in enumerate(zip(sources, (*smems, psi_ref, state_ref)))
    ]
    for copy in copies:
        copy.start()
    cols, lat_rows, width = state_ref.shape
    part = part_ref.shape[1]
    chan = lax.axis_index("chan")
    wide_scr[cols * lat_rows :, :] = jnp.zeros(
        (wide_scr.shape[0] - cols * lat_rows, width), F32
    )
    for copy in copies[:4]:
        copy.wait()
    firsts = [first + (HALO - PAIR) * (n == 0) for n, first in enumerate(needed_rows(2, lat_rows))]
    if sides == 1:
        firsts = [(1 - lax.axis_index("lat")) * (lat_rows - PAIR)]
    rows = [first + m for first in firsts for m in range(PAIR)]
    bands = band_rows((*smems, psi_ref), slots, rows)
    for n in range(sides):
        put_pair(pair_scr, bands[n * PAIR : (n + 1) * PAIR])
        bands_ref[n] = pair_scr[...].astype(BF16)
    copies[4].wait()
    turn(state_ref, 0, cols, wide_scr)
    for r in range(lat_rows):
        part_ref[r] = turned_row(wide_scr, lat_rows, r, (half - WIDE) * chan, part)
        edge_ref[r] = turned_row(wide_scr, lat_rows, r, (cols - WIDE) * chan, WIDE)


def edges_kernel(
    sides, half, part_ref, edge_ref, other_ref, bands_ref, fields_ref, lon_ref, *rest
):
    lat_refs, corner_refs, (wide_scr,) = rest[:sides], rest[sides : 2 * sides], rest[2 * sides :]
    cols, lat_rows, width = other_ref.shape
    lon_total = fields_ref.shape[1]
    part = part_ref.shape[1]
    chan = lax.axis_index("chan")
    wide_scr[cols * lat_rows :, :] = jnp.zeros(
        (wide_scr.shape[0] - cols * lat_rows, width), F32
    )

    def build(core):
        start = 0 if core == 0 else half - WIDE
        edge = 0 if core == 0 else cols - WIDE
        stop = start + part if core == 0 else cols
        at = WIDE if core == 0 else 0
        own = slice(core * width, (core + 1) * width)
        lane = slice((1 - core) * width, (2 - core) * width)
        turn(other_ref, start, stop, wide_scr)
        for r in range(lat_rows):
            lon_ref[r, :, own] = edge_ref[r]
            lon_ref[r, :, lane] = turned_row(wide_scr, lat_rows, r, edge, WIDE)
            fields_ref[r, at : at + part, own] = part_ref[r]
            fields_ref[r, at : at + part, lane] = turned_row(wide_scr, lat_rows, r, start, part)
        empty = slice(0, WIDE) if core == 0 else slice(part, lon_total)
        fields_ref[:, empty, :] = jnp.zeros((lat_rows, WIDE, 2 * width), BF16)

    @pl.when(chan == 0)
    def _():
        build(0)

    @pl.when(chan == 1)
    def _():
        build(1)

    at = pl.multiple_of((1 - chan) * WIDE, WIDE)
    for n, first in enumerate(needed_rows(sides, lat_rows)):
        for t in range(HALO):
            lat_refs[n][t * part : (t + 1) * part, :] = fields_ref[first + t, pl.ds(at, part), :]
            corner_refs[n][t] = lon_ref[first + t]
        lat_refs[n][HALO * part :, :] = bands_ref[n]


def needed_rows(sides, lat_rows):
    if sides == 1:
        return [(1 - lax.axis_index("lat")) * (lat_rows - HALO)]
    return [lat_rows - HALO, 0]


def tables_kernel(sides, sup_hbm, count_hbm, reach_hbm, psi_hbm, weights_hbm, _, *refs):
    (weights_ref, tables_ref, order_ref), refs = refs[:3], refs[3:]
    smems, (psi_ref, slots, pairs_scr, sems) = refs[:3], refs[3:]
    sources = (sup_hbm, count_hbm, reach_hbm, psi_hbm, weights_hbm)
    copies = [
        pltpu.make_async_copy(source, dest, sems.at[n])
        for n, (source, dest) in enumerate(zip(sources, (*smems, psi_ref, weights_ref)))
    ]
    for copy in copies:
        copy.start()
    lat_rows, _, basis, _ = psi_ref.shape
    lat = lax.axis_index("lat")
    order = by_row(GROUP * basis)
    order_ref[...] = by_row(PAIR * basis)
    for copy in copies[:4]:
        copy.wait()
    bands = band_rows((*smems, psi_ref), slots, range(lat_rows))
    pairs = lat_rows // PAIR
    for p in range(pairs):
        put_pair(pairs_scr.at[p], bands[p * PAIR : (p + 1) * PAIR])

    def group(g):
        first, second = pairs_scr[2 * g], pairs_scr[2 * g + 1]
        return jnp.concatenate([first, pltpu.roll(second, PAIR * WINDOW, 1)], axis=0)

    if sides == 1:
        tables_ref[0] = toeplitz(group(lat), order)
        tables_ref[1] = toeplitz(group(1 - lat), order)
        mid, near = pairs_scr[2 - lat], pairs_scr[(pairs - 1) * (1 - lat)]
        tables_ref[2] = toeplitz(jnp.concatenate([mid, near], axis=0), order)
    else:
        for g in range(lat_rows // GROUP):
            tables_ref[g] = toeplitz(group(g), order)
    copies[4].wait()


def gelu(x):
    return 0.5 * x * (1.0 + jnp.tanh(0.7978845608028654 * (x + 0.044715 * (x * x * x))))


def add_lat_halo(rows, lat_ref, part):
    at = pl.ds(pl.multiple_of((1 - lax.axis_index("chan")) * WIDE, WIDE), part)
    for t, row in enumerate(rows):
        row[at, :] = lat_ref[t * part : (t + 1) * part, :]


def halo_table(lat_ref, order):
    count = order.shape[0] // BLOCK
    return toeplitz(lat_ref[lat_ref.shape[0] - count :, :].astype(F32), order)


def add_lon_halo(cols, half, rows, halos):
    chan = lax.axis_index("chan")
    count = cols - half + WIDE
    whole = count // BLOCK * BLOCK

    @pl.when(chan == 0)
    def _():
        for row, halo in zip(rows, halos):
            row[0:WIDE, :] = halo[...]

    @pl.when(chan == 1)
    def _():
        for row, halo in zip(rows, halos):
            lon_total, chans = row.shape
            before = row[whole : whole + BLOCK, :].astype(F32)[0 : count - whole, :]
            empty = jnp.zeros((lon_total - count - WIDE, chans), F32)
            row[whole:lon_total, :] = jnp.concatenate(
                [before, halo[...].astype(F32), empty], axis=0
            ).astype(BF16)


def conv(source, table, base, in_rows, feats, first, out_rows, jb, put):
    chans = source.shape[2]
    basis = table.shape[0] // (out_rows * BLOCK)
    taken = source[pl.ds(base, in_rows), jb * BLOCK : jb * BLOCK + WINDOW, :]
    taken = taken.reshape(in_rows * WINDOW, chans)
    result = jnp.dot(table, taken, preferred_element_type=F32).astype(BF16)
    at = slice(put * BLOCK, (put + 1) * BLOCK)
    for m in range(out_rows):
        for k in range(basis):
            begin = (m * basis + k) * BLOCK
            feats[first + m, at, k * chans : (k + 1) * chans] = result[begin : begin + BLOCK, :]


def mix(weights_ref, layer, feats, row, blocks, befores, store):
    _, basis, chans, _ = weights_ref.shape
    count, lons = len(befores), len(blocks) * BLOCK
    mixed = jnp.dot(
        feats[row : row + count, 0:lons, :].reshape(count * lons, basis * chans),
        weights_ref[layer].reshape(basis * chans, chans),
        preferred_element_type=F32,
    )
    for n, before in enumerate(befores):
        before = before[...].astype(F32)
        for put, jb in enumerate(blocks):
            at, begin = SHIFT + jb * BLOCK, n * lons + put * BLOCK
            value = before[at : at + BLOCK, :] + gelu(mixed[begin : begin + BLOCK, :])
            store(n, jb, value)


def into(ref, rows):
    def store(n, jb, value):
        ref[rows[n], jb * BLOCK : (jb + 1) * BLOCK, :] = value.astype(BF16)

    return store


def into_turned(turned, rows, lat_rows):
    def store(n, jb, value):
        width = value.shape[1] // 2
        for c in range(2):
            turned[c, pl.ds(jb * BLOCK * lat_rows + rows[n], BLOCK, stride=lat_rows), :] = value[
                :, c * width : (c + 1) * width
            ]

    return store


def hand_out(turned, keep_ref, send_ref):
    chan = lax.axis_index("chan")
    keep_ref[...] = turned[chan].reshape(keep_ref.shape).astype(BF16)
    send_ref[...] = turned[1 - chan].reshape(send_ref.shape).astype(BF16)


def far1_kernel(
    half,
    cols,
    own_ref,
    lon_ref,
    tables_ref,
    weights_ref,
    ext_ref,
    next_ref,
    fields,
    feats,
):
    lat_rows, lon_total, chans = own_ref.shape
    lat = lax.axis_index("lat")
    lon1 = lon_total - BLOCK

    for t in range(SPAN):
        fields[t] = jnp.zeros((lon_total, chans), BF16)
        fields[SPAN + lat_rows + t] = jnp.zeros((lon_total, chans), BF16)
    fields[SPAN : SPAN + lat_rows] = own_ref[...]
    add_lon_halo(
        cols,
        half,
        [fields.at[SPAN + r] for r in range(lat_rows)],
        [lon_ref.at[r] for r in range(lat_rows)],
    )
    ext_ref[...] = fields[SPAN : SPAN + lat_rows]

    far = GROUP * lat
    mid = GROUP - PAIR * lat
    rows6 = PAIR + 2 * SPAN
    blocks = range(lon1 // BLOCK)
    for jb in blocks:
        conv(fields, tables_ref[0], far, GROUP + 2 * SPAN, feats, 0, GROUP, jb, jb)
        table = tables_ref[2, 0 : tables_ref.shape[1] // 2, 0 : rows6 * WINDOW]
        conv(fields, table, mid, rows6, feats, GROUP, PAIR, jb, jb)
    for t in range(SPAN):
        next_ref[(GROUP + SPAN) * lat + t] = jnp.zeros((lon1, chans), BF16)
    dests = [SPAN + t for t in range(GROUP)]
    dests += [(GROUP + SPAN) * (1 - lat) + t for t in range(PAIR)]
    befores = [SPAN + far + t for t in range(GROUP)] + [SPAN + mid + t for t in range(PAIR)]
    for t in range(0, GROUP + PAIR, PAIR):
        rows = [fields.at[r] for r in befores[t : t + PAIR]]
        mix(weights_ref, 0, feats, t, blocks, rows, into(next_ref, dests[t : t + PAIR]))


def far2_kernel(half, next_ref, tables_ref, weights_ref, turned_ref, feats):
    lat_rows = next_ref.shape[0]
    lat = lax.axis_index("lat")
    blocks = range(half // BLOCK)
    for jb in blocks:
        conv(next_ref, tables_ref[0], 0, GROUP + 2 * SPAN, feats, 0, GROUP, jb, jb)
    for t in range(0, GROUP, PAIR):
        befores = [next_ref.at[SPAN + t + m] for m in range(PAIR)]
        rows = [GROUP * lat + t + m for m in range(PAIR)]
        mix(weights_ref, 1, feats, t, blocks, befores, into_turned(turned_ref, rows, lat_rows))


def near_rows(fields, near, table, tables_ref, weights_ref, feats, turned, blocks1, blocks2):
    lat_rows = near.shape[0]
    lat = lax.axis_index("lat")
    rows6 = PAIR + 2 * SPAN
    last_table = tables_ref[2, tables_ref.shape[1] // 2 :, 0 : rows6 * WINDOW]
    last = SPAN * lat
    beyond = SPAN * (1 - lat)
    for put, jb in enumerate(blocks1):
        conv(fields, last_table, last, rows6, feats, 0, PAIR, jb, put)
        conv(fields, table[:, 0 : rows6 * WINDOW], beyond, rows6, feats, PAIR, PAIR, jb, put)
    starts = [last] * PAIR + [beyond] * PAIR
    befores = [fields.at[SPAN + start + n % PAIR] for n, start in enumerate(starts)]
    dests = [GROUP * (1 - lat) + SPAN * lat + m for m in range(PAIR)]
    dests += [(GROUP + SPAN) * (1 - lat) + m for m in range(PAIR)]
    mix(weights_ref, 0, feats, 0, blocks1, befores, into(near, dests))
    for put, jb in enumerate(blocks2):
        conv(near, tables_ref[1], 0, GROUP + 2 * SPAN, feats, 0, GROUP, jb, put)
    befores = [near.at[SPAN + t] for t in range(GROUP)]
    rows = [GROUP * (1 - lat) + t for t in range(GROUP)]
    mix(weights_ref, 1, feats, 0, blocks2, befores, into_turned(turned, rows, lat_rows))


def inner(count):
    return range(1, count - 2)


def outer(count):
    return [0, count - 2, count - 1]


def near1_kernel(
    half,
    ext_ref,
    next_ref,
    lat_ref,
    tables_ref,
    weights_ref,
    order_ref,
    turned_in,
    fields_ref,
    near_ref,
    table_ref,
    turned_ref,
    feats,
):
    lat_rows, lon_total, _ = ext_ref.shape
    lat = lax.axis_index("lat")
    halo = HALO * (1 - lat)
    own = HALO * lat
    for t in range(HALO):
        fields_ref[own + t] = ext_ref[HALO * (1 - lat) + t]
    add_lat_halo([fields_ref.at[halo + t] for t in range(HALO)], lat_ref, half + WIDE)
    table_ref[...] = halo_table(lat_ref, order_ref[...])
    for t in range(GROUP):
        near_ref[GROUP * lat + t] = next_ref[GROUP * (1 - lat) + t]
    near_rows(
        fields_ref,
        near_ref,
        table_ref,
        tables_ref,
        weights_ref,
        feats,
        turned_ref,
        inner(lon_total // BLOCK - 1),
        inner(half // BLOCK),
    )


def near2_kernel(
    half,
    cols,
    corner_ref,
    table_ref,
    tables_ref,
    weights_ref,
    fields_in,
    near_in,
    turned_in,
    fields_ref,
    near_ref,
    turned_ref,
    keep_ref,
    send_ref,
    feats,
):
    halo = HALO * (1 - lax.axis_index("lat"))
    add_lon_halo(
        cols,
        half,
        [fields_ref.at[halo + t] for t in range(HALO)],
        [corner_ref.at[t] for t in range(HALO)],
    )
    near_rows(
        fields_ref,
        near_ref,
        table_ref,
        tables_ref,
        weights_ref,
        feats,
        turned_ref,
        outer(fields_ref.shape[1] // BLOCK - 1),
        outer(half // BLOCK),
    )
    hand_out(turned_ref, keep_ref, send_ref)


def all_kernel(half, cols, own_ref, lon_ref, *rest):
    lat_refs, corner_refs = rest[:2], rest[2:4]
    tables_ref, weights_ref, order_ref, keep_ref, send_ref, fields, feats, after, turned = rest[4:]
    lat_rows, lon_total, chans = own_ref.shape
    groups = lat_rows // GROUP
    lon1 = lon_total - BLOCK
    halo_base = [0, lat_rows + HALO]
    win_base = [0, lat_rows + HALO - SPAN]
    out_base = [0, lat_rows + SPAN]
    rows6 = PAIR + 2 * SPAN

    fields[HALO : HALO + lat_rows] = own_ref[...]
    rows = [fields.at[HALO + r] for r in range(lat_rows)]
    halos = [lon_ref.at[r] for r in range(lat_rows)]
    for n in range(2):
        halo_rows = [fields.at[halo_base[n] + t] for t in range(HALO)]
        add_lat_halo(halo_rows, lat_refs[n], half + WIDE)
        rows += halo_rows
        halos += [corner_refs[n].at[t] for t in range(HALO)]
    add_lon_halo(cols, half, rows, halos)
    halo_tables = [
        halo_table(lat_refs[n], order_ref[...])[:, 0 : rows6 * WINDOW] for n in range(2)
    ]
    blocks = range(lon1 // BLOCK)
    for jb in blocks:
        for g in range(groups):
            base = HALO - SPAN + g * GROUP
            conv(
                fields, tables_ref[g], base, GROUP + 2 * SPAN, feats, g * GROUP, GROUP, jb, jb
            )
        for n in range(2):
            first = lat_rows + n * PAIR
            conv(fields, halo_tables[n], win_base[n], rows6, feats, first, PAIR, jb, jb)
    dests = [SPAN + i for i in range(lat_rows)]
    dests += [out_base[n] + m for n in range(2) for m in range(PAIR)]
    for i in range(0, len(dests), PAIR):
        befores = [fields.at[dest + SPAN] for dest in dests[i : i + PAIR]]
        mix(weights_ref, 0, feats, i, blocks, befores, into(after, dests[i : i + PAIR]))
    blocks = range(half // BLOCK)
    for jb in blocks:
        for g in range(groups):
            base = g * GROUP
            conv(after, tables_ref[g], base, GROUP + 2 * SPAN, feats, base, GROUP, jb, jb)
    for i in range(0, lat_rows, PAIR):
        befores = [after.at[SPAN + i + m] for m in range(PAIR)]
        rows = [i + m for m in range(PAIR)]
        mix(weights_ref, 1, feats, i, blocks, befores, into_turned(turned, rows, lat_rows))
    hand_out(turned, keep_ref, send_ref)


def join_kernel(keep_ref, got_ref, out_hbm, sems):
    half = keep_ref.shape[0]
    rest = out_hbm.shape[0] - half
    chan = lax.axis_index("chan")

    def copy(first, second):
        copies = [
            pltpu.make_async_copy(first, out_hbm.at[0:half], sems.at[0]),
            pltpu.make_async_copy(second.at[0:rest], out_hbm.at[half : half + rest], sems.at[1]),
        ]
        for c in copies:
            c.start()
        for c in copies:
            c.wait()

    @pl.when(chan == 0)
    def _():
        copy(keep_ref, got_ref)

    @pl.when(chan == 1)
    def _():
        copy(got_ref, keep_ref)


def per_device(state, sup_rows, sup_count, lon_reach, psi, weights):
    lat_rows, cols, width = state.shape
    basis = psi.shape[2]
    chans = weights.shape[2]
    lats, lons = lax.axis_size("lat"), lax.axis_size("lon")
    sides = 1 if lats == 2 else 2
    groups = lat_rows // GROUP
    lanes = (GROUP + 2 * SPAN) * WINDOW
    half = -(-cols // (2 * BLOCK)) * BLOCK
    part = half + WIDE
    lon_total = half + 2 * WIDE
    lon1 = lon_total - BLOCK
    tabs = groups + 1 if sides == 1 else groups
    swap = [(0, 1), (1, 0)]
    params = pltpu.CompilerParams(vmem_limit_bytes=VMEM_LIMIT)

    def shape(*dims):
        return jax.ShapeDtypeStruct(dims, BF16)

    def to_lat(step):
        if lats == 2:
            return [(a, 1 - a) for a in range(lats)]
        return [(a, a + step) for a in range(lats) if 0 <= a + step < lats]

    forth = [((z, 1), ((z + 1) % lons, 0)) for z in range(lons)]
    back = [((z, 0), ((z - 1) % lons, 1)) for z in range(lons)]
    to_lon = forth + back

    own = jnp.transpose(state, (1, 0, 2))
    other = lax.ppermute(own, "chan", swap)

    def scratch(*dims):
        return pltpu.VMEM(dims, F32)

    wide = scratch((half + part) * lat_rows, width)
    smalls = [sup_rows, sup_count, lon_reach]
    part_own, edge_own, bands = pl.pallas_call(
        functools.partial(own_kernel, sides, half),
        out_shape=[
            shape(lat_rows, part, width),
            shape(lat_rows, WIDE, width),
            shape(sides, PAIR * basis, lanes),
        ],
        in_specs=[hbm()] * 5,
        out_specs=[vmem()] * 3,
        scratch_shapes=[pltpu.SMEM(x.shape, x.dtype) for x in smalls]
        + [
            scratch(*psi.shape),
            pltpu.VMEM(own.shape, BF16),
            scratch(sides * PAIR, 2 * SPAN + 1, basis, lanes),
            scratch(PAIR * basis, lanes),
            wide,
            pltpu.SemaphoreType.DMA((5,)),
        ],
        compiler_params=params,
        name="own",
    )(*[in_hbm(x) for x in smalls + [psi, own]])

    fields, lon_edge, *sends = pl.pallas_call(
        functools.partial(edges_kernel, sides, half),
        out_shape=[shape(lat_rows, lon_total, chans), shape(lat_rows, WIDE, chans)]
        + [shape(HALO * part + PAIR * basis, chans)] * sides
        + [shape(HALO, WIDE, chans)] * sides,
        in_specs=[vmem()] * 4,
        out_specs=[vmem()] * (2 + 2 * sides),
        scratch_shapes=[wide],
        compiler_params=params,
        name="edges",
    )(part_own, edge_own, other, bands)

    steps = [1, -1][:sides]
    lat_halos = [lax.ppermute(x, "lat", to_lat(step)) for x, step in zip(sends, steps)]
    lon_halo = lax.ppermute(
        lon_edge, ("lon", "chan"), [(z * 2 + c, y * 2 + d) for (z, c), (y, d) in to_lon]
    )

    corners = [
        lax.ppermute(
            x,
            ("lon", "lat", "chan"),
            [
                ((z * lats + a) * 2 + c, (y * lats + b) * 2 + d)
                for a, b in to_lat(step)
                for (z, c), (y, d) in to_lon
            ],
        )
        for x, step in zip(sends[sides:], steps)
    ]

    weights_in, tables, order = pl.pallas_call(
        functools.partial(tables_kernel, sides),
        out_shape=[
            shape(*weights.shape),
            shape(tabs, GROUP * basis * BLOCK, lanes),
            shape(PAIR * basis * BLOCK, PAIR * basis * BLOCK),
        ],
        in_specs=[hbm()] * 5 + [vmem()],
        out_specs=[vmem()] * 3,
        scratch_shapes=[pltpu.SMEM(x.shape, x.dtype) for x in smalls]
        + [
            scratch(*psi.shape),
            scratch(lat_rows, 2 * SPAN + 1, basis, lanes),
            scratch(lat_rows // PAIR, PAIR * basis, lanes),
            pltpu.SemaphoreType.DMA((5,)),
        ],
        compiler_params=params,
        name="tables",
    )(*[in_hbm(x) for x in smalls + [psi, weights]], lon_edge)

    piece = shape(half, lat_rows, width)
    turned = (2, half * lat_rows, width)
    if sides == 1:
        ext, after = pl.pallas_call(
            functools.partial(far1_kernel, half, cols),
            out_shape=[shape(lat_rows, lon_total, chans), shape(lat_rows, lon1, chans)],
            in_specs=[vmem()] * 4,
            out_specs=[vmem()] * 2,
            scratch_shapes=[
                pltpu.VMEM((lat_rows + 2 * SPAN, lon_total, chans), BF16),
                pltpu.VMEM((GROUP + PAIR, lon1, basis * chans), BF16),
            ],
            compiler_params=params,
            name="far_rows_1",
        )(fields, lon_halo, tables, weights_in)
        done = pl.pallas_call(
            functools.partial(far2_kernel, half),
            out_shape=jax.ShapeDtypeStruct(turned, F32),
            in_specs=[vmem()] * 3,
            out_specs=vmem(),
            scratch_shapes=[pltpu.VMEM((GROUP, half, basis * chans), BF16)],
            compiler_params=params,
            name="far_rows_2",
        )(after, tables, weights_in)
        near_shapes = [shape(2 * HALO, lon_total, chans), shape(GROUP + 2 * SPAN, lon1, chans)]
        near_feats = pltpu.VMEM((GROUP, lon1, basis * chans), BF16)
        ext, near, halo_tab, done = pl.pallas_call(
            functools.partial(near1_kernel, half),
            out_shape=near_shapes
            + [
                shape(PAIR * basis * BLOCK, lanes),
                jax.ShapeDtypeStruct(turned, F32),
            ],
            in_specs=[vmem()] * 7,
            out_specs=[vmem()] * 4,
            scratch_shapes=[near_feats],
            input_output_aliases={6: 3},
            compiler_params=params,
            name="near_rows_1",
        )(ext, after, lat_halos[0], tables, weights_in, order, done)
        *_, keep, send = pl.pallas_call(
            functools.partial(near2_kernel, half, cols),
            out_shape=near_shapes + [jax.ShapeDtypeStruct(turned, F32)] + [piece] * 2,
            in_specs=[vmem()] * 7,
            out_specs=[vmem()] * 5,
            scratch_shapes=[near_feats],
            input_output_aliases={4: 0, 5: 1, 6: 2},
            compiler_params=params,
            name="near_rows_2",
        )(corners[0], halo_tab, tables, weights_in, ext, near, done)
    else:
        keep, send = pl.pallas_call(
            functools.partial(all_kernel, half, cols),
            out_shape=[piece] * 2,
            in_specs=[vmem()] * (5 + 2 * sides),
            out_specs=[vmem()] * 2,
            scratch_shapes=[
                pltpu.VMEM((lat_rows + 2 * HALO, lon_total, chans), BF16),
                pltpu.VMEM((lat_rows + 2 * PAIR, lon1, basis * chans), BF16),
                pltpu.VMEM((lat_rows + 2 * SPAN, lon1, chans), BF16),
                scratch(*turned),
            ],
            compiler_params=params,
            name="all_rows",
        )(fields, lon_halo, *lat_halos, *corners, tables, weights_in, order)
    got = lax.ppermute(send, "chan", swap)

    out = pl.pallas_call(
        join_kernel,
        out_shape=shape(cols, lat_rows, width),
        in_specs=[vmem()] * 2,
        out_specs=hbm(),
        scratch_shapes=[pltpu.SemaphoreType.DMA((2,))],
        compiler_params=params,
        name="join",
    )(keep, got)
    return jnp.transpose(out, (1, 0, 2))


def solution(mesh):
    return jax.shard_map(
        per_device,
        mesh=mesh,
        in_specs=(
            P(("groups", "lat"), "lon", "chan"),
            P("lat", None),
            P("lat"),
            P("lat"),
            P("lat", None, None, None),
            P(),
        ),
        out_specs=P(("groups", "lat"), "lon", "chan"),
        check_vma=False,
    )
```

```python
import functools

import jax
import jax.numpy as jnp
from jax import lax
from jax.experimental import pallas as pl
from jax.experimental.pallas import tpu as pltpu
from jax.sharding import PartitionSpec as P

LAYERS = 2
SPAN = 2
HALO = LAYERS * SPAN
BLOCK = 16
WINDOW = 2 * BLOCK
GROUP = 4
PAIR = 2
WIDE = BLOCK
SHIFT = BLOCK // 2
VMEM_LIMIT = 48 * 1024 * 1024
BF16 = jnp.bfloat16
F32 = jnp.float32


def vmem():
    return pl.BlockSpec(memory_space=pltpu.VMEM)


def smem():
    return pl.BlockSpec(memory_space=pltpu.SMEM)


def hbm():
    return pl.BlockSpec(memory_space=pltpu.HBM)


def in_hbm(x):
    return pltpu.with_memory_space_constraint(x, pltpu.HBM)


def by_row(count):
    total = count * BLOCK
    out_row = lax.broadcasted_iota(jnp.int32, (total, total), 0)
    in_row = lax.broadcasted_iota(jnp.int32, (total, total), 1)
    source = (out_row % BLOCK) * count + out_row // BLOCK
    return (in_row == source).astype(F32).astype(BF16)


def toeplitz(rows_tab, order):
    moved = jnp.concatenate(
        [rows_tab if jj == 0 else pltpu.roll(rows_tab, jj, 1) for jj in range(BLOCK)], axis=0
    ).astype(BF16)
    return jnp.dot(order, moved, preferred_element_type=F32).astype(BF16)


def band_rows(refs, slots, rows):
    sup_ref, count_ref, reach_ref, psi_ref = refs
    lat_rows, sup, basis, offsets = psi_ref.shape
    lanes = slots.shape[3]
    slots[...] = jnp.zeros_like(slots)
    for n, i in enumerate(rows):
        row = lax.axis_index("lat") * lat_rows + i
        values = [psi_ref[i, s] for s in range(sup)]
        places = [jnp.where(s < count_ref[i], sup_ref[i, s] - row, -lat_rows) for s in range(sup)]
        for rel in range(2 * SPAN + 1):
            total = jnp.zeros((basis, offsets), F32)
            for value, at in zip(values, places):
                total = total + jnp.where(at == rel - SPAN, value, 0.0)
            slots[n, rel, :, 0:offsets] = total
    off = lax.broadcasted_iota(jnp.int32, (basis, lanes), 1) % WINDOW - offsets // 2
    bands = []
    for n, i in enumerate(rows):
        band = slots[n, 0]
        for rel in range(1, 2 * SPAN + 1):
            band = band + pltpu.roll(slots[n, rel], rel * WINDOW, 1)
        bands.append(jnp.where(jnp.abs(off) <= reach_ref[i], band, 0.0))
    return bands


def put_pair(scr, bands):
    for m, band in enumerate(bands):
        basis = band.shape[0]
        scr[m * basis : (m + 1) * basis, :] = (
            band if m == 0 else pltpu.roll(band, m * WINDOW, 1)
        )


def turn(ref, lon_from, lon_to, wide_scr):
    _, lat_rows, width = ref.shape
    wide_scr[lon_from * lat_rows : lon_to * lat_rows, :] = (
        ref[lon_from:lon_to].astype(F32).reshape((lon_to - lon_from) * lat_rows, width)
    )


def turned_row(wide_scr, lat_rows, row, start, count):
    return wide_scr[pl.ds(start * lat_rows + row, count, stride=lat_rows), :].astype(BF16)


def own_kernel(sides, half, *refs):
    sources, (part_ref, edge_ref), refs = refs[:5], refs[5:7], refs[7:]
    lat_refs, refs = refs[:sides], refs[sides:]
    smems, (psi_ref, state_ref, slots, pair_scr, wide_scr, sems) = refs[:3], refs[3:]
    copies = [
        pltpu.make_async_copy(source, dest, sems.at[n])
        for n, (source, dest) in enumerate(zip(sources, (*smems, psi_ref, state_ref)))
    ]
    for copy in copies:
        copy.start()
    cols, lat_rows, width = state_ref.shape
    part = part_ref.shape[1]
    chan = lax.axis_index("chan")
    wide_scr[cols * lat_rows :, :] = jnp.zeros(
        (wide_scr.shape[0] - cols * lat_rows, width), F32
    )
    for copy in copies[:4]:
        copy.wait()
    firsts = [first + (HALO - PAIR) * (n == 0) for n, first in enumerate(needed_rows(2, lat_rows))]
    if sides == 1:
        firsts = [(1 - lax.axis_index("lat")) * (lat_rows - PAIR)]
    rows = [first + m for first in firsts for m in range(PAIR)]
    bands = band_rows((*smems, psi_ref), slots, rows)
    for n in range(sides):
        put_pair(pair_scr, bands[n * PAIR : (n + 1) * PAIR])
        count, lanes = pair_scr.shape
        for x in range(lanes // width):
            begin = HALO * part + x * count
            lat_refs[n][begin : begin + count, :] = pair_scr[
                :, x * width : (x + 1) * width
            ].astype(BF16)
    copies[4].wait()
    turn(state_ref, 0, cols, wide_scr)
    for n, first in enumerate(needed_rows(sides, lat_rows)):
        for t in range(HALO):
            lat_refs[n][t * part : (t + 1) * part, :] = turned_row(
                wide_scr, lat_rows, first + t, (half - WIDE) * chan, part
            )
    for r in range(lat_rows):
        part_ref[r] = turned_row(wide_scr, lat_rows, r, (half - WIDE) * chan, part)
        edge_ref[r] = turned_row(wide_scr, lat_rows, r, (cols - WIDE) * chan, WIDE)


def edges_kernel(
    sides, half, part_ref, edge_ref, other_ref, fields_ref, lon_ref, *rest
):
    lat_refs, corner_refs, (wide_scr,) = rest[:sides], rest[sides : 2 * sides], rest[2 * sides :]
    cols, lat_rows, width = other_ref.shape
    lon_total = fields_ref.shape[1]
    part = part_ref.shape[1]
    chan = lax.axis_index("chan")
    wide_scr[cols * lat_rows :, :] = jnp.zeros(
        (wide_scr.shape[0] - cols * lat_rows, width), F32
    )

    def build(core):
        start = 0 if core == 0 else half - WIDE
        edge = 0 if core == 0 else cols - WIDE
        stop = start + part if core == 0 else cols
        at = WIDE if core == 0 else 0
        own = slice(core * width, (core + 1) * width)
        lane = slice((1 - core) * width, (2 - core) * width)
        turn(other_ref, start, stop, wide_scr)
        for r in range(lat_rows):
            lon_ref[r, :, own] = edge_ref[r]
            lon_ref[r, :, lane] = turned_row(wide_scr, lat_rows, r, edge, WIDE)
            fields_ref[r, at : at + part, own] = part_ref[r]
            fields_ref[r, at : at + part, lane] = turned_row(wide_scr, lat_rows, r, start, part)
        for n, first in enumerate(needed_rows(sides, lat_rows)):
            for t in range(HALO):
                lat_refs[n][t * part : (t + 1) * part, :] = turned_row(
                    wide_scr, lat_rows, first + t, start, part
                )
        empty = slice(0, WIDE) if core == 0 else slice(part, lon_total)
        fields_ref[:, empty, :] = jnp.zeros((lat_rows, WIDE, 2 * width), BF16)

    @pl.when(chan == 0)
    def _():
        build(0)

    @pl.when(chan == 1)
    def _():
        build(1)

    for n, first in enumerate(needed_rows(sides, lat_rows)):
        for t in range(HALO):
            corner_refs[n][t] = lon_ref[first + t]


def needed_rows(sides, lat_rows):
    if sides == 1:
        return [(1 - lax.axis_index("lat")) * (lat_rows - HALO)]
    return [lat_rows - HALO, 0]


def tables_kernel(sides, sup_hbm, count_hbm, reach_hbm, psi_hbm, weights_hbm, _, *refs):
    (weights_ref, tables_ref, order_ref), refs = refs[:3], refs[3:]
    smems, (psi_ref, slots, pairs_scr, sems) = refs[:3], refs[3:]
    sources = (sup_hbm, count_hbm, reach_hbm, psi_hbm, weights_hbm)
    copies = [
        pltpu.make_async_copy(source, dest, sems.at[n])
        for n, (source, dest) in enumerate(zip(sources, (*smems, psi_ref, weights_ref)))
    ]
    for copy in copies:
        copy.start()
    lat_rows, _, basis, _ = psi_ref.shape
    lat = lax.axis_index("lat")
    order = by_row(GROUP * basis)
    order_ref[...] = by_row(PAIR * basis)
    for copy in copies[:4]:
        copy.wait()
    bands = band_rows((*smems, psi_ref), slots, range(lat_rows))
    pairs = lat_rows // PAIR
    for p in range(pairs):
        put_pair(pairs_scr.at[p], bands[p * PAIR : (p + 1) * PAIR])

    def group(g):
        first, second = pairs_scr[2 * g], pairs_scr[2 * g + 1]
        return jnp.concatenate([first, pltpu.roll(second, PAIR * WINDOW, 1)], axis=0)

    if sides == 1:
        tables_ref[0] = toeplitz(group(lat), order)
        tables_ref[1] = toeplitz(group(1 - lat), order)
        mid, near = pairs_scr[2 - lat], pairs_scr[(pairs - 1) * (1 - lat)]
        tables_ref[2] = toeplitz(jnp.concatenate([mid, near], axis=0), order)
    else:
        for g in range(lat_rows // GROUP):
            tables_ref[g] = toeplitz(group(g), order)
    copies[4].wait()


def gelu(x):
    return 0.5 * x * (1.0 + jnp.tanh(0.7978845608028654 * (x + 0.044715 * (x * x * x))))


def add_lat_halo(rows, lat_refs, part):
    chan = lax.axis_index("chan")
    at = pl.ds(pl.multiple_of((1 - chan) * WIDE, WIDE), part)
    for core, ref in zip((chan, 1 - chan), lat_refs):
        width = ref.shape[1]
        lane = pl.ds(pl.multiple_of(core * width, width), width)
        for t, row in enumerate(rows):
            row[at, lane] = ref[t * part : (t + 1) * part, :]


def halo_table(lat_refs, order):
    count = order.shape[0] // BLOCK
    total, first = (ref.shape[0] for ref in lat_refs)
    parts = [lat_refs[0][x : x + count, :].astype(F32) for x in range(first, total, count)]
    return toeplitz(jnp.concatenate(parts, axis=1), order)


def add_lon_halo(cols, half, rows, halos):
    chan = lax.axis_index("chan")
    count = cols - half + WIDE
    whole = count // BLOCK * BLOCK

    @pl.when(chan == 0)
    def _():
        for row, halo in zip(rows, halos):
            row[0:WIDE, :] = halo[...]

    @pl.when(chan == 1)
    def _():
        for row, halo in zip(rows, halos):
            lon_total, chans = row.shape
            before = row[whole : whole + BLOCK, :].astype(F32)[0 : count - whole, :]
            empty = jnp.zeros((lon_total - count - WIDE, chans), F32)
            row[whole:lon_total, :] = jnp.concatenate(
                [before, halo[...].astype(F32), empty], axis=0
            ).astype(BF16)


def conv(source, table, base, in_rows, feats, first, out_rows, jb, put):
    chans = source.shape[2]
    basis = table.shape[0] // (out_rows * BLOCK)
    taken = source[pl.ds(base, in_rows), jb * BLOCK : jb * BLOCK + WINDOW, :]
    taken = taken.reshape(in_rows * WINDOW, chans)
    result = jnp.dot(table, taken, preferred_element_type=F32).astype(BF16)
    at = slice(put * BLOCK, (put + 1) * BLOCK)
    for m in range(out_rows):
        for k in range(basis):
            begin = (m * basis + k) * BLOCK
            feats[first + m, at, k * chans : (k + 1) * chans] = result[begin : begin + BLOCK, :]


def mix(weights_ref, layer, feats, row, blocks, befores, store):
    _, basis, chans, _ = weights_ref.shape
    count, lons = len(befores), len(blocks) * BLOCK
    mixed = jnp.dot(
        feats[row : row + count, 0:lons, :].reshape(count * lons, basis * chans),
        weights_ref[layer].reshape(basis * chans, chans),
        preferred_element_type=F32,
    )
    for n, before in enumerate(befores):
        before = before[...].astype(F32)
        for put, jb in enumerate(blocks):
            at, begin = SHIFT + jb * BLOCK, n * lons + put * BLOCK
            value = before[at : at + BLOCK, :] + gelu(mixed[begin : begin + BLOCK, :])
            store(n, jb, value)


def into(ref, rows):
    def store(n, jb, value):
        ref[rows[n], jb * BLOCK : (jb + 1) * BLOCK, :] = value.astype(BF16)

    return store


def into_turned(turned, rows, lat_rows):
    def store(n, jb, value):
        width = value.shape[1] // 2
        for c in range(2):
            turned[c, pl.ds(jb * BLOCK * lat_rows + rows[n], BLOCK, stride=lat_rows), :] = value[
                :, c * width : (c + 1) * width
            ]

    return store


def hand_out(turned, keep_ref, send_ref):
    chan = lax.axis_index("chan")
    keep_ref[...] = turned[chan].reshape(keep_ref.shape).astype(BF16)
    send_ref[...] = turned[1 - chan].reshape(send_ref.shape).astype(BF16)


def inner(count):
    return range(1, count - 2)


def outer(count):
    return [0, count - 2, count - 1]


def far_rows(fields, after, tables_ref, weights_ref, feats, turned, blocks1, blocks2):
    lat_rows = after.shape[0]
    lat = lax.axis_index("lat")
    far = GROUP * lat
    mid = GROUP - PAIR * lat
    rows6 = PAIR + 2 * SPAN
    mid_table = tables_ref[2, 0 : tables_ref.shape[1] // 2, 0 : rows6 * WINDOW]
    for put, jb in enumerate(blocks1):
        conv(fields, tables_ref[0], far, GROUP + 2 * SPAN, feats, 0, GROUP, jb, put)
        conv(fields, mid_table, mid, rows6, feats, GROUP, PAIR, jb, put)
    dests = [SPAN + t for t in range(GROUP)]
    dests += [(GROUP + SPAN) * (1 - lat) + t for t in range(PAIR)]
    befores = [SPAN + far + t for t in range(GROUP)] + [SPAN + mid + t for t in range(PAIR)]
    step = len(dests) // 2
    for t in range(0, len(dests), step):
        rows = [fields.at[r] for r in befores[t : t + step]]
        mix(weights_ref, 0, feats, t, blocks1, rows, into(after, dests[t : t + step]))
    for put, jb in enumerate(blocks2):
        conv(after, tables_ref[0], 0, GROUP + 2 * SPAN, feats, 0, GROUP, jb, put)
    befores = [after.at[SPAN + t] for t in range(GROUP)]
    rows = [far + t for t in range(GROUP)]
    mix(weights_ref, 1, feats, 0, blocks2, befores, into_turned(turned, rows, lat_rows))


def far1_kernel(
    half, own_ref, tables_ref, weights_ref, fields_ref, after_ref, turned_ref, feats
):
    lat_rows, lon_total, chans = own_ref.shape
    empty = jnp.zeros((lon_total, chans), BF16)
    for t in range(SPAN):
        fields_ref[t] = empty
        fields_ref[SPAN + lat_rows + t] = empty
        after_ref[(GROUP + SPAN) * lax.axis_index("lat") + t] = empty[: lon_total - BLOCK]
    fields_ref[SPAN : SPAN + lat_rows] = own_ref[...]
    far_rows(
        fields_ref,
        after_ref,
        tables_ref,
        weights_ref,
        feats,
        turned_ref,
        inner(lon_total // BLOCK - 1),
        inner(half // BLOCK),
    )


def far2_kernel(
    half,
    cols,
    lon_ref,
    tables_ref,
    weights_ref,
    fields_in,
    after_in,
    turned_in,
    fields_ref,
    after_ref,
    turned_ref,
    feats,
):
    lat_rows = lon_ref.shape[0]
    add_lon_halo(
        cols,
        half,
        [fields_ref.at[SPAN + r] for r in range(lat_rows)],
        [lon_ref.at[r] for r in range(lat_rows)],
    )
    far_rows(
        fields_ref,
        after_ref,
        tables_ref,
        weights_ref,
        feats,
        turned_ref,
        outer(fields_ref.shape[1] // BLOCK - 1),
        outer(half // BLOCK),
    )


def near_rows(fields, near, table, tables_ref, weights_ref, feats, turned, blocks1, blocks2):
    lat_rows = near.shape[0]
    lat = lax.axis_index("lat")
    rows6 = PAIR + 2 * SPAN
    last_table = tables_ref[2, tables_ref.shape[1] // 2 :, 0 : rows6 * WINDOW]
    last = SPAN * lat
    beyond = SPAN * (1 - lat)
    for put, jb in enumerate(blocks1):
        conv(fields, last_table, last, rows6, feats, 0, PAIR, jb, put)
        conv(fields, table[:, 0 : rows6 * WINDOW], beyond, rows6, feats, PAIR, PAIR, jb, put)
    starts = [last] * PAIR + [beyond] * PAIR
    befores = [fields.at[SPAN + start + n % PAIR] for n, start in enumerate(starts)]
    dests = [GROUP * (1 - lat) + SPAN * lat + m for m in range(PAIR)]
    dests += [(GROUP + SPAN) * (1 - lat) + m for m in range(PAIR)]
    mix(weights_ref, 0, feats, 0, blocks1, befores, into(near, dests))
    for put, jb in enumerate(blocks2):
        conv(near, tables_ref[1], 0, GROUP + 2 * SPAN, feats, 0, GROUP, jb, put)
    befores = [near.at[SPAN + t] for t in range(GROUP)]
    rows = [GROUP * (1 - lat) + t for t in range(GROUP)]
    mix(weights_ref, 1, feats, 0, blocks2, befores, into_turned(turned, rows, lat_rows))


def near1_kernel(
    half,
    ext_ref,
    after_ref,
    lat_own_ref,
    lat_other_ref,
    tables_ref,
    weights_ref,
    order_ref,
    turned_in,
    fields_ref,
    near_ref,
    table_ref,
    turned_ref,
    feats,
):
    lon_total = ext_ref.shape[1]
    lat = lax.axis_index("lat")
    lat_refs = (lat_own_ref, lat_other_ref)
    halo = HALO * (1 - lat)
    own = HALO * lat
    for t in range(HALO):
        fields_ref[own + t] = ext_ref[SPAN + HALO * (1 - lat) + t]
    add_lat_halo([fields_ref.at[halo + t] for t in range(HALO)], lat_refs, half + WIDE)
    table_ref[...] = halo_table(lat_refs, order_ref[...])
    for t in range(GROUP):
        near_ref[GROUP * lat + t] = after_ref[GROUP * (1 - lat) + t]
    near_rows(
        fields_ref,
        near_ref,
        table_ref,
        tables_ref,
        weights_ref,
        feats,
        turned_ref,
        inner(lon_total // BLOCK - 1),
        inner(half // BLOCK),
    )


def near2_kernel(
    half,
    cols,
    corner_ref,
    table_ref,
    tables_ref,
    weights_ref,
    fields_in,
    near_in,
    turned_in,
    fields_ref,
    near_ref,
    turned_ref,
    keep_ref,
    send_ref,
    feats,
):
    halo = HALO * (1 - lax.axis_index("lat"))
    add_lon_halo(
        cols,
        half,
        [fields_ref.at[halo + t] for t in range(HALO)],
        [corner_ref.at[t] for t in range(HALO)],
    )
    near_rows(
        fields_ref,
        near_ref,
        table_ref,
        tables_ref,
        weights_ref,
        feats,
        turned_ref,
        outer(fields_ref.shape[1] // BLOCK - 1),
        outer(half // BLOCK),
    )
    hand_out(turned_ref, keep_ref, send_ref)


def all_kernel(half, cols, own_ref, lon_ref, *rest):
    lat_refs, corner_refs = (rest[0:2], rest[2:4]), rest[4:6]
    tables_ref, weights_ref, order_ref, keep_ref, send_ref, fields, feats, after, turned = rest[6:]
    lat_rows, lon_total, chans = own_ref.shape
    groups = lat_rows // GROUP
    lon1 = lon_total - BLOCK
    halo_base = [0, lat_rows + HALO]
    win_base = [0, lat_rows + HALO - SPAN]
    out_base = [0, lat_rows + SPAN]
    rows6 = PAIR + 2 * SPAN

    fields[HALO : HALO + lat_rows] = own_ref[...]
    rows = [fields.at[HALO + r] for r in range(lat_rows)]
    halos = [lon_ref.at[r] for r in range(lat_rows)]
    for n in range(2):
        halo_rows = [fields.at[halo_base[n] + t] for t in range(HALO)]
        add_lat_halo(halo_rows, lat_refs[n], half + WIDE)
        rows += halo_rows
        halos += [corner_refs[n].at[t] for t in range(HALO)]
    add_lon_halo(cols, half, rows, halos)
    halo_tables = [
        halo_table(lat_refs[n], order_ref[...])[:, 0 : rows6 * WINDOW] for n in range(2)
    ]
    blocks = range(lon1 // BLOCK)
    for jb in blocks:
        for g in range(groups):
            base = HALO - SPAN + g * GROUP
            conv(
                fields, tables_ref[g], base, GROUP + 2 * SPAN, feats, g * GROUP, GROUP, jb, jb
            )
        for n in range(2):
            first = lat_rows + n * PAIR
            conv(fields, halo_tables[n], win_base[n], rows6, feats, first, PAIR, jb, jb)
    dests = [SPAN + i for i in range(lat_rows)]
    dests += [out_base[n] + m for n in range(2) for m in range(PAIR)]
    for i in range(0, len(dests), PAIR):
        befores = [fields.at[dest + SPAN] for dest in dests[i : i + PAIR]]
        mix(weights_ref, 0, feats, i, blocks, befores, into(after, dests[i : i + PAIR]))
    blocks = range(half // BLOCK)
    for jb in blocks:
        for g in range(groups):
            base = g * GROUP
            conv(after, tables_ref[g], base, GROUP + 2 * SPAN, feats, base, GROUP, jb, jb)
    for i in range(0, lat_rows, PAIR):
        befores = [after.at[SPAN + i + m] for m in range(PAIR)]
        rows = [i + m for m in range(PAIR)]
        mix(weights_ref, 1, feats, i, blocks, befores, into_turned(turned, rows, lat_rows))
    hand_out(turned, keep_ref, send_ref)


def join_kernel(keep_ref, got_ref, out_hbm, sems):
    half = keep_ref.shape[0]
    rest = out_hbm.shape[0] - half
    chan = lax.axis_index("chan")

    def copy(first, second):
        copies = [
            pltpu.make_async_copy(first, out_hbm.at[0:half], sems.at[0]),
            pltpu.make_async_copy(second.at[0:rest], out_hbm.at[half : half + rest], sems.at[1]),
        ]
        for c in copies:
            c.start()
        for c in copies:
            c.wait()

    @pl.when(chan == 0)
    def _():
        copy(keep_ref, got_ref)

    @pl.when(chan == 1)
    def _():
        copy(got_ref, keep_ref)


def per_device(state, sup_rows, sup_count, lon_reach, psi, weights):
    lat_rows, cols, width = state.shape
    basis = psi.shape[2]
    chans = weights.shape[2]
    lats, lons = lax.axis_size("lat"), lax.axis_size("lon")
    sides = 1 if lats == 2 else 2
    groups = lat_rows // GROUP
    lanes = (GROUP + 2 * SPAN) * WINDOW
    half = -(-cols // (2 * BLOCK)) * BLOCK
    part = half + WIDE
    lon_total = half + 2 * WIDE
    lon1 = lon_total - BLOCK
    tabs = groups + 1 if sides == 1 else groups
    swap = [(0, 1), (1, 0)]
    params = pltpu.CompilerParams(vmem_limit_bytes=VMEM_LIMIT)

    def shape(*dims):
        return jax.ShapeDtypeStruct(dims, BF16)

    def to_lat(step):
        if lats == 2:
            return [(a, 1 - a) for a in range(lats)]
        return [(a, a + step) for a in range(lats) if 0 <= a + step < lats]

    forth = [((z, 1), ((z + 1) % lons, 0)) for z in range(lons)]
    back = [((z, 0), ((z - 1) % lons, 1)) for z in range(lons)]
    to_lon = forth + back

    own = jnp.transpose(state, (1, 0, 2))
    other = lax.ppermute(own, "chan", swap)

    def scratch(*dims):
        return pltpu.VMEM(dims, F32)

    wide = scratch((half + part) * lat_rows, width)
    smalls = [sup_rows, sup_count, lon_reach]
    part_own, edge_own, *lat_owns = pl.pallas_call(
        functools.partial(own_kernel, sides, half),
        out_shape=[
            shape(lat_rows, part, width),
            shape(lat_rows, WIDE, width),
        ]
        + [shape(HALO * part + PAIR * basis * lanes // width, width)] * sides,
        in_specs=[hbm()] * 5,
        out_specs=[vmem()] * (2 + sides),
        scratch_shapes=[pltpu.SMEM(x.shape, x.dtype) for x in smalls]
        + [
            scratch(*psi.shape),
            pltpu.VMEM(own.shape, BF16),
            scratch(sides * PAIR, 2 * SPAN + 1, basis, lanes),
            scratch(PAIR * basis, lanes),
            wide,
            pltpu.SemaphoreType.DMA((5,)),
        ],
        compiler_params=params,
        name="own",
    )(*[in_hbm(x) for x in smalls + [psi, own]])

    fields, lon_edge, *sends = pl.pallas_call(
        functools.partial(edges_kernel, sides, half),
        out_shape=[shape(lat_rows, lon_total, chans), shape(lat_rows, WIDE, chans)]
        + [shape(HALO * part, width)] * sides
        + [shape(HALO, WIDE, chans)] * sides,
        in_specs=[vmem()] * 3,
        out_specs=[vmem()] * (2 + 2 * sides),
        scratch_shapes=[wide],
        compiler_params=params,
        name="edges",
    )(part_own, edge_own, other)

    steps = [1, -1][:sides]
    lat_halos = [
        [lax.ppermute(x, "lat", to_lat(step)) for x in pair]
        for pair, step in zip(zip(lat_owns, sends), steps)
    ]
    lon_halo = lax.ppermute(
        lon_edge, ("lon", "chan"), [(z * 2 + c, y * 2 + d) for (z, c), (y, d) in to_lon]
    )

    corners = [
        lax.ppermute(
            x,
            ("lon", "lat", "chan"),
            [
                ((z * lats + a) * 2 + c, (y * lats + b) * 2 + d)
                for a, b in to_lat(step)
                for (z, c), (y, d) in to_lon
            ],
        )
        for x, step in zip(sends[sides:], steps)
    ]

    weights_in, tables, order = pl.pallas_call(
        functools.partial(tables_kernel, sides),
        out_shape=[
            shape(*weights.shape),
            shape(tabs, GROUP * basis * BLOCK, lanes),
            shape(PAIR * basis * BLOCK, PAIR * basis * BLOCK),
        ],
        in_specs=[hbm()] * 5 + [vmem()],
        out_specs=[vmem()] * 3,
        scratch_shapes=[pltpu.SMEM(x.shape, x.dtype) for x in smalls]
        + [
            scratch(*psi.shape),
            scratch(lat_rows, 2 * SPAN + 1, basis, lanes),
            scratch(lat_rows // PAIR, PAIR * basis, lanes),
            pltpu.SemaphoreType.DMA((5,)),
        ],
        compiler_params=params,
        name="tables",
    )(*[in_hbm(x) for x in smalls + [psi, weights]], lon_edge)

    piece = shape(half, lat_rows, width)
    turned = (2, half * lat_rows, width)
    if sides == 1:
        far_shapes = [
            shape(lat_rows + 2 * SPAN, lon_total, chans),
            shape(lat_rows, lon1, chans),
            jax.ShapeDtypeStruct(turned, F32),
        ]
        far_feats = pltpu.VMEM((GROUP + PAIR, lon1, basis * chans), BF16)
        far = pl.pallas_call(
            functools.partial(far1_kernel, half),
            out_shape=far_shapes,
            in_specs=[vmem()] * 3,
            out_specs=[vmem()] * 3,
            scratch_shapes=[far_feats],
            compiler_params=params,
            name="far_rows_1",
        )(fields, tables, weights_in)
        ext, after, done = pl.pallas_call(
            functools.partial(far2_kernel, half, cols),
            out_shape=far_shapes,
            in_specs=[vmem()] * 6,
            out_specs=[vmem()] * 3,
            scratch_shapes=[far_feats],
            input_output_aliases={3: 0, 4: 1, 5: 2},
            compiler_params=params,
            name="far_rows_2",
        )(lon_halo, tables, weights_in, *far)
        near_shapes = [shape(2 * HALO, lon_total, chans), shape(GROUP + 2 * SPAN, lon1, chans)]
        near_feats = pltpu.VMEM((GROUP, lon1, basis * chans), BF16)
        ext, near, halo_tab, done = pl.pallas_call(
            functools.partial(near1_kernel, half),
            out_shape=near_shapes
            + [
                shape(PAIR * basis * BLOCK, lanes),
                jax.ShapeDtypeStruct(turned, F32),
            ],
            in_specs=[vmem()] * 8,
            out_specs=[vmem()] * 4,
            scratch_shapes=[near_feats],
            input_output_aliases={7: 3},
            compiler_params=params,
            name="near_rows_1",
        )(ext, after, *lat_halos[0], tables, weights_in, order, done)
        *_, keep, send = pl.pallas_call(
            functools.partial(near2_kernel, half, cols),
            out_shape=near_shapes + [jax.ShapeDtypeStruct(turned, F32)] + [piece] * 2,
            in_specs=[vmem()] * 7,
            out_specs=[vmem()] * 5,
            scratch_shapes=[near_feats],
            input_output_aliases={4: 0, 5: 1, 6: 2},
            compiler_params=params,
            name="near_rows_2",
        )(corners[0], halo_tab, tables, weights_in, ext, near, done)
    else:
        keep, send = pl.pallas_call(
            functools.partial(all_kernel, half, cols),
            out_shape=[piece] * 2,
            in_specs=[vmem()] * (5 + 3 * sides),
            out_specs=[vmem()] * 2,
            scratch_shapes=[
                pltpu.VMEM((lat_rows + 2 * HALO, lon_total, chans), BF16),
                pltpu.VMEM((lat_rows + 2 * PAIR, lon1, basis * chans), BF16),
                pltpu.VMEM((lat_rows + 2 * SPAN, lon1, chans), BF16),
                scratch(*turned),
            ],
            compiler_params=params,
            name="all_rows",
        )(fields, lon_halo, *sum(lat_halos, []), *corners, tables, weights_in, order)
    got = lax.ppermute(send, "chan", swap)

    out = pl.pallas_call(
        join_kernel,
        out_shape=shape(cols, lat_rows, width),
        in_specs=[vmem()] * 2,
        out_specs=hbm(),
        scratch_shapes=[pltpu.SemaphoreType.DMA((2,))],
        compiler_params=params,
        name="join",
    )(keep, got)
    return jnp.transpose(out, (1, 0, 2))


def solution(mesh):
    return jax.shard_map(
        per_device,
        mesh=mesh,
        in_specs=(
            P(("groups", "lat"), "lon", "chan"),
            P("lat", None),
            P("lat"),
            P("lat"),
            P("lat", None, None, None),
            P(),
        ),
        out_specs=P(("groups", "lat"), "lon", "chan"),
        check_vma=False,
    )
```

```python
import functools

import jax
import jax.numpy as jnp
from jax import lax
from jax.experimental import pallas as pl
from jax.experimental.pallas import tpu as pltpu
from jax.sharding import PartitionSpec as P

LAYERS = 2
SPAN = 2
HALO = LAYERS * SPAN
BLOCK = 16
WINDOW = 2 * BLOCK
GROUP = 4
PAIR = 2
WIDE = BLOCK
SHIFT = BLOCK // 2
VMEM_LIMIT = 48 * 1024 * 1024
BF16 = jnp.bfloat16
F32 = jnp.float32


def vmem():
    return pl.BlockSpec(memory_space=pltpu.VMEM)


def smem():
    return pl.BlockSpec(memory_space=pltpu.SMEM)


def hbm():
    return pl.BlockSpec(memory_space=pltpu.HBM)


def in_hbm(x):
    return pltpu.with_memory_space_constraint(x, pltpu.HBM)


def by_row(count):
    total = count * BLOCK
    out_row = lax.broadcasted_iota(jnp.int32, (total, total), 0)
    in_row = lax.broadcasted_iota(jnp.int32, (total, total), 1)
    source = (out_row % BLOCK) * count + out_row // BLOCK
    return (in_row == source).astype(F32).astype(BF16)


def toeplitz(rows_tab, order):
    moved = jnp.concatenate(
        [rows_tab if jj == 0 else pltpu.roll(rows_tab, jj, 1) for jj in range(BLOCK)], axis=0
    ).astype(BF16)
    return jnp.dot(order, moved, preferred_element_type=F32).astype(BF16)


def band_rows(refs, slots, rows):
    sup_ref, count_ref, reach_ref, psi_ref = refs
    lat_rows, sup, basis, offsets = psi_ref.shape
    lanes = slots.shape[3]
    slots[...] = jnp.zeros_like(slots)
    for n, i in enumerate(rows):
        row = lax.axis_index("lat") * lat_rows + i
        values = [psi_ref[i, s] for s in range(sup)]
        places = [jnp.where(s < count_ref[i], sup_ref[i, s] - row, -lat_rows) for s in range(sup)]
        for rel in range(2 * SPAN + 1):
            total = jnp.zeros((basis, offsets), F32)
            for value, at in zip(values, places):
                total = total + jnp.where(at == rel - SPAN, value, 0.0)
            slots[n, rel, :, 0:offsets] = total
    off = lax.broadcasted_iota(jnp.int32, (basis, lanes), 1) % WINDOW - offsets // 2
    bands = []
    for n, i in enumerate(rows):
        band = slots[n, 0]
        for rel in range(1, 2 * SPAN + 1):
            band = band + pltpu.roll(slots[n, rel], rel * WINDOW, 1)
        bands.append(jnp.where(jnp.abs(off) <= reach_ref[i], band, 0.0))
    return bands


def put_pair(scr, bands):
    for m, band in enumerate(bands):
        basis = band.shape[0]
        scr[m * basis : (m + 1) * basis, :] = (
            band if m == 0 else pltpu.roll(band, m * WINDOW, 1)
        )


def turn(ref, lon_from, lon_to, wide_scr):
    _, lat_rows, width = ref.shape
    wide_scr[lon_from * lat_rows : lon_to * lat_rows, :] = (
        ref[lon_from:lon_to].astype(F32).reshape((lon_to - lon_from) * lat_rows, width)
    )


def turned_row(wide_scr, lat_rows, row, start, count):
    return wide_scr[pl.ds(start * lat_rows + row, count, stride=lat_rows), :].astype(BF16)


def own_kernel(sides, half, *refs):
    sources, (part_ref, edge_ref, bands_ref), refs = refs[:5], refs[5:8], refs[8:]
    smems, (psi_ref, state_ref, slots, pair_scr, wide_scr, sems) = refs[:3], refs[3:]
    copies = [
        pltpu.make_async_copy(source, dest, sems.at[n])
        for n, (source, dest) in enumerate(zip(sources, (*smems, psi_ref, state_ref)))
    ]
    for copy in copies:
        copy.start()
    cols, lat_rows, width = state_ref.shape
    part = part_ref.shape[1]
    chan = lax.axis_index("chan")
    wide_scr[cols * lat_rows :, :] = jnp.zeros(
        (wide_scr.shape[0] - cols * lat_rows, width), F32
    )
    for copy in copies[:4]:
        copy.wait()
    firsts = [first + (HALO - PAIR) * (n == 0) for n, first in enumerate(needed_rows(2, lat_rows))]
    if sides == 1:
        firsts = [(1 - lax.axis_index("lat")) * (lat_rows - PAIR)]
    rows = [first + m for first in firsts for m in range(PAIR)]
    bands = band_rows((*smems, psi_ref), slots, rows)
    for n in range(sides):
        put_pair(pair_scr, bands[n * PAIR : (n + 1) * PAIR])
        bands_ref[n] = pair_scr[...].astype(BF16)
    copies[4].wait()
    turn(state_ref, 0, cols, wide_scr)
    for r in range(lat_rows):
        part_ref[r] = turned_row(wide_scr, lat_rows, r, (half - WIDE) * chan, part)
        edge_ref[r] = turned_row(wide_scr, lat_rows, r, (cols - WIDE) * chan, WIDE)


def edges_kernel(
    sides, half, part_ref, edge_ref, other_ref, bands_ref, fields_ref, lon_ref, *rest
):
    lat_refs, corner_refs, (wide_scr,) = rest[:sides], rest[sides : 2 * sides], rest[2 * sides :]
    cols, lat_rows, width = other_ref.shape
    lon_total = fields_ref.shape[1]
    part = part_ref.shape[1]
    chan = lax.axis_index("chan")
    wide_scr[cols * lat_rows :, :] = jnp.zeros(
        (wide_scr.shape[0] - cols * lat_rows, width), F32
    )

    def build(core):
        start = 0 if core == 0 else half - WIDE
        edge = 0 if core == 0 else cols - WIDE
        stop = start + part if core == 0 else cols
        at = WIDE if core == 0 else 0
        own = slice(core * width, (core + 1) * width)
        lane = slice((1 - core) * width, (2 - core) * width)
        turn(other_ref, start, stop, wide_scr)
        for r in range(lat_rows):
            lon_ref[r, :, own] = edge_ref[r]
            lon_ref[r, :, lane] = turned_row(wide_scr, lat_rows, r, edge, WIDE)
            fields_ref[r, at : at + part, own] = part_ref[r]
            fields_ref[r, at : at + part, lane] = turned_row(wide_scr, lat_rows, r, start, part)
        empty = slice(0, WIDE) if core == 0 else slice(part, lon_total)
        fields_ref[:, empty, :] = jnp.zeros((lat_rows, WIDE, 2 * width), BF16)

    @pl.when(chan == 0)
    def _():
        build(0)

    @pl.when(chan == 1)
    def _():
        build(1)

    at = pl.multiple_of((1 - chan) * WIDE, WIDE)
    for n, first in enumerate(needed_rows(sides, lat_rows)):
        for t in range(HALO):
            lat_refs[n][t * part : (t + 1) * part, :] = fields_ref[first + t, pl.ds(at, part), :]
            corner_refs[n][t] = lon_ref[first + t]
        lat_refs[n][HALO * part :, :] = bands_ref[n]


def needed_rows(sides, lat_rows):
    if sides == 1:
        return [(1 - lax.axis_index("lat")) * (lat_rows - HALO)]
    return [lat_rows - HALO, 0]


def tables_kernel(sides, sup_hbm, count_hbm, reach_hbm, psi_hbm, weights_hbm, _, *refs):
    (weights_ref, tables_ref, order_ref), refs = refs[:3], refs[3:]
    smems, (psi_ref, slots, pairs_scr, sems) = refs[:3], refs[3:]
    sources = (sup_hbm, count_hbm, reach_hbm, psi_hbm, weights_hbm)
    copies = [
        pltpu.make_async_copy(source, dest, sems.at[n])
        for n, (source, dest) in enumerate(zip(sources, (*smems, psi_ref, weights_ref)))
    ]
    for copy in copies:
        copy.start()
    lat_rows, _, basis, _ = psi_ref.shape
    lat = lax.axis_index("lat")
    order = by_row(GROUP * basis)
    order_ref[...] = by_row(PAIR * basis)
    for copy in copies[:4]:
        copy.wait()
    bands = band_rows((*smems, psi_ref), slots, range(lat_rows))
    pairs = lat_rows // PAIR
    for p in range(pairs):
        put_pair(pairs_scr.at[p], bands[p * PAIR : (p + 1) * PAIR])

    def group(g):
        first, second = pairs_scr[2 * g], pairs_scr[2 * g + 1]
        return jnp.concatenate([first, pltpu.roll(second, PAIR * WINDOW, 1)], axis=0)

    if sides == 1:
        tables_ref[0] = toeplitz(group(lat), order)
        tables_ref[1] = toeplitz(group(1 - lat), order)
        mid, near = pairs_scr[2 - lat], pairs_scr[(pairs - 1) * (1 - lat)]
        tables_ref[2] = toeplitz(jnp.concatenate([mid, near], axis=0), order)
    else:
        for g in range(lat_rows // GROUP):
            tables_ref[g] = toeplitz(group(g), order)
    copies[4].wait()


def gelu(x):
    return 0.5 * x * (1.0 + jnp.tanh(0.7978845608028654 * (x + 0.044715 * (x * x * x))))


def add_lat_halo(rows, lat_ref, part):
    at = pl.ds(pl.multiple_of((1 - lax.axis_index("chan")) * WIDE, WIDE), part)
    for t, row in enumerate(rows):
        row[at, :] = lat_ref[t * part : (t + 1) * part, :]


def halo_table(lat_ref, order):
    count = order.shape[0] // BLOCK
    return toeplitz(lat_ref[lat_ref.shape[0] - count :, :].astype(F32), order)


def add_lon_halo(cols, half, rows, halos):
    chan = lax.axis_index("chan")
    count = cols - half + WIDE
    whole = count // BLOCK * BLOCK

    @pl.when(chan == 0)
    def _():
        for row, halo in zip(rows, halos):
            row[0:WIDE, :] = halo[...]

    @pl.when(chan == 1)
    def _():
        for row, halo in zip(rows, halos):
            lon_total, chans = row.shape
            before = row[whole : whole + BLOCK, :].astype(F32)[0 : count - whole, :]
            empty = jnp.zeros((lon_total - count - WIDE, chans), F32)
            row[whole:lon_total, :] = jnp.concatenate(
                [before, halo[...].astype(F32), empty], axis=0
            ).astype(BF16)


def conv(source, table, base, in_rows, feats, first, out_rows, jb, put):
    chans = source.shape[2]
    basis = table.shape[0] // (out_rows * BLOCK)
    taken = source[pl.ds(base, in_rows), jb * BLOCK : jb * BLOCK + WINDOW, :]
    taken = taken.reshape(in_rows * WINDOW, chans)
    result = jnp.dot(table, taken, preferred_element_type=F32).astype(BF16)
    at = slice(put * BLOCK, (put + 1) * BLOCK)
    for m in range(out_rows):
        for k in range(basis):
            begin = (m * basis + k) * BLOCK
            feats[first + m, at, k * chans : (k + 1) * chans] = result[begin : begin + BLOCK, :]


def mix(weights_ref, layer, feats, row, blocks, befores, store):
    _, basis, chans, _ = weights_ref.shape
    count, lons = len(befores), len(blocks) * BLOCK
    mixed = jnp.dot(
        feats[row : row + count, 0:lons, :].reshape(count * lons, basis * chans),
        weights_ref[layer].reshape(basis * chans, chans),
        preferred_element_type=F32,
    )
    for n, before in enumerate(befores):
        before = before[...].astype(F32)
        for put, jb in enumerate(blocks):
            at, begin = SHIFT + jb * BLOCK, n * lons + put * BLOCK
            value = before[at : at + BLOCK, :] + gelu(mixed[begin : begin + BLOCK, :])
            store(n, jb, value)


def into(ref, rows):
    def store(n, jb, value):
        ref[rows[n], jb * BLOCK : (jb + 1) * BLOCK, :] = value.astype(BF16)

    return store


def into_turned(turned, rows, lat_rows):
    def store(n, jb, value):
        width = value.shape[1] // 2
        for c in range(2):
            turned[c, pl.ds(jb * BLOCK * lat_rows + rows[n], BLOCK, stride=lat_rows), :] = value[
                :, c * width : (c + 1) * width
            ]

    return store


def hand_out(turned, keep_ref, send_ref):
    chan = lax.axis_index("chan")
    keep_ref[...] = turned[chan].reshape(keep_ref.shape).astype(BF16)
    send_ref[...] = turned[1 - chan].reshape(send_ref.shape).astype(BF16)


def for_each_lat(body):
    for value in range(2):
        pl.when(lax.axis_index("lat") == value)(functools.partial(body, value))


def far_kernel(
    half,
    cols,
    own_ref,
    lon_ref,
    tables_ref,
    weights_ref,
    ext_ref,
    next_ref,
    turned_ref,
    fields,
    feats,
):
    lat_rows, lon_total, chans = own_ref.shape
    lon1 = lon_total - BLOCK

    for t in range(SPAN):
        fields[t] = jnp.zeros((lon_total, chans), BF16)
        fields[SPAN + lat_rows + t] = jnp.zeros((lon_total, chans), BF16)
    fields[SPAN : SPAN + lat_rows] = own_ref[...]
    add_lon_halo(
        cols,
        half,
        [fields.at[SPAN + r] for r in range(lat_rows)],
        [lon_ref.at[r] for r in range(lat_rows)],
    )
    ext_ref[...] = fields[SPAN : SPAN + lat_rows]

    @for_each_lat
    def _(lat):
        far = GROUP * lat
        mid = GROUP - PAIR * lat
        rows6 = PAIR + 2 * SPAN
        blocks = range(lon1 // BLOCK)
        mid_table = tables_ref[2, 0 : tables_ref.shape[1] // 2, 0 : rows6 * WINDOW]
        for jb in blocks:
            conv(fields, tables_ref[0], far, GROUP + 2 * SPAN, feats, 0, GROUP, jb, jb)
            conv(fields, mid_table, mid, rows6, feats, GROUP, PAIR, jb, jb)
        for t in range(SPAN):
            next_ref[(GROUP + SPAN) * lat + t] = jnp.zeros((lon1, chans), BF16)
        dests = [SPAN + t for t in range(GROUP)]
        dests += [(GROUP + SPAN) * (1 - lat) + t for t in range(PAIR)]
        befores = [SPAN + far + t for t in range(GROUP)] + [SPAN + mid + t for t in range(PAIR)]
        for t in range(0, GROUP + PAIR, PAIR):
            rows = [fields.at[r] for r in befores[t : t + PAIR]]
            mix(weights_ref, 0, feats, t, blocks, rows, into(next_ref, dests[t : t + PAIR]))
        blocks = range(half // BLOCK)
        for jb in blocks:
            conv(next_ref, tables_ref[0], 0, GROUP + 2 * SPAN, feats, 0, GROUP, jb, jb)
        for t in range(0, GROUP, PAIR):
            befores = [next_ref.at[SPAN + t + m] for m in range(PAIR)]
            rows = [GROUP * lat + t + m for m in range(PAIR)]
            mix(
                weights_ref, 1, feats, t, blocks, befores, into_turned(turned_ref, rows, lat_rows)
            )


def near_rows(lat, fields, near, table, tables_ref, weights_ref, feats, turned, blocks1, blocks2):
    lat_rows = near.shape[0]
    rows6 = PAIR + 2 * SPAN
    last_table = tables_ref[2, tables_ref.shape[1] // 2 :, 0 : rows6 * WINDOW]
    last = SPAN * lat
    beyond = SPAN * (1 - lat)
    for put, jb in enumerate(blocks1):
        conv(fields, last_table, last, rows6, feats, 0, PAIR, jb, put)
    for put, jb in enumerate(blocks1):
        conv(fields, table[:, 0 : rows6 * WINDOW], beyond, rows6, feats, PAIR, PAIR, jb, put)
    starts = [last] * PAIR + [beyond] * PAIR
    befores = [fields.at[SPAN + start + n % PAIR] for n, start in enumerate(starts)]
    dests = [GROUP * (1 - lat) + SPAN * lat + m for m in range(PAIR)]
    dests += [(GROUP + SPAN) * (1 - lat) + m for m in range(PAIR)]
    for t in range(0, GROUP, PAIR):
        rows = slice(t, t + PAIR)
        mix(weights_ref, 0, feats, t, blocks1, befores[rows], into(near, dests[rows]))
    for put, jb in enumerate(blocks2):
        conv(near, tables_ref[1], 0, GROUP + 2 * SPAN, feats, 0, GROUP, jb, put)
    for t in range(0, GROUP, PAIR):
        befores = [near.at[SPAN + t + m] for m in range(PAIR)]
        rows = [GROUP * (1 - lat) + t + m for m in range(PAIR)]
        mix(weights_ref, 1, feats, t, blocks2, befores, into_turned(turned, rows, lat_rows))


def inner(count):
    return range(1, count - 2)


def outer(count):
    return [0, count - 2, count - 1]


def near1_kernel(
    half,
    ext_ref,
    next_ref,
    lat_ref,
    tables_ref,
    weights_ref,
    order_ref,
    turned_in,
    fields_ref,
    near_ref,
    table_ref,
    turned_ref,
    feats,
):
    lon_total = ext_ref.shape[1]

    @for_each_lat
    def _(lat):
        halo = HALO * (1 - lat)
        own = HALO * lat
        for t in range(HALO):
            fields_ref[own + t] = ext_ref[HALO * (1 - lat) + t]
        add_lat_halo([fields_ref.at[halo + t] for t in range(HALO)], lat_ref, half + WIDE)
        table = halo_table(lat_ref, order_ref[...])
        table_ref[...] = table
        for t in range(GROUP):
            near_ref[GROUP * lat + t] = next_ref[GROUP * (1 - lat) + t]
        near_rows(
            lat,
            fields_ref,
            near_ref,
            table,
            tables_ref,
            weights_ref,
            feats,
            turned_ref,
            inner(lon_total // BLOCK - 1),
            inner(half // BLOCK),
        )


def near2_kernel(
    half,
    cols,
    corner_ref,
    table_ref,
    tables_ref,
    weights_ref,
    fields_in,
    near_in,
    turned_in,
    fields_ref,
    near_ref,
    turned_ref,
    keep_ref,
    send_ref,
    feats,
):
    @for_each_lat
    def _(lat):
        halo = HALO * (1 - lat)
        add_lon_halo(
            cols,
            half,
            [fields_ref.at[halo + t] for t in range(HALO)],
            [corner_ref.at[t] for t in range(HALO)],
        )
        near_rows(
            lat,
            fields_ref,
            near_ref,
            table_ref[...],
            tables_ref,
            weights_ref,
            feats,
            turned_ref,
            outer(fields_ref.shape[1] // BLOCK - 1),
            outer(half // BLOCK),
        )

    hand_out(turned_ref, keep_ref, send_ref)


def all_kernel(half, cols, own_ref, lon_ref, *rest):
    lat_refs, corner_refs = rest[:2], rest[2:4]
    tables_ref, weights_ref, order_ref, keep_ref, send_ref, fields, feats, after, turned = rest[4:]
    lat_rows, lon_total, chans = own_ref.shape
    groups = lat_rows // GROUP
    lon1 = lon_total - BLOCK
    halo_base = [0, lat_rows + HALO]
    win_base = [0, lat_rows + HALO - SPAN]
    out_base = [0, lat_rows + SPAN]
    rows6 = PAIR + 2 * SPAN

    fields[HALO : HALO + lat_rows] = own_ref[...]
    rows = [fields.at[HALO + r] for r in range(lat_rows)]
    halos = [lon_ref.at[r] for r in range(lat_rows)]
    for n in range(2):
        halo_rows = [fields.at[halo_base[n] + t] for t in range(HALO)]
        add_lat_halo(halo_rows, lat_refs[n], half + WIDE)
        rows += halo_rows
        halos += [corner_refs[n].at[t] for t in range(HALO)]
    add_lon_halo(cols, half, rows, halos)
    halo_tables = [
        halo_table(lat_refs[n], order_ref[...])[:, 0 : rows6 * WINDOW] for n in range(2)
    ]
    blocks = range(lon1 // BLOCK)
    for jb in blocks:
        for g in range(groups):
            base = HALO - SPAN + g * GROUP
            conv(
                fields, tables_ref[g], base, GROUP + 2 * SPAN, feats, g * GROUP, GROUP, jb, jb
            )
        for n in range(2):
            first = lat_rows + n * PAIR
            conv(fields, halo_tables[n], win_base[n], rows6, feats, first, PAIR, jb, jb)
    dests = [SPAN + i for i in range(lat_rows)]
    dests += [out_base[n] + m for n in range(2) for m in range(PAIR)]
    for i in range(0, len(dests), PAIR):
        befores = [fields.at[dest + SPAN] for dest in dests[i : i + PAIR]]
        mix(weights_ref, 0, feats, i, blocks, befores, into(after, dests[i : i + PAIR]))
    blocks = range(half // BLOCK)
    for jb in blocks:
        for g in range(groups):
            base = g * GROUP
            conv(after, tables_ref[g], base, GROUP + 2 * SPAN, feats, base, GROUP, jb, jb)
    for i in range(0, lat_rows, PAIR):
        befores = [after.at[SPAN + i + m] for m in range(PAIR)]
        rows = [i + m for m in range(PAIR)]
        mix(weights_ref, 1, feats, i, blocks, befores, into_turned(turned, rows, lat_rows))
    hand_out(turned, keep_ref, send_ref)


def join_kernel(keep_ref, got_ref, out_hbm, sems):
    half = keep_ref.shape[0]
    rest = out_hbm.shape[0] - half
    chan = lax.axis_index("chan")

    def copy(first, second):
        copies = [
            pltpu.make_async_copy(first, out_hbm.at[0:half], sems.at[0]),
            pltpu.make_async_copy(second.at[0:rest], out_hbm.at[half : half + rest], sems.at[1]),
        ]
        for c in copies:
            c.start()
        for c in copies:
            c.wait()

    @pl.when(chan == 0)
    def _():
        copy(keep_ref, got_ref)

    @pl.when(chan == 1)
    def _():
        copy(got_ref, keep_ref)


def per_device(state, sup_rows, sup_count, lon_reach, psi, weights):
    lat_rows, cols, width = state.shape
    basis = psi.shape[2]
    chans = weights.shape[2]
    lats, lons = lax.axis_size("lat"), lax.axis_size("lon")
    sides = 1 if lats == 2 else 2
    groups = lat_rows // GROUP
    lanes = (GROUP + 2 * SPAN) * WINDOW
    half = -(-cols // (2 * BLOCK)) * BLOCK
    part = half + WIDE
    lon_total = half + 2 * WIDE
    lon1 = lon_total - BLOCK
    tabs = groups + 1 if sides == 1 else groups
    swap = [(0, 1), (1, 0)]
    params = pltpu.CompilerParams(vmem_limit_bytes=VMEM_LIMIT)

    def shape(*dims):
        return jax.ShapeDtypeStruct(dims, BF16)

    def to_lat(step):
        if lats == 2:
            return [(a, 1 - a) for a in range(lats)]
        return [(a, a + step) for a in range(lats) if 0 <= a + step < lats]

    forth = [((z, 1), ((z + 1) % lons, 0)) for z in range(lons)]
    back = [((z, 0), ((z - 1) % lons, 1)) for z in range(lons)]
    to_lon = forth + back

    own = jnp.transpose(state, (1, 0, 2))
    other = lax.ppermute(own, "chan", swap)

    def scratch(*dims):
        return pltpu.VMEM(dims, F32)

    wide = scratch((half + part) * lat_rows, width)
    smalls = [sup_rows, sup_count, lon_reach]
    part_own, edge_own, bands = pl.pallas_call(
        functools.partial(own_kernel, sides, half),
        out_shape=[
            shape(lat_rows, part, width),
            shape(lat_rows, WIDE, width),
            shape(sides, PAIR * basis, lanes),
        ],
        in_specs=[hbm()] * 5,
        out_specs=[vmem()] * 3,
        scratch_shapes=[pltpu.SMEM(x.shape, x.dtype) for x in smalls]
        + [
            scratch(*psi.shape),
            pltpu.VMEM(own.shape, BF16),
            scratch(sides * PAIR, 2 * SPAN + 1, basis, lanes),
            scratch(PAIR * basis, lanes),
            wide,
            pltpu.SemaphoreType.DMA((5,)),
        ],
        compiler_params=params,
        name="own",
    )(*[in_hbm(x) for x in smalls + [psi, own]])

    fields, lon_edge, *sends = pl.pallas_call(
        functools.partial(edges_kernel, sides, half),
        out_shape=[shape(lat_rows, lon_total, chans), shape(lat_rows, WIDE, chans)]
        + [shape(HALO * part + PAIR * basis, chans)] * sides
        + [shape(HALO, WIDE, chans)] * sides,
        in_specs=[vmem()] * 4,
        out_specs=[vmem()] * (2 + 2 * sides),
        scratch_shapes=[wide],
        compiler_params=params,
        name="edges",
    )(part_own, edge_own, other, bands)

    steps = [1, -1][:sides]
    lat_halos = [lax.ppermute(x, "lat", to_lat(step)) for x, step in zip(sends, steps)]
    lon_halo = lax.ppermute(
        lon_edge, ("lon", "chan"), [(z * 2 + c, y * 2 + d) for (z, c), (y, d) in to_lon]
    )

    corners = [
        lax.ppermute(
            x,
            ("lon", "lat", "chan"),
            [
                ((z * lats + a) * 2 + c, (y * lats + b) * 2 + d)
                for a, b in to_lat(step)
                for (z, c), (y, d) in to_lon
            ],
        )
        for x, step in zip(sends[sides:], steps)
    ]

    weights_in, tables, order = pl.pallas_call(
        functools.partial(tables_kernel, sides),
        out_shape=[
            shape(*weights.shape),
            shape(tabs, GROUP * basis * BLOCK, lanes),
            shape(PAIR * basis * BLOCK, PAIR * basis * BLOCK),
        ],
        in_specs=[hbm()] * 5 + [vmem()],
        out_specs=[vmem()] * 3,
        scratch_shapes=[pltpu.SMEM(x.shape, x.dtype) for x in smalls]
        + [
            scratch(*psi.shape),
            scratch(lat_rows, 2 * SPAN + 1, basis, lanes),
            scratch(lat_rows // PAIR, PAIR * basis, lanes),
            pltpu.SemaphoreType.DMA((5,)),
        ],
        compiler_params=params,
        name="tables",
    )(*[in_hbm(x) for x in smalls + [psi, weights]], lon_edge)

    piece = shape(half, lat_rows, width)
    turned = (2, half * lat_rows, width)
    if sides == 1:
        ext, after, done = pl.pallas_call(
            functools.partial(far_kernel, half, cols),
            out_shape=[
                shape(lat_rows, lon_total, chans),
                shape(lat_rows, lon1, chans),
                jax.ShapeDtypeStruct(turned, F32),
            ],
            in_specs=[vmem()] * 4,
            out_specs=[vmem()] * 3,
            scratch_shapes=[
                pltpu.VMEM((lat_rows + 2 * SPAN, lon_total, chans), BF16),
                pltpu.VMEM((GROUP + PAIR, lon1, basis * chans), BF16),
            ],
            compiler_params=params,
            name="far_rows",
        )(fields, lon_halo, tables, weights_in)
        near_shapes = [shape(2 * HALO, lon_total, chans), shape(GROUP + 2 * SPAN, lon1, chans)]
        near_feats = pltpu.VMEM((GROUP, lon1, basis * chans), BF16)
        ext, near, halo_tab, done = pl.pallas_call(
            functools.partial(near1_kernel, half),
            out_shape=near_shapes
            + [
                shape(PAIR * basis * BLOCK, lanes),
                jax.ShapeDtypeStruct(turned, F32),
            ],
            in_specs=[vmem()] * 7,
            out_specs=[vmem()] * 4,
            scratch_shapes=[near_feats],
            input_output_aliases={6: 3},
            compiler_params=params,
            name="near_rows_1",
        )(ext, after, lat_halos[0], tables, weights_in, order, done)
        *_, keep, send = pl.pallas_call(
            functools.partial(near2_kernel, half, cols),
            out_shape=near_shapes + [jax.ShapeDtypeStruct(turned, F32)] + [piece] * 2,
            in_specs=[vmem()] * 7,
            out_specs=[vmem()] * 5,
            scratch_shapes=[near_feats],
            input_output_aliases={4: 0, 5: 1, 6: 2},
            compiler_params=params,
            name="near_rows_2",
        )(corners[0], halo_tab, tables, weights_in, ext, near, done)
    else:
        keep, send = pl.pallas_call(
            functools.partial(all_kernel, half, cols),
            out_shape=[piece] * 2,
            in_specs=[vmem()] * (5 + 2 * sides),
            out_specs=[vmem()] * 2,
            scratch_shapes=[
                pltpu.VMEM((lat_rows + 2 * HALO, lon_total, chans), BF16),
                pltpu.VMEM((lat_rows + 2 * PAIR, lon1, basis * chans), BF16),
                pltpu.VMEM((lat_rows + 2 * SPAN, lon1, chans), BF16),
                scratch(*turned),
            ],
            compiler_params=params,
            name="all_rows",
        )(fields, lon_halo, *lat_halos, *corners, tables, weights_in, order)
    got = lax.ppermute(send, "chan", swap)

    out = pl.pallas_call(
        join_kernel,
        out_shape=shape(cols, lat_rows, width),
        in_specs=[vmem()] * 2,
        out_specs=hbm(),
        scratch_shapes=[pltpu.SemaphoreType.DMA((2,))],
        compiler_params=params,
        name="join",
    )(keep, got)
    return jnp.transpose(out, (1, 0, 2))


def solution(mesh):
    return jax.shard_map(
        per_device,
        mesh=mesh,
        in_specs=(
            P(("groups", "lat"), "lon", "chan"),
            P("lat", None),
            P("lat"),
            P("lat"),
            P("lat", None, None, None),
            P(),
        ),
        out_specs=P(("groups", "lat"), "lon", "chan"),
        check_vma=False,
    )
```

```python
import functools

import jax
import jax.numpy as jnp
from jax import lax
from jax.experimental import pallas as pl
from jax.experimental.pallas import tpu as pltpu
from jax.sharding import PartitionSpec as P

LAYERS = 2
SPAN = 2
HALO = LAYERS * SPAN
BLOCK = 16
WINDOW = 2 * BLOCK
GROUP = 4
PAIR = 2
WIDE = BLOCK
SHIFT = BLOCK // 2
VMEM_LIMIT = 48 * 1024 * 1024
BF16 = jnp.bfloat16
F32 = jnp.float32


def vmem():
    return pl.BlockSpec(memory_space=pltpu.VMEM)


def smem():
    return pl.BlockSpec(memory_space=pltpu.SMEM)


def hbm():
    return pl.BlockSpec(memory_space=pltpu.HBM)


def in_hbm(x):
    return pltpu.with_memory_space_constraint(x, pltpu.HBM)


def by_row(count):
    total = count * BLOCK
    out_row = lax.broadcasted_iota(jnp.int32, (total, total), 0)
    in_row = lax.broadcasted_iota(jnp.int32, (total, total), 1)
    source = (out_row % BLOCK) * count + out_row // BLOCK
    return (in_row == source).astype(F32).astype(BF16)


def toeplitz(rows_tab, order):
    moved = jnp.concatenate(
        [rows_tab if jj == 0 else pltpu.roll(rows_tab, jj, 1) for jj in range(BLOCK)], axis=0
    ).astype(BF16)
    return jnp.dot(order, moved, preferred_element_type=F32).astype(BF16)


def band_rows(refs, slots, rows):
    sup_ref, count_ref, reach_ref, psi_ref = refs
    lat_rows, sup, basis, offsets = psi_ref.shape
    lanes = slots.shape[3]
    slots[...] = jnp.zeros_like(slots)
    for n, i in enumerate(rows):
        row = lax.axis_index("lat") * lat_rows + i
        values = [psi_ref[i, s] for s in range(sup)]
        places = [jnp.where(s < count_ref[i], sup_ref[i, s] - row, -lat_rows) for s in range(sup)]
        for rel in range(2 * SPAN + 1):
            total = jnp.zeros((basis, offsets), F32)
            for value, at in zip(values, places):
                total = total + jnp.where(at == rel - SPAN, value, 0.0)
            slots[n, rel, :, 0:offsets] = total
    off = lax.broadcasted_iota(jnp.int32, (basis, lanes), 1) % WINDOW - offsets // 2
    bands = []
    for n, i in enumerate(rows):
        band = slots[n, 0]
        for rel in range(1, 2 * SPAN + 1):
            band = band + pltpu.roll(slots[n, rel], rel * WINDOW, 1)
        bands.append(jnp.where(jnp.abs(off) <= reach_ref[i], band, 0.0))
    return bands


def put_pair(scr, bands):
    for m, band in enumerate(bands):
        basis = band.shape[0]
        scr[m * basis : (m + 1) * basis, :] = (
            band if m == 0 else pltpu.roll(band, m * WINDOW, 1)
        )


def turn(ref, lon_from, lon_to, wide_scr):
    _, lat_rows, width = ref.shape
    wide_scr[lon_from * lat_rows : lon_to * lat_rows, :] = (
        ref[lon_from:lon_to].astype(F32).reshape((lon_to - lon_from) * lat_rows, width)
    )


def turned_row(wide_scr, lat_rows, row, start, count):
    return wide_scr[pl.ds(start * lat_rows + row, count, stride=lat_rows), :].astype(BF16)


def own_kernel(sides, half, *refs):
    sources, (part_ref, edge_ref, bands_ref), refs = refs[:5], refs[5:8], refs[8:]
    smems, (psi_ref, state_ref, slots, pair_scr, wide_scr, sems) = refs[:3], refs[3:]
    copies = [
        pltpu.make_async_copy(source, dest, sems.at[n])
        for n, (source, dest) in enumerate(zip(sources, (*smems, psi_ref, state_ref)))
    ]
    for copy in copies:
        copy.start()
    cols, lat_rows, width = state_ref.shape
    part = part_ref.shape[1]
    chan = lax.axis_index("chan")
    wide_scr[cols * lat_rows :, :] = jnp.zeros(
        (wide_scr.shape[0] - cols * lat_rows, width), F32
    )
    for copy in copies[:4]:
        copy.wait()
    firsts = [first + (HALO - PAIR) * (n == 0) for n, first in enumerate(needed_rows(2, lat_rows))]
    if sides == 1:
        firsts = [(1 - lax.axis_index("lat")) * (lat_rows - PAIR)]
    rows = [first + m for first in firsts for m in range(PAIR)]
    bands = band_rows((*smems, psi_ref), slots, rows)
    for n in range(sides):
        put_pair(pair_scr, bands[n * PAIR : (n + 1) * PAIR])
        bands_ref[n] = pair_scr[...].astype(BF16)
    copies[4].wait()
    turn(state_ref, 0, cols, wide_scr)
    for r in range(lat_rows):
        part_ref[r] = turned_row(wide_scr, lat_rows, r, (half - WIDE) * chan, part)
        edge_ref[r] = turned_row(wide_scr, lat_rows, r, (cols - WIDE) * chan, WIDE)


def edges_kernel(
    sides, half, part_ref, edge_ref, other_ref, bands_ref, fields_ref, lon_ref, *rest
):
    lat_refs, corner_refs, (wide_scr,) = rest[:sides], rest[sides : 2 * sides], rest[2 * sides :]
    cols, lat_rows, width = other_ref.shape
    lon_total = fields_ref.shape[1]
    part = part_ref.shape[1]
    chan = lax.axis_index("chan")
    wide_scr[cols * lat_rows :, :] = jnp.zeros(
        (wide_scr.shape[0] - cols * lat_rows, width), F32
    )

    def build(core):
        start = 0 if core == 0 else half - WIDE
        edge = 0 if core == 0 else cols - WIDE
        stop = start + part if core == 0 else cols
        at = WIDE if core == 0 else 0
        own = slice(core * width, (core + 1) * width)
        lane = slice((1 - core) * width, (2 - core) * width)
        turn(other_ref, start, stop, wide_scr)
        for r in range(lat_rows):
            lon_ref[r, :, own] = edge_ref[r]
            lon_ref[r, :, lane] = turned_row(wide_scr, lat_rows, r, edge, WIDE)
            fields_ref[r, at : at + part, own] = part_ref[r]
            fields_ref[r, at : at + part, lane] = turned_row(wide_scr, lat_rows, r, start, part)
        empty = slice(0, WIDE) if core == 0 else slice(part, lon_total)
        fields_ref[:, empty, :] = jnp.zeros((lat_rows, WIDE, 2 * width), BF16)

    @pl.when(chan == 0)
    def _():
        build(0)

    @pl.when(chan == 1)
    def _():
        build(1)

    at = pl.multiple_of((1 - chan) * WIDE, WIDE)
    for n, first in enumerate(needed_rows(sides, lat_rows)):
        for t in range(HALO):
            lat_refs[n][t * part : (t + 1) * part, :] = fields_ref[first + t, pl.ds(at, part), :]
            corner_refs[n][t] = lon_ref[first + t]
        lat_refs[n][HALO * part :, :] = bands_ref[n]


def needed_rows(sides, lat_rows):
    if sides == 1:
        return [(1 - lax.axis_index("lat")) * (lat_rows - HALO)]
    return [lat_rows - HALO, 0]


def tables_kernel(sides, sup_hbm, count_hbm, reach_hbm, psi_hbm, weights_hbm, _, *refs):
    (weights_ref, tables_ref, order_ref), refs = refs[:3], refs[3:]
    smems, (psi_ref, slots, pairs_scr, sems) = refs[:3], refs[3:]
    sources = (sup_hbm, count_hbm, reach_hbm, psi_hbm, weights_hbm)
    copies = [
        pltpu.make_async_copy(source, dest, sems.at[n])
        for n, (source, dest) in enumerate(zip(sources, (*smems, psi_ref, weights_ref)))
    ]
    for copy in copies:
        copy.start()
    lat_rows, _, basis, _ = psi_ref.shape
    lat = lax.axis_index("lat")
    order = by_row(GROUP * basis)
    order_ref[...] = by_row(PAIR * basis)
    for copy in copies[:4]:
        copy.wait()
    bands = band_rows((*smems, psi_ref), slots, range(lat_rows))
    for p in range(lat_rows // PAIR):
        put_pair(pairs_scr.at[p], bands[p * PAIR : (p + 1) * PAIR])

    def group(g):
        first, second = pairs_scr[2 * g], pairs_scr[2 * g + 1]
        return jnp.concatenate([first, pltpu.roll(second, PAIR * WINDOW, 1)], axis=0)

    if sides == 1:
        tables_ref[0] = toeplitz(group(lat), order)
        tables_ref[1] = toeplitz(group(1 - lat), order)
    else:
        for g in range(lat_rows // GROUP):
            tables_ref[g] = toeplitz(group(g), order)
    copies[4].wait()


def gelu(x):
    return 0.5 * x * (1.0 + jnp.tanh(0.7978845608028654 * (x + 0.044715 * (x * x * x))))


def add_lat_halo(rows, lat_ref, part):
    at = pl.ds(pl.multiple_of((1 - lax.axis_index("chan")) * WIDE, WIDE), part)
    for t, row in enumerate(rows):
        row[at, :] = lat_ref[t * part : (t + 1) * part, :]


def halo_table(lat_ref, order):
    count = order.shape[0] // BLOCK
    return toeplitz(lat_ref[lat_ref.shape[0] - count :, :].astype(F32), order)


def add_lon_halo(cols, half, rows, halos):
    chan = lax.axis_index("chan")
    count = cols - half + WIDE
    whole = count // BLOCK * BLOCK

    @pl.when(chan == 0)
    def _():
        for row, halo in zip(rows, halos):
            row[0:WIDE, :] = halo[...]

    @pl.when(chan == 1)
    def _():
        for row, halo in zip(rows, halos):
            lon_total, chans = row.shape
            before = row[whole : whole + BLOCK, :].astype(F32)[0 : count - whole, :]
            empty = jnp.zeros((lon_total - count - WIDE, chans), F32)
            row[whole:lon_total, :] = jnp.concatenate(
                [before, halo[...].astype(F32), empty], axis=0
            ).astype(BF16)


def conv(source, table, base, in_rows, feats, first, out_rows, jb, put):
    chans = source.shape[2]
    basis = table.shape[0] // (out_rows * BLOCK)
    taken = source[pl.ds(base, in_rows), jb * BLOCK : jb * BLOCK + WINDOW, :]
    taken = taken.reshape(in_rows * WINDOW, chans)
    result = jnp.dot(table, taken, preferred_element_type=F32).astype(BF16)
    at = slice(put * BLOCK, (put + 1) * BLOCK)
    for m in range(out_rows):
        for k in range(basis):
            begin = (m * basis + k) * BLOCK
            feats[first + m, at, k * chans : (k + 1) * chans] = result[begin : begin + BLOCK, :]


def mix(weights_ref, layer, feats, row, blocks, befores, store):
    _, basis, chans, _ = weights_ref.shape
    count, lons = len(befores), len(blocks) * BLOCK
    mixed = jnp.dot(
        feats[row : row + count, 0:lons, :].reshape(count * lons, basis * chans),
        weights_ref[layer].reshape(basis * chans, chans),
        preferred_element_type=F32,
    )
    for n, before in enumerate(befores):
        before = before[...].astype(F32)
        for put, jb in enumerate(blocks):
            at, begin = SHIFT + jb * BLOCK, n * lons + put * BLOCK
            value = before[at : at + BLOCK, :] + gelu(mixed[begin : begin + BLOCK, :])
            store(n, jb, value)


def into(ref, rows):
    def store(n, jb, value):
        ref[rows[n], jb * BLOCK : (jb + 1) * BLOCK, :] = value.astype(BF16)

    return store


def into_turned(turned, rows, lat_rows):
    def store(n, jb, value):
        width = value.shape[1] // 2
        for c in range(2):
            turned[c, pl.ds(jb * BLOCK * lat_rows + rows[n], BLOCK, stride=lat_rows), :] = value[
                :, c * width : (c + 1) * width
            ]

    return store


def hand_out(turned, keep_ref, send_ref):
    chan = lax.axis_index("chan")
    keep_ref[...] = turned[chan].reshape(keep_ref.shape).astype(BF16)
    send_ref[...] = turned[1 - chan].reshape(send_ref.shape).astype(BF16)


def for_each_lat(body):
    for value in range(2):
        pl.when(lax.axis_index("lat") == value)(functools.partial(body, value))


def inner(count):
    return range(1, count - 2)


def outer(count):
    return [0, count - 2, count - 1]


def half_table(tables_ref, second):
    rows = tables_ref.shape[1] // 2
    return tables_ref[1, rows * second : rows * (second + 1), :]


def far_rows(lat, fields, after, tables_ref, weights_ref, feats, turned, blocks1, blocks2):
    lat_rows = after.shape[0]
    far = GROUP * lat
    near = GROUP - far
    mid = GROUP - PAIR * lat
    rows8 = GROUP + 2 * SPAN
    for put, jb in enumerate(blocks1):
        conv(fields, tables_ref[0], far, rows8, feats, 0, GROUP, jb, put)
        conv(fields, half_table(tables_ref, lat), near, rows8, feats, GROUP, PAIR, jb, put)
    dests = [SPAN + t for t in range(GROUP)]
    dests += [(GROUP + SPAN) * (1 - lat) + t for t in range(PAIR)]
    befores = [SPAN + far + t for t in range(GROUP)] + [SPAN + mid + t for t in range(PAIR)]
    step = len(dests) // 2
    for t in range(0, len(dests), step):
        rows = [fields.at[r] for r in befores[t : t + step]]
        mix(weights_ref, 0, feats, t, blocks1, rows, into(after, dests[t : t + step]))
    for put, jb in enumerate(blocks2):
        conv(after, tables_ref[0], 0, rows8, feats, 0, GROUP, jb, put)
    for t in range(0, GROUP, PAIR):
        befores = [after.at[SPAN + t + m] for m in range(PAIR)]
        rows = [far + t + m for m in range(PAIR)]
        mix(weights_ref, 1, feats, t, blocks2, befores, into_turned(turned, rows, lat_rows))


def far1_kernel(
    half, own_ref, tables_ref, weights_ref, fields_ref, after_ref, turned_ref, feats
):
    lat_rows, lon_total, chans = own_ref.shape
    for t in range(SPAN):
        fields_ref[t] = jnp.zeros((lon_total, chans), BF16)
        fields_ref[SPAN + lat_rows + t] = jnp.zeros((lon_total, chans), BF16)
    fields_ref[SPAN : SPAN + lat_rows] = own_ref[...]

    @for_each_lat
    def _(lat):
        for t in range(SPAN):
            after_ref[(GROUP + SPAN) * lat + t] = jnp.zeros((lon_total - BLOCK, chans), BF16)
        far_rows(
            lat,
            fields_ref,
            after_ref,
            tables_ref,
            weights_ref,
            feats,
            turned_ref,
            inner(lon_total // BLOCK - 1),
            inner(half // BLOCK),
        )


def far2_kernel(
    half,
    cols,
    lon_ref,
    tables_ref,
    weights_ref,
    fields_in,
    after_in,
    turned_in,
    fields_ref,
    after_ref,
    turned_ref,
    feats,
):
    lat_rows = lon_ref.shape[0]
    add_lon_halo(
        cols,
        half,
        [fields_ref.at[SPAN + r] for r in range(lat_rows)],
        [lon_ref.at[r] for r in range(lat_rows)],
    )

    @for_each_lat
    def _(lat):
        far_rows(
            lat,
            fields_ref,
            after_ref,
            tables_ref,
            weights_ref,
            feats,
            turned_ref,
            outer(fields_ref.shape[1] // BLOCK - 1),
            outer(half // BLOCK),
        )


def near_rows(lat, fields, near, table, tables_ref, weights_ref, feats, turned, blocks1, blocks2):
    lat_rows = near.shape[0]
    rows6, rows8 = PAIR + 2 * SPAN, GROUP + 2 * SPAN
    group = SPAN * lat
    beyond = HALO * (1 - lat)
    for put, jb in enumerate(blocks1):
        conv(fields, half_table(tables_ref, 1 - lat), group, rows8, feats, 0, PAIR, jb, put)
    for put, jb in enumerate(blocks1):
        conv(fields, table[:, 0 : rows6 * WINDOW], beyond, rows6, feats, PAIR, PAIR, jb, put)
    befores = [fields.at[HALO + m] for m in range(PAIR)]
    befores += [fields.at[beyond + SPAN + m] for m in range(PAIR)]
    dests = [GROUP * (1 - lat) + SPAN * lat + m for m in range(PAIR)]
    dests += [(GROUP + SPAN) * (1 - lat) + m for m in range(PAIR)]
    for t in range(0, GROUP, PAIR):
        rows = slice(t, t + PAIR)
        mix(weights_ref, 0, feats, t, blocks1, befores[rows], into(near, dests[rows]))
    for put, jb in enumerate(blocks2):
        conv(near, tables_ref[1], 0, GROUP + 2 * SPAN, feats, 0, GROUP, jb, put)
    for t in range(0, GROUP, PAIR):
        befores = [near.at[SPAN + t + m] for m in range(PAIR)]
        rows = [GROUP * (1 - lat) + t + m for m in range(PAIR)]
        mix(weights_ref, 1, feats, t, blocks2, befores, into_turned(turned, rows, lat_rows))


def near1_kernel(
    half,
    ext_ref,
    next_ref,
    lat_ref,
    tables_ref,
    weights_ref,
    order_ref,
    turned_in,
    fields_ref,
    near_ref,
    table_ref,
    turned_ref,
    feats,
):
    lon_total = ext_ref.shape[1]

    @for_each_lat
    def _(lat):
        halo = (HALO + SPAN) * (1 - lat)
        own = HALO * lat
        for t in range(HALO + SPAN):
            fields_ref[own + t] = ext_ref[SPAN + SPAN * (1 - lat) + t]
        add_lat_halo([fields_ref.at[halo + t] for t in range(HALO)], lat_ref, half + WIDE)
        table = halo_table(lat_ref, order_ref[...])
        table_ref[...] = table
        for t in range(GROUP):
            near_ref[GROUP * lat + t] = next_ref[GROUP * (1 - lat) + t]
        near_rows(
            lat,
            fields_ref,
            near_ref,
            table,
            tables_ref,
            weights_ref,
            feats,
            turned_ref,
            inner(lon_total // BLOCK - 1),
            inner(half // BLOCK),
        )


def near2_kernel(
    half,
    cols,
    corner_ref,
    table_ref,
    tables_ref,
    weights_ref,
    fields_in,
    near_in,
    turned_in,
    fields_ref,
    near_ref,
    turned_ref,
    keep_ref,
    send_ref,
    feats,
):
    @for_each_lat
    def _(lat):
        halo = (HALO + SPAN) * (1 - lat)
        add_lon_halo(
            cols,
            half,
            [fields_ref.at[halo + t] for t in range(HALO)],
            [corner_ref.at[t] for t in range(HALO)],
        )
        near_rows(
            lat,
            fields_ref,
            near_ref,
            table_ref[...],
            tables_ref,
            weights_ref,
            feats,
            turned_ref,
            outer(fields_ref.shape[1] // BLOCK - 1),
            outer(half // BLOCK),
        )

    hand_out(turned_ref, keep_ref, send_ref)


def all_kernel(half, cols, own_ref, lon_ref, *rest):
    lat_refs, corner_refs = rest[:2], rest[2:4]
    tables_ref, weights_ref, order_ref, keep_ref, send_ref, fields, feats, after, turned = rest[4:]
    lat_rows, lon_total, chans = own_ref.shape
    groups = lat_rows // GROUP
    lon1 = lon_total - BLOCK
    halo_base = [0, lat_rows + HALO]
    win_base = [0, lat_rows + HALO - SPAN]
    out_base = [0, lat_rows + SPAN]
    rows6 = PAIR + 2 * SPAN

    fields[HALO : HALO + lat_rows] = own_ref[...]
    rows = [fields.at[HALO + r] for r in range(lat_rows)]
    halos = [lon_ref.at[r] for r in range(lat_rows)]
    for n in range(2):
        halo_rows = [fields.at[halo_base[n] + t] for t in range(HALO)]
        add_lat_halo(halo_rows, lat_refs[n], half + WIDE)
        rows += halo_rows
        halos += [corner_refs[n].at[t] for t in range(HALO)]
    add_lon_halo(cols, half, rows, halos)
    halo_tables = [
        halo_table(lat_refs[n], order_ref[...])[:, 0 : rows6 * WINDOW] for n in range(2)
    ]
    blocks = range(lon1 // BLOCK)
    for jb in blocks:
        for g in range(groups):
            base = HALO - SPAN + g * GROUP
            conv(
                fields, tables_ref[g], base, GROUP + 2 * SPAN, feats, g * GROUP, GROUP, jb, jb
            )
        for n in range(2):
            first = lat_rows + n * PAIR
            conv(fields, halo_tables[n], win_base[n], rows6, feats, first, PAIR, jb, jb)
    dests = [SPAN + i for i in range(lat_rows)]
    dests += [out_base[n] + m for n in range(2) for m in range(PAIR)]
    for i in range(0, len(dests), PAIR):
        befores = [fields.at[dest + SPAN] for dest in dests[i : i + PAIR]]
        mix(weights_ref, 0, feats, i, blocks, befores, into(after, dests[i : i + PAIR]))
    blocks = range(half // BLOCK)
    for jb in blocks:
        for g in range(groups):
            base = g * GROUP
            conv(after, tables_ref[g], base, GROUP + 2 * SPAN, feats, base, GROUP, jb, jb)
    for i in range(0, lat_rows, PAIR):
        befores = [after.at[SPAN + i + m] for m in range(PAIR)]
        rows = [i + m for m in range(PAIR)]
        mix(weights_ref, 1, feats, i, blocks, befores, into_turned(turned, rows, lat_rows))
    hand_out(turned, keep_ref, send_ref)


def join_kernel(keep_ref, got_ref, out_hbm, sems):
    half = keep_ref.shape[0]
    rest = out_hbm.shape[0] - half
    chan = lax.axis_index("chan")

    def copy(first, second):
        copies = [
            pltpu.make_async_copy(first, out_hbm.at[0:half], sems.at[0]),
            pltpu.make_async_copy(second.at[0:rest], out_hbm.at[half : half + rest], sems.at[1]),
        ]
        for c in copies:
            c.start()
        for c in copies:
            c.wait()

    @pl.when(chan == 0)
    def _():
        copy(keep_ref, got_ref)

    @pl.when(chan == 1)
    def _():
        copy(got_ref, keep_ref)


def per_device(state, sup_rows, sup_count, lon_reach, psi, weights):
    lat_rows, cols, width = state.shape
    basis = psi.shape[2]
    chans = weights.shape[2]
    lats, lons = lax.axis_size("lat"), lax.axis_size("lon")
    sides = 1 if lats == 2 else 2
    groups = lat_rows // GROUP
    lanes = (GROUP + 2 * SPAN) * WINDOW
    half = -(-cols // (2 * BLOCK)) * BLOCK
    part = half + WIDE
    lon_total = half + 2 * WIDE
    lon1 = lon_total - BLOCK
    swap = [(0, 1), (1, 0)]
    params = pltpu.CompilerParams(vmem_limit_bytes=VMEM_LIMIT)

    def shape(*dims):
        return jax.ShapeDtypeStruct(dims, BF16)

    def to_lat(step):
        if lats == 2:
            return [(a, 1 - a) for a in range(lats)]
        return [(a, a + step) for a in range(lats) if 0 <= a + step < lats]

    forth = [((z, 1), ((z + 1) % lons, 0)) for z in range(lons)]
    back = [((z, 0), ((z - 1) % lons, 1)) for z in range(lons)]
    to_lon = forth + back

    own = jnp.transpose(state, (1, 0, 2))
    other = lax.ppermute(own, "chan", swap)

    def scratch(*dims):
        return pltpu.VMEM(dims, F32)

    wide = scratch((half + part) * lat_rows, width)
    smalls = [sup_rows, sup_count, lon_reach]
    part_own, edge_own, bands = pl.pallas_call(
        functools.partial(own_kernel, sides, half),
        out_shape=[
            shape(lat_rows, part, width),
            shape(lat_rows, WIDE, width),
            shape(sides, PAIR * basis, lanes),
        ],
        in_specs=[hbm()] * 5,
        out_specs=[vmem()] * 3,
        scratch_shapes=[pltpu.SMEM(x.shape, x.dtype) for x in smalls]
        + [
            scratch(*psi.shape),
            pltpu.VMEM(own.shape, BF16),
            scratch(sides * PAIR, 2 * SPAN + 1, basis, lanes),
            scratch(PAIR * basis, lanes),
            wide,
            pltpu.SemaphoreType.DMA((5,)),
        ],
        compiler_params=params,
        name="own",
    )(*[in_hbm(x) for x in smalls + [psi, own]])

    fields, lon_edge, *sends = pl.pallas_call(
        functools.partial(edges_kernel, sides, half),
        out_shape=[shape(lat_rows, lon_total, chans), shape(lat_rows, WIDE, chans)]
        + [shape(HALO * part + PAIR * basis, chans)] * sides
        + [shape(HALO, WIDE, chans)] * sides,
        in_specs=[vmem()] * 4,
        out_specs=[vmem()] * (2 + 2 * sides),
        scratch_shapes=[wide],
        compiler_params=params,
        name="edges",
    )(part_own, edge_own, other, bands)

    steps = [1, -1][:sides]
    lat_halos = [lax.ppermute(x, "lat", to_lat(step)) for x, step in zip(sends, steps)]
    lon_halo = lax.ppermute(
        lon_edge, ("lon", "chan"), [(z * 2 + c, y * 2 + d) for (z, c), (y, d) in to_lon]
    )

    corners = [
        lax.ppermute(
            x,
            ("lon", "lat", "chan"),
            [
                ((z * lats + a) * 2 + c, (y * lats + b) * 2 + d)
                for a, b in to_lat(step)
                for (z, c), (y, d) in to_lon
            ],
        )
        for x, step in zip(sends[sides:], steps)
    ]

    weights_in, tables, order = pl.pallas_call(
        functools.partial(tables_kernel, sides),
        out_shape=[
            shape(*weights.shape),
            shape(groups, GROUP * basis * BLOCK, lanes),
            shape(PAIR * basis * BLOCK, PAIR * basis * BLOCK),
        ],
        in_specs=[hbm()] * 5 + [vmem()],
        out_specs=[vmem()] * 3,
        scratch_shapes=[pltpu.SMEM(x.shape, x.dtype) for x in smalls]
        + [
            scratch(*psi.shape),
            scratch(lat_rows, 2 * SPAN + 1, basis, lanes),
            scratch(lat_rows // PAIR, PAIR * basis, lanes),
            pltpu.SemaphoreType.DMA((5,)),
        ],
        compiler_params=params,
        name="tables",
    )(*[in_hbm(x) for x in smalls + [psi, weights]], lon_edge)

    piece = shape(half, lat_rows, width)
    turned = (2, half * lat_rows, width)
    if sides == 1:
        far_shapes = [
            shape(lat_rows + 2 * SPAN, lon_total, chans),
            shape(lat_rows, lon1, chans),
            jax.ShapeDtypeStruct(turned, F32),
        ]
        far_feats = pltpu.VMEM((GROUP + PAIR, lon1, basis * chans), BF16)
        far = pl.pallas_call(
            functools.partial(far1_kernel, half),
            out_shape=far_shapes,
            in_specs=[vmem()] * 3,
            out_specs=[vmem()] * 3,
            scratch_shapes=[far_feats],
            compiler_params=params,
            name="far_rows_1",
        )(fields, tables, weights_in)
        ext, after, done = pl.pallas_call(
            functools.partial(far2_kernel, half, cols),
            out_shape=far_shapes,
            in_specs=[vmem()] * 6,
            out_specs=[vmem()] * 3,
            scratch_shapes=[far_feats],
            input_output_aliases={3: 0, 4: 1, 5: 2},
            compiler_params=params,
            name="far_rows_2",
        )(lon_halo, tables, weights_in, *far)
        near_shapes = [shape(2 * HALO + SPAN, lon_total, chans), shape(GROUP + 2 * SPAN, lon1, chans)]
        near_feats = pltpu.VMEM((GROUP, lon1, basis * chans), BF16)
        ext, near, halo_tab, done = pl.pallas_call(
            functools.partial(near1_kernel, half),
            out_shape=near_shapes
            + [
                shape(PAIR * basis * BLOCK, lanes),
                jax.ShapeDtypeStruct(turned, F32),
            ],
            in_specs=[vmem()] * 7,
            out_specs=[vmem()] * 4,
            scratch_shapes=[near_feats],
            input_output_aliases={6: 3},
            compiler_params=params,
            name="near_rows_1",
        )(ext, after, lat_halos[0], tables, weights_in, order, done)
        *_, keep, send = pl.pallas_call(
            functools.partial(near2_kernel, half, cols),
            out_shape=near_shapes + [jax.ShapeDtypeStruct(turned, F32)] + [piece] * 2,
            in_specs=[vmem()] * 7,
            out_specs=[vmem()] * 5,
            scratch_shapes=[near_feats],
            input_output_aliases={4: 0, 5: 1, 6: 2},
            compiler_params=params,
            name="near_rows_2",
        )(corners[0], halo_tab, tables, weights_in, ext, near, done)
    else:
        keep, send = pl.pallas_call(
            functools.partial(all_kernel, half, cols),
            out_shape=[piece] * 2,
            in_specs=[vmem()] * (5 + 2 * sides),
            out_specs=[vmem()] * 2,
            scratch_shapes=[
                pltpu.VMEM((lat_rows + 2 * HALO, lon_total, chans), BF16),
                pltpu.VMEM((lat_rows + 2 * PAIR, lon1, basis * chans), BF16),
                pltpu.VMEM((lat_rows + 2 * SPAN, lon1, chans), BF16),
                scratch(*turned),
            ],
            compiler_params=params,
            name="all_rows",
        )(fields, lon_halo, *lat_halos, *corners, tables, weights_in, order)
    got = lax.ppermute(send, "chan", swap)

    out = pl.pallas_call(
        join_kernel,
        out_shape=shape(cols, lat_rows, width),
        in_specs=[vmem()] * 2,
        out_specs=hbm(),
        scratch_shapes=[pltpu.SemaphoreType.DMA((2,))],
        compiler_params=params,
        name="join",
    )(keep, got)
    return jnp.transpose(out, (1, 0, 2))


def solution(mesh):
    return jax.shard_map(
        per_device,
        mesh=mesh,
        in_specs=(
            P(("groups", "lat"), "lon", "chan"),
            P("lat", None),
            P("lat"),
            P("lat"),
            P("lat", None, None, None),
            P(),
        ),
        out_specs=P(("groups", "lat"), "lon", "chan"),
        check_vma=False,
    )
```

```python
import functools

import jax
import jax.numpy as jnp
from jax import lax
from jax.experimental import pallas as pl
from jax.experimental.pallas import tpu as pltpu
from jax.sharding import PartitionSpec as P

LAYERS = 2
SPAN = 2
HALO = LAYERS * SPAN
BLOCK = 16
WINDOW = 2 * BLOCK
GROUP = 4
PAIR = 2
WIDE = BLOCK
SHIFT = BLOCK // 2
VMEM_LIMIT = 48 * 1024 * 1024
BF16 = jnp.bfloat16
F32 = jnp.float32


def vmem():
    return pl.BlockSpec(memory_space=pltpu.VMEM)


def smem():
    return pl.BlockSpec(memory_space=pltpu.SMEM)


def hbm():
    return pl.BlockSpec(memory_space=pltpu.HBM)


def in_hbm(x):
    return pltpu.with_memory_space_constraint(x, pltpu.HBM)


def by_row(count):
    total = count * BLOCK
    out_row = lax.broadcasted_iota(jnp.int32, (total, total), 0)
    in_row = lax.broadcasted_iota(jnp.int32, (total, total), 1)
    source = (out_row % BLOCK) * count + out_row // BLOCK
    return (in_row == source).astype(F32).astype(BF16)


def toeplitz(rows_tab, order):
    moved = jnp.concatenate(
        [rows_tab if jj == 0 else pltpu.roll(rows_tab, jj, 1) for jj in range(BLOCK)], axis=0
    ).astype(BF16)
    return jnp.dot(order, moved, preferred_element_type=F32).astype(BF16)


def band_rows(refs, slots, rows):
    sup_ref, count_ref, reach_ref, psi_ref = refs
    lat_rows, sup, basis, offsets = psi_ref.shape
    lanes = slots.shape[3]
    slots[...] = jnp.zeros_like(slots)
    for n, i in enumerate(rows):
        row = lax.axis_index("lat") * lat_rows + i
        values = [psi_ref[i, s] for s in range(sup)]
        places = [jnp.where(s < count_ref[i], sup_ref[i, s] - row, -lat_rows) for s in range(sup)]
        for rel in range(2 * SPAN + 1):
            total = jnp.zeros((basis, offsets), F32)
            for value, at in zip(values, places):
                total = total + jnp.where(at == rel - SPAN, value, 0.0)
            slots[n, rel, :, 0:offsets] = total
    off = lax.broadcasted_iota(jnp.int32, (basis, lanes), 1) % WINDOW - offsets // 2
    bands = []
    for n, i in enumerate(rows):
        band = slots[n, 0]
        for rel in range(1, 2 * SPAN + 1):
            band = band + pltpu.roll(slots[n, rel], rel * WINDOW, 1)
        bands.append(jnp.where(jnp.abs(off) <= reach_ref[i], band, 0.0))
    return bands


def put_pair(scr, bands):
    for m, band in enumerate(bands):
        basis = band.shape[0]
        scr[m * basis : (m + 1) * basis, :] = (
            band if m == 0 else pltpu.roll(band, m * WINDOW, 1)
        )


def turn(ref, lon_from, lon_to, wide_scr):
    _, lat_rows, width = ref.shape
    wide_scr[lon_from * lat_rows : lon_to * lat_rows, :] = (
        ref[lon_from:lon_to].astype(F32).reshape((lon_to - lon_from) * lat_rows, width)
    )


def turned_row(wide_scr, lat_rows, row, start, count):
    return wide_scr[pl.ds(start * lat_rows + row, count, stride=lat_rows), :].astype(BF16)


def own_kernel(sides, half, *refs):
    sources, (part_ref, edge_ref), refs = refs[:5], refs[5:7], refs[7:]
    lat_refs, refs = refs[:sides], refs[sides:]
    smems, (psi_ref, state_ref, slots, pair_scr, wide_scr, sems) = refs[:3], refs[3:]
    copies = [
        pltpu.make_async_copy(source, dest, sems.at[n])
        for n, (source, dest) in enumerate(zip(sources, (*smems, psi_ref, state_ref)))
    ]
    for copy in copies:
        copy.start()
    cols, lat_rows, width = state_ref.shape
    part = part_ref.shape[1]
    chan = lax.axis_index("chan")
    wide_scr[cols * lat_rows :, :] = jnp.zeros(
        (wide_scr.shape[0] - cols * lat_rows, width), F32
    )
    for copy in copies[:4]:
        copy.wait()
    firsts = [first + (HALO - PAIR) * (n == 0) for n, first in enumerate(needed_rows(2, lat_rows))]
    if sides == 1:
        firsts = [(1 - lax.axis_index("lat")) * (lat_rows - PAIR)]
    rows = [first + m for first in firsts for m in range(PAIR)]
    bands = band_rows((*smems, psi_ref), slots, rows)
    for n in range(sides):
        put_pair(pair_scr, bands[n * PAIR : (n + 1) * PAIR])
        per = pair_scr.shape[0] // HALO
        for t in range(HALO):
            extra = [
                pair_scr[row : row + 1, x : x + width]
                for row in range(per * t, per * (t + 1))
                for x in range(0, pair_scr.shape[1], width)
            ]
            lat_refs[n][t, cols:, :] = jnp.concatenate(extra, axis=0).astype(BF16)
    copies[4].wait()
    turn(state_ref, 0, cols, wide_scr)
    for n, first in enumerate(needed_rows(sides, lat_rows)):
        for t in range(HALO):
            lat_refs[n][t, 0:cols, :] = turned_row(wide_scr, lat_rows, first + t, 0, cols)
    for r in range(lat_rows):
        part_ref[r] = turned_row(wide_scr, lat_rows, r, (half - WIDE) * chan, part)
        edge_ref[r] = turned_row(wide_scr, lat_rows, r, (cols - WIDE) * chan, WIDE)


def edges_kernel(
    sides, half, part_ref, edge_ref, other_ref, fields_ref, lon_ref, *rest
):
    corner_refs, (wide_scr,) = rest[:sides], rest[sides:]
    cols, lat_rows, width = other_ref.shape
    lon_total = fields_ref.shape[1]
    part = part_ref.shape[1]
    chan = lax.axis_index("chan")
    wide_scr[cols * lat_rows :, :] = jnp.zeros(
        (wide_scr.shape[0] - cols * lat_rows, width), F32
    )

    def build(core):
        start = 0 if core == 0 else half - WIDE
        edge = 0 if core == 0 else cols - WIDE
        stop = start + part if core == 0 else cols
        at = WIDE if core == 0 else 0
        own = slice(core * width, (core + 1) * width)
        lane = slice((1 - core) * width, (2 - core) * width)
        turn(other_ref, start, stop, wide_scr)
        for r in range(lat_rows):
            lon_ref[r, :, own] = edge_ref[r]
            lon_ref[r, :, lane] = turned_row(wide_scr, lat_rows, r, edge, WIDE)
            fields_ref[r, at : at + part, own] = part_ref[r]
            fields_ref[r, at : at + part, lane] = turned_row(wide_scr, lat_rows, r, start, part)
        empty = slice(0, WIDE) if core == 0 else slice(part, lon_total)
        fields_ref[:, empty, :] = jnp.zeros((lat_rows, WIDE, 2 * width), BF16)

    @pl.when(chan == 0)
    def _():
        build(0)

    @pl.when(chan == 1)
    def _():
        build(1)

    for n, first in enumerate(needed_rows(sides, lat_rows)):
        for t in range(HALO):
            corner_refs[n][t] = lon_ref[first + t]


def core_part(core, cols, half):
    start = 0 if core == 0 else half - WIDE
    return start, min(cols - start, half + WIDE)


def for_each_core(body):
    for value in range(2):
        pl.when(lax.axis_index("chan") == value)(functools.partial(body, value))


def relay_kernel(half, cols, halo_ref, _, *out_refs):
    @for_each_core
    def _(core):
        start, count = core_part(1 - core, cols, half)
        for t, out_ref in enumerate(out_refs):
            out_ref[0:count, :] = halo_ref[t, start : start + count, :]


def needed_rows(sides, lat_rows):
    if sides == 1:
        return [(1 - lax.axis_index("lat")) * (lat_rows - HALO)]
    return [lat_rows - HALO, 0]


def tables_kernel(sides, sup_hbm, count_hbm, reach_hbm, psi_hbm, weights_hbm, _, *refs):
    (weights_ref, tables_ref, order_ref), refs = refs[:3], refs[3:]
    smems, (psi_ref, slots, pairs_scr, sems) = refs[:3], refs[3:]
    sources = (sup_hbm, count_hbm, reach_hbm, psi_hbm, weights_hbm)
    copies = [
        pltpu.make_async_copy(source, dest, sems.at[n])
        for n, (source, dest) in enumerate(zip(sources, (*smems, psi_ref, weights_ref)))
    ]
    for copy in copies:
        copy.start()
    lat_rows, _, basis, _ = psi_ref.shape
    lat = lax.axis_index("lat")
    order = by_row(GROUP * basis)
    order_ref[...] = by_row(PAIR * basis)
    for copy in copies[:4]:
        copy.wait()
    bands = band_rows((*smems, psi_ref), slots, range(lat_rows))
    for p in range(lat_rows // PAIR):
        put_pair(pairs_scr.at[p], bands[p * PAIR : (p + 1) * PAIR])

    def group(g):
        first, second = pairs_scr[2 * g], pairs_scr[2 * g + 1]
        return jnp.concatenate([first, pltpu.roll(second, PAIR * WINDOW, 1)], axis=0)

    if sides == 1:
        tables_ref[0] = toeplitz(group(lat), order)
        tables_ref[1] = toeplitz(group(1 - lat), order)
    else:
        for g in range(lat_rows // GROUP):
            tables_ref[g] = toeplitz(group(g), order)
    copies[4].wait()


def gelu(x):
    return 0.5 * x * (1.0 + jnp.tanh(0.7978845608028654 * (x + 0.044715 * (x * x * x))))


def add_lat_halo(cols, half, rows, halo_ref, other_refs):
    width = halo_ref.shape[2]

    @for_each_core
    def _(core):
        start, count = core_part(core, cols, half)
        at = WIDE if core == 0 else 0
        own = slice(core * width, (core + 1) * width)
        other = slice((1 - core) * width, (2 - core) * width)
        for t, row in enumerate(rows):
            row[at : at + count, own] = halo_ref[t, start : start + count, :]
            row[at : at + count, other] = other_refs[t][0:count, :]


def halo_table(cols, halo_ref, order):
    count = order.shape[0] // BLOCK
    per = count // HALO
    rows = []
    for t in range(HALO):
        flat = halo_ref[t, cols:, :].astype(F32)
        wide = flat.shape[0] // per
        for q in range(per):
            parts = [flat[q * wide + x : q * wide + x + 1, :] for x in range(wide)]
            rows.append(jnp.concatenate(parts, axis=1))
    return toeplitz(jnp.concatenate(rows, axis=0), order)


def add_lon_halo(cols, half, rows, halos):
    chan = lax.axis_index("chan")
    count = cols - half + WIDE
    whole = count // BLOCK * BLOCK

    @pl.when(chan == 0)
    def _():
        for row, halo in zip(rows, halos):
            row[0:WIDE, :] = halo[...]

    @pl.when(chan == 1)
    def _():
        for row, halo in zip(rows, halos):
            lon_total, chans = row.shape
            before = row[whole : whole + BLOCK, :].astype(F32)[0 : count - whole, :]
            empty = jnp.zeros((lon_total - count - WIDE, chans), F32)
            row[whole:lon_total, :] = jnp.concatenate(
                [before, halo[...].astype(F32), empty], axis=0
            ).astype(BF16)


def conv(source, table, base, in_rows, feats, first, out_rows, jb, put):
    chans = source.shape[2]
    basis = table.shape[0] // (out_rows * BLOCK)
    taken = source[pl.ds(base, in_rows), jb * BLOCK : jb * BLOCK + WINDOW, :]
    taken = taken.reshape(in_rows * WINDOW, chans)
    result = jnp.dot(table, taken, preferred_element_type=F32).astype(BF16)
    at = slice(put * BLOCK, (put + 1) * BLOCK)
    for m in range(out_rows):
        for k in range(basis):
            begin = (m * basis + k) * BLOCK
            feats[first + m, at, k * chans : (k + 1) * chans] = result[begin : begin + BLOCK, :]


def mix(weights_ref, layer, feats, row, blocks, befores, store):
    _, basis, chans, _ = weights_ref.shape
    count, lons = len(befores), len(blocks) * BLOCK
    mixed = jnp.dot(
        feats[row : row + count, 0:lons, :].reshape(count * lons, basis * chans),
        weights_ref[layer].reshape(basis * chans, chans),
        preferred_element_type=F32,
    )
    for n, before in enumerate(befores):
        before = before[...].astype(F32)
        for put, jb in enumerate(blocks):
            at, begin = SHIFT + jb * BLOCK, n * lons + put * BLOCK
            value = before[at : at + BLOCK, :] + gelu(mixed[begin : begin + BLOCK, :])
            store(n, jb, value)


def into(ref, rows):
    def store(n, jb, value):
        ref[rows[n], jb * BLOCK : (jb + 1) * BLOCK, :] = value.astype(BF16)

    return store


def into_turned(turned, rows, lat_rows):
    def store(n, jb, value):
        width = value.shape[1] // 2
        for c in range(2):
            turned[c, pl.ds(jb * BLOCK * lat_rows + rows[n], BLOCK, stride=lat_rows), :] = value[
                :, c * width : (c + 1) * width
            ]

    return store


def hand_out(turned, keep_ref, send_ref):
    chan = lax.axis_index("chan")
    keep_ref[...] = turned[chan].reshape(keep_ref.shape).astype(BF16)
    send_ref[...] = turned[1 - chan].reshape(send_ref.shape).astype(BF16)


def for_each_lat(body):
    for value in range(2):
        pl.when(lax.axis_index("lat") == value)(functools.partial(body, value))


def inner(count):
    return range(1, count - 2)


def outer(count):
    return [0, count - 2, count - 1]


def half_table(tables_ref, second):
    rows = tables_ref.shape[1] // 2
    return tables_ref[1, rows * second : rows * (second + 1), :]


def far_rows(lat, fields, after, tables_ref, weights_ref, feats, turned, blocks1, blocks2):
    lat_rows = after.shape[0]
    far = GROUP * lat
    near = GROUP - far
    mid = GROUP - PAIR * lat
    rows8 = GROUP + 2 * SPAN
    for put, jb in enumerate(blocks1):
        conv(fields, tables_ref[0], far, rows8, feats, 0, GROUP, jb, put)
        conv(fields, half_table(tables_ref, lat), near, rows8, feats, GROUP, PAIR, jb, put)
    dests = [SPAN + t for t in range(GROUP)]
    dests += [(GROUP + SPAN) * (1 - lat) + t for t in range(PAIR)]
    befores = [SPAN + far + t for t in range(GROUP)] + [SPAN + mid + t for t in range(PAIR)]
    step = len(dests) // 2
    for t in range(0, len(dests), step):
        rows = [fields.at[r] for r in befores[t : t + step]]
        mix(weights_ref, 0, feats, t, blocks1, rows, into(after, dests[t : t + step]))
    for put, jb in enumerate(blocks2):
        conv(after, tables_ref[0], 0, rows8, feats, 0, GROUP, jb, put)
    for t in range(0, GROUP, PAIR):
        befores = [after.at[SPAN + t + m] for m in range(PAIR)]
        rows = [far + t + m for m in range(PAIR)]
        mix(weights_ref, 1, feats, t, blocks2, befores, into_turned(turned, rows, lat_rows))


def far1_kernel(
    half, own_ref, tables_ref, weights_ref, fields_ref, after_ref, turned_ref, feats
):
    lat_rows, lon_total, chans = own_ref.shape
    for t in range(SPAN):
        fields_ref[t] = jnp.zeros((lon_total, chans), BF16)
        fields_ref[SPAN + lat_rows + t] = jnp.zeros((lon_total, chans), BF16)
    fields_ref[SPAN : SPAN + lat_rows] = own_ref[...]

    @for_each_lat
    def _(lat):
        for t in range(SPAN):
            after_ref[(GROUP + SPAN) * lat + t] = jnp.zeros((lon_total - BLOCK, chans), BF16)
        far_rows(
            lat,
            fields_ref,
            after_ref,
            tables_ref,
            weights_ref,
            feats,
            turned_ref,
            inner(lon_total // BLOCK - 1),
            inner(half // BLOCK),
        )


def far2_kernel(
    half,
    cols,
    lon_ref,
    tables_ref,
    weights_ref,
    fields_in,
    after_in,
    turned_in,
    fields_ref,
    after_ref,
    turned_ref,
    feats,
):
    lat_rows = lon_ref.shape[0]
    add_lon_halo(
        cols,
        half,
        [fields_ref.at[SPAN + r] for r in range(lat_rows)],
        [lon_ref.at[r] for r in range(lat_rows)],
    )

    @for_each_lat
    def _(lat):
        far_rows(
            lat,
            fields_ref,
            after_ref,
            tables_ref,
            weights_ref,
            feats,
            turned_ref,
            outer(fields_ref.shape[1] // BLOCK - 1),
            outer(half // BLOCK),
        )


def near_rows(lat, fields, near, table, tables_ref, weights_ref, feats, turned, blocks1, blocks2):
    lat_rows = near.shape[0]
    rows6, rows8 = PAIR + 2 * SPAN, GROUP + 2 * SPAN
    group = SPAN * lat
    beyond = HALO * (1 - lat)
    for put, jb in enumerate(blocks1):
        conv(fields, half_table(tables_ref, 1 - lat), group, rows8, feats, 0, PAIR, jb, put)
    for put, jb in enumerate(blocks1):
        conv(fields, table[:, 0 : rows6 * WINDOW], beyond, rows6, feats, PAIR, PAIR, jb, put)
    befores = [fields.at[HALO + m] for m in range(PAIR)]
    befores += [fields.at[beyond + SPAN + m] for m in range(PAIR)]
    dests = [GROUP * (1 - lat) + SPAN * lat + m for m in range(PAIR)]
    dests += [(GROUP + SPAN) * (1 - lat) + m for m in range(PAIR)]
    for t in range(0, GROUP, PAIR):
        rows = slice(t, t + PAIR)
        mix(weights_ref, 0, feats, t, blocks1, befores[rows], into(near, dests[rows]))
    for put, jb in enumerate(blocks2):
        conv(near, tables_ref[1], 0, GROUP + 2 * SPAN, feats, 0, GROUP, jb, put)
    for t in range(0, GROUP, PAIR):
        befores = [near.at[SPAN + t + m] for m in range(PAIR)]
        rows = [GROUP * (1 - lat) + t + m for m in range(PAIR)]
        mix(weights_ref, 1, feats, t, blocks2, befores, into_turned(turned, rows, lat_rows))


def near_kernel(
    half,
    cols,
    ext_ref,
    next_ref,
    halo_ref,
    corner_ref,
    tables_ref,
    weights_ref,
    order_ref,
    *rest,
):
    other_refs, (_, turned_ref, keep_ref, send_ref, fields, near, feats) = rest[:HALO], rest[HALO:]
    lon_total = ext_ref.shape[1]

    @for_each_lat
    def _(lat):
        halo = (HALO + SPAN) * (1 - lat)
        own = HALO * lat
        for t in range(HALO + SPAN):
            fields[own + t] = ext_ref[SPAN + SPAN * (1 - lat) + t]
        rows = [fields.at[halo + t] for t in range(HALO)]
        add_lat_halo(cols, half, rows, halo_ref, other_refs)
        add_lon_halo(cols, half, rows, [corner_ref.at[t] for t in range(HALO)])
        for t in range(GROUP):
            near[GROUP * lat + t] = next_ref[GROUP * (1 - lat) + t]
        near_rows(
            lat,
            fields,
            near,
            halo_table(cols, halo_ref, order_ref[...]),
            tables_ref,
            weights_ref,
            feats,
            turned_ref,
            range(lon_total // BLOCK - 1),
            range(half // BLOCK),
        )

    hand_out(turned_ref, keep_ref, send_ref)


def all_kernel(half, cols, own_ref, lon_ref, *rest):
    lat_refs, corner_refs, rest = rest[0:2], rest[2:4], rest[4:]
    other_refs, rest = rest[: 2 * HALO], rest[2 * HALO :]
    tables_ref, weights_ref, order_ref, keep_ref, send_ref, fields, feats, after, turned = rest
    lat_rows, lon_total, chans = own_ref.shape
    groups = lat_rows // GROUP
    lon1 = lon_total - BLOCK
    halo_base = [0, lat_rows + HALO]
    win_base = [0, lat_rows + HALO - SPAN]
    out_base = [0, lat_rows + SPAN]
    rows6 = PAIR + 2 * SPAN

    fields[HALO : HALO + lat_rows] = own_ref[...]
    rows = [fields.at[HALO + r] for r in range(lat_rows)]
    halos = [lon_ref.at[r] for r in range(lat_rows)]
    for n in range(2):
        halo_rows = [fields.at[halo_base[n] + t] for t in range(HALO)]
        add_lat_halo(
            cols, half, halo_rows, lat_refs[n], other_refs[n * HALO : (n + 1) * HALO]
        )
        rows += halo_rows
        halos += [corner_refs[n].at[t] for t in range(HALO)]
    add_lon_halo(cols, half, rows, halos)
    halo_tables = [
        halo_table(cols, lat_refs[n], order_ref[...])[:, 0 : rows6 * WINDOW] for n in range(2)
    ]
    blocks = range(lon1 // BLOCK)
    for jb in blocks:
        for g in range(groups):
            base = HALO - SPAN + g * GROUP
            conv(
                fields, tables_ref[g], base, GROUP + 2 * SPAN, feats, g * GROUP, GROUP, jb, jb
            )
        for n in range(2):
            first = lat_rows + n * PAIR
            conv(fields, halo_tables[n], win_base[n], rows6, feats, first, PAIR, jb, jb)
    dests = [SPAN + i for i in range(lat_rows)]
    dests += [out_base[n] + m for n in range(2) for m in range(PAIR)]
    for i in range(0, len(dests), PAIR):
        befores = [fields.at[dest + SPAN] for dest in dests[i : i + PAIR]]
        mix(weights_ref, 0, feats, i, blocks, befores, into(after, dests[i : i + PAIR]))
    blocks = range(half // BLOCK)
    for jb in blocks:
        for g in range(groups):
            base = g * GROUP
            conv(after, tables_ref[g], base, GROUP + 2 * SPAN, feats, base, GROUP, jb, jb)
    for i in range(0, lat_rows, PAIR):
        befores = [after.at[SPAN + i + m] for m in range(PAIR)]
        rows = [i + m for m in range(PAIR)]
        mix(weights_ref, 1, feats, i, blocks, befores, into_turned(turned, rows, lat_rows))
    hand_out(turned, keep_ref, send_ref)


def join_kernel(keep_ref, got_ref, out_hbm, sems):
    half = keep_ref.shape[0]
    rest = out_hbm.shape[0] - half
    chan = lax.axis_index("chan")

    def copy(first, second):
        copies = [
            pltpu.make_async_copy(first, out_hbm.at[0:half], sems.at[0]),
            pltpu.make_async_copy(second.at[0:rest], out_hbm.at[half : half + rest], sems.at[1]),
        ]
        for c in copies:
            c.start()
        for c in copies:
            c.wait()

    @pl.when(chan == 0)
    def _():
        copy(keep_ref, got_ref)

    @pl.when(chan == 1)
    def _():
        copy(got_ref, keep_ref)


def per_device(state, sup_rows, sup_count, lon_reach, psi, weights):
    lat_rows, cols, width = state.shape
    basis = psi.shape[2]
    chans = weights.shape[2]
    lats, lons = lax.axis_size("lat"), lax.axis_size("lon")
    sides = 1 if lats == 2 else 2
    groups = lat_rows // GROUP
    lanes = (GROUP + 2 * SPAN) * WINDOW
    half = -(-cols // (2 * BLOCK)) * BLOCK
    part = half + WIDE
    lon_total = half + 2 * WIDE
    lon1 = lon_total - BLOCK
    swap = [(0, 1), (1, 0)]
    params = pltpu.CompilerParams(vmem_limit_bytes=VMEM_LIMIT)

    def shape(*dims):
        return jax.ShapeDtypeStruct(dims, BF16)

    def to_lat(step):
        if lats == 2:
            return [(a, 1 - a) for a in range(lats)]
        return [(a, a + step) for a in range(lats) if 0 <= a + step < lats]

    forth = [((z, 1), ((z + 1) % lons, 0)) for z in range(lons)]
    back = [((z, 0), ((z - 1) % lons, 1)) for z in range(lons)]
    to_lon = forth + back

    own = jnp.transpose(state, (1, 0, 2))
    other = lax.ppermute(own, "chan", swap)

    def scratch(*dims):
        return pltpu.VMEM(dims, F32)

    wide = scratch((half + part) * lat_rows, width)
    smalls = [sup_rows, sup_count, lon_reach]
    extra = PAIR * basis * lanes // (HALO * width)
    part_own, edge_own, *sends = pl.pallas_call(
        functools.partial(own_kernel, sides, half),
        out_shape=[
            shape(lat_rows, part, width),
            shape(lat_rows, WIDE, width),
        ]
        + [shape(HALO, cols + extra, width)] * sides,
        in_specs=[hbm()] * 5,
        out_specs=[vmem()] * (2 + sides),
        scratch_shapes=[pltpu.SMEM(x.shape, x.dtype) for x in smalls]
        + [
            scratch(*psi.shape),
            pltpu.VMEM(own.shape, BF16),
            scratch(sides * PAIR, 2 * SPAN + 1, basis, lanes),
            scratch(PAIR * basis, lanes),
            wide,
            pltpu.SemaphoreType.DMA((5,)),
        ],
        compiler_params=params,
        name="own",
    )(*[in_hbm(x) for x in smalls + [psi, own]])

    steps = [1, -1][:sides]
    lat_halos = [lax.ppermute(x, "lat", to_lat(step)) for x, step in zip(sends, steps)]

    fields, lon_edge, *corners = pl.pallas_call(
        functools.partial(edges_kernel, sides, half),
        out_shape=[shape(lat_rows, lon_total, chans), shape(lat_rows, WIDE, chans)]
        + [shape(HALO, WIDE, chans)] * sides,
        in_specs=[vmem()] * 3,
        out_specs=[vmem()] * (2 + sides),
        scratch_shapes=[wide],
        compiler_params=params,
        name="edges",
    )(part_own, edge_own, other)

    lon_halo = lax.ppermute(
        lon_edge, ("lon", "chan"), [(z * 2 + c, y * 2 + d) for (z, c), (y, d) in to_lon]
    )

    corners = [
        lax.ppermute(
            x,
            ("lon", "lat", "chan"),
            [
                ((z * lats + a) * 2 + c, (y * lats + b) * 2 + d)
                for a, b in to_lat(step)
                for (z, c), (y, d) in to_lon
            ],
        )
        for x, step in zip(corners, steps)
    ]

    weights_in, tables, order = pl.pallas_call(
        functools.partial(tables_kernel, sides),
        out_shape=[
            shape(*weights.shape),
            shape(groups, GROUP * basis * BLOCK, lanes),
            shape(PAIR * basis * BLOCK, PAIR * basis * BLOCK),
        ],
        in_specs=[hbm()] * 5 + [vmem()],
        out_specs=[vmem()] * 3,
        scratch_shapes=[pltpu.SMEM(x.shape, x.dtype) for x in smalls]
        + [
            scratch(*psi.shape),
            scratch(lat_rows, 2 * SPAN + 1, basis, lanes),
            scratch(lat_rows // PAIR, PAIR * basis, lanes),
            pltpu.SemaphoreType.DMA((5,)),
        ],
        compiler_params=params,
        name="tables",
    )(*[in_hbm(x) for x in smalls + [psi, weights]], lon_edge)

    def to_other_core(halo, after):
        relayed = pl.pallas_call(
            functools.partial(relay_kernel, half, cols),
            out_shape=[shape(part, width)] * HALO,
            in_specs=[vmem()] * 2,
            out_specs=[vmem()] * HALO,
            compiler_params=params,
            name="relay",
        )(halo, after)
        return [lax.ppermute(x, "chan", swap) for x in relayed]

    piece = shape(half, lat_rows, width)
    turned = (2, half * lat_rows, width)
    if sides == 1:
        far_shapes = [
            shape(lat_rows + 2 * SPAN, lon_total, chans),
            shape(lat_rows, lon1, chans),
            jax.ShapeDtypeStruct(turned, F32),
        ]
        far_feats = pltpu.VMEM((GROUP + PAIR, lon1, basis * chans), BF16)
        far = pl.pallas_call(
            functools.partial(far1_kernel, half),
            out_shape=far_shapes,
            in_specs=[vmem()] * 3,
            out_specs=[vmem()] * 3,
            scratch_shapes=[far_feats],
            compiler_params=params,
            name="far_rows_1",
        )(fields, tables, weights_in)
        lat_other = to_other_core(lat_halos[0], far[1])
        ext, after, done = pl.pallas_call(
            functools.partial(far2_kernel, half, cols),
            out_shape=far_shapes,
            in_specs=[vmem()] * 6,
            out_specs=[vmem()] * 3,
            scratch_shapes=[far_feats],
            input_output_aliases={3: 0, 4: 1, 5: 2},
            compiler_params=params,
            name="far_rows_2",
        )(lon_halo, tables, weights_in, *far)
        _, keep, send = pl.pallas_call(
            functools.partial(near_kernel, half, cols),
            out_shape=[jax.ShapeDtypeStruct(turned, F32)] + [piece] * 2,
            in_specs=[vmem()] * (8 + HALO),
            out_specs=[vmem()] * 3,
            scratch_shapes=[
                pltpu.VMEM((2 * HALO + SPAN, lon_total, chans), BF16),
                pltpu.VMEM((GROUP + 2 * SPAN, lon1, chans), BF16),
                pltpu.VMEM((GROUP, lon1, basis * chans), BF16),
            ],
            input_output_aliases={7 + HALO: 0},
            compiler_params=params,
            name="near_rows",
        )(
            ext,
            after,
            lat_halos[0],
            corners[0],
            tables,
            weights_in,
            order,
            *lat_other,
            done,
        )
    else:
        lat_others = sum([to_other_core(h, tables) for h in lat_halos], [])
        keep, send = pl.pallas_call(
            functools.partial(all_kernel, half, cols),
            out_shape=[piece] * 2,
            in_specs=[vmem()] * (5 + (2 + HALO) * sides),
            out_specs=[vmem()] * 2,
            scratch_shapes=[
                pltpu.VMEM((lat_rows + 2 * HALO, lon_total, chans), BF16),
                pltpu.VMEM((lat_rows + 2 * PAIR, lon1, basis * chans), BF16),
                pltpu.VMEM((lat_rows + 2 * SPAN, lon1, chans), BF16),
                scratch(*turned),
            ],
            compiler_params=params,
            name="all_rows",
        )(fields, lon_halo, *lat_halos, *corners, *lat_others, tables, weights_in, order)
    got = lax.ppermute(send, "chan", swap)

    out = pl.pallas_call(
        join_kernel,
        out_shape=shape(cols, lat_rows, width),
        in_specs=[vmem()] * 2,
        out_specs=hbm(),
        scratch_shapes=[pltpu.SemaphoreType.DMA((2,))],
        compiler_params=params,
        name="join",
    )(keep, got)
    return jnp.transpose(out, (1, 0, 2))


def solution(mesh):
    return jax.shard_map(
        per_device,
        mesh=mesh,
        in_specs=(
            P(("groups", "lat"), "lon", "chan"),
            P("lat", None),
            P("lat"),
            P("lat"),
            P("lat", None, None, None),
            P(),
        ),
        out_specs=P(("groups", "lat"), "lon", "chan"),
        check_vma=False,
    )
```

```python
import functools

import jax
import jax.numpy as jnp
from jax import lax
from jax.experimental import pallas as pl
from jax.experimental.pallas import tpu as pltpu
from jax.sharding import PartitionSpec as P

LAYERS = 2
SPAN = 2
HALO = LAYERS * SPAN
BLOCK = 16
WINDOW = 2 * BLOCK
GROUP = 4
PAIR = 2
WIDE = BLOCK
LATE = 2 * BLOCK
SHIFT = BLOCK // 2
VMEM_LIMIT = 48 * 1024 * 1024
BF16 = jnp.bfloat16
F32 = jnp.float32


def vmem():
    return pl.BlockSpec(memory_space=pltpu.VMEM)


def smem():
    return pl.BlockSpec(memory_space=pltpu.SMEM)


def hbm():
    return pl.BlockSpec(memory_space=pltpu.HBM)


def in_hbm(x):
    return pltpu.with_memory_space_constraint(x, pltpu.HBM)


def by_row(count):
    total = count * BLOCK
    out_row = lax.broadcasted_iota(jnp.int32, (total, total), 0)
    in_row = lax.broadcasted_iota(jnp.int32, (total, total), 1)
    source = (out_row % BLOCK) * count + out_row // BLOCK
    return (in_row == source).astype(F32).astype(BF16)


def toeplitz(rows_tab, order):
    moved = jnp.concatenate(
        [rows_tab if jj == 0 else pltpu.roll(rows_tab, jj, 1) for jj in range(BLOCK)], axis=0
    ).astype(BF16)
    return jnp.dot(order, moved, preferred_element_type=F32).astype(BF16)


def band_rows(refs, slots, rows):
    sup_ref, count_ref, reach_ref, psi_ref = refs
    lat_rows, sup, basis, offsets = psi_ref.shape
    lanes = slots.shape[3]
    slots[...] = jnp.zeros_like(slots)
    for n, i in enumerate(rows):
        row = lax.axis_index("lat") * lat_rows + i
        values = [psi_ref[i, s] for s in range(sup)]
        places = [jnp.where(s < count_ref[i], sup_ref[i, s] - row, -lat_rows) for s in range(sup)]
        for rel in range(2 * SPAN + 1):
            total = jnp.zeros((basis, offsets), F32)
            for value, at in zip(values, places):
                total = total + jnp.where(at == rel - SPAN, value, 0.0)
            slots[n, rel, :, 0:offsets] = total
    off = lax.broadcasted_iota(jnp.int32, (basis, lanes), 1) % WINDOW - offsets // 2
    bands = []
    for n, i in enumerate(rows):
        band = slots[n, 0]
        for rel in range(1, 2 * SPAN + 1):
            band = band + pltpu.roll(slots[n, rel], rel * WINDOW, 1)
        bands.append(jnp.where(jnp.abs(off) <= reach_ref[i], band, 0.0))
    return bands


def put_pair(scr, bands):
    for m, band in enumerate(bands):
        basis = band.shape[0]
        scr[m * basis : (m + 1) * basis, :] = (
            band if m == 0 else pltpu.roll(band, m * WINDOW, 1)
        )


def turn(ref, lon_from, lon_to, wide_scr):
    _, lat_rows, width = ref.shape
    wide_scr[lon_from * lat_rows : lon_to * lat_rows, :] = (
        ref[lon_from:lon_to].astype(F32).reshape((lon_to - lon_from) * lat_rows, width)
    )


def turned_row(wide_scr, lat_rows, row, start, count):
    return wide_scr[pl.ds(start * lat_rows + row, count, stride=lat_rows), :].astype(BF16)


def own_kernel(sides, half, *refs):
    sources, (part_ref, edge_ref, bands_ref), refs = refs[:5], refs[5:8], refs[8:]
    smems, (psi_ref, state_ref, slots, pair_scr, wide_scr, sems) = refs[:3], refs[3:]
    copies = [
        pltpu.make_async_copy(source, dest, sems.at[n])
        for n, (source, dest) in enumerate(zip(sources, (*smems, psi_ref, state_ref)))
    ]
    for copy in copies:
        copy.start()
    cols, lat_rows, width = state_ref.shape
    part = part_ref.shape[1]
    chan = lax.axis_index("chan")
    wide_scr[cols * lat_rows :, :] = jnp.zeros(
        (wide_scr.shape[0] - cols * lat_rows, width), F32
    )
    for copy in copies[:4]:
        copy.wait()
    firsts = [first + (HALO - PAIR) * (n == 0) for n, first in enumerate(needed_rows(2, lat_rows))]
    if sides == 1:
        firsts = [(1 - lax.axis_index("lat")) * (lat_rows - PAIR)]
    rows = [first + m for first in firsts for m in range(PAIR)]
    bands = band_rows((*smems, psi_ref), slots, rows)
    for n in range(sides):
        put_pair(pair_scr, bands[n * PAIR : (n + 1) * PAIR])
        bands_ref[n] = pair_scr[...].astype(BF16)
    copies[4].wait()
    turn(state_ref, 0, cols, wide_scr)
    for r in range(lat_rows):
        part_ref[r] = turned_row(wide_scr, lat_rows, r, (half - WIDE) * chan, part)
        edge_ref[r] = turned_row(wide_scr, lat_rows, r, (cols - WIDE) * chan, WIDE)


def edges_kernel(
    sides, half, part_ref, edge_ref, other_ref, bands_ref, fields_ref, lon_ref, *rest
):
    lat_refs, corner_refs, (wide_scr,) = rest[:sides], rest[sides : 2 * sides], rest[2 * sides :]
    cols, lat_rows, width = other_ref.shape
    lon_total = fields_ref.shape[1]
    part = part_ref.shape[1]
    chan = lax.axis_index("chan")
    wide_scr[cols * lat_rows :, :] = jnp.zeros(
        (wide_scr.shape[0] - cols * lat_rows, width), F32
    )

    def build(core):
        start = 0 if core == 0 else half - WIDE
        edge = 0 if core == 0 else cols - WIDE
        stop = start + part if core == 0 else cols
        at = WIDE if core == 0 else 0
        own = slice(core * width, (core + 1) * width)
        lane = slice((1 - core) * width, (2 - core) * width)
        turn(other_ref, start, stop, wide_scr)
        for r in range(lat_rows):
            lon_ref[r, :, own] = edge_ref[r]
            lon_ref[r, :, lane] = turned_row(wide_scr, lat_rows, r, edge, WIDE)
            fields_ref[r, at : at + part, own] = part_ref[r]
            fields_ref[r, at : at + part, lane] = turned_row(wide_scr, lat_rows, r, start, part)
        empty = slice(0, WIDE) if core == 0 else slice(part, lon_total)
        fields_ref[:, empty, :] = jnp.zeros((lat_rows, WIDE, 2 * width), BF16)

    @pl.when(chan == 0)
    def _():
        build(0)

    @pl.when(chan == 1)
    def _():
        build(1)

    at = pl.multiple_of((1 - chan) * WIDE, WIDE)
    for n, first in enumerate(needed_rows(sides, lat_rows)):
        for t in range(HALO):
            lat_refs[n][t * part : (t + 1) * part, :] = fields_ref[first + t, pl.ds(at, part), :]
            corner_refs[n][t] = lon_ref[first + t]
        lat_refs[n][HALO * part :, :] = bands_ref[n]


def needed_rows(sides, lat_rows):
    if sides == 1:
        return [(1 - lax.axis_index("lat")) * (lat_rows - HALO)]
    return [lat_rows - HALO, 0]


def tables_kernel(sides, sup_hbm, count_hbm, reach_hbm, psi_hbm, weights_hbm, _, *refs):
    (weights_ref, tables_ref, order_ref), refs = refs[:3], refs[3:]
    smems, (psi_ref, slots, pairs_scr, sems) = refs[:3], refs[3:]
    sources = (sup_hbm, count_hbm, reach_hbm, psi_hbm, weights_hbm)
    copies = [
        pltpu.make_async_copy(source, dest, sems.at[n])
        for n, (source, dest) in enumerate(zip(sources, (*smems, psi_ref, weights_ref)))
    ]
    for copy in copies:
        copy.start()
    lat_rows, _, basis, _ = psi_ref.shape
    lat = lax.axis_index("lat")
    order = by_row(GROUP * basis)
    order_ref[...] = by_row(PAIR * basis)
    for copy in copies[:4]:
        copy.wait()
    bands = band_rows((*smems, psi_ref), slots, range(lat_rows))
    for p in range(lat_rows // PAIR):
        put_pair(pairs_scr.at[p], bands[p * PAIR : (p + 1) * PAIR])

    def group(g):
        first, second = pairs_scr[2 * g], pairs_scr[2 * g + 1]
        return jnp.concatenate([first, pltpu.roll(second, PAIR * WINDOW, 1)], axis=0)

    if sides == 1:
        tables_ref[0] = toeplitz(group(lat), order)
        tables_ref[1] = toeplitz(group(1 - lat), order)
    else:
        for g in range(lat_rows // GROUP):
            tables_ref[g] = toeplitz(group(g), order)
    copies[4].wait()


def gelu(x):
    return 0.5 * x * (1.0 + jnp.tanh(0.7978845608028654 * (x + 0.044715 * (x * x * x))))


def add_lat_halo(rows, lat_ref, part, core):
    at = WIDE if core == 0 else 0
    for t, row in enumerate(rows):
        row[at : at + part, :] = lat_ref[t * part : (t + 1) * part, :]


def halo_table(lat_ref, order):
    count = order.shape[0] // BLOCK
    return toeplitz(lat_ref[lat_ref.shape[0] - count :, :].astype(F32), order)


def add_lon_halo(cols, half, rows, halos, core):
    count = cols - half + WIDE
    whole = count // BLOCK * BLOCK
    for row, halo in zip(rows, halos):
        if core == 0:
            row[0:WIDE, :] = halo[...]
            continue
        lon_total, chans = row.shape
        before = row[whole : whole + BLOCK, :].astype(F32)[0 : count - whole, :]
        empty = jnp.zeros((lon_total - count - WIDE, chans), F32)
        row[whole:lon_total, :] = jnp.concatenate(
            [before, halo[...].astype(F32), empty], axis=0
        ).astype(BF16)


def conv(source, table, base, in_rows, feats, first, out_rows, jb, put):
    chans = source.shape[2]
    basis = table.shape[0] // (out_rows * BLOCK)
    taken = source[pl.ds(base, in_rows), jb * BLOCK : jb * BLOCK + WINDOW, :]
    taken = taken.reshape(in_rows * WINDOW, chans)
    result = jnp.dot(table, taken, preferred_element_type=F32).astype(BF16)
    at = slice(put * BLOCK, (put + 1) * BLOCK)
    for m in range(out_rows):
        for k in range(basis):
            begin = (m * basis + k) * BLOCK
            feats[first + m, at, k * chans : (k + 1) * chans] = result[begin : begin + BLOCK, :]


def mix(weights_ref, layer, feats, row, blocks, befores, store):
    _, basis, chans, _ = weights_ref.shape
    count, lons = len(befores), len(blocks) * BLOCK
    mixed = jnp.dot(
        feats[row : row + count, 0:lons, :].reshape(count * lons, basis * chans),
        weights_ref[layer].reshape(basis * chans, chans),
        preferred_element_type=F32,
    )
    for n, before in enumerate(befores):
        before = before[...].astype(F32)
        for put, jb in enumerate(blocks):
            at, begin = SHIFT + jb * BLOCK, n * lons + put * BLOCK
            value = before[at : at + BLOCK, :] + gelu(mixed[begin : begin + BLOCK, :])
            store(n, jb, value)


def into(ref, rows):
    def store(n, jb, value):
        ref[rows[n], jb * BLOCK : (jb + 1) * BLOCK, :] = value.astype(BF16)

    return store


def into_turned(turned, rows, lat_rows):
    def store(n, jb, value):
        width = value.shape[1] // 2
        for c in range(2):
            turned[c, pl.ds(jb * BLOCK * lat_rows + rows[n], BLOCK, stride=lat_rows), :] = value[
                :, c * width : (c + 1) * width
            ]

    return store


def hand_out(turned, keep_ref, send_ref, core, start, count):
    lat_rows, width = keep_ref.shape[1:]
    at = slice(start * lat_rows, (start + count) * lat_rows)
    for ref, which in ((keep_ref, core), (send_ref, 1 - core)):
        piece = turned[which, at, :].reshape(count, lat_rows, width)
        ref[start : start + count] = piece.astype(BF16)


def late_blocks(core, count):
    return [0] if core == 0 else [count - 2, count - 1]


def early_blocks(core, count):
    late = late_blocks(core, count)
    return [jb for jb in range(count) if jb not in late]


def late_start(core, half):
    return 0 if core == 0 else half - LATE


def for_each_core(body):
    for value in range(2):
        pl.when(lax.axis_index("chan") == value)(functools.partial(body, value))


def for_each_lat(body):
    for value in range(2):
        pl.when(lax.axis_index("lat") == value)(functools.partial(body, value))


def half_table(tables_ref, second):
    rows = tables_ref.shape[1] // 2
    return tables_ref[1, rows * second : rows * (second + 1), :]


def far_rows(lat, fields, after, tables_ref, weights_ref, feats, turned, blocks1, blocks2):
    lat_rows = after.shape[0]
    far = GROUP * lat
    near = GROUP - far
    mid = GROUP - PAIR * lat
    rows8 = GROUP + 2 * SPAN
    for put, jb in enumerate(blocks1):
        conv(fields, tables_ref[0], far, rows8, feats, 0, GROUP, jb, put)
        conv(fields, half_table(tables_ref, lat), near, rows8, feats, GROUP, PAIR, jb, put)
    dests = [SPAN + t for t in range(GROUP)]
    dests += [(GROUP + SPAN) * (1 - lat) + t for t in range(PAIR)]
    befores = [SPAN + far + t for t in range(GROUP)] + [SPAN + mid + t for t in range(PAIR)]
    step = len(dests) // 2
    for t in range(0, len(dests), step):
        rows = [fields.at[r] for r in befores[t : t + step]]
        mix(weights_ref, 0, feats, t, blocks1, rows, into(after, dests[t : t + step]))
    for put, jb in enumerate(blocks2):
        conv(after, tables_ref[0], 0, rows8, feats, 0, GROUP, jb, put)
    for t in range(0, GROUP, PAIR):
        befores = [after.at[SPAN + t + m] for m in range(PAIR)]
        rows = [far + t + m for m in range(PAIR)]
        mix(weights_ref, 1, feats, t, blocks2, befores, into_turned(turned, rows, lat_rows))


def far1_kernel(
    half, own_ref, tables_ref, weights_ref, fields_ref, after_ref, turned_ref, feats
):
    lat_rows, lon_total, chans = own_ref.shape
    for t in range(SPAN):
        fields_ref[t] = jnp.zeros((lon_total, chans), BF16)
        fields_ref[SPAN + lat_rows + t] = jnp.zeros((lon_total, chans), BF16)
    fields_ref[SPAN : SPAN + lat_rows] = own_ref[...]

    def body(lat, core):
        for t in range(SPAN):
            after_ref[(GROUP + SPAN) * lat + t] = jnp.zeros((lon_total - BLOCK, chans), BF16)
        far_rows(
            lat,
            fields_ref,
            after_ref,
            tables_ref,
            weights_ref,
            feats,
            turned_ref,
            early_blocks(core, lon_total // BLOCK - 1),
            early_blocks(core, half // BLOCK),
        )

    for_each_core(lambda core: for_each_lat(functools.partial(body, core=core)))


def far2_kernel(
    half,
    cols,
    lon_ref,
    tables_ref,
    weights_ref,
    fields_in,
    after_in,
    turned_in,
    fields_ref,
    after_ref,
    turned_ref,
    feats,
):
    lat_rows = lon_ref.shape[0]

    def body(lat, core):
        add_lon_halo(
            cols,
            half,
            [fields_ref.at[SPAN + r] for r in range(lat_rows)],
            [lon_ref.at[r] for r in range(lat_rows)],
            core,
        )
        far_rows(
            lat,
            fields_ref,
            after_ref,
            tables_ref,
            weights_ref,
            feats,
            turned_ref,
            late_blocks(core, fields_ref.shape[1] // BLOCK - 1),
            late_blocks(core, half // BLOCK),
        )

    for_each_core(lambda core: for_each_lat(functools.partial(body, core=core)))


def near_rows(lat, fields, near, table, tables_ref, weights_ref, feats, turned, blocks1, blocks2):
    lat_rows = near.shape[0]
    rows6, rows8 = PAIR + 2 * SPAN, GROUP + 2 * SPAN
    group = SPAN * lat
    beyond = HALO * (1 - lat)
    for put, jb in enumerate(blocks1):
        conv(fields, half_table(tables_ref, 1 - lat), group, rows8, feats, 0, PAIR, jb, put)
    for put, jb in enumerate(blocks1):
        conv(fields, table[:, 0 : rows6 * WINDOW], beyond, rows6, feats, PAIR, PAIR, jb, put)
    befores = [fields.at[HALO + m] for m in range(PAIR)]
    befores += [fields.at[beyond + SPAN + m] for m in range(PAIR)]
    dests = [GROUP * (1 - lat) + SPAN * lat + m for m in range(PAIR)]
    dests += [(GROUP + SPAN) * (1 - lat) + m for m in range(PAIR)]
    for t in range(0, GROUP, PAIR):
        rows = slice(t, t + PAIR)
        mix(weights_ref, 0, feats, t, blocks1, befores[rows], into(near, dests[rows]))
    for put, jb in enumerate(blocks2):
        conv(near, tables_ref[1], 0, GROUP + 2 * SPAN, feats, 0, GROUP, jb, put)
    for t in range(0, GROUP, PAIR):
        befores = [near.at[SPAN + t + m] for m in range(PAIR)]
        rows = [GROUP * (1 - lat) + t + m for m in range(PAIR)]
        mix(weights_ref, 1, feats, t, blocks2, befores, into_turned(turned, rows, lat_rows))


def near1_kernel(
    half,
    ext_ref,
    next_ref,
    lat_ref,
    tables_ref,
    weights_ref,
    order_ref,
    turned_in,
    fields_ref,
    near_ref,
    table_ref,
    turned_ref,
    keep_ref,
    send_ref,
    feats,
):
    lon_total = ext_ref.shape[1]

    def body(lat, core):
        halo = (HALO + SPAN) * (1 - lat)
        own = HALO * lat
        for t in range(HALO + SPAN):
            fields_ref[own + t] = ext_ref[SPAN + SPAN * (1 - lat) + t]
        add_lat_halo([fields_ref.at[halo + t] for t in range(HALO)], lat_ref, half + WIDE, core)
        table = halo_table(lat_ref, order_ref[...])
        table_ref[...] = table
        for t in range(GROUP):
            near_ref[GROUP * lat + t] = next_ref[GROUP * (1 - lat) + t]
        near_rows(
            lat,
            fields_ref,
            near_ref,
            table,
            tables_ref,
            weights_ref,
            feats,
            turned_ref,
            early_blocks(core, lon_total // BLOCK - 1),
            early_blocks(core, half // BLOCK),
        )
        hand_out(turned_ref, keep_ref, send_ref, core, 0, half)

    for_each_core(lambda core: for_each_lat(functools.partial(body, core=core)))


def near2_kernel(
    half,
    cols,
    corner_ref,
    table_ref,
    tables_ref,
    weights_ref,
    fields_in,
    near_in,
    turned_in,
    keep_in,
    send_in,
    fields_ref,
    near_ref,
    turned_ref,
    keep_ref,
    send_ref,
    feats,
):
    def body(lat, core):
        halo = (HALO + SPAN) * (1 - lat)
        add_lon_halo(
            cols,
            half,
            [fields_ref.at[halo + t] for t in range(HALO)],
            [corner_ref.at[t] for t in range(HALO)],
            core,
        )
        near_rows(
            lat,
            fields_ref,
            near_ref,
            table_ref[...],
            tables_ref,
            weights_ref,
            feats,
            turned_ref,
            late_blocks(core, fields_ref.shape[1] // BLOCK - 1),
            late_blocks(core, half // BLOCK),
        )
        hand_out(turned_ref, keep_ref, send_ref, core, late_start(core, half), LATE)

    for_each_core(lambda core: for_each_lat(functools.partial(body, core=core)))


def all_kernel(half, cols, own_ref, lon_ref, *rest):
    lat_refs, corner_refs = rest[:2], rest[2:4]
    (tables_ref, weights_ref, order_ref), rest = rest[4:7], rest[7:]
    keep_ref, send_ref, fields, feats, after, turned = rest
    lat_rows, lon_total, chans = own_ref.shape
    groups = lat_rows // GROUP
    lon1 = lon_total - BLOCK
    halo_base = [0, lat_rows + HALO]
    win_base = [0, lat_rows + HALO - SPAN]
    out_base = [0, lat_rows + SPAN]
    rows6 = PAIR + 2 * SPAN

    fields[HALO : HALO + lat_rows] = own_ref[...]

    @for_each_core
    def _(core):
        rows = [fields.at[HALO + r] for r in range(lat_rows)]
        halos = [lon_ref.at[r] for r in range(lat_rows)]
        for n in range(2):
            halo_rows = [fields.at[halo_base[n] + t] for t in range(HALO)]
            add_lat_halo(halo_rows, lat_refs[n], half + WIDE, core)
            rows += halo_rows
            halos += [corner_refs[n].at[t] for t in range(HALO)]
        add_lon_halo(cols, half, rows, halos, core)

    halo_tables = [
        halo_table(lat_refs[n], order_ref[...])[:, 0 : rows6 * WINDOW] for n in range(2)
    ]
    blocks = range(lon1 // BLOCK)
    for jb in blocks:
        for g in range(groups):
            base = HALO - SPAN + g * GROUP
            conv(
                fields, tables_ref[g], base, GROUP + 2 * SPAN, feats, g * GROUP, GROUP, jb, jb
            )
        for n in range(2):
            first = lat_rows + n * PAIR
            conv(fields, halo_tables[n], win_base[n], rows6, feats, first, PAIR, jb, jb)
    dests = [SPAN + i for i in range(lat_rows)]
    dests += [out_base[n] + m for n in range(2) for m in range(PAIR)]
    for i in range(0, len(dests), PAIR):
        befores = [fields.at[dest + SPAN] for dest in dests[i : i + PAIR]]
        mix(weights_ref, 0, feats, i, blocks, befores, into(after, dests[i : i + PAIR]))
    blocks = range(half // BLOCK)
    for jb in blocks:
        for g in range(groups):
            base = g * GROUP
            conv(after, tables_ref[g], base, GROUP + 2 * SPAN, feats, base, GROUP, jb, jb)
    for i in range(0, lat_rows, PAIR):
        befores = [after.at[SPAN + i + m] for m in range(PAIR)]
        rows = [i + m for m in range(PAIR)]
        mix(weights_ref, 1, feats, i, blocks, befores, into_turned(turned, rows, lat_rows))

    @for_each_core
    def _(core):
        hand_out(turned, keep_ref, send_ref, core, 0, half)


def join_kernel(keep_ref, got_ref, out_hbm, sems):
    half = keep_ref.shape[0]
    rest = out_hbm.shape[0] - half

    @for_each_core
    def _(core):
        first, second = (keep_ref, got_ref) if core == 0 else (got_ref, keep_ref)
        copies = [
            pltpu.make_async_copy(first, out_hbm.at[0:half], sems.at[0]),
            pltpu.make_async_copy(second.at[0:rest], out_hbm.at[half : half + rest], sems.at[1]),
        ]
        for copy in copies:
            copy.start()
        for copy in copies:
            copy.wait()


def per_device(state, sup_rows, sup_count, lon_reach, psi, weights):
    lat_rows, cols, width = state.shape
    basis = psi.shape[2]
    chans = weights.shape[2]
    lats, lons = lax.axis_size("lat"), lax.axis_size("lon")
    sides = 1 if lats == 2 else 2
    groups = lat_rows // GROUP
    lanes = (GROUP + 2 * SPAN) * WINDOW
    half = -(-cols // (2 * BLOCK)) * BLOCK
    part = half + WIDE
    lon_total = half + 2 * WIDE
    lon1 = lon_total - BLOCK
    swap = [(0, 1), (1, 0)]
    params = pltpu.CompilerParams(vmem_limit_bytes=VMEM_LIMIT)

    def shape(*dims):
        return jax.ShapeDtypeStruct(dims, BF16)

    def to_lat(step):
        if lats == 2:
            return [(a, 1 - a) for a in range(lats)]
        return [(a, a + step) for a in range(lats) if 0 <= a + step < lats]

    forth = [((z, 1), ((z + 1) % lons, 0)) for z in range(lons)]
    back = [((z, 0), ((z - 1) % lons, 1)) for z in range(lons)]
    to_lon = forth + back

    own = jnp.transpose(state, (1, 0, 2))
    other = lax.ppermute(own, "chan", swap)

    def scratch(*dims):
        return pltpu.VMEM(dims, F32)

    wide = scratch((half + part) * lat_rows, width)
    smalls = [sup_rows, sup_count, lon_reach]
    part_own, edge_own, bands = pl.pallas_call(
        functools.partial(own_kernel, sides, half),
        out_shape=[
            shape(lat_rows, part, width),
            shape(lat_rows, WIDE, width),
            shape(sides, PAIR * basis, lanes),
        ],
        in_specs=[hbm()] * 5,
        out_specs=[vmem()] * 3,
        scratch_shapes=[pltpu.SMEM(x.shape, x.dtype) for x in smalls]
        + [
            scratch(*psi.shape),
            pltpu.VMEM(own.shape, BF16),
            scratch(sides * PAIR, 2 * SPAN + 1, basis, lanes),
            scratch(PAIR * basis, lanes),
            wide,
            pltpu.SemaphoreType.DMA((5,)),
        ],
        compiler_params=params,
        name="own",
    )(*[in_hbm(x) for x in smalls + [psi, own]])

    fields, lon_edge, *sends = pl.pallas_call(
        functools.partial(edges_kernel, sides, half),
        out_shape=[shape(lat_rows, lon_total, chans), shape(lat_rows, WIDE, chans)]
        + [shape(HALO * part + PAIR * basis, chans)] * sides
        + [shape(HALO, WIDE, chans)] * sides,
        in_specs=[vmem()] * 4,
        out_specs=[vmem()] * (2 + 2 * sides),
        scratch_shapes=[wide],
        compiler_params=params,
        name="edges",
    )(part_own, edge_own, other, bands)

    steps = [1, -1][:sides]
    lat_halos = [lax.ppermute(x, "lat", to_lat(step)) for x, step in zip(sends, steps)]
    lon_halo = lax.ppermute(
        lon_edge, ("lon", "chan"), [(z * 2 + c, y * 2 + d) for (z, c), (y, d) in to_lon]
    )

    corners = [
        lax.ppermute(
            x,
            ("lon", "lat", "chan"),
            [
                ((z * lats + a) * 2 + c, (y * lats + b) * 2 + d)
                for a, b in to_lat(step)
                for (z, c), (y, d) in to_lon
            ],
        )
        for x, step in zip(sends[sides:], steps)
    ]

    weights_in, tables, order = pl.pallas_call(
        functools.partial(tables_kernel, sides),
        out_shape=[
            shape(*weights.shape),
            shape(groups, GROUP * basis * BLOCK, lanes),
            shape(PAIR * basis * BLOCK, PAIR * basis * BLOCK),
        ],
        in_specs=[hbm()] * 5 + [vmem()],
        out_specs=[vmem()] * 3,
        scratch_shapes=[pltpu.SMEM(x.shape, x.dtype) for x in smalls]
        + [
            scratch(*psi.shape),
            scratch(lat_rows, 2 * SPAN + 1, basis, lanes),
            scratch(lat_rows // PAIR, PAIR * basis, lanes),
            pltpu.SemaphoreType.DMA((5,)),
        ],
        compiler_params=params,
        name="tables",
    )(*[in_hbm(x) for x in smalls + [psi, weights]], lon_edge)

    piece = shape(half, lat_rows, width)
    turned = (2, half * lat_rows, width)
    if sides == 1:
        far_shapes = [
            shape(lat_rows + 2 * SPAN, lon_total, chans),
            shape(lat_rows, lon1, chans),
            jax.ShapeDtypeStruct(turned, F32),
        ]
        far_feats = pltpu.VMEM((GROUP + PAIR, lon1, basis * chans), BF16)
        far = pl.pallas_call(
            functools.partial(far1_kernel, half),
            out_shape=far_shapes,
            in_specs=[vmem()] * 3,
            out_specs=[vmem()] * 3,
            scratch_shapes=[far_feats],
            compiler_params=params,
            name="far_rows_1",
        )(fields, tables, weights_in)
        ext, after, done = pl.pallas_call(
            functools.partial(far2_kernel, half, cols),
            out_shape=far_shapes,
            in_specs=[vmem()] * 6,
            out_specs=[vmem()] * 3,
            scratch_shapes=[far_feats],
            input_output_aliases={3: 0, 4: 1, 5: 2},
            compiler_params=params,
            name="far_rows_2",
        )(lon_halo, tables, weights_in, *far)
        near_shapes = [shape(2 * HALO + SPAN, lon_total, chans), shape(GROUP + 2 * SPAN, lon1, chans)]
        near_feats = pltpu.VMEM((GROUP, lon1, basis * chans), BF16)
        ext, near, halo_tab, done, keep, send = pl.pallas_call(
            functools.partial(near1_kernel, half),
            out_shape=near_shapes
            + [shape(PAIR * basis * BLOCK, lanes), jax.ShapeDtypeStruct(turned, F32)]
            + [piece] * 2,
            in_specs=[vmem()] * 7,
            out_specs=[vmem()] * 6,
            scratch_shapes=[near_feats],
            input_output_aliases={6: 3},
            compiler_params=params,
            name="near_rows_1",
        )(ext, after, lat_halos[0], tables, weights_in, order, done)
        *_, keep, send = pl.pallas_call(
            functools.partial(near2_kernel, half, cols),
            out_shape=near_shapes + [jax.ShapeDtypeStruct(turned, F32)] + [piece] * 2,
            in_specs=[vmem()] * 9,
            out_specs=[vmem()] * 5,
            scratch_shapes=[near_feats],
            input_output_aliases={4: 0, 5: 1, 6: 2, 7: 3, 8: 4},
            compiler_params=params,
            name="near_rows_2",
        )(corners[0], halo_tab, tables, weights_in, ext, near, done, keep, send)
    else:
        keep, send = pl.pallas_call(
            functools.partial(all_kernel, half, cols),
            out_shape=[piece] * 2,
            in_specs=[vmem()] * (5 + 2 * sides),
            out_specs=[vmem()] * 2,
            scratch_shapes=[
                pltpu.VMEM((lat_rows + 2 * HALO, lon_total, chans), BF16),
                pltpu.VMEM((lat_rows + 2 * PAIR, lon1, basis * chans), BF16),
                pltpu.VMEM((lat_rows + 2 * SPAN, lon1, chans), BF16),
                scratch(*turned),
            ],
            compiler_params=params,
            name="all_rows",
        )(fields, lon_halo, *lat_halos, *corners, tables, weights_in, order)
    got = lax.ppermute(send, "chan", swap)

    out = pl.pallas_call(
        join_kernel,
        out_shape=shape(cols, lat_rows, width),
        in_specs=[vmem()] * 2,
        out_specs=hbm(),
        scratch_shapes=[pltpu.SemaphoreType.DMA((2,))],
        compiler_params=params,
        name="join",
    )(keep, got)
    return jnp.transpose(out, (1, 0, 2))


def solution(mesh):
    return jax.shard_map(
        per_device,
        mesh=mesh,
        in_specs=(
            P(("groups", "lat"), "lon", "chan"),
            P("lat", None),
            P("lat"),
            P("lat"),
            P("lat", None, None, None),
            P(),
        ),
        out_specs=P(("groups", "lat"), "lon", "chan"),
        check_vma=False,
    )
```

```python
import functools

import jax
import jax.numpy as jnp
from jax import lax
from jax.experimental import pallas as pl
from jax.experimental.pallas import tpu as pltpu
from jax.sharding import PartitionSpec as P

LAYERS = 2
SPAN = 2
HALO = LAYERS * SPAN
BLOCK = 16
WINDOW = 2 * BLOCK
GROUP = 4
PAIR = 2
WIDE = BLOCK
LATE = 2 * BLOCK
SHIFT = BLOCK // 2
VMEM_LIMIT = 48 * 1024 * 1024
BF16 = jnp.bfloat16
F32 = jnp.float32


def vmem():
    return pl.BlockSpec(memory_space=pltpu.VMEM)


def smem():
    return pl.BlockSpec(memory_space=pltpu.SMEM)


def hbm():
    return pl.BlockSpec(memory_space=pltpu.HBM)


def in_hbm(x):
    return pltpu.with_memory_space_constraint(x, pltpu.HBM)


def by_row(count):
    total = count * BLOCK
    out_row = lax.broadcasted_iota(jnp.int32, (total, total), 0)
    in_row = lax.broadcasted_iota(jnp.int32, (total, total), 1)
    source = (out_row % BLOCK) * count + out_row // BLOCK
    return (in_row == source).astype(F32).astype(BF16)


def toeplitz(rows_tab, order):
    moved = jnp.concatenate(
        [rows_tab if jj == 0 else pltpu.roll(rows_tab, jj, 1) for jj in range(BLOCK)], axis=0
    ).astype(BF16)
    return jnp.dot(order, moved, preferred_element_type=F32).astype(BF16)


def band_rows(refs, slots, rows):
    sup_ref, count_ref, reach_ref, psi_ref = refs
    lat_rows, sup, basis, offsets = psi_ref.shape
    lanes = slots.shape[3]
    slots[...] = jnp.zeros_like(slots)
    for n, i in enumerate(rows):
        row = lax.axis_index("lat") * lat_rows + i
        values = [psi_ref[i, s] for s in range(sup)]
        places = [jnp.where(s < count_ref[i], sup_ref[i, s] - row, -lat_rows) for s in range(sup)]
        for rel in range(2 * SPAN + 1):
            total = jnp.zeros((basis, offsets), F32)
            for value, at in zip(values, places):
                total = total + jnp.where(at == rel - SPAN, value, 0.0)
            slots[n, rel, :, 0:offsets] = total
    off = lax.broadcasted_iota(jnp.int32, (basis, lanes), 1) % WINDOW - offsets // 2
    bands = []
    for n, i in enumerate(rows):
        band = slots[n, 0]
        for rel in range(1, 2 * SPAN + 1):
            band = band + pltpu.roll(slots[n, rel], rel * WINDOW, 1)
        bands.append(jnp.where(jnp.abs(off) <= reach_ref[i], band, 0.0))
    return bands


def put_pair(scr, bands):
    for m, band in enumerate(bands):
        basis = band.shape[0]
        scr[m * basis : (m + 1) * basis, :] = (
            band if m == 0 else pltpu.roll(band, m * WINDOW, 1)
        )


def turn(ref, lon_from, lon_to, wide_scr):
    _, lat_rows, width = ref.shape
    wide_scr[lon_from * lat_rows : lon_to * lat_rows, :] = (
        ref[lon_from:lon_to].astype(F32).reshape((lon_to - lon_from) * lat_rows, width)
    )


def turned_row(wide_scr, lat_rows, row, start, count):
    return wide_scr[pl.ds(start * lat_rows + row, count, stride=lat_rows), :].astype(BF16)


def own_kernel(sides, half, *refs):
    sources, outs, refs = refs[:6], refs[6:11], refs[11:]
    part_ref, edge_ref, rows_ref, bands_ref, weights_ref = outs
    smems, (psi_ref, state_ref, slots, pairs_scr, wide_scr, sems) = refs[:3], refs[3:]
    copies = [
        pltpu.make_async_copy(source, dest, sems.at[n])
        for n, (source, dest) in enumerate(
            zip(sources, (*smems, psi_ref, state_ref, weights_ref))
        )
    ]
    for copy in copies:
        copy.start()
    cols, lat_rows, width = state_ref.shape
    part = part_ref.shape[1]
    chan = lax.axis_index("chan")
    lat = lax.axis_index("lat")
    wide_scr[cols * lat_rows :, :] = jnp.zeros(
        (wide_scr.shape[0] - cols * lat_rows, width), F32
    )
    for copy in copies[:4]:
        copy.wait()
    bands = band_rows((*smems, psi_ref), slots, range(lat_rows))
    pairs = lat_rows // PAIR
    for p in range(pairs):
        put_pair(pairs_scr.at[p], bands[p * PAIR : (p + 1) * PAIR])
    for g in range(lat_rows // GROUP):
        source = 2 * ((g + lat) % 2 if sides == 1 else g)
        first, second = pairs_scr[source], pairs_scr[source + 1]
        rows_ref[g] = jnp.concatenate([first, pltpu.roll(second, PAIR * WINDOW, 1)], axis=0)
    edges = [(pairs - 1) * (1 - lat)] if sides == 1 else [pairs - 1, 0]
    for n in range(sides):
        bands_ref[n] = pairs_scr[edges[n]].astype(BF16)
    copies[4].wait()
    turn(state_ref, 0, cols, wide_scr)
    for r in range(lat_rows):
        part_ref[r] = turned_row(wide_scr, lat_rows, r, (half - WIDE) * chan, part)
        edge_ref[r] = turned_row(wide_scr, lat_rows, r, (cols - WIDE) * chan, WIDE)
    copies[5].wait()


def edges_kernel(
    sides, half, part_ref, edge_ref, other_ref, bands_ref, fields_ref, lon_ref, *rest
):
    lat_refs, corner_refs, (wide_scr,) = rest[:sides], rest[sides : 2 * sides], rest[2 * sides :]
    cols, lat_rows, width = other_ref.shape
    lon_total = fields_ref.shape[1]
    part = part_ref.shape[1]
    chan = lax.axis_index("chan")
    wide_scr[cols * lat_rows :, :] = jnp.zeros(
        (wide_scr.shape[0] - cols * lat_rows, width), F32
    )

    def build(core):
        start = 0 if core == 0 else half - WIDE
        edge = 0 if core == 0 else cols - WIDE
        stop = start + part if core == 0 else cols
        at = WIDE if core == 0 else 0
        own = slice(core * width, (core + 1) * width)
        lane = slice((1 - core) * width, (2 - core) * width)
        turn(other_ref, start, stop, wide_scr)
        for r in range(lat_rows):
            lon_ref[r, :, own] = edge_ref[r]
            lon_ref[r, :, lane] = turned_row(wide_scr, lat_rows, r, edge, WIDE)
            fields_ref[r, at : at + part, own] = part_ref[r]
            fields_ref[r, at : at + part, lane] = turned_row(wide_scr, lat_rows, r, start, part)
        empty = slice(0, WIDE) if core == 0 else slice(part, lon_total)
        fields_ref[:, empty, :] = jnp.zeros((lat_rows, WIDE, 2 * width), BF16)

    @pl.when(chan == 0)
    def _():
        build(0)

    @pl.when(chan == 1)
    def _():
        build(1)

    at = pl.multiple_of((1 - chan) * WIDE, WIDE)
    for n, first in enumerate(needed_rows(sides, lat_rows)):
        for t in range(HALO):
            lat_refs[n][t * part : (t + 1) * part, :] = fields_ref[first + t, pl.ds(at, part), :]
            corner_refs[n][t] = lon_ref[first + t]
        lat_refs[n][HALO * part :, :] = bands_ref[n]


def needed_rows(sides, lat_rows):
    if sides == 1:
        return [(1 - lax.axis_index("lat")) * (lat_rows - HALO)]
    return [lat_rows - HALO, 0]


def tables_kernel(rows_ref, _, tables_ref, order_ref):
    groups, rows, _ = rows_ref.shape
    order = by_row(rows)
    for g in range(groups):
        tables_ref[g] = toeplitz(rows_ref[g], order)
    order_ref[...] = by_row(order_ref.shape[0] // BLOCK)


def gelu(x):
    return 0.5 * x * (1.0 + jnp.tanh(0.7978845608028654 * (x + 0.044715 * (x * x * x))))


def add_lat_halo(rows, lat_ref, part, core):
    at = WIDE if core == 0 else 0
    for t, row in enumerate(rows):
        row[at : at + part, :] = lat_ref[t * part : (t + 1) * part, :]


def halo_table(lat_ref, order):
    count = order.shape[0] // BLOCK
    return toeplitz(lat_ref[lat_ref.shape[0] - count :, :].astype(F32), order)


def add_lon_halo(cols, half, rows, halos, core):
    count = cols - half + WIDE
    whole = count // BLOCK * BLOCK
    for row, halo in zip(rows, halos):
        if core == 0:
            row[0:WIDE, :] = halo[...]
            continue
        lon_total, chans = row.shape
        before = row[whole : whole + BLOCK, :].astype(F32)[0 : count - whole, :]
        empty = jnp.zeros((lon_total - count - WIDE, chans), F32)
        row[whole:lon_total, :] = jnp.concatenate(
            [before, halo[...].astype(F32), empty], axis=0
        ).astype(BF16)


def conv(source, table, base, in_rows, feats, first, out_rows, jb, put):
    chans = source.shape[2]
    basis = table.shape[0] // (out_rows * BLOCK)
    taken = source[pl.ds(base, in_rows), jb * BLOCK : jb * BLOCK + WINDOW, :]
    taken = taken.reshape(in_rows * WINDOW, chans)
    result = jnp.dot(table, taken, preferred_element_type=F32).astype(BF16)
    at = slice(put * BLOCK, (put + 1) * BLOCK)
    for m in range(out_rows):
        for k in range(basis):
            begin = (m * basis + k) * BLOCK
            feats[first + m, at, k * chans : (k + 1) * chans] = result[begin : begin + BLOCK, :]


def mix(weights_ref, layer, feats, row, blocks, befores, store):
    _, basis, chans, _ = weights_ref.shape
    count, lons = len(befores), len(blocks) * BLOCK
    mixed = jnp.dot(
        feats[row : row + count, 0:lons, :].reshape(count * lons, basis * chans),
        weights_ref[layer].reshape(basis * chans, chans),
        preferred_element_type=F32,
    )
    for n, before in enumerate(befores):
        before = before[...].astype(F32)
        for put, jb in enumerate(blocks):
            at, begin = SHIFT + jb * BLOCK, n * lons + put * BLOCK
            value = before[at : at + BLOCK, :] + gelu(mixed[begin : begin + BLOCK, :])
            store(n, jb, value)


def into(ref, rows):
    def store(n, jb, value):
        ref[rows[n], jb * BLOCK : (jb + 1) * BLOCK, :] = value.astype(BF16)

    return store


def into_turned(turned, rows, lat_rows):
    def store(n, jb, value):
        width = value.shape[1] // 2
        for c in range(2):
            turned[c, pl.ds(jb * BLOCK * lat_rows + rows[n], BLOCK, stride=lat_rows), :] = value[
                :, c * width : (c + 1) * width
            ]

    return store


def hand_out(turned, keep_ref, send_ref, core, start, count):
    lat_rows, width = keep_ref.shape[1:]
    at = slice(start * lat_rows, (start + count) * lat_rows)
    for ref, which in ((keep_ref, core), (send_ref, 1 - core)):
        piece = turned[which, at, :].reshape(count, lat_rows, width)
        ref[start : start + count] = piece.astype(BF16)


def late_blocks(core, count):
    return [0] if core == 0 else [count - 2, count - 1]


def early_blocks(core, count):
    late = late_blocks(core, count)
    return [jb for jb in range(count) if jb not in late]


def late_start(core, half):
    return 0 if core == 0 else half - LATE


def for_each_core(body):
    for value in range(2):
        pl.when(lax.axis_index("chan") == value)(functools.partial(body, value))


def for_each_lat(body):
    for value in range(2):
        pl.when(lax.axis_index("lat") == value)(functools.partial(body, value))


def half_table(tables_ref, second):
    rows = tables_ref.shape[1] // 2
    return tables_ref[1, rows * second : rows * (second + 1), :]


def far_rows(
    lat, fields, after, tables_ref, weights_ref, feats, turned, blocks1, blocks2, parts
):
    lat_rows = after.shape[0]
    far = GROUP * lat
    near = GROUP - far
    mid = GROUP - PAIR * lat
    rows8 = GROUP + 2 * SPAN
    for put, jb in enumerate(blocks1):
        conv(fields, tables_ref[0], far, rows8, feats, 0, GROUP, jb, put)
        conv(fields, half_table(tables_ref, lat), near, rows8, feats, GROUP, PAIR, jb, put)
    dests = [SPAN + t for t in range(GROUP)]
    dests += [(GROUP + SPAN) * (1 - lat) + t for t in range(PAIR)]
    befores = [SPAN + far + t for t in range(GROUP)] + [SPAN + mid + t for t in range(PAIR)]
    step = len(dests) // parts
    for t in range(0, len(dests), step):
        rows = [fields.at[r] for r in befores[t : t + step]]
        mix(weights_ref, 0, feats, t, blocks1, rows, into(after, dests[t : t + step]))
    for put, jb in enumerate(blocks2):
        conv(after, tables_ref[0], 0, rows8, feats, 0, GROUP, jb, put)
    step = GROUP // parts
    for t in range(0, GROUP, step):
        befores = [after.at[SPAN + t + m] for m in range(step)]
        rows = [far + t + m for m in range(step)]
        mix(weights_ref, 1, feats, t, blocks2, befores, into_turned(turned, rows, lat_rows))


def far1_kernel(
    half, own_ref, tables_ref, weights_ref, fields_ref, after_ref, turned_ref, feats
):
    lat_rows, lon_total, chans = own_ref.shape
    for t in range(SPAN):
        fields_ref[t] = jnp.zeros((lon_total, chans), BF16)
        fields_ref[SPAN + lat_rows + t] = jnp.zeros((lon_total, chans), BF16)
    fields_ref[SPAN : SPAN + lat_rows] = own_ref[...]

    def body(lat, core):
        for t in range(SPAN):
            after_ref[(GROUP + SPAN) * lat + t] = jnp.zeros((lon_total - BLOCK, chans), BF16)
        far_rows(
            lat,
            fields_ref,
            after_ref,
            tables_ref,
            weights_ref,
            feats,
            turned_ref,
            early_blocks(core, lon_total // BLOCK - 1),
            early_blocks(core, half // BLOCK),
            2,
        )

    for_each_core(lambda core: for_each_lat(functools.partial(body, core=core)))


def far2_kernel(
    half,
    cols,
    lon_ref,
    tables_ref,
    weights_ref,
    fields_in,
    after_in,
    turned_in,
    fields_ref,
    after_ref,
    turned_ref,
    feats,
):
    lat_rows = lon_ref.shape[0]

    def body(lat, core):
        add_lon_halo(
            cols,
            half,
            [fields_ref.at[SPAN + r] for r in range(lat_rows)],
            [lon_ref.at[r] for r in range(lat_rows)],
            core,
        )
        far_rows(
            lat,
            fields_ref,
            after_ref,
            tables_ref,
            weights_ref,
            feats,
            turned_ref,
            late_blocks(core, fields_ref.shape[1] // BLOCK - 1),
            late_blocks(core, half // BLOCK),
            1,
        )

    for_each_core(lambda core: for_each_lat(functools.partial(body, core=core)))


def near_rows(
    lat, fields, near, table, tables_ref, weights_ref, feats, turned, blocks1, blocks2, parts
):
    lat_rows = near.shape[0]
    rows6, rows8 = PAIR + 2 * SPAN, GROUP + 2 * SPAN
    group = SPAN * lat
    beyond = HALO * (1 - lat)
    for put, jb in enumerate(blocks1):
        conv(fields, half_table(tables_ref, 1 - lat), group, rows8, feats, 0, PAIR, jb, put)
    for put, jb in enumerate(blocks1):
        conv(fields, table[:, 0 : rows6 * WINDOW], beyond, rows6, feats, PAIR, PAIR, jb, put)
    befores = [fields.at[HALO + m] for m in range(PAIR)]
    befores += [fields.at[beyond + SPAN + m] for m in range(PAIR)]
    dests = [GROUP * (1 - lat) + SPAN * lat + m for m in range(PAIR)]
    dests += [(GROUP + SPAN) * (1 - lat) + m for m in range(PAIR)]
    step = GROUP // parts
    for t in range(0, GROUP, step):
        rows = slice(t, t + step)
        mix(weights_ref, 0, feats, t, blocks1, befores[rows], into(near, dests[rows]))
    for put, jb in enumerate(blocks2):
        conv(near, tables_ref[1], 0, GROUP + 2 * SPAN, feats, 0, GROUP, jb, put)
    for t in range(0, GROUP, step):
        befores = [near.at[SPAN + t + m] for m in range(step)]
        rows = [GROUP * (1 - lat) + t + m for m in range(step)]
        mix(weights_ref, 1, feats, t, blocks2, befores, into_turned(turned, rows, lat_rows))


def near1_kernel(
    half,
    ext_ref,
    next_ref,
    lat_ref,
    tables_ref,
    weights_ref,
    order_ref,
    turned_in,
    fields_ref,
    near_ref,
    table_ref,
    turned_ref,
    keep_ref,
    send_ref,
    feats,
):
    lon_total = ext_ref.shape[1]

    def body(lat, core):
        halo = (HALO + SPAN) * (1 - lat)
        own = HALO * lat
        for t in range(HALO + SPAN):
            fields_ref[own + t] = ext_ref[SPAN + SPAN * (1 - lat) + t]
        add_lat_halo([fields_ref.at[halo + t] for t in range(HALO)], lat_ref, half + WIDE, core)
        table = halo_table(lat_ref, order_ref[...])
        table_ref[...] = table
        for t in range(GROUP):
            near_ref[GROUP * lat + t] = next_ref[GROUP * (1 - lat) + t]
        near_rows(
            lat,
            fields_ref,
            near_ref,
            table,
            tables_ref,
            weights_ref,
            feats,
            turned_ref,
            early_blocks(core, lon_total // BLOCK - 1),
            early_blocks(core, half // BLOCK),
            2,
        )
        hand_out(turned_ref, keep_ref, send_ref, core, 0, half)

    for_each_core(lambda core: for_each_lat(functools.partial(body, core=core)))


def near2_kernel(
    half,
    cols,
    corner_ref,
    table_ref,
    tables_ref,
    weights_ref,
    fields_in,
    near_in,
    turned_in,
    keep_in,
    send_in,
    fields_ref,
    near_ref,
    turned_ref,
    keep_ref,
    send_ref,
    feats,
):
    def body(lat, core):
        halo = (HALO + SPAN) * (1 - lat)
        add_lon_halo(
            cols,
            half,
            [fields_ref.at[halo + t] for t in range(HALO)],
            [corner_ref.at[t] for t in range(HALO)],
            core,
        )
        near_rows(
            lat,
            fields_ref,
            near_ref,
            table_ref[...],
            tables_ref,
            weights_ref,
            feats,
            turned_ref,
            late_blocks(core, fields_ref.shape[1] // BLOCK - 1),
            late_blocks(core, half // BLOCK),
            1,
        )
        hand_out(turned_ref, keep_ref, send_ref, core, late_start(core, half), LATE)

    for_each_core(lambda core: for_each_lat(functools.partial(body, core=core)))


def all_kernel(half, cols, own_ref, lon_ref, *rest):
    lat_refs, corner_refs = rest[:2], rest[2:4]
    (tables_ref, weights_ref, order_ref), rest = rest[4:7], rest[7:]
    keep_ref, send_ref, fields, feats, after, turned = rest
    lat_rows, lon_total, chans = own_ref.shape
    groups = lat_rows // GROUP
    lon1 = lon_total - BLOCK
    halo_base = [0, lat_rows + HALO]
    win_base = [0, lat_rows + HALO - SPAN]
    out_base = [0, lat_rows + SPAN]
    rows6 = PAIR + 2 * SPAN

    fields[HALO : HALO + lat_rows] = own_ref[...]

    @for_each_core
    def _(core):
        rows = [fields.at[HALO + r] for r in range(lat_rows)]
        halos = [lon_ref.at[r] for r in range(lat_rows)]
        for n in range(2):
            halo_rows = [fields.at[halo_base[n] + t] for t in range(HALO)]
            add_lat_halo(halo_rows, lat_refs[n], half + WIDE, core)
            rows += halo_rows
            halos += [corner_refs[n].at[t] for t in range(HALO)]
        add_lon_halo(cols, half, rows, halos, core)

    halo_tables = [
        halo_table(lat_refs[n], order_ref[...])[:, 0 : rows6 * WINDOW] for n in range(2)
    ]
    blocks = range(lon1 // BLOCK)
    for jb in blocks:
        for g in range(groups):
            base = HALO - SPAN + g * GROUP
            conv(
                fields, tables_ref[g], base, GROUP + 2 * SPAN, feats, g * GROUP, GROUP, jb, jb
            )
        for n in range(2):
            first = lat_rows + n * PAIR
            conv(fields, halo_tables[n], win_base[n], rows6, feats, first, PAIR, jb, jb)
    dests = [SPAN + i for i in range(lat_rows)]
    dests += [out_base[n] + m for n in range(2) for m in range(PAIR)]
    for i in range(0, len(dests), PAIR):
        befores = [fields.at[dest + SPAN] for dest in dests[i : i + PAIR]]
        mix(weights_ref, 0, feats, i, blocks, befores, into(after, dests[i : i + PAIR]))
    blocks = range(half // BLOCK)
    for jb in blocks:
        for g in range(groups):
            base = g * GROUP
            conv(after, tables_ref[g], base, GROUP + 2 * SPAN, feats, base, GROUP, jb, jb)
    for i in range(0, lat_rows, PAIR):
        befores = [after.at[SPAN + i + m] for m in range(PAIR)]
        rows = [i + m for m in range(PAIR)]
        mix(weights_ref, 1, feats, i, blocks, befores, into_turned(turned, rows, lat_rows))

    @for_each_core
    def _(core):
        hand_out(turned, keep_ref, send_ref, core, 0, half)


def join_kernel(keep_ref, got_ref, out_hbm, sems):
    half = keep_ref.shape[0]
    rest = out_hbm.shape[0] - half

    @for_each_core
    def _(core):
        first, second = (keep_ref, got_ref) if core == 0 else (got_ref, keep_ref)
        copies = [
            pltpu.make_async_copy(first, out_hbm.at[0:half], sems.at[0]),
            pltpu.make_async_copy(second.at[0:rest], out_hbm.at[half : half + rest], sems.at[1]),
        ]
        for copy in copies:
            copy.start()
        for copy in copies:
            copy.wait()


def per_device(state, sup_rows, sup_count, lon_reach, psi, weights):
    lat_rows, cols, width = state.shape
    basis = psi.shape[2]
    chans = weights.shape[2]
    lats, lons = lax.axis_size("lat"), lax.axis_size("lon")
    sides = 1 if lats == 2 else 2
    groups = lat_rows // GROUP
    lanes = (GROUP + 2 * SPAN) * WINDOW
    half = -(-cols // (2 * BLOCK)) * BLOCK
    part = half + WIDE
    lon_total = half + 2 * WIDE
    lon1 = lon_total - BLOCK
    swap = [(0, 1), (1, 0)]
    params = pltpu.CompilerParams(vmem_limit_bytes=VMEM_LIMIT)

    def shape(*dims):
        return jax.ShapeDtypeStruct(dims, BF16)

    def to_lat(step):
        if lats == 2:
            return [(a, 1 - a) for a in range(lats)]
        return [(a, a + step) for a in range(lats) if 0 <= a + step < lats]

    forth = [((z, 1), ((z + 1) % lons, 0)) for z in range(lons)]
    back = [((z, 0), ((z - 1) % lons, 1)) for z in range(lons)]
    to_lon = forth + back

    own = jnp.transpose(state, (1, 0, 2))
    other = lax.ppermute(own, "chan", swap)

    def scratch(*dims):
        return pltpu.VMEM(dims, F32)

    wide = scratch((half + part) * lat_rows, width)
    smalls = [sup_rows, sup_count, lon_reach]
    part_own, edge_own, rows, bands, weights_in = pl.pallas_call(
        functools.partial(own_kernel, sides, half),
        out_shape=[
            shape(lat_rows, part, width),
            shape(lat_rows, WIDE, width),
            jax.ShapeDtypeStruct((groups, GROUP * basis, lanes), F32),
            shape(sides, PAIR * basis, lanes),
            shape(*weights.shape),
        ],
        in_specs=[hbm()] * 6,
        out_specs=[vmem()] * 5,
        scratch_shapes=[pltpu.SMEM(x.shape, x.dtype) for x in smalls]
        + [
            scratch(*psi.shape),
            pltpu.VMEM(own.shape, BF16),
            scratch(lat_rows, 2 * SPAN + 1, basis, lanes),
            scratch(lat_rows // PAIR, PAIR * basis, lanes),
            wide,
            pltpu.SemaphoreType.DMA((6,)),
        ],
        compiler_params=params,
        name="own",
    )(*[in_hbm(x) for x in smalls + [psi, own, weights]])

    fields, lon_edge, *sends = pl.pallas_call(
        functools.partial(edges_kernel, sides, half),
        out_shape=[shape(lat_rows, lon_total, chans), shape(lat_rows, WIDE, chans)]
        + [shape(HALO * part + PAIR * basis, chans)] * sides
        + [shape(HALO, WIDE, chans)] * sides,
        in_specs=[vmem()] * 4,
        out_specs=[vmem()] * (2 + 2 * sides),
        scratch_shapes=[wide],
        compiler_params=params,
        name="edges",
    )(part_own, edge_own, other, bands)

    steps = [1, -1][:sides]
    lat_halos = [lax.ppermute(x, "lat", to_lat(step)) for x, step in zip(sends, steps)]
    lon_halo = lax.ppermute(
        lon_edge, ("lon", "chan"), [(z * 2 + c, y * 2 + d) for (z, c), (y, d) in to_lon]
    )

    corners = [
        lax.ppermute(
            x,
            ("lon", "lat", "chan"),
            [
                ((z * lats + a) * 2 + c, (y * lats + b) * 2 + d)
                for a, b in to_lat(step)
                for (z, c), (y, d) in to_lon
            ],
        )
        for x, step in zip(sends[sides:], steps)
    ]

    tables, order = pl.pallas_call(
        tables_kernel,
        out_shape=[
            shape(groups, GROUP * basis * BLOCK, lanes),
            shape(PAIR * basis * BLOCK, PAIR * basis * BLOCK),
        ],
        in_specs=[vmem()] * 2,
        out_specs=[vmem()] * 2,
        compiler_params=params,
        name="tables",
    )(rows, lon_edge)

    piece = shape(half, lat_rows, width)
    turned = (2, half * lat_rows, width)
    if sides == 1:
        far_shapes = [
            shape(lat_rows + 2 * SPAN, lon_total, chans),
            shape(lat_rows, lon1, chans),
            jax.ShapeDtypeStruct(turned, F32),
        ]
        far_feats = pltpu.VMEM((GROUP + PAIR, lon1, basis * chans), BF16)
        far = pl.pallas_call(
            functools.partial(far1_kernel, half),
            out_shape=far_shapes,
            in_specs=[vmem()] * 3,
            out_specs=[vmem()] * 3,
            scratch_shapes=[far_feats],
            compiler_params=params,
            name="far_rows_1",
        )(fields, tables, weights_in)
        ext, after, done = pl.pallas_call(
            functools.partial(far2_kernel, half, cols),
            out_shape=far_shapes,
            in_specs=[vmem()] * 6,
            out_specs=[vmem()] * 3,
            scratch_shapes=[far_feats],
            input_output_aliases={3: 0, 4: 1, 5: 2},
            compiler_params=params,
            name="far_rows_2",
        )(lon_halo, tables, weights_in, *far)
        near_shapes = [shape(2 * HALO + SPAN, lon_total, chans), shape(GROUP + 2 * SPAN, lon1, chans)]
        near_feats = pltpu.VMEM((GROUP, lon1, basis * chans), BF16)
        ext, near, halo_tab, done, keep, send = pl.pallas_call(
            functools.partial(near1_kernel, half),
            out_shape=near_shapes
            + [shape(PAIR * basis * BLOCK, lanes), jax.ShapeDtypeStruct(turned, F32)]
            + [piece] * 2,
            in_specs=[vmem()] * 7,
            out_specs=[vmem()] * 6,
            scratch_shapes=[near_feats],
            input_output_aliases={6: 3},
            compiler_params=params,
            name="near_rows_1",
        )(ext, after, lat_halos[0], tables, weights_in, order, done)
        *_, keep, send = pl.pallas_call(
            functools.partial(near2_kernel, half, cols),
            out_shape=near_shapes + [jax.ShapeDtypeStruct(turned, F32)] + [piece] * 2,
            in_specs=[vmem()] * 9,
            out_specs=[vmem()] * 5,
            scratch_shapes=[near_feats],
            input_output_aliases={4: 0, 5: 1, 6: 2, 7: 3, 8: 4},
            compiler_params=params,
            name="near_rows_2",
        )(corners[0], halo_tab, tables, weights_in, ext, near, done, keep, send)
    else:
        keep, send = pl.pallas_call(
            functools.partial(all_kernel, half, cols),
            out_shape=[piece] * 2,
            in_specs=[vmem()] * (5 + 2 * sides),
            out_specs=[vmem()] * 2,
            scratch_shapes=[
                pltpu.VMEM((lat_rows + 2 * HALO, lon_total, chans), BF16),
                pltpu.VMEM((lat_rows + 2 * PAIR, lon1, basis * chans), BF16),
                pltpu.VMEM((lat_rows + 2 * SPAN, lon1, chans), BF16),
                scratch(*turned),
            ],
            compiler_params=params,
            name="all_rows",
        )(fields, lon_halo, *lat_halos, *corners, tables, weights_in, order)
    got = lax.ppermute(send, "chan", swap)

    out = pl.pallas_call(
        join_kernel,
        out_shape=shape(cols, lat_rows, width),
        in_specs=[vmem()] * 2,
        out_specs=hbm(),
        scratch_shapes=[pltpu.SemaphoreType.DMA((2,))],
        compiler_params=params,
        name="join",
    )(keep, got)
    return jnp.transpose(out, (1, 0, 2))


def solution(mesh):
    return jax.shard_map(
        per_device,
        mesh=mesh,
        in_specs=(
            P(("groups", "lat"), "lon", "chan"),
            P("lat", None),
            P("lat"),
            P("lat"),
            P("lat", None, None, None),
            P(),
        ),
        out_specs=P(("groups", "lat"), "lon", "chan"),
        check_vma=False,
    )
```

```python
import functools

import jax
import jax.numpy as jnp
from jax import lax
from jax.experimental import pallas as pl
from jax.experimental.pallas import tpu as pltpu
from jax.sharding import PartitionSpec as P

LAYERS = 2
SPAN = 2
HALO = LAYERS * SPAN
BLOCK = 16
WINDOW = 2 * BLOCK
GROUP = 4
PAIR = 2
WIDE = BLOCK
LATE = 2 * BLOCK
SHIFT = BLOCK // 2
VMEM_LIMIT = 48 * 1024 * 1024
BF16 = jnp.bfloat16
F32 = jnp.float32


def vmem():
    return pl.BlockSpec(memory_space=pltpu.VMEM)


def smem():
    return pl.BlockSpec(memory_space=pltpu.SMEM)


def hbm():
    return pl.BlockSpec(memory_space=pltpu.HBM)


def in_hbm(x):
    return pltpu.with_memory_space_constraint(x, pltpu.HBM)


def by_row(count):
    total = count * BLOCK
    out_row = lax.broadcasted_iota(jnp.int32, (total, total), 0)
    in_row = lax.broadcasted_iota(jnp.int32, (total, total), 1)
    source = (out_row % BLOCK) * count + out_row // BLOCK
    return (in_row == source).astype(F32).astype(BF16)


def toeplitz(rows_tab, order):
    moved = jnp.concatenate(
        [rows_tab if jj == 0 else pltpu.roll(rows_tab, jj, 1) for jj in range(BLOCK)], axis=0
    ).astype(BF16)
    return jnp.dot(order, moved, preferred_element_type=F32).astype(BF16)


def band_rows(refs, slots, rows):
    sup_ref, count_ref, reach_ref, psi_ref = refs
    lat_rows, sup, basis, offsets = psi_ref.shape
    lanes = slots.shape[3]
    slots[...] = jnp.zeros_like(slots)
    for n, i in enumerate(rows):
        row = lax.axis_index("lat") * lat_rows + i
        values = [psi_ref[i, s] for s in range(sup)]
        places = [jnp.where(s < count_ref[i], sup_ref[i, s] - row, -lat_rows) for s in range(sup)]
        for rel in range(2 * SPAN + 1):
            total = jnp.zeros((basis, offsets), F32)
            for value, at in zip(values, places):
                total = total + jnp.where(at == rel - SPAN, value, 0.0)
            slots[n, rel, :, 0:offsets] = total
    off = lax.broadcasted_iota(jnp.int32, (basis, lanes), 1) % WINDOW - offsets // 2
    bands = []
    for n, i in enumerate(rows):
        band = slots[n, 0]
        for rel in range(1, 2 * SPAN + 1):
            band = band + pltpu.roll(slots[n, rel], rel * WINDOW, 1)
        bands.append(jnp.where(jnp.abs(off) <= reach_ref[i], band, 0.0))
    return bands


def put_pair(scr, bands):
    for m, band in enumerate(bands):
        basis = band.shape[0]
        scr[m * basis : (m + 1) * basis, :] = (
            band if m == 0 else pltpu.roll(band, m * WINDOW, 1)
        )


def turn(ref, lon_from, lon_to, wide_scr):
    _, lat_rows, width = ref.shape
    wide_scr[lon_from * lat_rows : lon_to * lat_rows, :] = (
        ref[lon_from:lon_to].astype(F32).reshape((lon_to - lon_from) * lat_rows, width)
    )


def turned_row(wide_scr, lat_rows, row, start, count):
    return wide_scr[pl.ds(start * lat_rows + row, count, stride=lat_rows), :].astype(BF16)


def own_kernel(sides, half, *refs):
    sources, outs, refs = refs[:6], refs[6:11], refs[11:]
    part_ref, edge_ref, rows_ref, bands_ref, weights_ref = outs
    smems, (psi_ref, state_ref, slots, pairs_scr, wide_scr, sems) = refs[:3], refs[3:]
    copies = [
        pltpu.make_async_copy(source, dest, sems.at[n])
        for n, (source, dest) in enumerate(
            zip(sources, (*smems, psi_ref, state_ref, weights_ref))
        )
    ]
    for copy in copies:
        copy.start()
    cols, lat_rows, width = state_ref.shape
    part = part_ref.shape[1]
    chan = lax.axis_index("chan")
    lat = lax.axis_index("lat")
    wide_scr[cols * lat_rows :, :] = jnp.zeros(
        (wide_scr.shape[0] - cols * lat_rows, width), F32
    )
    for copy in copies[:4]:
        copy.wait()
    bands = band_rows((*smems, psi_ref), slots, range(lat_rows))
    pairs = lat_rows // PAIR
    for p in range(pairs):
        put_pair(pairs_scr.at[p], bands[p * PAIR : (p + 1) * PAIR])
    for g in range(lat_rows // GROUP):
        source = 2 * ((g + lat) % 2 if sides == 1 else g)
        first, second = pairs_scr[source], pairs_scr[source + 1]
        rows_ref[g] = jnp.concatenate([first, pltpu.roll(second, PAIR * WINDOW, 1)], axis=0)
    edges = [(pairs - 1) * (1 - lat)] if sides == 1 else [pairs - 1, 0]
    for n in range(sides):
        bands_ref[n] = pairs_scr[edges[n]].astype(BF16)
    copies[4].wait()
    turn(state_ref, 0, cols, wide_scr)
    for r in range(lat_rows):
        part_ref[r] = turned_row(wide_scr, lat_rows, r, (half - WIDE) * chan, part)
        edge_ref[r] = turned_row(wide_scr, lat_rows, r, (cols - WIDE) * chan, WIDE)
    copies[5].wait()


def edges_kernel(
    sides, half, part_ref, edge_ref, other_ref, bands_ref, fields_ref, lon_ref, *rest
):
    lat_refs, corner_refs, (wide_scr,) = rest[:sides], rest[sides : 2 * sides], rest[2 * sides :]
    cols, lat_rows, width = other_ref.shape
    lon_total = fields_ref.shape[1]
    part = part_ref.shape[1]
    chan = lax.axis_index("chan")
    wide_scr[cols * lat_rows :, :] = jnp.zeros(
        (wide_scr.shape[0] - cols * lat_rows, width), F32
    )

    def build(core):
        start = 0 if core == 0 else half - WIDE
        edge = 0 if core == 0 else cols - WIDE
        stop = start + part if core == 0 else cols
        at = WIDE if core == 0 else 0
        own = slice(core * width, (core + 1) * width)
        lane = slice((1 - core) * width, (2 - core) * width)
        turn(other_ref, start, stop, wide_scr)
        for r in range(lat_rows):
            lon_ref[r, :, own] = edge_ref[r]
            lon_ref[r, :, lane] = turned_row(wide_scr, lat_rows, r, edge, WIDE)
            fields_ref[r, at : at + part, own] = part_ref[r]
            fields_ref[r, at : at + part, lane] = turned_row(wide_scr, lat_rows, r, start, part)
        empty = slice(0, WIDE) if core == 0 else slice(part, lon_total)
        fields_ref[:, empty, :] = jnp.zeros((lat_rows, WIDE, 2 * width), BF16)

    @pl.when(chan == 0)
    def _():
        build(0)

    @pl.when(chan == 1)
    def _():
        build(1)

    at = pl.multiple_of((1 - chan) * WIDE, WIDE)
    for n, first in enumerate(needed_rows(sides, lat_rows)):
        for t in range(HALO):
            lat_refs[n][t * part : (t + 1) * part, :] = fields_ref[first + t, pl.ds(at, part), :]
            corner_refs[n][t] = lon_ref[first + t]
        lat_refs[n][HALO * part :, :] = bands_ref[n]


def needed_rows(sides, lat_rows):
    if sides == 1:
        return [(1 - lax.axis_index("lat")) * (lat_rows - HALO)]
    return [lat_rows - HALO, 0]


def tables_kernel(rows_ref, _, tables_ref, order_ref):
    groups, rows, _ = rows_ref.shape
    order = by_row(rows)
    for g in range(groups):
        tables_ref[g] = toeplitz(rows_ref[g], order)
    order_ref[...] = by_row(order_ref.shape[0] // BLOCK)


def gelu(x):
    return 0.5 * x * (1.0 + jnp.tanh(0.7978845608028654 * (x + 0.044715 * (x * x * x))))


def add_lat_halo(rows, lat_ref, part, core):
    at = WIDE if core == 0 else 0
    for t, row in enumerate(rows):
        row[at : at + part, :] = lat_ref[t * part : (t + 1) * part, :]


def halo_table(lat_ref, order):
    count = order.shape[0] // BLOCK
    return toeplitz(lat_ref[lat_ref.shape[0] - count :, :].astype(F32), order)


def add_lon_halo(cols, half, rows, halos, core):
    count = cols - half + WIDE
    whole = count // BLOCK * BLOCK
    for row, halo in zip(rows, halos):
        if core == 0:
            row[0:WIDE, :] = halo[...]
            continue
        lon_total, chans = row.shape
        before = row[whole : whole + BLOCK, :].astype(F32)[0 : count - whole, :]
        empty = jnp.zeros((lon_total - count - WIDE, chans), F32)
        row[whole:lon_total, :] = jnp.concatenate(
            [before, halo[...].astype(F32), empty], axis=0
        ).astype(BF16)


def conv(source, table, base, in_rows, feats, first, out_rows, jb, put):
    chans = source.shape[2]
    basis = table.shape[0] // (out_rows * BLOCK)
    taken = source[pl.ds(base, in_rows), jb * BLOCK : jb * BLOCK + WINDOW, :]
    taken = taken.reshape(in_rows * WINDOW, chans)
    result = jnp.dot(table, taken, preferred_element_type=F32).astype(BF16)
    at = slice(put * BLOCK, (put + 1) * BLOCK)
    for m in range(out_rows):
        for k in range(basis):
            begin = (m * basis + k) * BLOCK
            feats[first + m, at, k * chans : (k + 1) * chans] = result[begin : begin + BLOCK, :]


def mix(weights_ref, layer, feats, row, blocks, befores, store):
    _, basis, chans, _ = weights_ref.shape
    count, lons = len(befores), len(blocks) * BLOCK
    mixed = jnp.dot(
        feats[row : row + count, 0:lons, :].reshape(count * lons, basis * chans),
        weights_ref[layer].reshape(basis * chans, chans),
        preferred_element_type=F32,
    )
    for n, before in enumerate(befores):
        before = before[...].astype(F32)
        for put, jb in enumerate(blocks):
            at, begin = SHIFT + jb * BLOCK, n * lons + put * BLOCK
            value = before[at : at + BLOCK, :] + gelu(mixed[begin : begin + BLOCK, :])
            store(n, jb, value)


def into(ref, rows):
    def store(n, jb, value):
        ref[rows[n], jb * BLOCK : (jb + 1) * BLOCK, :] = value.astype(BF16)

    return store


def into_turned(turned, rows, lat_rows):
    def store(n, jb, value):
        width = value.shape[1] // 2
        for c in range(2):
            turned[c, pl.ds(jb * BLOCK * lat_rows + rows[n], BLOCK, stride=lat_rows), :] = value[
                :, c * width : (c + 1) * width
            ]

    return store


def hand_out(turned, ref, which, start):
    count, lat_rows, width = ref.shape
    piece = turned[which, start * lat_rows : (start + count) * lat_rows, :]
    ref[...] = piece.reshape(count, lat_rows, width).astype(BF16)


def hand_out_early(turned, keep_ref, send_refs, core):
    start = early_start(core)
    hand_out(turned, keep_ref, core, start)
    for send_ref in send_refs:
        hand_out(turned, send_ref, 1 - core, start)
        start += send_ref.shape[0]


def hand_out_late(turned, keep_ref, send_ref, core, half):
    hand_out(turned, keep_ref, core, late_start(core, half))
    hand_out(turned, send_ref, 1 - core, late_start(core, half))


def late_blocks(core, count):
    return [0] if core == 0 else [count - 2, count - 1]


def early_blocks(core, count):
    late = late_blocks(core, count)
    return [jb for jb in range(count) if jb not in late]


def late_start(core, half):
    return 0 if core == 0 else half - LATE


def early_start(core):
    return LATE if core == 0 else 0


def for_each_core(body):
    for value in range(2):
        pl.when(lax.axis_index("chan") == value)(functools.partial(body, value))


def for_each_lat(body):
    for value in range(2):
        pl.when(lax.axis_index("lat") == value)(functools.partial(body, value))


def half_table(tables_ref, second):
    rows = tables_ref.shape[1] // 2
    return tables_ref[1, rows * second : rows * (second + 1), :]


def far_rows(
    lat, fields, after, tables_ref, weights_ref, feats, turned, blocks1, blocks2, parts
):
    lat_rows = after.shape[0]
    far = GROUP * lat
    near = GROUP - far
    mid = GROUP - PAIR * lat
    rows8 = GROUP + 2 * SPAN
    for put, jb in enumerate(blocks1):
        conv(fields, tables_ref[0], far, rows8, feats, 0, GROUP, jb, put)
        conv(fields, half_table(tables_ref, lat), near, rows8, feats, GROUP, PAIR, jb, put)
    dests = [SPAN + t for t in range(GROUP)]
    dests += [(GROUP + SPAN) * (1 - lat) + t for t in range(PAIR)]
    befores = [SPAN + far + t for t in range(GROUP)] + [SPAN + mid + t for t in range(PAIR)]
    step = len(dests) // parts
    for t in range(0, len(dests), step):
        rows = [fields.at[r] for r in befores[t : t + step]]
        mix(weights_ref, 0, feats, t, blocks1, rows, into(after, dests[t : t + step]))
    for put, jb in enumerate(blocks2):
        conv(after, tables_ref[0], 0, rows8, feats, 0, GROUP, jb, put)
    step = GROUP // parts
    for t in range(0, GROUP, step):
        befores = [after.at[SPAN + t + m] for m in range(step)]
        rows = [far + t + m for m in range(step)]
        mix(weights_ref, 1, feats, t, blocks2, befores, into_turned(turned, rows, lat_rows))


def far1_kernel(
    half, own_ref, tables_ref, weights_ref, fields_ref, after_ref, turned_ref, feats
):
    lat_rows, lon_total, chans = own_ref.shape
    for t in range(SPAN):
        fields_ref[t] = jnp.zeros((lon_total, chans), BF16)
        fields_ref[SPAN + lat_rows + t] = jnp.zeros((lon_total, chans), BF16)
    fields_ref[SPAN : SPAN + lat_rows] = own_ref[...]

    def body(lat, core):
        for t in range(SPAN):
            after_ref[(GROUP + SPAN) * lat + t] = jnp.zeros((lon_total - BLOCK, chans), BF16)
        far_rows(
            lat,
            fields_ref,
            after_ref,
            tables_ref,
            weights_ref,
            feats,
            turned_ref,
            early_blocks(core, lon_total // BLOCK - 1),
            early_blocks(core, half // BLOCK),
            2,
        )

    for_each_core(lambda core: for_each_lat(functools.partial(body, core=core)))


def far2_kernel(
    half,
    cols,
    lon_ref,
    tables_ref,
    weights_ref,
    fields_in,
    after_in,
    turned_in,
    fields_ref,
    after_ref,
    turned_ref,
    feats,
):
    lat_rows = lon_ref.shape[0]

    def body(lat, core):
        add_lon_halo(
            cols,
            half,
            [fields_ref.at[SPAN + r] for r in range(lat_rows)],
            [lon_ref.at[r] for r in range(lat_rows)],
            core,
        )
        far_rows(
            lat,
            fields_ref,
            after_ref,
            tables_ref,
            weights_ref,
            feats,
            turned_ref,
            late_blocks(core, fields_ref.shape[1] // BLOCK - 1),
            late_blocks(core, half // BLOCK),
            1,
        )

    for_each_core(lambda core: for_each_lat(functools.partial(body, core=core)))


def near_rows(
    lat, fields, near, table, tables_ref, weights_ref, feats, turned, blocks1, blocks2, parts
):
    lat_rows = near.shape[0]
    rows6, rows8 = PAIR + 2 * SPAN, GROUP + 2 * SPAN
    group = SPAN * lat
    beyond = HALO * (1 - lat)
    for put, jb in enumerate(blocks1):
        conv(fields, half_table(tables_ref, 1 - lat), group, rows8, feats, 0, PAIR, jb, put)
    for put, jb in enumerate(blocks1):
        conv(fields, table[:, 0 : rows6 * WINDOW], beyond, rows6, feats, PAIR, PAIR, jb, put)
    befores = [fields.at[HALO + m] for m in range(PAIR)]
    befores += [fields.at[beyond + SPAN + m] for m in range(PAIR)]
    dests = [GROUP * (1 - lat) + SPAN * lat + m for m in range(PAIR)]
    dests += [(GROUP + SPAN) * (1 - lat) + m for m in range(PAIR)]
    step = GROUP // parts
    for t in range(0, GROUP, step):
        rows = slice(t, t + step)
        mix(weights_ref, 0, feats, t, blocks1, befores[rows], into(near, dests[rows]))
    for put, jb in enumerate(blocks2):
        conv(near, tables_ref[1], 0, GROUP + 2 * SPAN, feats, 0, GROUP, jb, put)
    for t in range(0, GROUP, step):
        befores = [near.at[SPAN + t + m] for m in range(step)]
        rows = [GROUP * (1 - lat) + t + m for m in range(step)]
        mix(weights_ref, 1, feats, t, blocks2, befores, into_turned(turned, rows, lat_rows))


def near1_kernel(
    half,
    ext_ref,
    next_ref,
    lat_ref,
    tables_ref,
    weights_ref,
    order_ref,
    turned_in,
    fields_ref,
    near_ref,
    table_ref,
    turned_ref,
    keep_ref,
    *rest,
):
    *send_refs, feats = rest
    lon_total = ext_ref.shape[1]

    def body(lat, core):
        halo = (HALO + SPAN) * (1 - lat)
        own = HALO * lat
        for t in range(HALO + SPAN):
            fields_ref[own + t] = ext_ref[SPAN + SPAN * (1 - lat) + t]
        add_lat_halo([fields_ref.at[halo + t] for t in range(HALO)], lat_ref, half + WIDE, core)
        table = halo_table(lat_ref, order_ref[...])
        table_ref[...] = table
        for t in range(GROUP):
            near_ref[GROUP * lat + t] = next_ref[GROUP * (1 - lat) + t]
        near_rows(
            lat,
            fields_ref,
            near_ref,
            table,
            tables_ref,
            weights_ref,
            feats,
            turned_ref,
            early_blocks(core, lon_total // BLOCK - 1),
            early_blocks(core, half // BLOCK),
            2,
        )
        hand_out_early(turned_ref, keep_ref, send_refs, core)

    for_each_core(lambda core: for_each_lat(functools.partial(body, core=core)))


def near2_kernel(
    half,
    cols,
    corner_ref,
    table_ref,
    tables_ref,
    weights_ref,
    fields_in,
    near_in,
    turned_in,
    fields_ref,
    near_ref,
    turned_ref,
    keep_ref,
    send_ref,
    feats,
):
    def body(lat, core):
        halo = (HALO + SPAN) * (1 - lat)
        add_lon_halo(
            cols,
            half,
            [fields_ref.at[halo + t] for t in range(HALO)],
            [corner_ref.at[t] for t in range(HALO)],
            core,
        )
        near_rows(
            lat,
            fields_ref,
            near_ref,
            table_ref[...],
            tables_ref,
            weights_ref,
            feats,
            turned_ref,
            late_blocks(core, fields_ref.shape[1] // BLOCK - 1),
            late_blocks(core, half // BLOCK),
            1,
        )
        hand_out_late(turned_ref, keep_ref, send_ref, core, half)

    for_each_core(lambda core: for_each_lat(functools.partial(body, core=core)))


def all_kernel(half, cols, own_ref, lon_ref, *rest):
    lat_refs, corner_refs = rest[:2], rest[2:4]
    (tables_ref, weights_ref, order_ref), rest = rest[4:7], rest[7:]
    (late_keep_ref, late_send_ref, keep_ref), rest = rest[:3], rest[3:]
    *send_refs, fields, feats, after, turned = rest
    lat_rows, lon_total, chans = own_ref.shape
    groups = lat_rows // GROUP
    lon1 = lon_total - BLOCK
    halo_base = [0, lat_rows + HALO]
    win_base = [0, lat_rows + HALO - SPAN]
    out_base = [0, lat_rows + SPAN]
    rows6 = PAIR + 2 * SPAN

    fields[HALO : HALO + lat_rows] = own_ref[...]

    @for_each_core
    def _(core):
        rows = [fields.at[HALO + r] for r in range(lat_rows)]
        halos = [lon_ref.at[r] for r in range(lat_rows)]
        for n in range(2):
            halo_rows = [fields.at[halo_base[n] + t] for t in range(HALO)]
            add_lat_halo(halo_rows, lat_refs[n], half + WIDE, core)
            rows += halo_rows
            halos += [corner_refs[n].at[t] for t in range(HALO)]
        add_lon_halo(cols, half, rows, halos, core)

    halo_tables = [
        halo_table(lat_refs[n], order_ref[...])[:, 0 : rows6 * WINDOW] for n in range(2)
    ]
    blocks = range(lon1 // BLOCK)
    for jb in blocks:
        for g in range(groups):
            base = HALO - SPAN + g * GROUP
            conv(
                fields, tables_ref[g], base, GROUP + 2 * SPAN, feats, g * GROUP, GROUP, jb, jb
            )
        for n in range(2):
            first = lat_rows + n * PAIR
            conv(fields, halo_tables[n], win_base[n], rows6, feats, first, PAIR, jb, jb)
    dests = [SPAN + i for i in range(lat_rows)]
    dests += [out_base[n] + m for n in range(2) for m in range(PAIR)]
    for i in range(0, len(dests), PAIR):
        befores = [fields.at[dest + SPAN] for dest in dests[i : i + PAIR]]
        mix(weights_ref, 0, feats, i, blocks, befores, into(after, dests[i : i + PAIR]))
    blocks = range(half // BLOCK)
    for jb in blocks:
        for g in range(groups):
            base = g * GROUP
            conv(after, tables_ref[g], base, GROUP + 2 * SPAN, feats, base, GROUP, jb, jb)
    for i in range(0, lat_rows, PAIR):
        befores = [after.at[SPAN + i + m] for m in range(PAIR)]
        rows = [i + m for m in range(PAIR)]
        mix(weights_ref, 1, feats, i, blocks, befores, into_turned(turned, rows, lat_rows))

    @for_each_core
    def _(core):
        hand_out_late(turned, late_keep_ref, late_send_ref, core, half)
        hand_out_early(turned, keep_ref, send_refs, core)


def write(copies, sems):
    copies = [
        pltpu.make_async_copy(source, dest, sems.at[n])
        for n, (source, dest) in enumerate(copies)
    ]
    for copy in copies:
        copy.start()
    for copy in copies:
        copy.wait()


def early_kernel(half, keep_ref, got_ref, out_hbm, sems):
    @for_each_core
    def _(core):
        copies = []
        for which, ref in ((core, keep_ref), (1 - core, got_ref)):
            at = which * half + early_start(which)
            copies.append((ref, out_hbm.at[at : at + ref.shape[0]]))
        write(copies, sems)


def late_kernel(half, early_ref, keep_ref, got_ref, out_in, out_hbm, sems):
    cols = out_hbm.shape[0]

    @for_each_core
    def _(core):
        at = (1 - core) * half + early_start(1 - core) + half - LATE
        copies = [(early_ref, out_hbm.at[at - early_ref.shape[0] : at])]
        for which, ref in ((core, keep_ref), (1 - core, got_ref)):
            at = which * half + late_start(which, half)
            count = min(LATE, cols - at)
            copies.append((ref.at[0:count], out_hbm.at[at : at + count]))
        write(copies, sems)


def per_device(state, sup_rows, sup_count, lon_reach, psi, weights):
    lat_rows, cols, width = state.shape
    basis = psi.shape[2]
    chans = weights.shape[2]
    lats, lons = lax.axis_size("lat"), lax.axis_size("lon")
    sides = 1 if lats == 2 else 2
    groups = lat_rows // GROUP
    lanes = (GROUP + 2 * SPAN) * WINDOW
    half = -(-cols // (2 * BLOCK)) * BLOCK
    part = half + WIDE
    lon_total = half + 2 * WIDE
    lon1 = lon_total - BLOCK
    swap = [(0, 1), (1, 0)]
    params = pltpu.CompilerParams(vmem_limit_bytes=VMEM_LIMIT)

    def shape(*dims):
        return jax.ShapeDtypeStruct(dims, BF16)

    def to_lat(step):
        if lats == 2:
            return [(a, 1 - a) for a in range(lats)]
        return [(a, a + step) for a in range(lats) if 0 <= a + step < lats]

    forth = [((z, 1), ((z + 1) % lons, 0)) for z in range(lons)]
    back = [((z, 0), ((z - 1) % lons, 1)) for z in range(lons)]
    to_lon = forth + back

    own = jnp.transpose(state, (1, 0, 2))
    other = lax.ppermute(own, "chan", swap)

    def scratch(*dims):
        return pltpu.VMEM(dims, F32)

    wide = scratch((half + part) * lat_rows, width)
    smalls = [sup_rows, sup_count, lon_reach]
    part_own, edge_own, rows, bands, weights_in = pl.pallas_call(
        functools.partial(own_kernel, sides, half),
        out_shape=[
            shape(lat_rows, part, width),
            shape(lat_rows, WIDE, width),
            jax.ShapeDtypeStruct((groups, GROUP * basis, lanes), F32),
            shape(sides, PAIR * basis, lanes),
            shape(*weights.shape),
        ],
        in_specs=[hbm()] * 6,
        out_specs=[vmem()] * 5,
        scratch_shapes=[pltpu.SMEM(x.shape, x.dtype) for x in smalls]
        + [
            scratch(*psi.shape),
            pltpu.VMEM(own.shape, BF16),
            scratch(lat_rows, 2 * SPAN + 1, basis, lanes),
            scratch(lat_rows // PAIR, PAIR * basis, lanes),
            wide,
            pltpu.SemaphoreType.DMA((6,)),
        ],
        compiler_params=params,
        name="own",
    )(*[in_hbm(x) for x in smalls + [psi, own, weights]])

    fields, lon_edge, *sends = pl.pallas_call(
        functools.partial(edges_kernel, sides, half),
        out_shape=[shape(lat_rows, lon_total, chans), shape(lat_rows, WIDE, chans)]
        + [shape(HALO * part + PAIR * basis, chans)] * sides
        + [shape(HALO, WIDE, chans)] * sides,
        in_specs=[vmem()] * 4,
        out_specs=[vmem()] * (2 + 2 * sides),
        scratch_shapes=[wide],
        compiler_params=params,
        name="edges",
    )(part_own, edge_own, other, bands)

    steps = [1, -1][:sides]
    lat_halos = [lax.ppermute(x, "lat", to_lat(step)) for x, step in zip(sends, steps)]
    lon_halo = lax.ppermute(
        lon_edge, ("lon", "chan"), [(z * 2 + c, y * 2 + d) for (z, c), (y, d) in to_lon]
    )

    corners = [
        lax.ppermute(
            x,
            ("lon", "lat", "chan"),
            [
                ((z * lats + a) * 2 + c, (y * lats + b) * 2 + d)
                for a, b in to_lat(step)
                for (z, c), (y, d) in to_lon
            ],
        )
        for x, step in zip(sends[sides:], steps)
    ]

    tables, order = pl.pallas_call(
        tables_kernel,
        out_shape=[
            shape(groups, GROUP * basis * BLOCK, lanes),
            shape(PAIR * basis * BLOCK, PAIR * basis * BLOCK),
        ],
        in_specs=[vmem()] * 2,
        out_specs=[vmem()] * 2,
        compiler_params=params,
        name="tables",
    )(rows, lon_edge)

    early = half - LATE
    late_shapes = [shape(LATE, lat_rows, width)] * 2
    early_shapes = [shape(early, lat_rows, width)]
    early_shapes += [shape(n, lat_rows, width) for n in (early - BLOCK, BLOCK)]
    turned = (2, half * lat_rows, width)
    if sides == 1:
        far_shapes = [
            shape(lat_rows + 2 * SPAN, lon_total, chans),
            shape(lat_rows, lon1, chans),
            jax.ShapeDtypeStruct(turned, F32),
        ]
        far_feats = pltpu.VMEM((GROUP + PAIR, lon1, basis * chans), BF16)
        far = pl.pallas_call(
            functools.partial(far1_kernel, half),
            out_shape=far_shapes,
            in_specs=[vmem()] * 3,
            out_specs=[vmem()] * 3,
            scratch_shapes=[far_feats],
            compiler_params=params,
            name="far_rows_1",
        )(fields, tables, weights_in)
        ext, after, done = pl.pallas_call(
            functools.partial(far2_kernel, half, cols),
            out_shape=far_shapes,
            in_specs=[vmem()] * 6,
            out_specs=[vmem()] * 3,
            scratch_shapes=[far_feats],
            input_output_aliases={3: 0, 4: 1, 5: 2},
            compiler_params=params,
            name="far_rows_2",
        )(lon_halo, tables, weights_in, *far)
        near_shapes = [shape(2 * HALO + SPAN, lon_total, chans), shape(GROUP + 2 * SPAN, lon1, chans)]
        near_feats = pltpu.VMEM((GROUP, lon1, basis * chans), BF16)
        ext, near, halo_tab, done, keep, *sends = pl.pallas_call(
            functools.partial(near1_kernel, half),
            out_shape=near_shapes
            + [shape(PAIR * basis * BLOCK, lanes), jax.ShapeDtypeStruct(turned, F32)]
            + early_shapes,
            in_specs=[vmem()] * 7,
            out_specs=[vmem()] * (4 + len(early_shapes)),
            scratch_shapes=[near_feats],
            input_output_aliases={6: 3},
            compiler_params=params,
            name="near_rows_1",
        )(ext, after, lat_halos[0], tables, weights_in, order, done)
        *_, late_keep, late_send = pl.pallas_call(
            functools.partial(near2_kernel, half, cols),
            out_shape=near_shapes + [jax.ShapeDtypeStruct(turned, F32)] + late_shapes,
            in_specs=[vmem()] * 7,
            out_specs=[vmem()] * 5,
            scratch_shapes=[near_feats],
            input_output_aliases={4: 0, 5: 1, 6: 2},
            compiler_params=params,
            name="near_rows_2",
        )(corners[0], halo_tab, tables, weights_in, ext, near, done)
    else:
        late_keep, late_send, keep, *sends = pl.pallas_call(
            functools.partial(all_kernel, half, cols),
            out_shape=late_shapes + early_shapes,
            in_specs=[vmem()] * (5 + 2 * sides),
            out_specs=[vmem()] * (2 + len(early_shapes)),
            scratch_shapes=[
                pltpu.VMEM((lat_rows + 2 * HALO, lon_total, chans), BF16),
                pltpu.VMEM((lat_rows + 2 * PAIR, lon1, basis * chans), BF16),
                pltpu.VMEM((lat_rows + 2 * SPAN, lon1, chans), BF16),
                scratch(*turned),
            ],
            compiler_params=params,
            name="all_rows",
        )(fields, lon_halo, *lat_halos, *corners, tables, weights_in, order)
    gots = [lax.ppermute(x, "chan", swap) for x in sends]
    late_got = lax.ppermute(late_send, "chan", swap)

    out_type = shape(cols, lat_rows, width)
    out = pl.pallas_call(
        functools.partial(early_kernel, half),
        out_shape=out_type,
        in_specs=[vmem()] * 2,
        out_specs=hbm(),
        scratch_shapes=[pltpu.SemaphoreType.DMA((2,))],
        compiler_params=params,
        name="write_early",
    )(keep, gots[0])
    out = pl.pallas_call(
        functools.partial(late_kernel, half),
        out_shape=out_type,
        in_specs=[vmem()] * 3 + [hbm()],
        out_specs=hbm(),
        scratch_shapes=[pltpu.SemaphoreType.DMA((3,))],
        input_output_aliases={3: 0},
        compiler_params=params,
        name="write_late",
    )(gots[1], late_keep, late_got, out)
    return jnp.transpose(out, (1, 0, 2))


def solution(mesh):
    return jax.shard_map(
        per_device,
        mesh=mesh,
        in_specs=(
            P(("groups", "lat"), "lon", "chan"),
            P("lat", None),
            P("lat"),
            P("lat"),
            P("lat", None, None, None),
            P(),
        ),
        out_specs=P(("groups", "lat"), "lon", "chan"),
        check_vma=False,
    )
```

```python
import functools

import jax
import jax.numpy as jnp
from jax import lax
from jax.experimental import pallas as pl
from jax.experimental.pallas import tpu as pltpu
from jax.sharding import PartitionSpec as P

LAYERS = 2
SPAN = 2
HALO = LAYERS * SPAN
BLOCK = 16
WINDOW = 2 * BLOCK
GROUP = 4
PAIR = 2
WIDE = BLOCK
LATE = 46
SHIFT = BLOCK // 2
VMEM_LIMIT = 48 * 1024 * 1024
BF16 = jnp.bfloat16
F32 = jnp.float32


def vmem():
    return pl.BlockSpec(memory_space=pltpu.VMEM)


def smem():
    return pl.BlockSpec(memory_space=pltpu.SMEM)


def hbm():
    return pl.BlockSpec(memory_space=pltpu.HBM)


def in_hbm(x):
    return pltpu.with_memory_space_constraint(x, pltpu.HBM)


def by_row(count):
    total = count * BLOCK
    out_row = lax.broadcasted_iota(jnp.int32, (total, total), 0)
    in_row = lax.broadcasted_iota(jnp.int32, (total, total), 1)
    source = (out_row % BLOCK) * count + out_row // BLOCK
    return (in_row == source).astype(F32).astype(BF16)


def toeplitz(rows_tab, order):
    moved = jnp.concatenate(
        [rows_tab if jj == 0 else pltpu.roll(rows_tab, jj, 1) for jj in range(BLOCK)], axis=0
    ).astype(BF16)
    return jnp.dot(order, moved, preferred_element_type=F32).astype(BF16)


def band_rows(refs, slots, rows):
    sup_ref, count_ref, reach_ref, psi_ref = refs
    lat_rows, sup, basis, offsets = psi_ref.shape
    lanes = slots.shape[3]
    slots[...] = jnp.zeros_like(slots)
    for n, i in enumerate(rows):
        row = lax.axis_index("lat") * lat_rows + i
        values = [psi_ref[i, s] for s in range(sup)]
        places = [jnp.where(s < count_ref[i], sup_ref[i, s] - row, -lat_rows) for s in range(sup)]
        for rel in range(2 * SPAN + 1):
            total = jnp.zeros((basis, offsets), F32)
            for value, at in zip(values, places):
                total = total + jnp.where(at == rel - SPAN, value, 0.0)
            slots[n, rel, :, 0:offsets] = total
    off = lax.broadcasted_iota(jnp.int32, (basis, lanes), 1) % WINDOW - offsets // 2
    bands = []
    for n, i in enumerate(rows):
        band = slots[n, 0]
        for rel in range(1, 2 * SPAN + 1):
            band = band + pltpu.roll(slots[n, rel], rel * WINDOW, 1)
        bands.append(jnp.where(jnp.abs(off) <= reach_ref[i], band, 0.0))
    return bands


def put_pair(scr, bands):
    for m, band in enumerate(bands):
        basis = band.shape[0]
        scr[m * basis : (m + 1) * basis, :] = (
            band if m == 0 else pltpu.roll(band, m * WINDOW, 1)
        )


def turn(ref, lon_from, lon_to, wide_scr):
    _, lat_rows, width = ref.shape
    wide_scr[lon_from * lat_rows : lon_to * lat_rows, :] = (
        ref[lon_from:lon_to].astype(F32).reshape((lon_to - lon_from) * lat_rows, width)
    )


def turned_row(wide_scr, lat_rows, row, start, count):
    return wide_scr[pl.ds(start * lat_rows + row, count, stride=lat_rows), :].astype(BF16)


def own_kernel(sides, half, *refs):
    sources, outs, refs = refs[:5], refs[5:9], refs[9:]
    part_ref, edge_ref, rows_ref, bands_ref = outs
    smems, (psi_ref, state_ref, slots, pairs_scr, wide_scr, sems) = refs[:3], refs[3:]
    copies = [
        pltpu.make_async_copy(source, dest, sems.at[n])
        for n, (source, dest) in enumerate(zip(sources, (*smems, psi_ref, state_ref)))
    ]
    for copy in copies:
        copy.start()
    cols, lat_rows, width = state_ref.shape
    part = part_ref.shape[1]
    chan = lax.axis_index("chan")
    lat = lax.axis_index("lat")
    wide_scr[cols * lat_rows :, :] = jnp.zeros(
        (wide_scr.shape[0] - cols * lat_rows, width), F32
    )
    for copy in copies[:4]:
        copy.wait()
    bands = band_rows((*smems, psi_ref), slots, range(lat_rows))
    pairs = lat_rows // PAIR
    for p in range(pairs):
        put_pair(pairs_scr.at[p], bands[p * PAIR : (p + 1) * PAIR])
    for g in range(lat_rows // GROUP):
        source = 2 * ((g + lat) % 2 if sides == 1 else g)
        first, second = pairs_scr[source], pairs_scr[source + 1]
        rows_ref[g] = jnp.concatenate([first, pltpu.roll(second, PAIR * WINDOW, 1)], axis=0)
    edges = [(pairs - 1) * (1 - lat)] if sides == 1 else [pairs - 1, 0]
    for n in range(sides):
        bands_ref[n] = pairs_scr[edges[n]].astype(BF16)
    copies[4].wait()
    turn(state_ref, 0, cols, wide_scr)
    for r in range(lat_rows):
        part_ref[r] = turned_row(wide_scr, lat_rows, r, (half - WIDE) * chan, part)
        edge_ref[r] = turned_row(wide_scr, lat_rows, r, (cols - WIDE) * chan, WIDE)


def edges_kernel(
    sides, half, part_ref, edge_ref, other_ref, bands_ref, fields_ref, lon_ref, *rest
):
    lat_refs, corner_refs, (wide_scr,) = rest[:sides], rest[sides : 2 * sides], rest[2 * sides :]
    cols, lat_rows, width = other_ref.shape
    lon_total = fields_ref.shape[1]
    part = part_ref.shape[1]
    chan = lax.axis_index("chan")
    wide_scr[cols * lat_rows :, :] = jnp.zeros(
        (wide_scr.shape[0] - cols * lat_rows, width), F32
    )

    def build(core):
        start = 0 if core == 0 else half - WIDE
        edge = 0 if core == 0 else cols - WIDE
        stop = start + part if core == 0 else cols
        at = WIDE if core == 0 else 0
        own = slice(core * width, (core + 1) * width)
        lane = slice((1 - core) * width, (2 - core) * width)
        turn(other_ref, start, stop, wide_scr)
        for r in range(lat_rows):
            lon_ref[r, :, own] = edge_ref[r]
            lon_ref[r, :, lane] = turned_row(wide_scr, lat_rows, r, edge, WIDE)
            fields_ref[r, at : at + part, own] = part_ref[r]
            fields_ref[r, at : at + part, lane] = turned_row(wide_scr, lat_rows, r, start, part)
        empty = slice(0, WIDE) if core == 0 else slice(part, lon_total)
        fields_ref[:, empty, :] = jnp.zeros((lat_rows, WIDE, 2 * width), BF16)

    @pl.when(chan == 0)
    def _():
        build(0)

    @pl.when(chan == 1)
    def _():
        build(1)

    at = pl.multiple_of((1 - chan) * WIDE, WIDE)
    for n, first in enumerate(needed_rows(sides, lat_rows)):
        for t in range(HALO):
            lat_refs[n][t * part : (t + 1) * part, :] = fields_ref[first + t, pl.ds(at, part), :]
            corner_refs[n][t] = lon_ref[first + t]
        lat_refs[n][HALO * part :, :] = bands_ref[n]


def needed_rows(sides, lat_rows):
    if sides == 1:
        return [(1 - lax.axis_index("lat")) * (lat_rows - HALO)]
    return [lat_rows - HALO, 0]


def tables_kernel(rows_ref, _, weights_hbm, tables_ref, order_ref, weights_ref, sem):
    fetch = pltpu.make_async_copy(weights_hbm, weights_ref, sem)
    fetch.start()
    groups, rows, _ = rows_ref.shape
    order = by_row(rows)
    for g in range(groups):
        tables_ref[g] = toeplitz(rows_ref[g], order)
    order_ref[...] = by_row(order_ref.shape[0] // BLOCK)
    fetch.wait()


def gelu(x):
    return 0.5 * x * (1.0 + jnp.tanh(0.7978845608028654 * (x + 0.044715 * (x * x * x))))


def add_lat_halo(rows, lat_ref, part, core):
    at = WIDE if core == 0 else 0
    for t, row in enumerate(rows):
        row[at : at + part, :] = lat_ref[t * part : (t + 1) * part, :]


def halo_table(lat_ref, order):
    count = order.shape[0] // BLOCK
    return toeplitz(lat_ref[lat_ref.shape[0] - count :, :].astype(F32), order)


def add_lon_halo(cols, half, rows, halos, core):
    count = cols - half + WIDE
    whole = count // BLOCK * BLOCK
    for row, halo in zip(rows, halos):
        if core == 0:
            row[0:WIDE, :] = halo[...]
            continue
        lon_total, chans = row.shape
        before = row[whole : whole + BLOCK, :].astype(F32)[0 : count - whole, :]
        empty = jnp.zeros((lon_total - count - WIDE, chans), F32)
        row[whole:lon_total, :] = jnp.concatenate(
            [before, halo[...].astype(F32), empty], axis=0
        ).astype(BF16)


def conv(source, table, base, in_rows, feats, first, out_rows, jb, put):
    chans = source.shape[2]
    basis = table.shape[0] // (out_rows * BLOCK)
    taken = source[pl.ds(base, in_rows), jb * BLOCK : jb * BLOCK + WINDOW, :]
    taken = taken.reshape(in_rows * WINDOW, chans)
    result = jnp.dot(table, taken, preferred_element_type=F32).astype(BF16)
    at = slice(put * BLOCK, (put + 1) * BLOCK)
    for m in range(out_rows):
        for k in range(basis):
            begin = (m * basis + k) * BLOCK
            feats[first + m, at, k * chans : (k + 1) * chans] = result[begin : begin + BLOCK, :]


def mix(weights_ref, layer, feats, row, blocks, befores, store):
    _, basis, chans, _ = weights_ref.shape
    count, lons = len(befores), len(blocks) * BLOCK
    mixed = jnp.dot(
        feats[row : row + count, 0:lons, :].reshape(count * lons, basis * chans),
        weights_ref[layer].reshape(basis * chans, chans),
        preferred_element_type=F32,
    )
    for n, before in enumerate(befores):
        before = before[...].astype(F32)
        for put, jb in enumerate(blocks):
            at, begin = SHIFT + jb * BLOCK, n * lons + put * BLOCK
            value = before[at : at + BLOCK, :] + gelu(mixed[begin : begin + BLOCK, :])
            store(n, jb, value)


def into(ref, rows):
    def store(n, jb, value):
        ref[rows[n], jb * BLOCK : (jb + 1) * BLOCK, :] = value.astype(BF16)

    return store


def into_turned(turned, rows, lat_rows):
    def store(n, jb, value):
        width = value.shape[1] // 2
        for c in range(2):
            turned[c, pl.ds(jb * BLOCK * lat_rows + rows[n], BLOCK, stride=lat_rows), :] = value[
                :, c * width : (c + 1) * width
            ]

    return store


def hand_out(turned, keep_ref, send_ref, core, start):
    count, lat_rows, width = keep_ref.shape
    at = slice(start * lat_rows, (start + count) * lat_rows)
    for ref, which in ((keep_ref, core), (send_ref, 1 - core)):
        ref[...] = turned[which, at, :].reshape(count, lat_rows, width).astype(BF16)


def late_blocks(core, count):
    return [0] if core == 0 else [count - 2, count - 1]


def early_blocks(core, count):
    late = late_blocks(core, count)
    return [jb for jb in range(count) if jb not in late]


def late_start(core, half):
    return 0 if core == 0 else half - LATE


def early_start(core):
    return LATE if core == 0 else 0


def for_each_core(body):
    for value in range(2):
        pl.when(lax.axis_index("chan") == value)(functools.partial(body, value))


def for_each_lat(body):
    for value in range(2):
        pl.when(lax.axis_index("lat") == value)(functools.partial(body, value))


def half_table(tables_ref, second):
    rows = tables_ref.shape[1] // 2
    return tables_ref[1, rows * second : rows * (second + 1), :]


def far_rows(
    lat, fields, after, tables_ref, weights_ref, feats, turned, blocks1, blocks2, parts
):
    lat_rows = after.shape[0]
    far = GROUP * lat
    near = GROUP - far
    mid = GROUP - PAIR * lat
    rows8 = GROUP + 2 * SPAN
    for put, jb in enumerate(blocks1):
        conv(fields, tables_ref[0], far, rows8, feats, 0, GROUP, jb, put)
        conv(fields, half_table(tables_ref, lat), near, rows8, feats, GROUP, PAIR, jb, put)
    dests = [SPAN + t for t in range(GROUP)]
    dests += [(GROUP + SPAN) * (1 - lat) + t for t in range(PAIR)]
    befores = [SPAN + far + t for t in range(GROUP)] + [SPAN + mid + t for t in range(PAIR)]
    step = len(dests) // parts
    for t in range(0, len(dests), step):
        rows = [fields.at[r] for r in befores[t : t + step]]
        mix(weights_ref, 0, feats, t, blocks1, rows, into(after, dests[t : t + step]))
    for put, jb in enumerate(blocks2):
        conv(after, tables_ref[0], 0, rows8, feats, 0, GROUP, jb, put)
    step = GROUP // parts
    for t in range(0, GROUP, step):
        befores = [after.at[SPAN + t + m] for m in range(step)]
        rows = [far + t + m for m in range(step)]
        mix(weights_ref, 1, feats, t, blocks2, befores, into_turned(turned, rows, lat_rows))


def far1_kernel(
    half, own_ref, tables_ref, weights_ref, fields_ref, after_ref, turned_ref, feats
):
    lat_rows, lon_total, chans = own_ref.shape
    for t in range(SPAN):
        fields_ref[t] = jnp.zeros((lon_total, chans), BF16)
        fields_ref[SPAN + lat_rows + t] = jnp.zeros((lon_total, chans), BF16)
    fields_ref[SPAN : SPAN + lat_rows] = own_ref[...]

    def body(lat, core):
        for t in range(SPAN):
            after_ref[(GROUP + SPAN) * lat + t] = jnp.zeros((lon_total - BLOCK, chans), BF16)
        far_rows(
            lat,
            fields_ref,
            after_ref,
            tables_ref,
            weights_ref,
            feats,
            turned_ref,
            early_blocks(core, lon_total // BLOCK - 1),
            early_blocks(core, half // BLOCK),
            2,
        )

    for_each_core(lambda core: for_each_lat(functools.partial(body, core=core)))


def far2_kernel(
    half,
    cols,
    lon_ref,
    tables_ref,
    weights_ref,
    fields_in,
    after_in,
    turned_in,
    fields_ref,
    after_ref,
    turned_ref,
    feats,
):
    lat_rows = lon_ref.shape[0]

    def body(lat, core):
        add_lon_halo(
            cols,
            half,
            [fields_ref.at[SPAN + r] for r in range(lat_rows)],
            [lon_ref.at[r] for r in range(lat_rows)],
            core,
        )
        far_rows(
            lat,
            fields_ref,
            after_ref,
            tables_ref,
            weights_ref,
            feats,
            turned_ref,
            late_blocks(core, fields_ref.shape[1] // BLOCK - 1),
            late_blocks(core, half // BLOCK),
            1,
        )

    for_each_core(lambda core: for_each_lat(functools.partial(body, core=core)))


def near_rows(
    lat, fields, near, table, tables_ref, weights_ref, feats, turned, blocks1, blocks2, parts
):
    lat_rows = near.shape[0]
    rows6, rows8 = PAIR + 2 * SPAN, GROUP + 2 * SPAN
    group = SPAN * lat
    beyond = HALO * (1 - lat)
    for put, jb in enumerate(blocks1):
        conv(fields, half_table(tables_ref, 1 - lat), group, rows8, feats, 0, PAIR, jb, put)
    for put, jb in enumerate(blocks1):
        conv(fields, table[:, 0 : rows6 * WINDOW], beyond, rows6, feats, PAIR, PAIR, jb, put)
    befores = [fields.at[HALO + m] for m in range(PAIR)]
    befores += [fields.at[beyond + SPAN + m] for m in range(PAIR)]
    dests = [GROUP * (1 - lat) + SPAN * lat + m for m in range(PAIR)]
    dests += [(GROUP + SPAN) * (1 - lat) + m for m in range(PAIR)]
    step = GROUP // parts
    for t in range(0, GROUP, step):
        rows = slice(t, t + step)
        mix(weights_ref, 0, feats, t, blocks1, befores[rows], into(near, dests[rows]))
    for put, jb in enumerate(blocks2):
        conv(near, tables_ref[1], 0, GROUP + 2 * SPAN, feats, 0, GROUP, jb, put)
    for t in range(0, GROUP, step):
        befores = [near.at[SPAN + t + m] for m in range(step)]
        rows = [GROUP * (1 - lat) + t + m for m in range(step)]
        mix(weights_ref, 1, feats, t, blocks2, befores, into_turned(turned, rows, lat_rows))


def near1_kernel(
    half,
    ext_ref,
    next_ref,
    lat_ref,
    tables_ref,
    weights_ref,
    order_ref,
    turned_in,
    fields_ref,
    near_ref,
    table_ref,
    turned_ref,
    keep_ref,
    send_ref,
    feats,
):
    lon_total = ext_ref.shape[1]

    def body(lat, core):
        halo = (HALO + SPAN) * (1 - lat)
        own = HALO * lat
        for t in range(HALO + SPAN):
            fields_ref[own + t] = ext_ref[SPAN + SPAN * (1 - lat) + t]
        add_lat_halo([fields_ref.at[halo + t] for t in range(HALO)], lat_ref, half + WIDE, core)
        table = halo_table(lat_ref, order_ref[...])
        table_ref[...] = table
        for t in range(GROUP):
            near_ref[GROUP * lat + t] = next_ref[GROUP * (1 - lat) + t]
        near_rows(
            lat,
            fields_ref,
            near_ref,
            table,
            tables_ref,
            weights_ref,
            feats,
            turned_ref,
            early_blocks(core, lon_total // BLOCK - 1),
            early_blocks(core, half // BLOCK),
            2,
        )
        hand_out(turned_ref, keep_ref, send_ref, core, early_start(core))

    for_each_core(lambda core: for_each_lat(functools.partial(body, core=core)))


def near2_kernel(
    half,
    cols,
    corner_ref,
    table_ref,
    tables_ref,
    weights_ref,
    fields_in,
    near_in,
    turned_in,
    fields_ref,
    near_ref,
    turned_ref,
    keep_ref,
    send_ref,
    feats,
):
    def body(lat, core):
        halo = (HALO + SPAN) * (1 - lat)
        add_lon_halo(
            cols,
            half,
            [fields_ref.at[halo + t] for t in range(HALO)],
            [corner_ref.at[t] for t in range(HALO)],
            core,
        )
        near_rows(
            lat,
            fields_ref,
            near_ref,
            table_ref[...],
            tables_ref,
            weights_ref,
            feats,
            turned_ref,
            late_blocks(core, fields_ref.shape[1] // BLOCK - 1),
            late_blocks(core, half // BLOCK),
            1,
        )
        hand_out(turned_ref, keep_ref, send_ref, core, late_start(core, half))

    for_each_core(lambda core: for_each_lat(functools.partial(body, core=core)))


def all_kernel(half, cols, own_ref, lon_ref, *rest):
    lat_refs, corner_refs = rest[:2], rest[2:4]
    (tables_ref, weights_ref, order_ref), rest = rest[4:7], rest[7:]
    (late_keep_ref, late_send_ref, keep_ref, send_ref), rest = rest[:4], rest[4:]
    fields, feats, after, turned = rest
    lat_rows, lon_total, chans = own_ref.shape
    groups = lat_rows // GROUP
    lon1 = lon_total - BLOCK
    halo_base = [0, lat_rows + HALO]
    win_base = [0, lat_rows + HALO - SPAN]
    out_base = [0, lat_rows + SPAN]
    rows6 = PAIR + 2 * SPAN

    fields[HALO : HALO + lat_rows] = own_ref[...]

    @for_each_core
    def _(core):
        rows = [fields.at[HALO + r] for r in range(lat_rows)]
        halos = [lon_ref.at[r] for r in range(lat_rows)]
        for n in range(2):
            halo_rows = [fields.at[halo_base[n] + t] for t in range(HALO)]
            add_lat_halo(halo_rows, lat_refs[n], half + WIDE, core)
            rows += halo_rows
            halos += [corner_refs[n].at[t] for t in range(HALO)]
        add_lon_halo(cols, half, rows, halos, core)

    halo_tables = [
        halo_table(lat_refs[n], order_ref[...])[:, 0 : rows6 * WINDOW] for n in range(2)
    ]
    blocks = range(lon1 // BLOCK)
    for jb in blocks:
        for g in range(groups):
            base = HALO - SPAN + g * GROUP
            conv(
                fields, tables_ref[g], base, GROUP + 2 * SPAN, feats, g * GROUP, GROUP, jb, jb
            )
        for n in range(2):
            first = lat_rows + n * PAIR
            conv(fields, halo_tables[n], win_base[n], rows6, feats, first, PAIR, jb, jb)
    dests = [SPAN + i for i in range(lat_rows)]
    dests += [out_base[n] + m for n in range(2) for m in range(PAIR)]
    for i in range(0, len(dests), PAIR):
        befores = [fields.at[dest + SPAN] for dest in dests[i : i + PAIR]]
        mix(weights_ref, 0, feats, i, blocks, befores, into(after, dests[i : i + PAIR]))
    blocks = range(half // BLOCK)
    for jb in blocks:
        for g in range(groups):
            base = g * GROUP
            conv(after, tables_ref[g], base, GROUP + 2 * SPAN, feats, base, GROUP, jb, jb)
    for i in range(0, lat_rows, PAIR):
        befores = [after.at[SPAN + i + m] for m in range(PAIR)]
        rows = [i + m for m in range(PAIR)]
        mix(weights_ref, 1, feats, i, blocks, befores, into_turned(turned, rows, lat_rows))

    @for_each_core
    def _(core):
        hand_out(turned, late_keep_ref, late_send_ref, core, late_start(core, half))
        hand_out(turned, keep_ref, send_ref, core, early_start(core))


def write(copies, sems):
    copies = [
        pltpu.make_async_copy(source, dest, sems.at[n])
        for n, (source, dest) in enumerate(copies)
    ]
    for copy in copies:
        copy.start()
    for copy in copies:
        copy.wait()


def early_kernel(half, keep_ref, got_ref, out_hbm, sems):
    @for_each_core
    def _(core):
        copies = []
        for which, ref in ((core, keep_ref), (1 - core, got_ref)):
            at = which * half + early_start(which)
            copies.append((ref, out_hbm.at[at : at + ref.shape[0]]))
        write(copies, sems)


def late_kernel(half, keep_ref, got_ref, out_in, out_hbm, sems):
    cols = out_hbm.shape[0]

    @for_each_core
    def _(core):
        copies = []
        for which, ref in ((core, keep_ref), (1 - core, got_ref)):
            at = which * half + late_start(which, half)
            count = min(LATE, cols - at)
            copies.append((ref.at[0:count], out_hbm.at[at : at + count]))
        write(copies, sems)


def per_device(state, sup_rows, sup_count, lon_reach, psi, weights):
    lat_rows, cols, width = state.shape
    basis = psi.shape[2]
    chans = weights.shape[2]
    lats, lons = lax.axis_size("lat"), lax.axis_size("lon")
    sides = 1 if lats == 2 else 2
    groups = lat_rows // GROUP
    lanes = (GROUP + 2 * SPAN) * WINDOW
    half = -(-cols // (2 * BLOCK)) * BLOCK
    part = half + WIDE
    lon_total = half + 2 * WIDE
    lon1 = lon_total - BLOCK
    swap = [(0, 1), (1, 0)]
    params = pltpu.CompilerParams(vmem_limit_bytes=VMEM_LIMIT)

    def shape(*dims):
        return jax.ShapeDtypeStruct(dims, BF16)

    def to_lat(step):
        if lats == 2:
            return [(a, 1 - a) for a in range(lats)]
        return [(a, a + step) for a in range(lats) if 0 <= a + step < lats]

    forth = [((z, 1), ((z + 1) % lons, 0)) for z in range(lons)]
    back = [((z, 0), ((z - 1) % lons, 1)) for z in range(lons)]
    to_lon = forth + back

    own = jnp.transpose(state, (1, 0, 2))
    other = lax.ppermute(own, "chan", swap)

    def scratch(*dims):
        return pltpu.VMEM(dims, F32)

    wide = scratch((half + part) * lat_rows, width)
    smalls = [sup_rows, sup_count, lon_reach]
    part_own, edge_own, rows, bands = pl.pallas_call(
        functools.partial(own_kernel, sides, half),
        out_shape=[
            shape(lat_rows, part, width),
            shape(lat_rows, WIDE, width),
            jax.ShapeDtypeStruct((groups, GROUP * basis, lanes), F32),
            shape(sides, PAIR * basis, lanes),
        ],
        in_specs=[hbm()] * 5,
        out_specs=[vmem()] * 4,
        scratch_shapes=[pltpu.SMEM(x.shape, x.dtype) for x in smalls]
        + [
            scratch(*psi.shape),
            pltpu.VMEM(own.shape, BF16),
            scratch(lat_rows, 2 * SPAN + 1, basis, lanes),
            scratch(lat_rows // PAIR, PAIR * basis, lanes),
            wide,
            pltpu.SemaphoreType.DMA((5,)),
        ],
        compiler_params=params,
        name="own",
    )(*[in_hbm(x) for x in smalls + [psi, own]])

    fields, lon_edge, *sends = pl.pallas_call(
        functools.partial(edges_kernel, sides, half),
        out_shape=[shape(lat_rows, lon_total, chans), shape(lat_rows, WIDE, chans)]
        + [shape(HALO * part + PAIR * basis, chans)] * sides
        + [shape(HALO, WIDE, chans)] * sides,
        in_specs=[vmem()] * 4,
        out_specs=[vmem()] * (2 + 2 * sides),
        scratch_shapes=[wide],
        compiler_params=params,
        name="edges",
    )(part_own, edge_own, other, bands)

    steps = [1, -1][:sides]
    lat_halos = [lax.ppermute(x, "lat", to_lat(step)) for x, step in zip(sends, steps)]
    lon_halo = lax.ppermute(
        lon_edge, ("lon", "chan"), [(z * 2 + c, y * 2 + d) for (z, c), (y, d) in to_lon]
    )

    corners = [
        lax.ppermute(
            x,
            ("lon", "lat", "chan"),
            [
                ((z * lats + a) * 2 + c, (y * lats + b) * 2 + d)
                for a, b in to_lat(step)
                for (z, c), (y, d) in to_lon
            ],
        )
        for x, step in zip(sends[sides:], steps)
    ]

    tables, order, weights_in = pl.pallas_call(
        tables_kernel,
        out_shape=[
            shape(groups, GROUP * basis * BLOCK, lanes),
            shape(PAIR * basis * BLOCK, PAIR * basis * BLOCK),
            shape(*weights.shape),
        ],
        in_specs=[vmem()] * 2 + [hbm()],
        out_specs=[vmem()] * 3,
        scratch_shapes=[pltpu.SemaphoreType.DMA],
        compiler_params=params,
        name="tables",
    )(rows, lon_edge, in_hbm(weights))

    late_shapes = [shape(LATE, lat_rows, width)] * 2
    early_shapes = [shape(half - LATE, lat_rows, width)] * 2
    turned = (2, half * lat_rows, width)
    if sides == 1:
        far_shapes = [
            shape(lat_rows + 2 * SPAN, lon_total, chans),
            shape(lat_rows, lon1, chans),
            jax.ShapeDtypeStruct(turned, F32),
        ]
        far_feats = pltpu.VMEM((GROUP + PAIR, lon1, basis * chans), BF16)
        far = pl.pallas_call(
            functools.partial(far1_kernel, half),
            out_shape=far_shapes,
            in_specs=[vmem()] * 3,
            out_specs=[vmem()] * 3,
            scratch_shapes=[far_feats],
            compiler_params=params,
            name="far_rows_1",
        )(fields, tables, weights_in)
        ext, after, done = pl.pallas_call(
            functools.partial(far2_kernel, half, cols),
            out_shape=far_shapes,
            in_specs=[vmem()] * 6,
            out_specs=[vmem()] * 3,
            scratch_shapes=[far_feats],
            input_output_aliases={3: 0, 4: 1, 5: 2},
            compiler_params=params,
            name="far_rows_2",
        )(lon_halo, tables, weights_in, *far)
        near_shapes = [shape(2 * HALO + SPAN, lon_total, chans), shape(GROUP + 2 * SPAN, lon1, chans)]
        near_feats = pltpu.VMEM((GROUP, lon1, basis * chans), BF16)
        ext, near, halo_tab, done, keep, send = pl.pallas_call(
            functools.partial(near1_kernel, half),
            out_shape=near_shapes
            + [shape(PAIR * basis * BLOCK, lanes), jax.ShapeDtypeStruct(turned, F32)]
            + early_shapes,
            in_specs=[vmem()] * 7,
            out_specs=[vmem()] * 6,
            scratch_shapes=[near_feats],
            input_output_aliases={6: 3},
            compiler_params=params,
            name="near_rows_1",
        )(ext, after, lat_halos[0], tables, weights_in, order, done)
        *_, late_keep, late_send = pl.pallas_call(
            functools.partial(near2_kernel, half, cols),
            out_shape=near_shapes + [jax.ShapeDtypeStruct(turned, F32)] + late_shapes,
            in_specs=[vmem()] * 7,
            out_specs=[vmem()] * 5,
            scratch_shapes=[near_feats],
            input_output_aliases={4: 0, 5: 1, 6: 2},
            compiler_params=params,
            name="near_rows_2",
        )(corners[0], halo_tab, tables, weights_in, ext, near, done)
    else:
        late_keep, late_send, keep, send = pl.pallas_call(
            functools.partial(all_kernel, half, cols),
            out_shape=late_shapes + early_shapes,
            in_specs=[vmem()] * (5 + 2 * sides),
            out_specs=[vmem()] * 4,
            scratch_shapes=[
                pltpu.VMEM((lat_rows + 2 * HALO, lon_total, chans), BF16),
                pltpu.VMEM((lat_rows + 2 * PAIR, lon1, basis * chans), BF16),
                pltpu.VMEM((lat_rows + 2 * SPAN, lon1, chans), BF16),
                scratch(*turned),
            ],
            compiler_params=params,
            name="all_rows",
        )(fields, lon_halo, *lat_halos, *corners, tables, weights_in, order)
    got = lax.ppermute(send, "chan", swap)
    late_got = lax.ppermute(late_send, "chan", swap)

    out_type = shape(cols, lat_rows, width)
    out = pl.pallas_call(
        functools.partial(early_kernel, half),
        out_shape=out_type,
        in_specs=[vmem()] * 2,
        out_specs=hbm(),
        scratch_shapes=[pltpu.SemaphoreType.DMA((2,))],
        compiler_params=params,
        name="write_early",
    )(keep, got)
    out = pl.pallas_call(
        functools.partial(late_kernel, half),
        out_shape=out_type,
        in_specs=[vmem()] * 2 + [hbm()],
        out_specs=hbm(),
        scratch_shapes=[pltpu.SemaphoreType.DMA((2,))],
        input_output_aliases={2: 0},
        compiler_params=params,
        name="write_late",
    )(late_keep, late_got, out)
    return jnp.transpose(out, (1, 0, 2))


def solution(mesh):
    return jax.shard_map(
        per_device,
        mesh=mesh,
        in_specs=(
            P(("groups", "lat"), "lon", "chan"),
            P("lat", None),
            P("lat"),
            P("lat"),
            P("lat", None, None, None),
            P(),
        ),
        out_specs=P(("groups", "lat"), "lon", "chan"),
        check_vma=False,
    )
```

```python
import functools

import jax
import jax.numpy as jnp
from jax import lax
from jax.experimental import pallas as pl
from jax.experimental.pallas import tpu as pltpu
from jax.sharding import PartitionSpec as P

LAYERS = 2
SPAN = 2
HALO = LAYERS * SPAN
BLOCK = 16
WINDOW = 2 * BLOCK
GROUP = 4
PAIR = 2
WIDE = BLOCK
LATE = 46
SHIFT = BLOCK // 2
VMEM_LIMIT = 48 * 1024 * 1024
BF16 = jnp.bfloat16
F32 = jnp.float32


def vmem():
    return pl.BlockSpec(memory_space=pltpu.VMEM)


def smem():
    return pl.BlockSpec(memory_space=pltpu.SMEM)


def hbm():
    return pl.BlockSpec(memory_space=pltpu.HBM)


def in_hbm(x):
    return pltpu.with_memory_space_constraint(x, pltpu.HBM)


def by_row(count):
    total = count * BLOCK
    out_row = lax.broadcasted_iota(jnp.int32, (total, total), 0)
    in_row = lax.broadcasted_iota(jnp.int32, (total, total), 1)
    source = (out_row % BLOCK) * count + out_row // BLOCK
    return (in_row == source).astype(F32).astype(BF16)


def toeplitz(rows_tab, order):
    moved = jnp.concatenate(
        [rows_tab if jj == 0 else pltpu.roll(rows_tab, jj, 1) for jj in range(BLOCK)], axis=0
    ).astype(BF16)
    return jnp.dot(order, moved, preferred_element_type=F32).astype(BF16)


def band_rows(refs, slots, rows):
    sup_ref, count_ref, reach_ref, psi_ref = refs
    lat_rows, sup, basis, offsets = psi_ref.shape
    lanes = slots.shape[3]
    slots[...] = jnp.zeros_like(slots)
    for n, i in enumerate(rows):
        row = lax.axis_index("lat") * lat_rows + i
        values = [psi_ref[i, s] for s in range(sup)]
        places = [jnp.where(s < count_ref[i], sup_ref[i, s] - row, -lat_rows) for s in range(sup)]
        for rel in range(2 * SPAN + 1):
            total = jnp.zeros((basis, offsets), F32)
            for value, at in zip(values, places):
                total = total + jnp.where(at == rel - SPAN, value, 0.0)
            slots[n, rel, :, 0:offsets] = total
    off = lax.broadcasted_iota(jnp.int32, (basis, lanes), 1) % WINDOW - offsets // 2
    bands = []
    for n, i in enumerate(rows):
        band = slots[n, 0]
        for rel in range(1, 2 * SPAN + 1):
            band = band + pltpu.roll(slots[n, rel], rel * WINDOW, 1)
        bands.append(jnp.where(jnp.abs(off) <= reach_ref[i], band, 0.0))
    return bands


def put_pair(scr, bands):
    for m, band in enumerate(bands):
        basis = band.shape[0]
        scr[m * basis : (m + 1) * basis, :] = (
            band if m == 0 else pltpu.roll(band, m * WINDOW, 1)
        )


def turn(ref, lon_from, lon_to, wide_scr):
    _, lat_rows, width = ref.shape
    wide_scr[lon_from * lat_rows : lon_to * lat_rows, :] = (
        ref[lon_from:lon_to].astype(F32).reshape((lon_to - lon_from) * lat_rows, width)
    )


def turned_row(wide_scr, lat_rows, row, start, count):
    return wide_scr[pl.ds(start * lat_rows + row, count, stride=lat_rows), :].astype(BF16)


def own_kernel(sides, half, *refs):
    sources, (part_ref, edge_ref, bands_ref), refs = refs[:5], refs[5:8], refs[8:]
    smems, (psi_ref, state_ref, slots, pair_scr, wide_scr, sems) = refs[:3], refs[3:]
    copies = [
        pltpu.make_async_copy(source, dest, sems.at[n])
        for n, (source, dest) in enumerate(zip(sources, (*smems, psi_ref, state_ref)))
    ]
    for copy in copies:
        copy.start()
    cols, lat_rows, width = state_ref.shape
    part = part_ref.shape[1]
    wide_scr[cols * lat_rows :, :] = jnp.zeros(
        (wide_scr.shape[0] - cols * lat_rows, width), F32
    )
    for copy in copies[:4]:
        copy.wait()
    firsts = [first + (HALO - PAIR) * (n == 0) for n, first in enumerate(needed_rows(2, lat_rows))]
    if sides == 1:
        firsts = [(1 - lax.axis_index("lat")) * (lat_rows - PAIR)]
    rows = [first + m for first in firsts for m in range(PAIR)]
    bands = band_rows((*smems, psi_ref), slots, rows)
    for n in range(sides):
        put_pair(pair_scr, bands[n * PAIR : (n + 1) * PAIR])
        bands_ref[n] = pair_scr[...].astype(BF16)
    copies[4].wait()

    @for_each_core
    def _(core):
        start = 0 if core == 0 else half - WIDE
        edge = 0 if core == 0 else cols - WIDE
        turn(state_ref, start, min(start + part, cols), wide_scr)
        for r in range(lat_rows):
            part_ref[r] = turned_row(wide_scr, lat_rows, r, start, part)
            edge_ref[r] = turned_row(wide_scr, lat_rows, r, edge, WIDE)


def edges_kernel(
    sides, half, part_ref, edge_ref, other_ref, bands_ref, fields_ref, lon_ref, *rest
):
    lat_refs, corner_refs, (wide_scr,) = rest[:sides], rest[sides : 2 * sides], rest[2 * sides :]
    cols, lat_rows, width = other_ref.shape
    lon_total = fields_ref.shape[1]
    part = part_ref.shape[1]
    chan = lax.axis_index("chan")
    wide_scr[cols * lat_rows :, :] = jnp.zeros(
        (wide_scr.shape[0] - cols * lat_rows, width), F32
    )

    def build(core):
        start = 0 if core == 0 else half - WIDE
        edge = 0 if core == 0 else cols - WIDE
        stop = start + part if core == 0 else cols
        at = WIDE if core == 0 else 0
        own = slice(core * width, (core + 1) * width)
        lane = slice((1 - core) * width, (2 - core) * width)
        turn(other_ref, start, stop, wide_scr)
        for r in range(lat_rows):
            lon_ref[r, :, own] = edge_ref[r]
            lon_ref[r, :, lane] = turned_row(wide_scr, lat_rows, r, edge, WIDE)
            fields_ref[r, at : at + part, own] = part_ref[r]
            fields_ref[r, at : at + part, lane] = turned_row(wide_scr, lat_rows, r, start, part)
        empty = slice(0, WIDE) if core == 0 else slice(part, lon_total)
        fields_ref[:, empty, :] = jnp.zeros((lat_rows, WIDE, 2 * width), BF16)

    @pl.when(chan == 0)
    def _():
        build(0)

    @pl.when(chan == 1)
    def _():
        build(1)

    at = pl.multiple_of((1 - chan) * WIDE, WIDE)
    for n, first in enumerate(needed_rows(sides, lat_rows)):
        for t in range(HALO):
            lat_refs[n][t * part : (t + 1) * part, :] = fields_ref[first + t, pl.ds(at, part), :]
            corner_refs[n][t] = lon_ref[first + t]
        lat_refs[n][HALO * part :, :] = bands_ref[n]


def needed_rows(sides, lat_rows):
    if sides == 1:
        return [(1 - lax.axis_index("lat")) * (lat_rows - HALO)]
    return [lat_rows - HALO, 0]


def tables_kernel(sides, sup_hbm, count_hbm, reach_hbm, psi_hbm, weights_hbm, _, *refs):
    (weights_ref, tables_ref, order_ref), refs = refs[:3], refs[3:]
    smems, (psi_ref, slots, pairs_scr, sems) = refs[:3], refs[3:]
    sources = (sup_hbm, count_hbm, reach_hbm, psi_hbm, weights_hbm)
    copies = [
        pltpu.make_async_copy(source, dest, sems.at[n])
        for n, (source, dest) in enumerate(zip(sources, (*smems, psi_ref, weights_ref)))
    ]
    for copy in copies:
        copy.start()
    lat_rows, _, basis, _ = psi_ref.shape
    lat = lax.axis_index("lat")
    order = by_row(GROUP * basis)
    order_ref[...] = by_row(PAIR * basis)
    for copy in copies[:4]:
        copy.wait()
    bands = band_rows((*smems, psi_ref), slots, range(lat_rows))
    for p in range(lat_rows // PAIR):
        put_pair(pairs_scr.at[p], bands[p * PAIR : (p + 1) * PAIR])

    def group(g):
        first, second = pairs_scr[2 * g], pairs_scr[2 * g + 1]
        return jnp.concatenate([first, pltpu.roll(second, PAIR * WINDOW, 1)], axis=0)

    if sides == 1:
        tables_ref[0] = toeplitz(group(lat), order)
        tables_ref[1] = toeplitz(group(1 - lat), order)
    else:
        for g in range(lat_rows // GROUP):
            tables_ref[g] = toeplitz(group(g), order)
    copies[4].wait()


def gelu(x):
    return 0.5 * x * (1.0 + jnp.tanh(0.7978845608028654 * (x + 0.044715 * (x * x * x))))


def add_lat_halo(rows, lat_ref, part, core):
    at = WIDE if core == 0 else 0
    for t, row in enumerate(rows):
        row[at : at + part, :] = lat_ref[t * part : (t + 1) * part, :]


def halo_table(lat_ref, order):
    count = order.shape[0] // BLOCK
    return toeplitz(lat_ref[lat_ref.shape[0] - count :, :].astype(F32), order)


def add_lon_halo(cols, half, rows, halos, core):
    count = cols - half + WIDE
    whole = count // BLOCK * BLOCK
    for row, halo in zip(rows, halos):
        if core == 0:
            row[0:WIDE, :] = halo[...]
            continue
        lon_total, chans = row.shape
        before = row[whole : whole + BLOCK, :].astype(F32)[0 : count - whole, :]
        empty = jnp.zeros((lon_total - count - WIDE, chans), F32)
        row[whole:lon_total, :] = jnp.concatenate(
            [before, halo[...].astype(F32), empty], axis=0
        ).astype(BF16)


def conv(source, table, base, in_rows, feats, first, out_rows, jb, put):
    chans = source.shape[2]
    basis = table.shape[0] // (out_rows * BLOCK)
    taken = source[pl.ds(base, in_rows), jb * BLOCK : jb * BLOCK + WINDOW, :]
    taken = taken.reshape(in_rows * WINDOW, chans)
    result = jnp.dot(table, taken, preferred_element_type=F32).astype(BF16)
    at = slice(put * BLOCK, (put + 1) * BLOCK)
    for m in range(out_rows):
        for k in range(basis):
            begin = (m * basis + k) * BLOCK
            feats[first + m, at, k * chans : (k + 1) * chans] = result[begin : begin + BLOCK, :]


def mix(weights_ref, layer, feats, row, blocks, befores, store):
    _, basis, chans, _ = weights_ref.shape
    count, lons = len(befores), len(blocks) * BLOCK
    mixed = jnp.dot(
        feats[row : row + count, 0:lons, :].reshape(count * lons, basis * chans),
        weights_ref[layer].reshape(basis * chans, chans),
        preferred_element_type=F32,
    )
    for n, before in enumerate(befores):
        before = before[...].astype(F32)
        for put, jb in enumerate(blocks):
            at, begin = SHIFT + jb * BLOCK, n * lons + put * BLOCK
            value = before[at : at + BLOCK, :] + gelu(mixed[begin : begin + BLOCK, :])
            store(n, jb, value)


def into(ref, rows):
    def store(n, jb, value):
        ref[rows[n], jb * BLOCK : (jb + 1) * BLOCK, :] = value.astype(BF16)

    return store


def into_turned(turned, rows, lat_rows):
    def store(n, jb, value):
        width = value.shape[1] // 2
        for c in range(2):
            turned[c, pl.ds(jb * BLOCK * lat_rows + rows[n], BLOCK, stride=lat_rows), :] = value[
                :, c * width : (c + 1) * width
            ]

    return store


def hand_out(turned, keep_ref, send_ref, core, start):
    count, lat_rows, width = keep_ref.shape
    at = slice(start * lat_rows, (start + count) * lat_rows)
    for ref, which in ((keep_ref, core), (send_ref, 1 - core)):
        ref[...] = turned[which, at, :].reshape(count, lat_rows, width).astype(BF16)


def late_blocks(core, count):
    return [0] if core == 0 else [count - 2, count - 1]


def early_blocks(core, count):
    late = late_blocks(core, count)
    return [jb for jb in range(count) if jb not in late]


def late_start(core, half):
    return 0 if core == 0 else half - LATE


def early_start(core):
    return LATE if core == 0 else 0


def for_each_core(body):
    for value in range(2):
        pl.when(lax.axis_index("chan") == value)(functools.partial(body, value))


def for_each_lat(body):
    for value in range(2):
        pl.when(lax.axis_index("lat") == value)(functools.partial(body, value))


def half_table(tables_ref, second):
    rows = tables_ref.shape[1] // 2
    return tables_ref[1, rows * second : rows * (second + 1), :]


def far_rows(
    lat, fields, after, tables_ref, weights_ref, feats, turned, blocks1, blocks2, parts
):
    lat_rows = after.shape[0]
    far = GROUP * lat
    near = GROUP - far
    mid = GROUP - PAIR * lat
    rows8 = GROUP + 2 * SPAN
    for put, jb in enumerate(blocks1):
        conv(fields, tables_ref[0], far, rows8, feats, 0, GROUP, jb, put)
        conv(fields, half_table(tables_ref, lat), near, rows8, feats, GROUP, PAIR, jb, put)
    dests = [SPAN + t for t in range(GROUP)]
    dests += [(GROUP + SPAN) * (1 - lat) + t for t in range(PAIR)]
    befores = [SPAN + far + t for t in range(GROUP)] + [SPAN + mid + t for t in range(PAIR)]
    step = len(dests) // parts
    for t in range(0, len(dests), step):
        rows = [fields.at[r] for r in befores[t : t + step]]
        mix(weights_ref, 0, feats, t, blocks1, rows, into(after, dests[t : t + step]))
    for put, jb in enumerate(blocks2):
        conv(after, tables_ref[0], 0, rows8, feats, 0, GROUP, jb, put)
    step = GROUP // parts
    for t in range(0, GROUP, step):
        befores = [after.at[SPAN + t + m] for m in range(step)]
        rows = [far + t + m for m in range(step)]
        mix(weights_ref, 1, feats, t, blocks2, befores, into_turned(turned, rows, lat_rows))


def far1_kernel(
    half, own_ref, tables_ref, weights_ref, fields_ref, after_ref, turned_ref, feats
):
    lat_rows, lon_total, chans = own_ref.shape
    for t in range(SPAN):
        fields_ref[t] = jnp.zeros((lon_total, chans), BF16)
        fields_ref[SPAN + lat_rows + t] = jnp.zeros((lon_total, chans), BF16)
    fields_ref[SPAN : SPAN + lat_rows] = own_ref[...]

    def body(lat, core):
        for t in range(SPAN):
            after_ref[(GROUP + SPAN) * lat + t] = jnp.zeros((lon_total - BLOCK, chans), BF16)
        far_rows(
            lat,
            fields_ref,
            after_ref,
            tables_ref,
            weights_ref,
            feats,
            turned_ref,
            early_blocks(core, lon_total // BLOCK - 1),
            early_blocks(core, half // BLOCK),
            2,
        )

    for_each_core(lambda core: for_each_lat(functools.partial(body, core=core)))


def far2_kernel(
    half,
    cols,
    lon_ref,
    tables_ref,
    weights_ref,
    fields_in,
    after_in,
    turned_in,
    fields_ref,
    after_ref,
    turned_ref,
    feats,
):
    lat_rows = lon_ref.shape[0]

    def body(lat, core):
        add_lon_halo(
            cols,
            half,
            [fields_ref.at[SPAN + r] for r in range(lat_rows)],
            [lon_ref.at[r] for r in range(lat_rows)],
            core,
        )
        far_rows(
            lat,
            fields_ref,
            after_ref,
            tables_ref,
            weights_ref,
            feats,
            turned_ref,
            late_blocks(core, fields_ref.shape[1] // BLOCK - 1),
            late_blocks(core, half // BLOCK),
            1,
        )

    for_each_core(lambda core: for_each_lat(functools.partial(body, core=core)))


def near_rows(
    lat, fields, near, table, tables_ref, weights_ref, feats, turned, blocks1, blocks2, parts
):
    lat_rows = near.shape[0]
    rows6, rows8 = PAIR + 2 * SPAN, GROUP + 2 * SPAN
    group = SPAN * lat
    beyond = HALO * (1 - lat)
    for put, jb in enumerate(blocks1):
        conv(fields, half_table(tables_ref, 1 - lat), group, rows8, feats, 0, PAIR, jb, put)
    for put, jb in enumerate(blocks1):
        conv(fields, table[:, 0 : rows6 * WINDOW], beyond, rows6, feats, PAIR, PAIR, jb, put)
    befores = [fields.at[HALO + m] for m in range(PAIR)]
    befores += [fields.at[beyond + SPAN + m] for m in range(PAIR)]
    dests = [GROUP * (1 - lat) + SPAN * lat + m for m in range(PAIR)]
    dests += [(GROUP + SPAN) * (1 - lat) + m for m in range(PAIR)]
    step = GROUP // parts
    for t in range(0, GROUP, step):
        rows = slice(t, t + step)
        mix(weights_ref, 0, feats, t, blocks1, befores[rows], into(near, dests[rows]))
    for put, jb in enumerate(blocks2):
        conv(near, tables_ref[1], 0, GROUP + 2 * SPAN, feats, 0, GROUP, jb, put)
    for t in range(0, GROUP, step):
        befores = [near.at[SPAN + t + m] for m in range(step)]
        rows = [GROUP * (1 - lat) + t + m for m in range(step)]
        mix(weights_ref, 1, feats, t, blocks2, befores, into_turned(turned, rows, lat_rows))


def near1_kernel(
    half,
    ext_ref,
    next_ref,
    lat_ref,
    tables_ref,
    weights_ref,
    order_ref,
    turned_in,
    fields_ref,
    near_ref,
    table_ref,
    turned_ref,
    keep_ref,
    send_ref,
    feats,
):
    lon_total = ext_ref.shape[1]

    def body(lat, core):
        halo = (HALO + SPAN) * (1 - lat)
        own = HALO * lat
        for t in range(HALO + SPAN):
            fields_ref[own + t] = ext_ref[SPAN + SPAN * (1 - lat) + t]
        add_lat_halo([fields_ref.at[halo + t] for t in range(HALO)], lat_ref, half + WIDE, core)
        table = halo_table(lat_ref, order_ref[...])
        table_ref[...] = table
        for t in range(GROUP):
            near_ref[GROUP * lat + t] = next_ref[GROUP * (1 - lat) + t]
        near_rows(
            lat,
            fields_ref,
            near_ref,
            table,
            tables_ref,
            weights_ref,
            feats,
            turned_ref,
            early_blocks(core, lon_total // BLOCK - 1),
            early_blocks(core, half // BLOCK),
            2,
        )
        hand_out(turned_ref, keep_ref, send_ref, core, early_start(core))

    for_each_core(lambda core: for_each_lat(functools.partial(body, core=core)))


def near2_kernel(
    half,
    cols,
    corner_ref,
    table_ref,
    tables_ref,
    weights_ref,
    fields_in,
    near_in,
    turned_in,
    fields_ref,
    near_ref,
    turned_ref,
    keep_ref,
    send_ref,
    feats,
):
    def body(lat, core):
        halo = (HALO + SPAN) * (1 - lat)
        add_lon_halo(
            cols,
            half,
            [fields_ref.at[halo + t] for t in range(HALO)],
            [corner_ref.at[t] for t in range(HALO)],
            core,
        )
        near_rows(
            lat,
            fields_ref,
            near_ref,
            table_ref[...],
            tables_ref,
            weights_ref,
            feats,
            turned_ref,
            late_blocks(core, fields_ref.shape[1] // BLOCK - 1),
            late_blocks(core, half // BLOCK),
            1,
        )
        hand_out(turned_ref, keep_ref, send_ref, core, late_start(core, half))

    for_each_core(lambda core: for_each_lat(functools.partial(body, core=core)))


def all_kernel(half, cols, own_ref, lon_ref, *rest):
    lat_refs, corner_refs = rest[:2], rest[2:4]
    (tables_ref, weights_ref, order_ref), rest = rest[4:7], rest[7:]
    (late_keep_ref, late_send_ref, keep_ref, send_ref), rest = rest[:4], rest[4:]
    fields, feats, after, turned = rest
    lat_rows, lon_total, chans = own_ref.shape
    groups = lat_rows // GROUP
    lon1 = lon_total - BLOCK
    halo_base = [0, lat_rows + HALO]
    win_base = [0, lat_rows + HALO - SPAN]
    out_base = [0, lat_rows + SPAN]
    rows6 = PAIR + 2 * SPAN

    fields[HALO : HALO + lat_rows] = own_ref[...]

    @for_each_core
    def _(core):
        rows = [fields.at[HALO + r] for r in range(lat_rows)]
        halos = [lon_ref.at[r] for r in range(lat_rows)]
        for n in range(2):
            halo_rows = [fields.at[halo_base[n] + t] for t in range(HALO)]
            add_lat_halo(halo_rows, lat_refs[n], half + WIDE, core)
            rows += halo_rows
            halos += [corner_refs[n].at[t] for t in range(HALO)]
        add_lon_halo(cols, half, rows, halos, core)

    halo_tables = [
        halo_table(lat_refs[n], order_ref[...])[:, 0 : rows6 * WINDOW] for n in range(2)
    ]
    blocks = range(lon1 // BLOCK)
    for jb in blocks:
        for g in range(groups):
            base = HALO - SPAN + g * GROUP
            conv(
                fields, tables_ref[g], base, GROUP + 2 * SPAN, feats, g * GROUP, GROUP, jb, jb
            )
        for n in range(2):
            first = lat_rows + n * PAIR
            conv(fields, halo_tables[n], win_base[n], rows6, feats, first, PAIR, jb, jb)
    dests = [SPAN + i for i in range(lat_rows)]
    dests += [out_base[n] + m for n in range(2) for m in range(PAIR)]
    for i in range(0, len(dests), PAIR):
        befores = [fields.at[dest + SPAN] for dest in dests[i : i + PAIR]]
        mix(weights_ref, 0, feats, i, blocks, befores, into(after, dests[i : i + PAIR]))
    blocks = range(half // BLOCK)
    for jb in blocks:
        for g in range(groups):
            base = g * GROUP
            conv(after, tables_ref[g], base, GROUP + 2 * SPAN, feats, base, GROUP, jb, jb)
    for i in range(0, lat_rows, PAIR):
        befores = [after.at[SPAN + i + m] for m in range(PAIR)]
        rows = [i + m for m in range(PAIR)]
        mix(weights_ref, 1, feats, i, blocks, befores, into_turned(turned, rows, lat_rows))

    @for_each_core
    def _(core):
        hand_out(turned, late_keep_ref, late_send_ref, core, late_start(core, half))
        hand_out(turned, keep_ref, send_ref, core, early_start(core))


def write(copies, sems):
    copies = [
        pltpu.make_async_copy(source, dest, sems.at[n])
        for n, (source, dest) in enumerate(copies)
    ]
    for copy in copies:
        copy.start()
    for copy in copies:
        copy.wait()


def early_kernel(half, keep_ref, got_ref, out_hbm, sems):
    @for_each_core
    def _(core):
        copies = []
        for which, ref in ((core, keep_ref), (1 - core, got_ref)):
            at = which * half + early_start(which)
            copies.append((ref, out_hbm.at[at : at + ref.shape[0]]))
        write(copies, sems)


def late_kernel(half, keep_ref, got_ref, out_in, out_hbm, sems):
    cols = out_hbm.shape[0]

    @for_each_core
    def _(core):
        copies = []
        for which, ref in ((core, keep_ref), (1 - core, got_ref)):
            at = which * half + late_start(which, half)
            count = min(LATE, cols - at)
            copies.append((ref.at[0:count], out_hbm.at[at : at + count]))
        write(copies, sems)


def per_device(state, sup_rows, sup_count, lon_reach, psi, weights):
    lat_rows, cols, width = state.shape
    basis = psi.shape[2]
    chans = weights.shape[2]
    lats, lons = lax.axis_size("lat"), lax.axis_size("lon")
    sides = 1 if lats == 2 else 2
    groups = lat_rows // GROUP
    lanes = (GROUP + 2 * SPAN) * WINDOW
    half = -(-cols // (2 * BLOCK)) * BLOCK
    part = half + WIDE
    lon_total = half + 2 * WIDE
    lon1 = lon_total - BLOCK
    swap = [(0, 1), (1, 0)]
    params = pltpu.CompilerParams(vmem_limit_bytes=VMEM_LIMIT)

    def shape(*dims):
        return jax.ShapeDtypeStruct(dims, BF16)

    def to_lat(step):
        if lats == 2:
            return [(a, 1 - a) for a in range(lats)]
        return [(a, a + step) for a in range(lats) if 0 <= a + step < lats]

    forth = [((z, 1), ((z + 1) % lons, 0)) for z in range(lons)]
    back = [((z, 0), ((z - 1) % lons, 1)) for z in range(lons)]
    to_lon = forth + back

    own = jnp.transpose(state, (1, 0, 2))
    other = lax.ppermute(own, "chan", swap)

    def scratch(*dims):
        return pltpu.VMEM(dims, F32)

    wide = scratch((half + part) * lat_rows, width)
    smalls = [sup_rows, sup_count, lon_reach]
    part_own, edge_own, bands = pl.pallas_call(
        functools.partial(own_kernel, sides, half),
        out_shape=[
            shape(lat_rows, part, width),
            shape(lat_rows, WIDE, width),
            shape(sides, PAIR * basis, lanes),
        ],
        in_specs=[hbm()] * 5,
        out_specs=[vmem()] * 3,
        scratch_shapes=[pltpu.SMEM(x.shape, x.dtype) for x in smalls]
        + [
            scratch(*psi.shape),
            pltpu.VMEM(own.shape, BF16),
            scratch(sides * PAIR, 2 * SPAN + 1, basis, lanes),
            scratch(PAIR * basis, lanes),
            wide,
            pltpu.SemaphoreType.DMA((5,)),
        ],
        compiler_params=params,
        name="own",
    )(*[in_hbm(x) for x in smalls + [psi, own]])

    fields, lon_edge, *sends = pl.pallas_call(
        functools.partial(edges_kernel, sides, half),
        out_shape=[shape(lat_rows, lon_total, chans), shape(lat_rows, WIDE, chans)]
        + [shape(HALO * part + PAIR * basis, chans)] * sides
        + [shape(HALO, WIDE, chans)] * sides,
        in_specs=[vmem()] * 4,
        out_specs=[vmem()] * (2 + 2 * sides),
        scratch_shapes=[wide],
        compiler_params=params,
        name="edges",
    )(part_own, edge_own, other, bands)

    steps = [1, -1][:sides]
    lat_halos = [lax.ppermute(x, "lat", to_lat(step)) for x, step in zip(sends, steps)]
    lon_halo = lax.ppermute(
        lon_edge, ("lon", "chan"), [(z * 2 + c, y * 2 + d) for (z, c), (y, d) in to_lon]
    )

    corners = [
        lax.ppermute(
            x,
            ("lon", "lat", "chan"),
            [
                ((z * lats + a) * 2 + c, (y * lats + b) * 2 + d)
                for a, b in to_lat(step)
                for (z, c), (y, d) in to_lon
            ],
        )
        for x, step in zip(sends[sides:], steps)
    ]

    weights_in, tables, order = pl.pallas_call(
        functools.partial(tables_kernel, sides),
        out_shape=[
            shape(*weights.shape),
            shape(groups, GROUP * basis * BLOCK, lanes),
            shape(PAIR * basis * BLOCK, PAIR * basis * BLOCK),
        ],
        in_specs=[hbm()] * 5 + [vmem()],
        out_specs=[vmem()] * 3,
        scratch_shapes=[pltpu.SMEM(x.shape, x.dtype) for x in smalls]
        + [
            scratch(*psi.shape),
            scratch(lat_rows, 2 * SPAN + 1, basis, lanes),
            scratch(lat_rows // PAIR, PAIR * basis, lanes),
            pltpu.SemaphoreType.DMA((5,)),
        ],
        compiler_params=params,
        name="tables",
    )(*[in_hbm(x) for x in smalls + [psi, weights]], lon_edge)

    late_shapes = [shape(LATE, lat_rows, width)] * 2
    early_shapes = [shape(half - LATE, lat_rows, width)] * 2
    turned = (2, half * lat_rows, width)
    if sides == 1:
        far_shapes = [
            shape(lat_rows + 2 * SPAN, lon_total, chans),
            shape(lat_rows, lon1, chans),
            jax.ShapeDtypeStruct(turned, F32),
        ]
        far_feats = pltpu.VMEM((GROUP + PAIR, lon1, basis * chans), BF16)
        far = pl.pallas_call(
            functools.partial(far1_kernel, half),
            out_shape=far_shapes,
            in_specs=[vmem()] * 3,
            out_specs=[vmem()] * 3,
            scratch_shapes=[far_feats],
            compiler_params=params,
            name="far_rows_1",
        )(fields, tables, weights_in)
        ext, after, done = pl.pallas_call(
            functools.partial(far2_kernel, half, cols),
            out_shape=far_shapes,
            in_specs=[vmem()] * 6,
            out_specs=[vmem()] * 3,
            scratch_shapes=[far_feats],
            input_output_aliases={3: 0, 4: 1, 5: 2},
            compiler_params=params,
            name="far_rows_2",
        )(lon_halo, tables, weights_in, *far)
        near_shapes = [shape(2 * HALO + SPAN, lon_total, chans), shape(GROUP + 2 * SPAN, lon1, chans)]
        near_feats = pltpu.VMEM((GROUP, lon1, basis * chans), BF16)
        ext, near, halo_tab, done, keep, send = pl.pallas_call(
            functools.partial(near1_kernel, half),
            out_shape=near_shapes
            + [shape(PAIR * basis * BLOCK, lanes), jax.ShapeDtypeStruct(turned, F32)]
            + early_shapes,
            in_specs=[vmem()] * 7,
            out_specs=[vmem()] * 6,
            scratch_shapes=[near_feats],
            input_output_aliases={6: 3},
            compiler_params=params,
            name="near_rows_1",
        )(ext, after, lat_halos[0], tables, weights_in, order, done)
        *_, late_keep, late_send = pl.pallas_call(
            functools.partial(near2_kernel, half, cols),
            out_shape=near_shapes + [jax.ShapeDtypeStruct(turned, F32)] + late_shapes,
            in_specs=[vmem()] * 7,
            out_specs=[vmem()] * 5,
            scratch_shapes=[near_feats],
            input_output_aliases={4: 0, 5: 1, 6: 2},
            compiler_params=params,
            name="near_rows_2",
        )(corners[0], halo_tab, tables, weights_in, ext, near, done)
    else:
        late_keep, late_send, keep, send = pl.pallas_call(
            functools.partial(all_kernel, half, cols),
            out_shape=late_shapes + early_shapes,
            in_specs=[vmem()] * (5 + 2 * sides),
            out_specs=[vmem()] * 4,
            scratch_shapes=[
                pltpu.VMEM((lat_rows + 2 * HALO, lon_total, chans), BF16),
                pltpu.VMEM((lat_rows + 2 * PAIR, lon1, basis * chans), BF16),
                pltpu.VMEM((lat_rows + 2 * SPAN, lon1, chans), BF16),
                scratch(*turned),
            ],
            compiler_params=params,
            name="all_rows",
        )(fields, lon_halo, *lat_halos, *corners, tables, weights_in, order)
    got = lax.ppermute(send, "chan", swap)
    late_got = lax.ppermute(late_send, "chan", swap)

    out_type = shape(cols, lat_rows, width)
    out = pl.pallas_call(
        functools.partial(early_kernel, half),
        out_shape=out_type,
        in_specs=[vmem()] * 2,
        out_specs=hbm(),
        scratch_shapes=[pltpu.SemaphoreType.DMA((2,))],
        compiler_params=params,
        name="write_early",
    )(keep, got)
    out = pl.pallas_call(
        functools.partial(late_kernel, half),
        out_shape=out_type,
        in_specs=[vmem()] * 2 + [hbm()],
        out_specs=hbm(),
        scratch_shapes=[pltpu.SemaphoreType.DMA((2,))],
        input_output_aliases={2: 0},
        compiler_params=params,
        name="write_late",
    )(late_keep, late_got, out)
    return jnp.transpose(out, (1, 0, 2))


def solution(mesh):
    return jax.shard_map(
        per_device,
        mesh=mesh,
        in_specs=(
            P(("groups", "lat"), "lon", "chan"),
            P("lat", None),
            P("lat"),
            P("lat"),
            P("lat", None, None, None),
            P(),
        ),
        out_specs=P(("groups", "lat"), "lon", "chan"),
        check_vma=False,
    )
```

```python
import functools

import jax
import jax.numpy as jnp
from jax import lax
from jax.experimental import pallas as pl
from jax.experimental.pallas import tpu as pltpu
from jax.sharding import PartitionSpec as P

LAYERS = 2
SPAN = 2
HALO = LAYERS * SPAN
BLOCK = 16
WINDOW = 2 * BLOCK
GROUP = 4
PAIR = 2
WIDE = BLOCK
LATE = 46
SHIFT = BLOCK // 2
VMEM_LIMIT = 48 * 1024 * 1024
BF16 = jnp.bfloat16
F32 = jnp.float32


def vmem():
    return pl.BlockSpec(memory_space=pltpu.VMEM)


def smem():
    return pl.BlockSpec(memory_space=pltpu.SMEM)


def hbm():
    return pl.BlockSpec(memory_space=pltpu.HBM)


def in_hbm(x):
    return pltpu.with_memory_space_constraint(x, pltpu.HBM)


def by_row(count):
    total = count * BLOCK
    out_row = lax.broadcasted_iota(jnp.int32, (total, total), 0)
    in_row = lax.broadcasted_iota(jnp.int32, (total, total), 1)
    source = (out_row % BLOCK) * count + out_row // BLOCK
    return (in_row == source).astype(F32).astype(BF16)


def toeplitz(rows_tab, order):
    moved = jnp.concatenate(
        [rows_tab if jj == 0 else pltpu.roll(rows_tab, jj, 1) for jj in range(BLOCK)], axis=0
    ).astype(BF16)
    return jnp.dot(order, moved, preferred_element_type=F32).astype(BF16)


def band_rows(refs, slots, rows):
    sup_ref, count_ref, reach_ref, psi_ref = refs
    lat_rows, sup, basis, offsets = psi_ref.shape
    lanes = slots.shape[3]
    slots[...] = jnp.zeros_like(slots)
    for n, i in enumerate(rows):
        row = lax.axis_index("lat") * lat_rows + i
        values = [psi_ref[i, s] for s in range(sup)]
        places = [jnp.where(s < count_ref[i], sup_ref[i, s] - row, -lat_rows) for s in range(sup)]
        for rel in range(2 * SPAN + 1):
            total = jnp.zeros((basis, offsets), F32)
            for value, at in zip(values, places):
                total = total + jnp.where(at == rel - SPAN, value, 0.0)
            slots[n, rel, :, 0:offsets] = total
    off = lax.broadcasted_iota(jnp.int32, (basis, lanes), 1) % WINDOW - offsets // 2
    bands = []
    for n, i in enumerate(rows):
        band = slots[n, 0]
        for rel in range(1, 2 * SPAN + 1):
            band = band + pltpu.roll(slots[n, rel], rel * WINDOW, 1)
        bands.append(jnp.where(jnp.abs(off) <= reach_ref[i], band, 0.0))
    return bands


def put_pair(scr, bands):
    for m, band in enumerate(bands):
        basis = band.shape[0]
        scr[m * basis : (m + 1) * basis, :] = (
            band if m == 0 else pltpu.roll(band, m * WINDOW, 1)
        )


def turn(ref, lon_from, lon_to, wide_scr):
    _, lat_rows, width = ref.shape
    wide_scr[lon_from * lat_rows : lon_to * lat_rows, :] = (
        ref[lon_from:lon_to].astype(F32).reshape((lon_to - lon_from) * lat_rows, width)
    )


def turned_row(wide_scr, lat_rows, row, start, count):
    return wide_scr[pl.ds(start * lat_rows + row, count, stride=lat_rows), :].astype(BF16)


def own_kernel(sides, half, *refs):
    sources, outs, refs = refs[:6], refs[6:11], refs[11:]
    part_ref, edge_ref, rows_ref, bands_ref, weights_ref = outs
    smems, (psi_ref, state_ref, slots, pairs_scr, wide_scr, sems) = refs[:3], refs[3:]
    copies = [
        pltpu.make_async_copy(source, dest, sems.at[n])
        for n, (source, dest) in enumerate(
            zip(sources, (*smems, psi_ref, state_ref, weights_ref))
        )
    ]
    for copy in copies:
        copy.start()
    cols, lat_rows, width = state_ref.shape
    part = part_ref.shape[1]
    chan = lax.axis_index("chan")
    lat = lax.axis_index("lat")
    wide_scr[cols * lat_rows :, :] = jnp.zeros(
        (wide_scr.shape[0] - cols * lat_rows, width), F32
    )
    for copy in copies[:4]:
        copy.wait()
    bands = band_rows((*smems, psi_ref), slots, range(lat_rows))
    pairs = lat_rows // PAIR
    for p in range(pairs):
        put_pair(pairs_scr.at[p], bands[p * PAIR : (p + 1) * PAIR])
    for g in range(lat_rows // GROUP):
        source = 2 * ((g + lat) % 2 if sides == 1 else g)
        first, second = pairs_scr[source], pairs_scr[source + 1]
        rows_ref[g] = jnp.concatenate([first, pltpu.roll(second, PAIR * WINDOW, 1)], axis=0)
    edges = [(pairs - 1) * (1 - lat)] if sides == 1 else [pairs - 1, 0]
    for n in range(sides):
        bands_ref[n] = pairs_scr[edges[n]].astype(BF16)
    copies[4].wait()
    turn(state_ref, 0, cols, wide_scr)
    for r in range(lat_rows):
        part_ref[r] = turned_row(wide_scr, lat_rows, r, (half - WIDE) * chan, part)
        edge_ref[r] = turned_row(wide_scr, lat_rows, r, (cols - WIDE) * chan, WIDE)
    copies[5].wait()


def edges_kernel(
    sides, half, part_ref, edge_ref, other_ref, bands_ref, fields_ref, lon_ref, *rest
):
    lat_refs, corner_refs, (wide_scr,) = rest[:sides], rest[sides : 2 * sides], rest[2 * sides :]
    cols, lat_rows, width = other_ref.shape
    lon_total = fields_ref.shape[1]
    part = part_ref.shape[1]
    chan = lax.axis_index("chan")
    wide_scr[cols * lat_rows :, :] = jnp.zeros(
        (wide_scr.shape[0] - cols * lat_rows, width), F32
    )

    def build(core):
        start = 0 if core == 0 else half - WIDE
        edge = 0 if core == 0 else cols - WIDE
        stop = start + part if core == 0 else cols
        at = WIDE if core == 0 else 0
        own = slice(core * width, (core + 1) * width)
        lane = slice((1 - core) * width, (2 - core) * width)
        turn(other_ref, start, stop, wide_scr)
        for r in range(lat_rows):
            lon_ref[r, :, own] = edge_ref[r]
            lon_ref[r, :, lane] = turned_row(wide_scr, lat_rows, r, edge, WIDE)
            fields_ref[r, at : at + part, own] = part_ref[r]
            fields_ref[r, at : at + part, lane] = turned_row(wide_scr, lat_rows, r, start, part)
        empty = slice(0, WIDE) if core == 0 else slice(part, lon_total)
        fields_ref[:, empty, :] = jnp.zeros((lat_rows, WIDE, 2 * width), BF16)

    @pl.when(chan == 0)
    def _():
        build(0)

    @pl.when(chan == 1)
    def _():
        build(1)

    at = pl.multiple_of((1 - chan) * WIDE, WIDE)
    for n, first in enumerate(needed_rows(sides, lat_rows)):
        for t in range(HALO):
            lat_refs[n][t * part : (t + 1) * part, :] = fields_ref[first + t, pl.ds(at, part), :]
            corner_refs[n][t] = lon_ref[first + t]
        lat_refs[n][HALO * part :, :] = bands_ref[n]


def needed_rows(sides, lat_rows):
    if sides == 1:
        return [(1 - lax.axis_index("lat")) * (lat_rows - HALO)]
    return [lat_rows - HALO, 0]


def tables_kernel(rows_ref, _, tables_ref, order_ref):
    groups, rows, _ = rows_ref.shape
    order = by_row(rows)
    for g in range(groups):
        tables_ref[g] = toeplitz(rows_ref[g], order)
    order_ref[...] = by_row(order_ref.shape[0] // BLOCK)


def gelu(x):
    return 0.5 * x * (1.0 + jnp.tanh(0.7978845608028654 * (x + 0.044715 * (x * x * x))))


def add_lat_halo(rows, lat_ref, part, core):
    at = WIDE if core == 0 else 0
    for t, row in enumerate(rows):
        row[at : at + part, :] = lat_ref[t * part : (t + 1) * part, :]


def halo_table(lat_ref, order):
    count = order.shape[0] // BLOCK
    return toeplitz(lat_ref[lat_ref.shape[0] - count :, :].astype(F32), order)


def add_lon_halo(cols, half, rows, halos, core):
    count = cols - half + WIDE
    whole = count // BLOCK * BLOCK
    for row, halo in zip(rows, halos):
        if core == 0:
            row[0:WIDE, :] = halo[...]
            continue
        lon_total, chans = row.shape
        before = row[whole : whole + BLOCK, :].astype(F32)[0 : count - whole, :]
        empty = jnp.zeros((lon_total - count - WIDE, chans), F32)
        row[whole:lon_total, :] = jnp.concatenate(
            [before, halo[...].astype(F32), empty], axis=0
        ).astype(BF16)


def conv(source, table, base, in_rows, feats, first, out_rows, jb, put):
    chans = source.shape[2]
    basis = table.shape[0] // (out_rows * BLOCK)
    taken = source[pl.ds(base, in_rows), jb * BLOCK : jb * BLOCK + WINDOW, :]
    taken = taken.reshape(in_rows * WINDOW, chans)
    result = jnp.dot(table, taken, preferred_element_type=F32).astype(BF16)
    at = slice(put * BLOCK, (put + 1) * BLOCK)
    for m in range(out_rows):
        for k in range(basis):
            begin = (m * basis + k) * BLOCK
            feats[first + m, at, k * chans : (k + 1) * chans] = result[begin : begin + BLOCK, :]


def mix(weights_ref, layer, feats, row, blocks, befores, store):
    _, basis, chans, _ = weights_ref.shape
    count, lons = len(befores), len(blocks) * BLOCK
    mixed = jnp.dot(
        feats[row : row + count, 0:lons, :].reshape(count * lons, basis * chans),
        weights_ref[layer].reshape(basis * chans, chans),
        preferred_element_type=F32,
    )
    for n, before in enumerate(befores):
        before = before[...].astype(F32)
        for put, jb in enumerate(blocks):
            at, begin = SHIFT + jb * BLOCK, n * lons + put * BLOCK
            value = before[at : at + BLOCK, :] + gelu(mixed[begin : begin + BLOCK, :])
            store(n, jb, value)


def into(ref, rows):
    def store(n, jb, value):
        ref[rows[n], jb * BLOCK : (jb + 1) * BLOCK, :] = value.astype(BF16)

    return store


def into_turned(turned, rows, lat_rows):
    def store(n, jb, value):
        width = value.shape[1] // 2
        for c in range(2):
            turned[c, pl.ds(jb * BLOCK * lat_rows + rows[n], BLOCK, stride=lat_rows), :] = value[
                :, c * width : (c + 1) * width
            ]

    return store


def hand_out(turned, keep_ref, send_ref, core, start):
    count, lat_rows, width = keep_ref.shape
    at = slice(start * lat_rows, (start + count) * lat_rows)
    for ref, which in ((keep_ref, core), (send_ref, 1 - core)):
        ref[...] = turned[which, at, :].reshape(count, lat_rows, width).astype(BF16)


def late_blocks(core, count):
    return [0] if core == 0 else [count - 2, count - 1]


def early_blocks(core, count):
    late = late_blocks(core, count)
    return [jb for jb in range(count) if jb not in late]


def late_start(core, half):
    return 0 if core == 0 else half - LATE


def early_start(core):
    return LATE if core == 0 else 0


def for_each_core(body):
    for value in range(2):
        pl.when(lax.axis_index("chan") == value)(functools.partial(body, value))


def for_each_lat(body):
    for value in range(2):
        pl.when(lax.axis_index("lat") == value)(functools.partial(body, value))


def half_table(tables_ref, second):
    rows = tables_ref.shape[1] // 2
    return tables_ref[1, rows * second : rows * (second + 1), :]


def far_rows(
    lat, fields, after, tables_ref, weights_ref, feats, turned, blocks1, blocks2, parts
):
    lat_rows = after.shape[0]
    far = GROUP * lat
    near = GROUP - far
    mid = GROUP - PAIR * lat
    rows8 = GROUP + 2 * SPAN
    for put, jb in enumerate(blocks1):
        conv(fields, tables_ref[0], far, rows8, feats, 0, GROUP, jb, put)
        conv(fields, half_table(tables_ref, lat), near, rows8, feats, GROUP, PAIR, jb, put)
    dests = [SPAN + t for t in range(GROUP)]
    dests += [(GROUP + SPAN) * (1 - lat) + t for t in range(PAIR)]
    befores = [SPAN + far + t for t in range(GROUP)] + [SPAN + mid + t for t in range(PAIR)]
    step = len(dests) // parts
    for t in range(0, len(dests), step):
        rows = [fields.at[r] for r in befores[t : t + step]]
        mix(weights_ref, 0, feats, t, blocks1, rows, into(after, dests[t : t + step]))
    for put, jb in enumerate(blocks2):
        conv(after, tables_ref[0], 0, rows8, feats, 0, GROUP, jb, put)
    step = GROUP // parts
    for t in range(0, GROUP, step):
        befores = [after.at[SPAN + t + m] for m in range(step)]
        rows = [far + t + m for m in range(step)]
        mix(weights_ref, 1, feats, t, blocks2, befores, into_turned(turned, rows, lat_rows))


def far1_kernel(
    half, own_ref, tables_ref, weights_ref, fields_ref, after_ref, turned_ref, feats
):
    lat_rows, lon_total, chans = own_ref.shape
    for t in range(SPAN):
        fields_ref[t] = jnp.zeros((lon_total, chans), BF16)
        fields_ref[SPAN + lat_rows + t] = jnp.zeros((lon_total, chans), BF16)
    fields_ref[SPAN : SPAN + lat_rows] = own_ref[...]

    def body(lat, core):
        for t in range(SPAN):
            after_ref[(GROUP + SPAN) * lat + t] = jnp.zeros((lon_total - BLOCK, chans), BF16)
        far_rows(
            lat,
            fields_ref,
            after_ref,
            tables_ref,
            weights_ref,
            feats,
            turned_ref,
            early_blocks(core, lon_total // BLOCK - 1),
            early_blocks(core, half // BLOCK),
            2,
        )

    for_each_core(lambda core: for_each_lat(functools.partial(body, core=core)))


def far2_kernel(
    half,
    cols,
    lon_ref,
    tables_ref,
    weights_ref,
    fields_in,
    after_in,
    turned_in,
    fields_ref,
    after_ref,
    turned_ref,
    feats,
):
    lat_rows = lon_ref.shape[0]

    def body(lat, core):
        add_lon_halo(
            cols,
            half,
            [fields_ref.at[SPAN + r] for r in range(lat_rows)],
            [lon_ref.at[r] for r in range(lat_rows)],
            core,
        )
        far_rows(
            lat,
            fields_ref,
            after_ref,
            tables_ref,
            weights_ref,
            feats,
            turned_ref,
            late_blocks(core, fields_ref.shape[1] // BLOCK - 1),
            late_blocks(core, half // BLOCK),
            1,
        )

    for_each_core(lambda core: for_each_lat(functools.partial(body, core=core)))


def near_rows(
    lat, fields, near, table, tables_ref, weights_ref, feats, turned, blocks1, blocks2, parts
):
    lat_rows = near.shape[0]
    rows6, rows8 = PAIR + 2 * SPAN, GROUP + 2 * SPAN
    group = SPAN * lat
    beyond = HALO * (1 - lat)
    for put, jb in enumerate(blocks1):
        conv(fields, half_table(tables_ref, 1 - lat), group, rows8, feats, 0, PAIR, jb, put)
    for put, jb in enumerate(blocks1):
        conv(fields, table[:, 0 : rows6 * WINDOW], beyond, rows6, feats, PAIR, PAIR, jb, put)
    befores = [fields.at[HALO + m] for m in range(PAIR)]
    befores += [fields.at[beyond + SPAN + m] for m in range(PAIR)]
    dests = [GROUP * (1 - lat) + SPAN * lat + m for m in range(PAIR)]
    dests += [(GROUP + SPAN) * (1 - lat) + m for m in range(PAIR)]
    step = GROUP // parts
    for t in range(0, GROUP, step):
        rows = slice(t, t + step)
        mix(weights_ref, 0, feats, t, blocks1, befores[rows], into(near, dests[rows]))
    for put, jb in enumerate(blocks2):
        conv(near, tables_ref[1], 0, GROUP + 2 * SPAN, feats, 0, GROUP, jb, put)
    for t in range(0, GROUP, step):
        befores = [near.at[SPAN + t + m] for m in range(step)]
        rows = [GROUP * (1 - lat) + t + m for m in range(step)]
        mix(weights_ref, 1, feats, t, blocks2, befores, into_turned(turned, rows, lat_rows))


def near1_kernel(
    half,
    ext_ref,
    next_ref,
    lat_ref,
    tables_ref,
    weights_ref,
    order_ref,
    turned_in,
    fields_ref,
    near_ref,
    table_ref,
    turned_ref,
    keep_ref,
    send_ref,
    feats,
):
    lon_total = ext_ref.shape[1]

    def body(lat, core):
        halo = (HALO + SPAN) * (1 - lat)
        own = HALO * lat
        for t in range(HALO + SPAN):
            fields_ref[own + t] = ext_ref[SPAN + SPAN * (1 - lat) + t]
        add_lat_halo([fields_ref.at[halo + t] for t in range(HALO)], lat_ref, half + WIDE, core)
        table = halo_table(lat_ref, order_ref[...])
        table_ref[...] = table
        for t in range(GROUP):
            near_ref[GROUP * lat + t] = next_ref[GROUP * (1 - lat) + t]
        near_rows(
            lat,
            fields_ref,
            near_ref,
            table,
            tables_ref,
            weights_ref,
            feats,
            turned_ref,
            early_blocks(core, lon_total // BLOCK - 1),
            early_blocks(core, half // BLOCK),
            2,
        )
        hand_out(turned_ref, keep_ref, send_ref, core, early_start(core))

    for_each_core(lambda core: for_each_lat(functools.partial(body, core=core)))


def near2_kernel(
    half,
    cols,
    corner_ref,
    table_ref,
    tables_ref,
    weights_ref,
    fields_in,
    near_in,
    turned_in,
    fields_ref,
    near_ref,
    turned_ref,
    keep_ref,
    send_ref,
    feats,
):
    def body(lat, core):
        halo = (HALO + SPAN) * (1 - lat)
        add_lon_halo(
            cols,
            half,
            [fields_ref.at[halo + t] for t in range(HALO)],
            [corner_ref.at[t] for t in range(HALO)],
            core,
        )
        near_rows(
            lat,
            fields_ref,
            near_ref,
            table_ref[...],
            tables_ref,
            weights_ref,
            feats,
            turned_ref,
            late_blocks(core, fields_ref.shape[1] // BLOCK - 1),
            late_blocks(core, half // BLOCK),
            1,
        )
        hand_out(turned_ref, keep_ref, send_ref, core, late_start(core, half))

    for_each_core(lambda core: for_each_lat(functools.partial(body, core=core)))


def all_kernel(half, cols, own_ref, lon_ref, *rest):
    lat_refs, corner_refs = rest[:2], rest[2:4]
    (tables_ref, weights_ref, order_ref), rest = rest[4:7], rest[7:]
    (late_keep_ref, late_send_ref, keep_ref, send_ref), rest = rest[:4], rest[4:]
    fields, feats, after, turned = rest
    lat_rows, lon_total, chans = own_ref.shape
    groups = lat_rows // GROUP
    lon1 = lon_total - BLOCK
    halo_base = [0, lat_rows + HALO]
    win_base = [0, lat_rows + HALO - SPAN]
    out_base = [0, lat_rows + SPAN]
    rows6 = PAIR + 2 * SPAN

    fields[HALO : HALO + lat_rows] = own_ref[...]

    @for_each_core
    def _(core):
        rows = [fields.at[HALO + r] for r in range(lat_rows)]
        halos = [lon_ref.at[r] for r in range(lat_rows)]
        for n in range(2):
            halo_rows = [fields.at[halo_base[n] + t] for t in range(HALO)]
            add_lat_halo(halo_rows, lat_refs[n], half + WIDE, core)
            rows += halo_rows
            halos += [corner_refs[n].at[t] for t in range(HALO)]
        add_lon_halo(cols, half, rows, halos, core)

    halo_tables = [
        halo_table(lat_refs[n], order_ref[...])[:, 0 : rows6 * WINDOW] for n in range(2)
    ]
    blocks = range(lon1 // BLOCK)
    for jb in blocks:
        for g in range(groups):
            base = HALO - SPAN + g * GROUP
            conv(
                fields, tables_ref[g], base, GROUP + 2 * SPAN, feats, g * GROUP, GROUP, jb, jb
            )
        for n in range(2):
            first = lat_rows + n * PAIR
            conv(fields, halo_tables[n], win_base[n], rows6, feats, first, PAIR, jb, jb)
    dests = [SPAN + i for i in range(lat_rows)]
    dests += [out_base[n] + m for n in range(2) for m in range(PAIR)]
    for i in range(0, len(dests), PAIR):
        befores = [fields.at[dest + SPAN] for dest in dests[i : i + PAIR]]
        mix(weights_ref, 0, feats, i, blocks, befores, into(after, dests[i : i + PAIR]))
    blocks = range(half // BLOCK)
    for jb in blocks:
        for g in range(groups):
            base = g * GROUP
            conv(after, tables_ref[g], base, GROUP + 2 * SPAN, feats, base, GROUP, jb, jb)
    for i in range(0, lat_rows, PAIR):
        befores = [after.at[SPAN + i + m] for m in range(PAIR)]
        rows = [i + m for m in range(PAIR)]
        mix(weights_ref, 1, feats, i, blocks, befores, into_turned(turned, rows, lat_rows))

    @for_each_core
    def _(core):
        hand_out(turned, late_keep_ref, late_send_ref, core, late_start(core, half))
        hand_out(turned, keep_ref, send_ref, core, early_start(core))


def write(copies, sems):
    copies = [
        pltpu.make_async_copy(source, dest, sems.at[n])
        for n, (source, dest) in enumerate(copies)
    ]
    for copy in copies:
        copy.start()
    for copy in copies:
        copy.wait()


def early_kernel(half, keep_ref, got_ref, out_hbm, sems):
    @for_each_core
    def _(core):
        copies = []
        for which, ref in ((core, keep_ref), (1 - core, got_ref)):
            at = which * half + early_start(which)
            copies.append((ref, out_hbm.at[at : at + ref.shape[0]]))
        write(copies, sems)


def late_kernel(half, keep_ref, got_ref, out_in, out_hbm, sems):
    cols = out_hbm.shape[0]

    @for_each_core
    def _(core):
        copies = []
        for which, ref in ((core, keep_ref), (1 - core, got_ref)):
            at = which * half + late_start(which, half)
            count = min(LATE, cols - at)
            copies.append((ref.at[0:count], out_hbm.at[at : at + count]))
        write(copies, sems)


def per_device(state, sup_rows, sup_count, lon_reach, psi, weights):
    lat_rows, cols, width = state.shape
    basis = psi.shape[2]
    chans = weights.shape[2]
    lats, lons = lax.axis_size("lat"), lax.axis_size("lon")
    sides = 1 if lats == 2 else 2
    groups = lat_rows // GROUP
    lanes = (GROUP + 2 * SPAN) * WINDOW
    half = -(-cols // (2 * BLOCK)) * BLOCK
    part = half + WIDE
    lon_total = half + 2 * WIDE
    lon1 = lon_total - BLOCK
    swap = [(0, 1), (1, 0)]
    params = pltpu.CompilerParams(vmem_limit_bytes=VMEM_LIMIT)

    def shape(*dims):
        return jax.ShapeDtypeStruct(dims, BF16)

    def to_lat(step):
        if lats == 2:
            return [(a, 1 - a) for a in range(lats)]
        return [(a, a + step) for a in range(lats) if 0 <= a + step < lats]

    forth = [((z, 1), ((z + 1) % lons, 0)) for z in range(lons)]
    back = [((z, 0), ((z - 1) % lons, 1)) for z in range(lons)]
    to_lon = forth + back

    own = jnp.transpose(state, (1, 0, 2))
    other = lax.ppermute(own, "chan", swap)

    def scratch(*dims):
        return pltpu.VMEM(dims, F32)

    wide = scratch((half + part) * lat_rows, width)
    smalls = [sup_rows, sup_count, lon_reach]
    part_own, edge_own, rows, bands, weights_in = pl.pallas_call(
        functools.partial(own_kernel, sides, half),
        out_shape=[
            shape(lat_rows, part, width),
            shape(lat_rows, WIDE, width),
            jax.ShapeDtypeStruct((groups, GROUP * basis, lanes), F32),
            shape(sides, PAIR * basis, lanes),
            shape(*weights.shape),
        ],
        in_specs=[hbm()] * 6,
        out_specs=[vmem()] * 5,
        scratch_shapes=[pltpu.SMEM(x.shape, x.dtype) for x in smalls]
        + [
            scratch(*psi.shape),
            pltpu.VMEM(own.shape, BF16),
            scratch(lat_rows, 2 * SPAN + 1, basis, lanes),
            scratch(lat_rows // PAIR, PAIR * basis, lanes),
            wide,
            pltpu.SemaphoreType.DMA((6,)),
        ],
        compiler_params=params,
        name="own",
    )(*[in_hbm(x) for x in smalls + [psi, own, weights]])

    fields, lon_edge, *sends = pl.pallas_call(
        functools.partial(edges_kernel, sides, half),
        out_shape=[shape(lat_rows, lon_total, chans), shape(lat_rows, WIDE, chans)]
        + [shape(HALO * part + PAIR * basis, chans)] * sides
        + [shape(HALO, WIDE, chans)] * sides,
        in_specs=[vmem()] * 4,
        out_specs=[vmem()] * (2 + 2 * sides),
        scratch_shapes=[wide],
        compiler_params=params,
        name="edges",
    )(part_own, edge_own, other, bands)

    steps = [1, -1][:sides]
    lat_halos = [lax.ppermute(x, "lat", to_lat(step)) for x, step in zip(sends, steps)]
    lon_halo = lax.ppermute(
        lon_edge, ("lon", "chan"), [(z * 2 + c, y * 2 + d) for (z, c), (y, d) in to_lon]
    )

    corners = [
        lax.ppermute(
            x,
            ("lon", "lat", "chan"),
            [
                ((z * lats + a) * 2 + c, (y * lats + b) * 2 + d)
                for a, b in to_lat(step)
                for (z, c), (y, d) in to_lon
            ],
        )
        for x, step in zip(sends[sides:], steps)
    ]

    tables, order = pl.pallas_call(
        tables_kernel,
        out_shape=[
            shape(groups, GROUP * basis * BLOCK, lanes),
            shape(PAIR * basis * BLOCK, PAIR * basis * BLOCK),
        ],
        in_specs=[vmem()] * 2,
        out_specs=[vmem()] * 2,
        compiler_params=params,
        name="tables",
    )(rows, lon_edge)

    late_shapes = [shape(LATE, lat_rows, width)] * 2
    early_shapes = [shape(half - LATE, lat_rows, width)] * 2
    turned = (2, half * lat_rows, width)
    if sides == 1:
        far_shapes = [
            shape(lat_rows + 2 * SPAN, lon_total, chans),
            shape(lat_rows, lon1, chans),
            jax.ShapeDtypeStruct(turned, F32),
        ]
        far_feats = pltpu.VMEM((GROUP + PAIR, lon1, basis * chans), BF16)
        far = pl.pallas_call(
            functools.partial(far1_kernel, half),
            out_shape=far_shapes,
            in_specs=[vmem()] * 3,
            out_specs=[vmem()] * 3,
            scratch_shapes=[far_feats],
            compiler_params=params,
            name="far_rows_1",
        )(fields, tables, weights_in)
        ext, after, done = pl.pallas_call(
            functools.partial(far2_kernel, half, cols),
            out_shape=far_shapes,
            in_specs=[vmem()] * 6,
            out_specs=[vmem()] * 3,
            scratch_shapes=[far_feats],
            input_output_aliases={3: 0, 4: 1, 5: 2},
            compiler_params=params,
            name="far_rows_2",
        )(lon_halo, tables, weights_in, *far)
        near_shapes = [shape(2 * HALO + SPAN, lon_total, chans), shape(GROUP + 2 * SPAN, lon1, chans)]
        near_feats = pltpu.VMEM((GROUP, lon1, basis * chans), BF16)
        ext, near, halo_tab, done, keep, send = pl.pallas_call(
            functools.partial(near1_kernel, half),
            out_shape=near_shapes
            + [shape(PAIR * basis * BLOCK, lanes), jax.ShapeDtypeStruct(turned, F32)]
            + early_shapes,
            in_specs=[vmem()] * 7,
            out_specs=[vmem()] * 6,
            scratch_shapes=[near_feats],
            input_output_aliases={6: 3},
            compiler_params=params,
            name="near_rows_1",
        )(ext, after, lat_halos[0], tables, weights_in, order, done)
        *_, late_keep, late_send = pl.pallas_call(
            functools.partial(near2_kernel, half, cols),
            out_shape=near_shapes + [jax.ShapeDtypeStruct(turned, F32)] + late_shapes,
            in_specs=[vmem()] * 7,
            out_specs=[vmem()] * 5,
            scratch_shapes=[near_feats],
            input_output_aliases={4: 0, 5: 1, 6: 2},
            compiler_params=params,
            name="near_rows_2",
        )(corners[0], halo_tab, tables, weights_in, ext, near, done)
    else:
        late_keep, late_send, keep, send = pl.pallas_call(
            functools.partial(all_kernel, half, cols),
            out_shape=late_shapes + early_shapes,
            in_specs=[vmem()] * (5 + 2 * sides),
            out_specs=[vmem()] * 4,
            scratch_shapes=[
                pltpu.VMEM((lat_rows + 2 * HALO, lon_total, chans), BF16),
                pltpu.VMEM((lat_rows + 2 * PAIR, lon1, basis * chans), BF16),
                pltpu.VMEM((lat_rows + 2 * SPAN, lon1, chans), BF16),
                scratch(*turned),
            ],
            compiler_params=params,
            name="all_rows",
        )(fields, lon_halo, *lat_halos, *corners, tables, weights_in, order)
    got = lax.ppermute(send, "chan", swap)
    late_got = lax.ppermute(late_send, "chan", swap)

    out_type = shape(cols, lat_rows, width)
    out = pl.pallas_call(
        functools.partial(early_kernel, half),
        out_shape=out_type,
        in_specs=[vmem()] * 2,
        out_specs=hbm(),
        scratch_shapes=[pltpu.SemaphoreType.DMA((2,))],
        compiler_params=params,
        name="write_early",
    )(keep, got)
    out = pl.pallas_call(
        functools.partial(late_kernel, half),
        out_shape=out_type,
        in_specs=[vmem()] * 2 + [hbm()],
        out_specs=hbm(),
        scratch_shapes=[pltpu.SemaphoreType.DMA((2,))],
        input_output_aliases={2: 0},
        compiler_params=params,
        name="write_late",
    )(late_keep, late_got, out)
    return jnp.transpose(out, (1, 0, 2))


def solution(mesh):
    return jax.shard_map(
        per_device,
        mesh=mesh,
        in_specs=(
            P(("groups", "lat"), "lon", "chan"),
            P("lat", None),
            P("lat"),
            P("lat"),
            P("lat", None, None, None),
            P(),
        ),
        out_specs=P(("groups", "lat"), "lon", "chan"),
        check_vma=False,
    )
```

```python
import functools

import jax
import jax.numpy as jnp
from jax import lax
from jax.experimental import pallas as pl
from jax.experimental.pallas import tpu as pltpu
from jax.sharding import PartitionSpec as P

LAYERS = 2
SPAN = 2
HALO = LAYERS * SPAN
BLOCK = 16
WINDOW = 2 * BLOCK
GROUP = 4
PAIR = 2
WIDE = BLOCK
LATE = 46
SHIFT = BLOCK // 2
VMEM_LIMIT = 48 * 1024 * 1024
BF16 = jnp.bfloat16
F32 = jnp.float32


def vmem():
    return pl.BlockSpec(memory_space=pltpu.VMEM)


def smem():
    return pl.BlockSpec(memory_space=pltpu.SMEM)


def hbm():
    return pl.BlockSpec(memory_space=pltpu.HBM)


def in_hbm(x):
    return pltpu.with_memory_space_constraint(x, pltpu.HBM)


def by_row(count):
    total = count * BLOCK
    out_row = lax.broadcasted_iota(jnp.int32, (total, total), 0)
    in_row = lax.broadcasted_iota(jnp.int32, (total, total), 1)
    source = (out_row % BLOCK) * count + out_row // BLOCK
    return (in_row == source).astype(F32).astype(BF16)


def toeplitz(rows_tab, order):
    moved = jnp.concatenate(
        [rows_tab if jj == 0 else pltpu.roll(rows_tab, jj, 1) for jj in range(BLOCK)], axis=0
    ).astype(BF16)
    return jnp.dot(order, moved, preferred_element_type=F32).astype(BF16)


def band_rows(refs, slots, rows):
    sup_ref, count_ref, reach_ref, psi_ref = refs
    lat_rows, sup, basis, offsets = psi_ref.shape
    lanes = slots.shape[3]
    slots[...] = jnp.zeros_like(slots)
    for n, i in enumerate(rows):
        row = lax.axis_index("lat") * lat_rows + i
        values = [psi_ref[i, s] for s in range(sup)]
        places = [jnp.where(s < count_ref[i], sup_ref[i, s] - row, -lat_rows) for s in range(sup)]
        for rel in range(2 * SPAN + 1):
            total = jnp.zeros((basis, offsets), F32)
            for value, at in zip(values, places):
                total = total + jnp.where(at == rel - SPAN, value, 0.0)
            slots[n, rel, :, 0:offsets] = total
    off = lax.broadcasted_iota(jnp.int32, (basis, lanes), 1) % WINDOW - offsets // 2
    bands = []
    for n, i in enumerate(rows):
        band = slots[n, 0]
        for rel in range(1, 2 * SPAN + 1):
            band = band + pltpu.roll(slots[n, rel], rel * WINDOW, 1)
        bands.append(jnp.where(jnp.abs(off) <= reach_ref[i], band, 0.0))
    return bands


def put_pair(scr, bands):
    for m, band in enumerate(bands):
        basis = band.shape[0]
        scr[m * basis : (m + 1) * basis, :] = (
            band if m == 0 else pltpu.roll(band, m * WINDOW, 1)
        )


def turn(ref, lon_from, lon_to, wide_scr):
    _, lat_rows, width = ref.shape
    wide_scr[lon_from * lat_rows : lon_to * lat_rows, :] = (
        ref[lon_from:lon_to].astype(F32).reshape((lon_to - lon_from) * lat_rows, width)
    )


def turned_row(wide_scr, lat_rows, row, start, count):
    return wide_scr[pl.ds(start * lat_rows + row, count, stride=lat_rows), :].astype(BF16)


def own_kernel(sides, half, *refs):
    sources, (part_ref, edge_ref, bands_ref), refs = refs[:5], refs[5:8], refs[8:]
    smems, (psi_ref, state_ref, slots, pair_scr, wide_scr, sems) = refs[:3], refs[3:]
    copies = [
        pltpu.make_async_copy(source, dest, sems.at[n])
        for n, (source, dest) in enumerate(zip(sources, (*smems, psi_ref, state_ref)))
    ]
    for copy in copies:
        copy.start()
    cols, lat_rows, width = state_ref.shape
    part = part_ref.shape[1]
    wide_scr[cols * lat_rows :, :] = jnp.zeros(
        (wide_scr.shape[0] - cols * lat_rows, width), F32
    )
    for copy in copies[:4]:
        copy.wait()
    firsts = [first + (HALO - PAIR) * (n == 0) for n, first in enumerate(needed_rows(2, lat_rows))]
    if sides == 1:
        firsts = [(1 - lax.axis_index("lat")) * (lat_rows - PAIR)]
    rows = [first + m for first in firsts for m in range(PAIR)]
    bands = band_rows((*smems, psi_ref), slots, rows)
    for n in range(sides):
        put_pair(pair_scr, bands[n * PAIR : (n + 1) * PAIR])
        bands_ref[n] = pair_scr[...].astype(BF16)
    copies[4].wait()

    @for_each_core
    def _(core):
        start = 0 if core == 0 else half - WIDE
        edge = 0 if core == 0 else cols - WIDE
        turn(state_ref, start, min(start + part, cols), wide_scr)
        for r in range(lat_rows):
            part_ref[r] = turned_row(wide_scr, lat_rows, r, start, part)
            edge_ref[r] = turned_row(wide_scr, lat_rows, r, edge, WIDE)


def edges_kernel(
    sides, half, part_ref, edge_ref, other_ref, bands_ref, fields_ref, lon_ref, *rest
):
    lat_refs, corner_refs, (wide_scr,) = rest[:sides], rest[sides : 2 * sides], rest[2 * sides :]
    cols, lat_rows, width = other_ref.shape
    lon_total = fields_ref.shape[1]
    part = part_ref.shape[1]
    chan = lax.axis_index("chan")
    wide_scr[cols * lat_rows :, :] = jnp.zeros(
        (wide_scr.shape[0] - cols * lat_rows, width), F32
    )

    def build(core):
        start = 0 if core == 0 else half - WIDE
        edge = 0 if core == 0 else cols - WIDE
        stop = start + part if core == 0 else cols
        at = WIDE if core == 0 else 0
        own = slice(core * width, (core + 1) * width)
        lane = slice((1 - core) * width, (2 - core) * width)
        turn(other_ref, start, stop, wide_scr)
        for r in range(lat_rows):
            lon_ref[r, :, own] = edge_ref[r]
            lon_ref[r, :, lane] = turned_row(wide_scr, lat_rows, r, edge, WIDE)
            fields_ref[r, at : at + part, own] = part_ref[r]
            fields_ref[r, at : at + part, lane] = turned_row(wide_scr, lat_rows, r, start, part)
        empty = slice(0, WIDE) if core == 0 else slice(part, lon_total)
        fields_ref[:, empty, :] = jnp.zeros((lat_rows, WIDE, 2 * width), BF16)

    @pl.when(chan == 0)
    def _():
        build(0)

    @pl.when(chan == 1)
    def _():
        build(1)

    at = pl.multiple_of((1 - chan) * WIDE, WIDE)
    for n, first in enumerate(needed_rows(sides, lat_rows)):
        for t in range(HALO):
            lat_refs[n][t * part : (t + 1) * part, :] = fields_ref[first + t, pl.ds(at, part), :]
            corner_refs[n][t] = lon_ref[first + t]
        lat_refs[n][HALO * part :, :] = bands_ref[n]


def needed_rows(sides, lat_rows):
    if sides == 1:
        return [(1 - lax.axis_index("lat")) * (lat_rows - HALO)]
    return [lat_rows - HALO, 0]


def tables_kernel(sides, sup_hbm, count_hbm, reach_hbm, psi_hbm, weights_hbm, _, *refs):
    (weights_ref, tables_ref, order_ref), refs = refs[:3], refs[3:]
    smems, (psi_ref, slots, pairs_scr, sems) = refs[:3], refs[3:]
    sources = (sup_hbm, count_hbm, reach_hbm, psi_hbm, weights_hbm)
    copies = [
        pltpu.make_async_copy(source, dest, sems.at[n])
        for n, (source, dest) in enumerate(zip(sources, (*smems, psi_ref, weights_ref)))
    ]
    for copy in copies:
        copy.start()
    lat_rows, _, basis, _ = psi_ref.shape
    lat = lax.axis_index("lat")
    order = by_row(GROUP * basis)
    order_ref[...] = by_row(PAIR * basis)
    for copy in copies[:4]:
        copy.wait()
    bands = band_rows((*smems, psi_ref), slots, range(lat_rows))
    for p in range(lat_rows // PAIR):
        put_pair(pairs_scr.at[p], bands[p * PAIR : (p + 1) * PAIR])

    def group(g):
        first, second = pairs_scr[2 * g], pairs_scr[2 * g + 1]
        return jnp.concatenate([first, pltpu.roll(second, PAIR * WINDOW, 1)], axis=0)

    if sides == 1:
        tables_ref[0] = toeplitz(group(lat), order)
        tables_ref[1] = toeplitz(group(1 - lat), order)
    else:
        for g in range(lat_rows // GROUP):
            tables_ref[g] = toeplitz(group(g), order)
    copies[4].wait()


def gelu(x):
    return 0.5 * x * (1.0 + jnp.tanh(0.7978845608028654 * (x + 0.044715 * (x * x * x))))


def add_lat_halo(rows, lat_ref, part, core):
    at = WIDE if core == 0 else 0
    for t, row in enumerate(rows):
        row[at : at + part, :] = lat_ref[t * part : (t + 1) * part, :]


def halo_table(lat_ref, order):
    count = order.shape[0] // BLOCK
    return toeplitz(lat_ref[lat_ref.shape[0] - count :, :].astype(F32), order)


def add_lon_halo(cols, half, rows, halos, core):
    count = cols - half + WIDE
    whole = count // BLOCK * BLOCK
    for row, halo in zip(rows, halos):
        if core == 0:
            row[0:WIDE, :] = halo[...]
            continue
        lon_total, chans = row.shape
        before = row[whole : whole + BLOCK, :].astype(F32)[0 : count - whole, :]
        empty = jnp.zeros((lon_total - count - WIDE, chans), F32)
        row[whole:lon_total, :] = jnp.concatenate(
            [before, halo[...].astype(F32), empty], axis=0
        ).astype(BF16)


def conv(source, table, base, in_rows, feats, first, out_rows, jb, put):
    chans = source.shape[2]
    basis = table.shape[0] // (out_rows * BLOCK)
    taken = source[pl.ds(base, in_rows), jb * BLOCK : jb * BLOCK + WINDOW, :]
    taken = taken.reshape(in_rows * WINDOW, chans)
    result = jnp.dot(table, taken, preferred_element_type=F32).astype(BF16)
    at = slice(put * BLOCK, (put + 1) * BLOCK)
    for m in range(out_rows):
        for k in range(basis):
            begin = (m * basis + k) * BLOCK
            feats[first + m, at, k * chans : (k + 1) * chans] = result[begin : begin + BLOCK, :]


def mix(weights_ref, layer, feats, row, blocks, befores, store):
    _, basis, chans, _ = weights_ref.shape
    count, lons = len(befores), len(blocks) * BLOCK
    mixed = jnp.dot(
        feats[row : row + count, 0:lons, :].reshape(count * lons, basis * chans),
        weights_ref[layer].reshape(basis * chans, chans),
        preferred_element_type=F32,
    )
    for n, before in enumerate(befores):
        before = before[...].astype(F32)
        for put, jb in enumerate(blocks):
            at, begin = SHIFT + jb * BLOCK, n * lons + put * BLOCK
            value = before[at : at + BLOCK, :] + gelu(mixed[begin : begin + BLOCK, :])
            store(n, jb, value)


def into(ref, rows):
    def store(n, jb, value):
        ref[rows[n], jb * BLOCK : (jb + 1) * BLOCK, :] = value.astype(BF16)

    return store


def into_turned(turned, rows, lat_rows):
    def store(n, jb, value):
        width = value.shape[1] // 2
        for c in range(2):
            turned[c, pl.ds(jb * BLOCK * lat_rows + rows[n], BLOCK, stride=lat_rows), :] = value[
                :, c * width : (c + 1) * width
            ]

    return store


def hand_out(turned, keep_ref, send_ref, core, start):
    count, lat_rows, width = keep_ref.shape
    at = slice(start * lat_rows, (start + count) * lat_rows)
    for ref, which in ((keep_ref, core), (send_ref, 1 - core)):
        ref[...] = turned[which, at, :].reshape(count, lat_rows, width).astype(BF16)


def late_blocks(core, count):
    return [0] if core == 0 else [count - 2, count - 1]


def early_blocks(core, count):
    late = late_blocks(core, count)
    return [jb for jb in range(count) if jb not in late]


def late_start(core, half):
    return 0 if core == 0 else half - LATE


def early_start(core):
    return LATE if core == 0 else 0


def for_each_core(body):
    for value in range(2):
        pl.when(lax.axis_index("chan") == value)(functools.partial(body, value))


def for_each_lat(body):
    for value in range(2):
        pl.when(lax.axis_index("lat") == value)(functools.partial(body, value))


def half_table(tables_ref, second):
    rows = tables_ref.shape[1] // 2
    return tables_ref[1, rows * second : rows * (second + 1), :]


def far_rows(
    lat, fields, after, tables_ref, weights_ref, feats, turned, blocks1, blocks2, parts
):
    lat_rows = after.shape[0]
    far = GROUP * lat
    near = GROUP - far
    mid = GROUP - PAIR * lat
    rows8 = GROUP + 2 * SPAN
    for put, jb in enumerate(blocks1):
        conv(fields, tables_ref[0], far, rows8, feats, 0, GROUP, jb, put)
        conv(fields, half_table(tables_ref, lat), near, rows8, feats, GROUP, PAIR, jb, put)
    dests = [SPAN + t for t in range(GROUP)]
    dests += [(GROUP + SPAN) * (1 - lat) + t for t in range(PAIR)]
    befores = [SPAN + far + t for t in range(GROUP)] + [SPAN + mid + t for t in range(PAIR)]
    step = len(dests) // parts
    for t in range(0, len(dests), step):
        rows = [fields.at[r] for r in befores[t : t + step]]
        mix(weights_ref, 0, feats, t, blocks1, rows, into(after, dests[t : t + step]))
    for put, jb in enumerate(blocks2):
        conv(after, tables_ref[0], 0, rows8, feats, 0, GROUP, jb, put)
    step = GROUP // parts
    for t in range(0, GROUP, step):
        befores = [after.at[SPAN + t + m] for m in range(step)]
        rows = [far + t + m for m in range(step)]
        mix(weights_ref, 1, feats, t, blocks2, befores, into_turned(turned, rows, lat_rows))


def far1_kernel(
    half, own_ref, tables_ref, weights_ref, fields_ref, after_ref, turned_ref, feats
):
    lat_rows, lon_total, chans = own_ref.shape
    for t in range(SPAN):
        fields_ref[t] = jnp.zeros((lon_total, chans), BF16)
        fields_ref[SPAN + lat_rows + t] = jnp.zeros((lon_total, chans), BF16)
    fields_ref[SPAN : SPAN + lat_rows] = own_ref[...]

    def body(lat, core):
        for t in range(SPAN):
            after_ref[(GROUP + SPAN) * lat + t] = jnp.zeros((lon_total - BLOCK, chans), BF16)
        far_rows(
            lat,
            fields_ref,
            after_ref,
            tables_ref,
            weights_ref,
            feats,
            turned_ref,
            early_blocks(core, lon_total // BLOCK - 1),
            early_blocks(core, half // BLOCK),
            1,
        )

    for_each_core(lambda core: for_each_lat(functools.partial(body, core=core)))


def far2_kernel(
    half,
    cols,
    lon_ref,
    tables_ref,
    weights_ref,
    fields_in,
    after_in,
    turned_in,
    fields_ref,
    after_ref,
    turned_ref,
    feats,
):
    lat_rows = lon_ref.shape[0]

    def body(lat, core):
        add_lon_halo(
            cols,
            half,
            [fields_ref.at[SPAN + r] for r in range(lat_rows)],
            [lon_ref.at[r] for r in range(lat_rows)],
            core,
        )
        far_rows(
            lat,
            fields_ref,
            after_ref,
            tables_ref,
            weights_ref,
            feats,
            turned_ref,
            late_blocks(core, fields_ref.shape[1] // BLOCK - 1),
            late_blocks(core, half // BLOCK),
            1,
        )

    for_each_core(lambda core: for_each_lat(functools.partial(body, core=core)))


def near_rows(
    lat, fields, near, table, tables_ref, weights_ref, feats, turned, blocks1, blocks2, parts
):
    lat_rows = near.shape[0]
    rows6, rows8 = PAIR + 2 * SPAN, GROUP + 2 * SPAN
    group = SPAN * lat
    beyond = HALO * (1 - lat)
    for put, jb in enumerate(blocks1):
        conv(fields, half_table(tables_ref, 1 - lat), group, rows8, feats, 0, PAIR, jb, put)
    for put, jb in enumerate(blocks1):
        conv(fields, table[:, 0 : rows6 * WINDOW], beyond, rows6, feats, PAIR, PAIR, jb, put)
    befores = [fields.at[HALO + m] for m in range(PAIR)]
    befores += [fields.at[beyond + SPAN + m] for m in range(PAIR)]
    dests = [GROUP * (1 - lat) + SPAN * lat + m for m in range(PAIR)]
    dests += [(GROUP + SPAN) * (1 - lat) + m for m in range(PAIR)]
    step = GROUP // parts
    for t in range(0, GROUP, step):
        rows = slice(t, t + step)
        mix(weights_ref, 0, feats, t, blocks1, befores[rows], into(near, dests[rows]))
    for put, jb in enumerate(blocks2):
        conv(near, tables_ref[1], 0, GROUP + 2 * SPAN, feats, 0, GROUP, jb, put)
    for t in range(0, GROUP, step):
        befores = [near.at[SPAN + t + m] for m in range(step)]
        rows = [GROUP * (1 - lat) + t + m for m in range(step)]
        mix(weights_ref, 1, feats, t, blocks2, befores, into_turned(turned, rows, lat_rows))


def near1_kernel(
    half,
    ext_ref,
    next_ref,
    lat_ref,
    tables_ref,
    weights_ref,
    order_ref,
    turned_in,
    fields_ref,
    near_ref,
    table_ref,
    turned_ref,
    keep_ref,
    send_ref,
    feats,
):
    lon_total = ext_ref.shape[1]

    def body(lat, core):
        halo = (HALO + SPAN) * (1 - lat)
        own = HALO * lat
        for t in range(HALO + SPAN):
            fields_ref[own + t] = ext_ref[SPAN + SPAN * (1 - lat) + t]
        add_lat_halo([fields_ref.at[halo + t] for t in range(HALO)], lat_ref, half + WIDE, core)
        table = halo_table(lat_ref, order_ref[...])
        table_ref[...] = table
        for t in range(GROUP):
            near_ref[GROUP * lat + t] = next_ref[GROUP * (1 - lat) + t]
        near_rows(
            lat,
            fields_ref,
            near_ref,
            table,
            tables_ref,
            weights_ref,
            feats,
            turned_ref,
            early_blocks(core, lon_total // BLOCK - 1),
            early_blocks(core, half // BLOCK),
            1,
        )
        hand_out(turned_ref, keep_ref, send_ref, core, early_start(core))

    for_each_core(lambda core: for_each_lat(functools.partial(body, core=core)))


def near2_kernel(
    half,
    cols,
    corner_ref,
    table_ref,
    tables_ref,
    weights_ref,
    fields_in,
    near_in,
    turned_in,
    fields_ref,
    near_ref,
    turned_ref,
    keep_ref,
    send_ref,
    feats,
):
    def body(lat, core):
        halo = (HALO + SPAN) * (1 - lat)
        add_lon_halo(
            cols,
            half,
            [fields_ref.at[halo + t] for t in range(HALO)],
            [corner_ref.at[t] for t in range(HALO)],
            core,
        )
        near_rows(
            lat,
            fields_ref,
            near_ref,
            table_ref[...],
            tables_ref,
            weights_ref,
            feats,
            turned_ref,
            late_blocks(core, fields_ref.shape[1] // BLOCK - 1),
            late_blocks(core, half // BLOCK),
            1,
        )
        hand_out(turned_ref, keep_ref, send_ref, core, late_start(core, half))

    for_each_core(lambda core: for_each_lat(functools.partial(body, core=core)))


def all_kernel(half, cols, own_ref, lon_ref, *rest):
    lat_refs, corner_refs = rest[:2], rest[2:4]
    (tables_ref, weights_ref, order_ref), rest = rest[4:7], rest[7:]
    (late_keep_ref, late_send_ref, keep_ref, send_ref), rest = rest[:4], rest[4:]
    fields, feats, after, turned = rest
    lat_rows, lon_total, chans = own_ref.shape
    groups = lat_rows // GROUP
    lon1 = lon_total - BLOCK
    halo_base = [0, lat_rows + HALO]
    win_base = [0, lat_rows + HALO - SPAN]
    out_base = [0, lat_rows + SPAN]
    rows6 = PAIR + 2 * SPAN

    fields[HALO : HALO + lat_rows] = own_ref[...]

    @for_each_core
    def _(core):
        rows = [fields.at[HALO + r] for r in range(lat_rows)]
        halos = [lon_ref.at[r] for r in range(lat_rows)]
        for n in range(2):
            halo_rows = [fields.at[halo_base[n] + t] for t in range(HALO)]
            add_lat_halo(halo_rows, lat_refs[n], half + WIDE, core)
            rows += halo_rows
            halos += [corner_refs[n].at[t] for t in range(HALO)]
        add_lon_halo(cols, half, rows, halos, core)

    halo_tables = [
        halo_table(lat_refs[n], order_ref[...])[:, 0 : rows6 * WINDOW] for n in range(2)
    ]
    blocks = range(lon1 // BLOCK)
    for jb in blocks:
        for g in range(groups):
            base = HALO - SPAN + g * GROUP
            conv(
                fields, tables_ref[g], base, GROUP + 2 * SPAN, feats, g * GROUP, GROUP, jb, jb
            )
        for n in range(2):
            first = lat_rows + n * PAIR
            conv(fields, halo_tables[n], win_base[n], rows6, feats, first, PAIR, jb, jb)
    dests = [SPAN + i for i in range(lat_rows)]
    dests += [out_base[n] + m for n in range(2) for m in range(PAIR)]
    for i in range(0, len(dests), PAIR):
        befores = [fields.at[dest + SPAN] for dest in dests[i : i + PAIR]]
        mix(weights_ref, 0, feats, i, blocks, befores, into(after, dests[i : i + PAIR]))
    blocks = range(half // BLOCK)
    for jb in blocks:
        for g in range(groups):
            base = g * GROUP
            conv(after, tables_ref[g], base, GROUP + 2 * SPAN, feats, base, GROUP, jb, jb)
    for i in range(0, lat_rows, PAIR):
        befores = [after.at[SPAN + i + m] for m in range(PAIR)]
        rows = [i + m for m in range(PAIR)]
        mix(weights_ref, 1, feats, i, blocks, befores, into_turned(turned, rows, lat_rows))

    @for_each_core
    def _(core):
        hand_out(turned, late_keep_ref, late_send_ref, core, late_start(core, half))
        hand_out(turned, keep_ref, send_ref, core, early_start(core))


def write(copies, sems):
    copies = [
        pltpu.make_async_copy(source, dest, sems.at[n])
        for n, (source, dest) in enumerate(copies)
    ]
    for copy in copies:
        copy.start()
    for copy in copies:
        copy.wait()


def early_kernel(half, keep_ref, got_ref, out_hbm, sems):
    @for_each_core
    def _(core):
        copies = []
        for which, ref in ((core, keep_ref), (1 - core, got_ref)):
            at = which * half + early_start(which)
            copies.append((ref, out_hbm.at[at : at + ref.shape[0]]))
        write(copies, sems)


def late_kernel(half, keep_ref, got_ref, out_in, out_hbm, sems):
    cols = out_hbm.shape[0]

    @for_each_core
    def _(core):
        copies = []
        for which, ref in ((core, keep_ref), (1 - core, got_ref)):
            at = which * half + late_start(which, half)
            count = min(LATE, cols - at)
            copies.append((ref.at[0:count], out_hbm.at[at : at + count]))
        write(copies, sems)


def per_device(state, sup_rows, sup_count, lon_reach, psi, weights):
    lat_rows, cols, width = state.shape
    basis = psi.shape[2]
    chans = weights.shape[2]
    lats, lons = lax.axis_size("lat"), lax.axis_size("lon")
    sides = 1 if lats == 2 else 2
    groups = lat_rows // GROUP
    lanes = (GROUP + 2 * SPAN) * WINDOW
    half = -(-cols // (2 * BLOCK)) * BLOCK
    part = half + WIDE
    lon_total = half + 2 * WIDE
    lon1 = lon_total - BLOCK
    swap = [(0, 1), (1, 0)]
    params = pltpu.CompilerParams(vmem_limit_bytes=VMEM_LIMIT)

    def shape(*dims):
        return jax.ShapeDtypeStruct(dims, BF16)

    def to_lat(step):
        if lats == 2:
            return [(a, 1 - a) for a in range(lats)]
        return [(a, a + step) for a in range(lats) if 0 <= a + step < lats]

    forth = [((z, 1), ((z + 1) % lons, 0)) for z in range(lons)]
    back = [((z, 0), ((z - 1) % lons, 1)) for z in range(lons)]
    to_lon = forth + back

    own = jnp.transpose(state, (1, 0, 2))
    other = lax.ppermute(own, "chan", swap)

    def scratch(*dims):
        return pltpu.VMEM(dims, F32)

    wide = scratch((half + part) * lat_rows, width)
    smalls = [sup_rows, sup_count, lon_reach]
    part_own, edge_own, bands = pl.pallas_call(
        functools.partial(own_kernel, sides, half),
        out_shape=[
            shape(lat_rows, part, width),
            shape(lat_rows, WIDE, width),
            shape(sides, PAIR * basis, lanes),
        ],
        in_specs=[hbm()] * 5,
        out_specs=[vmem()] * 3,
        scratch_shapes=[pltpu.SMEM(x.shape, x.dtype) for x in smalls]
        + [
            scratch(*psi.shape),
            pltpu.VMEM(own.shape, BF16),
            scratch(sides * PAIR, 2 * SPAN + 1, basis, lanes),
            scratch(PAIR * basis, lanes),
            wide,
            pltpu.SemaphoreType.DMA((5,)),
        ],
        compiler_params=params,
        name="own",
    )(*[in_hbm(x) for x in smalls + [psi, own]])

    fields, lon_edge, *sends = pl.pallas_call(
        functools.partial(edges_kernel, sides, half),
        out_shape=[shape(lat_rows, lon_total, chans), shape(lat_rows, WIDE, chans)]
        + [shape(HALO * part + PAIR * basis, chans)] * sides
        + [shape(HALO, WIDE, chans)] * sides,
        in_specs=[vmem()] * 4,
        out_specs=[vmem()] * (2 + 2 * sides),
        scratch_shapes=[wide],
        compiler_params=params,
        name="edges",
    )(part_own, edge_own, other, bands)

    steps = [1, -1][:sides]
    lat_halos = [lax.ppermute(x, "lat", to_lat(step)) for x, step in zip(sends, steps)]
    lon_halo = lax.ppermute(
        lon_edge, ("lon", "chan"), [(z * 2 + c, y * 2 + d) for (z, c), (y, d) in to_lon]
    )

    corners = [
        lax.ppermute(
            x,
            ("lon", "lat", "chan"),
            [
                ((z * lats + a) * 2 + c, (y * lats + b) * 2 + d)
                for a, b in to_lat(step)
                for (z, c), (y, d) in to_lon
            ],
        )
        for x, step in zip(sends[sides:], steps)
    ]

    weights_in, tables, order = pl.pallas_call(
        functools.partial(tables_kernel, sides),
        out_shape=[
            shape(*weights.shape),
            shape(groups, GROUP * basis * BLOCK, lanes),
            shape(PAIR * basis * BLOCK, PAIR * basis * BLOCK),
        ],
        in_specs=[hbm()] * 5 + [vmem()],
        out_specs=[vmem()] * 3,
        scratch_shapes=[pltpu.SMEM(x.shape, x.dtype) for x in smalls]
        + [
            scratch(*psi.shape),
            scratch(lat_rows, 2 * SPAN + 1, basis, lanes),
            scratch(lat_rows // PAIR, PAIR * basis, lanes),
            pltpu.SemaphoreType.DMA((5,)),
        ],
        compiler_params=params,
        name="tables",
    )(*[in_hbm(x) for x in smalls + [psi, weights]], lon_edge)

    late_shapes = [shape(LATE, lat_rows, width)] * 2
    early_shapes = [shape(half - LATE, lat_rows, width)] * 2
    turned = (2, half * lat_rows, width)
    if sides == 1:
        far_shapes = [
            shape(lat_rows + 2 * SPAN, lon_total, chans),
            shape(lat_rows, lon1, chans),
            jax.ShapeDtypeStruct(turned, F32),
        ]
        far_feats = pltpu.VMEM((GROUP + PAIR, lon1, basis * chans), BF16)
        far = pl.pallas_call(
            functools.partial(far1_kernel, half),
            out_shape=far_shapes,
            in_specs=[vmem()] * 3,
            out_specs=[vmem()] * 3,
            scratch_shapes=[far_feats],
            compiler_params=params,
            name="far_rows_1",
        )(fields, tables, weights_in)
        ext, after, done = pl.pallas_call(
            functools.partial(far2_kernel, half, cols),
            out_shape=far_shapes,
            in_specs=[vmem()] * 6,
            out_specs=[vmem()] * 3,
            scratch_shapes=[far_feats],
            input_output_aliases={3: 0, 4: 1, 5: 2},
            compiler_params=params,
            name="far_rows_2",
        )(lon_halo, tables, weights_in, *far)
        near_shapes = [shape(2 * HALO + SPAN, lon_total, chans), shape(GROUP + 2 * SPAN, lon1, chans)]
        near_feats = pltpu.VMEM((GROUP, lon1, basis * chans), BF16)
        ext, near, halo_tab, done, keep, send = pl.pallas_call(
            functools.partial(near1_kernel, half),
            out_shape=near_shapes
            + [shape(PAIR * basis * BLOCK, lanes), jax.ShapeDtypeStruct(turned, F32)]
            + early_shapes,
            in_specs=[vmem()] * 7,
            out_specs=[vmem()] * 6,
            scratch_shapes=[near_feats],
            input_output_aliases={6: 3},
            compiler_params=params,
            name="near_rows_1",
        )(ext, after, lat_halos[0], tables, weights_in, order, done)
        *_, late_keep, late_send = pl.pallas_call(
            functools.partial(near2_kernel, half, cols),
            out_shape=near_shapes + [jax.ShapeDtypeStruct(turned, F32)] + late_shapes,
            in_specs=[vmem()] * 7,
            out_specs=[vmem()] * 5,
            scratch_shapes=[near_feats],
            input_output_aliases={4: 0, 5: 1, 6: 2},
            compiler_params=params,
            name="near_rows_2",
        )(corners[0], halo_tab, tables, weights_in, ext, near, done)
    else:
        late_keep, late_send, keep, send = pl.pallas_call(
            functools.partial(all_kernel, half, cols),
            out_shape=late_shapes + early_shapes,
            in_specs=[vmem()] * (5 + 2 * sides),
            out_specs=[vmem()] * 4,
            scratch_shapes=[
                pltpu.VMEM((lat_rows + 2 * HALO, lon_total, chans), BF16),
                pltpu.VMEM((lat_rows + 2 * PAIR, lon1, basis * chans), BF16),
                pltpu.VMEM((lat_rows + 2 * SPAN, lon1, chans), BF16),
                scratch(*turned),
            ],
            compiler_params=params,
            name="all_rows",
        )(fields, lon_halo, *lat_halos, *corners, tables, weights_in, order)
    got = lax.ppermute(send, "chan", swap)
    late_got = lax.ppermute(late_send, "chan", swap)

    out_type = shape(cols, lat_rows, width)
    out = pl.pallas_call(
        functools.partial(early_kernel, half),
        out_shape=out_type,
        in_specs=[vmem()] * 2,
        out_specs=hbm(),
        scratch_shapes=[pltpu.SemaphoreType.DMA((2,))],
        compiler_params=params,
        name="write_early",
    )(keep, got)
    out = pl.pallas_call(
        functools.partial(late_kernel, half),
        out_shape=out_type,
        in_specs=[vmem()] * 2 + [hbm()],
        out_specs=hbm(),
        scratch_shapes=[pltpu.SemaphoreType.DMA((2,))],
        input_output_aliases={2: 0},
        compiler_params=params,
        name="write_late",
    )(late_keep, late_got, out)
    return jnp.transpose(out, (1, 0, 2))


def solution(mesh):
    return jax.shard_map(
        per_device,
        mesh=mesh,
        in_specs=(
            P(("groups", "lat"), "lon", "chan"),
            P("lat", None),
            P("lat"),
            P("lat"),
            P("lat", None, None, None),
            P(),
        ),
        out_specs=P(("groups", "lat"), "lon", "chan"),
        check_vma=False,
    )
```

```python
import functools

import jax
import jax.numpy as jnp
from jax import lax
from jax.experimental import pallas as pl
from jax.experimental.pallas import tpu as pltpu
from jax.sharding import PartitionSpec as P

LAYERS = 2
SPAN = 2
HALO = LAYERS * SPAN
BLOCK = 16
WINDOW = 2 * BLOCK
GROUP = 4
PAIR = 2
WIDE = BLOCK
LATE = 46
SHIFT = BLOCK // 2
VMEM_LIMIT = 48 * 1024 * 1024
BF16 = jnp.bfloat16
F32 = jnp.float32


def vmem():
    return pl.BlockSpec(memory_space=pltpu.VMEM)


def smem():
    return pl.BlockSpec(memory_space=pltpu.SMEM)


def hbm():
    return pl.BlockSpec(memory_space=pltpu.HBM)


def in_hbm(x):
    return pltpu.with_memory_space_constraint(x, pltpu.HBM)


def by_row(count):
    total = count * BLOCK
    out_row = lax.broadcasted_iota(jnp.int32, (total, total), 0)
    in_row = lax.broadcasted_iota(jnp.int32, (total, total), 1)
    source = (out_row % BLOCK) * count + out_row // BLOCK
    return (in_row == source).astype(F32).astype(BF16)


def toeplitz(rows_tab, order):
    moved = jnp.concatenate(
        [rows_tab if jj == 0 else pltpu.roll(rows_tab, jj, 1) for jj in range(BLOCK)], axis=0
    ).astype(BF16)
    return jnp.dot(order, moved, preferred_element_type=F32).astype(BF16)


def band_rows(refs, slots, rows):
    sup_ref, count_ref, reach_ref, psi_ref = refs
    lat_rows, sup, basis, offsets = psi_ref.shape
    lanes = slots.shape[3]
    slots[...] = jnp.zeros_like(slots)
    for n, i in enumerate(rows):
        row = lax.axis_index("lat") * lat_rows + i
        values = [psi_ref[i, s] for s in range(sup)]
        places = [jnp.where(s < count_ref[i], sup_ref[i, s] - row, -lat_rows) for s in range(sup)]
        for rel in range(2 * SPAN + 1):
            total = jnp.zeros((basis, offsets), F32)
            for value, at in zip(values, places):
                total = total + jnp.where(at == rel - SPAN, value, 0.0)
            slots[n, rel, :, 0:offsets] = total
    off = lax.broadcasted_iota(jnp.int32, (basis, lanes), 1) % WINDOW - offsets // 2
    bands = []
    for n, i in enumerate(rows):
        band = slots[n, 0]
        for rel in range(1, 2 * SPAN + 1):
            band = band + pltpu.roll(slots[n, rel], rel * WINDOW, 1)
        bands.append(jnp.where(jnp.abs(off) <= reach_ref[i], band, 0.0))
    return bands


def put_pair(scr, bands):
    for m, band in enumerate(bands):
        basis = band.shape[0]
        scr[m * basis : (m + 1) * basis, :] = (
            band if m == 0 else pltpu.roll(band, m * WINDOW, 1)
        )


def turn(ref, lon_from, lon_to, wide_scr):
    _, lat_rows, width = ref.shape
    wide_scr[lon_from * lat_rows : lon_to * lat_rows, :] = (
        ref[lon_from:lon_to].astype(F32).reshape((lon_to - lon_from) * lat_rows, width)
    )


def turned_row(wide_scr, lat_rows, row, start, count):
    return wide_scr[pl.ds(start * lat_rows + row, count, stride=lat_rows), :].astype(BF16)


def own_kernel(sides, half, *refs):
    sources, (part_ref, edge_ref, bands_ref), refs = refs[:5], refs[5:8], refs[8:]
    smems, (psi_ref, state_ref, slots, pair_scr, wide_scr, sems) = refs[:3], refs[3:]
    copies = [
        pltpu.make_async_copy(source, dest, sems.at[n])
        for n, (source, dest) in enumerate(zip(sources, (*smems, psi_ref, state_ref)))
    ]
    for copy in copies:
        copy.start()
    cols, lat_rows, width = state_ref.shape
    part = part_ref.shape[1]
    wide_scr[cols * lat_rows :, :] = jnp.zeros(
        (wide_scr.shape[0] - cols * lat_rows, width), F32
    )
    for copy in copies[:4]:
        copy.wait()
    firsts = [first + (HALO - PAIR) * (n == 0) for n, first in enumerate(needed_rows(2, lat_rows))]
    if sides == 1:
        firsts = [(1 - lax.axis_index("lat")) * (lat_rows - PAIR)]
    rows = [first + m for first in firsts for m in range(PAIR)]
    bands = band_rows((*smems, psi_ref), slots, rows)
    for n in range(sides):
        put_pair(pair_scr, bands[n * PAIR : (n + 1) * PAIR])
        bands_ref[n] = pair_scr[...].astype(BF16)
    copies[4].wait()

    @for_each_core
    def _(core):
        start = 0 if core == 0 else half - WIDE
        edge = 0 if core == 0 else cols - WIDE
        turn(state_ref, start, min(start + part, cols), wide_scr)
        for r in range(lat_rows):
            part_ref[r] = turned_row(wide_scr, lat_rows, r, start, part)
            edge_ref[r] = turned_row(wide_scr, lat_rows, r, edge, WIDE)


def edges_kernel(
    sides, half, part_ref, edge_ref, other_ref, bands_ref, fields_ref, lon_ref, *rest
):
    lat_refs, corner_refs, (wide_scr,) = rest[:sides], rest[sides : 2 * sides], rest[2 * sides :]
    cols, lat_rows, width = other_ref.shape
    lon_total = fields_ref.shape[1]
    part = part_ref.shape[1]
    chan = lax.axis_index("chan")
    wide_scr[cols * lat_rows :, :] = jnp.zeros(
        (wide_scr.shape[0] - cols * lat_rows, width), F32
    )

    def build(core):
        start = 0 if core == 0 else half - WIDE
        edge = 0 if core == 0 else cols - WIDE
        stop = start + part if core == 0 else cols
        at = WIDE if core == 0 else 0
        own = slice(core * width, (core + 1) * width)
        lane = slice((1 - core) * width, (2 - core) * width)
        turn(other_ref, start, stop, wide_scr)
        for r in range(lat_rows):
            lon_ref[r, :, own] = edge_ref[r]
            lon_ref[r, :, lane] = turned_row(wide_scr, lat_rows, r, edge, WIDE)
            fields_ref[r, at : at + part, own] = part_ref[r]
            fields_ref[r, at : at + part, lane] = turned_row(wide_scr, lat_rows, r, start, part)
        empty = slice(0, WIDE) if core == 0 else slice(part, lon_total)
        fields_ref[:, empty, :] = jnp.zeros((lat_rows, WIDE, 2 * width), BF16)

    @pl.when(chan == 0)
    def _():
        build(0)

    @pl.when(chan == 1)
    def _():
        build(1)

    at = pl.multiple_of((1 - chan) * WIDE, WIDE)
    for n, first in enumerate(needed_rows(sides, lat_rows)):
        for t in range(HALO):
            lat_refs[n][t * part : (t + 1) * part, :] = fields_ref[first + t, pl.ds(at, part), :]
            corner_refs[n][t] = lon_ref[first + t]
        lat_refs[n][HALO * part :, :] = bands_ref[n]


def needed_rows(sides, lat_rows):
    if sides == 1:
        return [(1 - lax.axis_index("lat")) * (lat_rows - HALO)]
    return [lat_rows - HALO, 0]


def tables_kernel(sides, sup_hbm, count_hbm, reach_hbm, psi_hbm, weights_hbm, _, *refs):
    (weights_ref, tables_ref, order_ref), refs = refs[:3], refs[3:]
    smems, (psi_ref, slots, pairs_scr, sems) = refs[:3], refs[3:]
    sources = (sup_hbm, count_hbm, reach_hbm, psi_hbm, weights_hbm)
    copies = [
        pltpu.make_async_copy(source, dest, sems.at[n])
        for n, (source, dest) in enumerate(zip(sources, (*smems, psi_ref, weights_ref)))
    ]
    for copy in copies:
        copy.start()
    lat_rows, _, basis, _ = psi_ref.shape
    lat = lax.axis_index("lat")
    order = by_row(GROUP * basis)
    order_ref[...] = by_row(PAIR * basis)
    for copy in copies[:4]:
        copy.wait()
    bands = band_rows((*smems, psi_ref), slots, range(lat_rows))
    for p in range(lat_rows // PAIR):
        put_pair(pairs_scr.at[p], bands[p * PAIR : (p + 1) * PAIR])

    def group(g):
        first, second = pairs_scr[2 * g], pairs_scr[2 * g + 1]
        return jnp.concatenate([first, pltpu.roll(second, PAIR * WINDOW, 1)], axis=0)

    if sides == 1:
        tables_ref[0] = toeplitz(group(lat), order)
        tables_ref[1] = toeplitz(group(1 - lat), order)
    else:
        for g in range(lat_rows // GROUP):
            tables_ref[g] = toeplitz(group(g), order)
    copies[4].wait()


def gelu(x):
    return 0.5 * x * (1.0 + jnp.tanh(0.7978845608028654 * (x + 0.044715 * (x * x * x))))


def add_lat_halo(rows, lat_ref, part, core):
    at = WIDE if core == 0 else 0
    for t, row in enumerate(rows):
        row[at : at + part, :] = lat_ref[t * part : (t + 1) * part, :]


def halo_table(lat_ref, order):
    count = order.shape[0] // BLOCK
    return toeplitz(lat_ref[lat_ref.shape[0] - count :, :].astype(F32), order)


def add_lon_halo(cols, half, rows, halos, core):
    count = cols - half + WIDE
    whole = count // BLOCK * BLOCK
    for row, halo in zip(rows, halos):
        if core == 0:
            row[0:WIDE, :] = halo[...]
            continue
        lon_total, chans = row.shape
        before = row[whole : whole + BLOCK, :].astype(F32)[0 : count - whole, :]
        empty = jnp.zeros((lon_total - count - WIDE, chans), F32)
        row[whole:lon_total, :] = jnp.concatenate(
            [before, halo[...].astype(F32), empty], axis=0
        ).astype(BF16)


def conv(source, table, base, in_rows, feats, first, out_rows, jb, put):
    chans = source.shape[2]
    basis = table.shape[0] // (out_rows * BLOCK)
    taken = source[pl.ds(base, in_rows), jb * BLOCK : jb * BLOCK + WINDOW, :]
    taken = taken.reshape(in_rows * WINDOW, chans)
    result = jnp.dot(table, taken, preferred_element_type=F32).astype(BF16)
    at = slice(put * BLOCK, (put + 1) * BLOCK)
    for m in range(out_rows):
        for k in range(basis):
            begin = (m * basis + k) * BLOCK
            feats[first + m, at, k * chans : (k + 1) * chans] = result[begin : begin + BLOCK, :]


def mix(weights_ref, layer, feats, row, blocks, befores, store):
    _, basis, chans, _ = weights_ref.shape
    count, lons = len(befores), len(blocks) * BLOCK
    mixed = jnp.dot(
        feats[row : row + count, 0:lons, :].reshape(count * lons, basis * chans),
        weights_ref[layer].reshape(basis * chans, chans),
        preferred_element_type=F32,
    )
    for n, before in enumerate(befores):
        before = before[...].astype(F32)
        for put, jb in enumerate(blocks):
            at, begin = SHIFT + jb * BLOCK, n * lons + put * BLOCK
            value = before[at : at + BLOCK, :] + gelu(mixed[begin : begin + BLOCK, :])
            store(n, jb, value)


def into(ref, rows):
    def store(n, jb, value):
        ref[rows[n], jb * BLOCK : (jb + 1) * BLOCK, :] = value.astype(BF16)

    return store


def into_turned(turned, rows, lat_rows):
    def store(n, jb, value):
        width = value.shape[1] // 2
        for c in range(2):
            turned[c, pl.ds(jb * BLOCK * lat_rows + rows[n], BLOCK, stride=lat_rows), :] = value[
                :, c * width : (c + 1) * width
            ]

    return store


def hand_out(turned, keep_ref, send_ref, core, start):
    count, lat_rows, width = keep_ref.shape
    at = slice(start * lat_rows, (start + count) * lat_rows)
    for ref, which in ((keep_ref, core), (send_ref, 1 - core)):
        ref[...] = turned[which, at, :].reshape(count, lat_rows, width).astype(BF16)


def late_blocks(core, count):
    return [0] if core == 0 else [count - 2, count - 1]


def early_blocks(core, count):
    late = late_blocks(core, count)
    return [jb for jb in range(count) if jb not in late]


def late_start(core, half):
    return 0 if core == 0 else half - LATE


def early_start(core):
    return LATE if core == 0 else 0


def for_each_core(body):
    for value in range(2):
        pl.when(lax.axis_index("chan") == value)(functools.partial(body, value))


def for_each_lat(body):
    for value in range(2):
        pl.when(lax.axis_index("lat") == value)(functools.partial(body, value))


def half_table(tables_ref, second):
    rows = tables_ref.shape[1] // 2
    return tables_ref[1, rows * second : rows * (second + 1), :]


def far_rows(
    lat, fields, after, tables_ref, weights_ref, feats, turned, blocks1, blocks2, parts
):
    lat_rows = after.shape[0]
    far = GROUP * lat
    near = GROUP - far
    mid = GROUP - PAIR * lat
    rows8 = GROUP + 2 * SPAN
    for put, jb in enumerate(blocks1):
        conv(fields, tables_ref[0], far, rows8, feats, 0, GROUP, jb, put)
        conv(fields, half_table(tables_ref, lat), near, rows8, feats, GROUP, PAIR, jb, put)
    dests = [SPAN + t for t in range(GROUP)]
    dests += [(GROUP + SPAN) * (1 - lat) + t for t in range(PAIR)]
    befores = [SPAN + far + t for t in range(GROUP)] + [SPAN + mid + t for t in range(PAIR)]
    step = len(dests) // parts
    for t in range(0, len(dests), step):
        rows = [fields.at[r] for r in befores[t : t + step]]
        mix(weights_ref, 0, feats, t, blocks1, rows, into(after, dests[t : t + step]))
    for put, jb in enumerate(blocks2):
        conv(after, tables_ref[0], 0, rows8, feats, 0, GROUP, jb, put)
    step = GROUP // parts
    for t in range(0, GROUP, step):
        befores = [after.at[SPAN + t + m] for m in range(step)]
        rows = [far + t + m for m in range(step)]
        mix(weights_ref, 1, feats, t, blocks2, befores, into_turned(turned, rows, lat_rows))


def far1_kernel(
    half, own_ref, tables_ref, weights_ref, fields_ref, after_ref, turned_ref, feats
):
    lat_rows, lon_total, chans = own_ref.shape
    for t in range(SPAN):
        fields_ref[t] = jnp.zeros((lon_total, chans), BF16)
        fields_ref[SPAN + lat_rows + t] = jnp.zeros((lon_total, chans), BF16)
    fields_ref[SPAN : SPAN + lat_rows] = own_ref[...]

    def body(lat, core):
        for t in range(SPAN):
            after_ref[(GROUP + SPAN) * lat + t] = jnp.zeros((lon_total - BLOCK, chans), BF16)
        far_rows(
            lat,
            fields_ref,
            after_ref,
            tables_ref,
            weights_ref,
            feats,
            turned_ref,
            early_blocks(core, lon_total // BLOCK - 1),
            early_blocks(core, half // BLOCK),
            3,
        )

    for_each_core(lambda core: for_each_lat(functools.partial(body, core=core)))


def far2_kernel(
    half,
    cols,
    lon_ref,
    tables_ref,
    weights_ref,
    fields_in,
    after_in,
    turned_in,
    fields_ref,
    after_ref,
    turned_ref,
    feats,
):
    lat_rows = lon_ref.shape[0]

    def body(lat, core):
        add_lon_halo(
            cols,
            half,
            [fields_ref.at[SPAN + r] for r in range(lat_rows)],
            [lon_ref.at[r] for r in range(lat_rows)],
            core,
        )
        far_rows(
            lat,
            fields_ref,
            after_ref,
            tables_ref,
            weights_ref,
            feats,
            turned_ref,
            late_blocks(core, fields_ref.shape[1] // BLOCK - 1),
            late_blocks(core, half // BLOCK),
            1,
        )

    for_each_core(lambda core: for_each_lat(functools.partial(body, core=core)))


def near_rows(
    lat, fields, near, table, tables_ref, weights_ref, feats, turned, blocks1, blocks2, parts
):
    lat_rows = near.shape[0]
    rows6, rows8 = PAIR + 2 * SPAN, GROUP + 2 * SPAN
    group = SPAN * lat
    beyond = HALO * (1 - lat)
    for put, jb in enumerate(blocks1):
        conv(fields, half_table(tables_ref, 1 - lat), group, rows8, feats, 0, PAIR, jb, put)
    for put, jb in enumerate(blocks1):
        conv(fields, table[:, 0 : rows6 * WINDOW], beyond, rows6, feats, PAIR, PAIR, jb, put)
    befores = [fields.at[HALO + m] for m in range(PAIR)]
    befores += [fields.at[beyond + SPAN + m] for m in range(PAIR)]
    dests = [GROUP * (1 - lat) + SPAN * lat + m for m in range(PAIR)]
    dests += [(GROUP + SPAN) * (1 - lat) + m for m in range(PAIR)]
    step = GROUP // parts
    for t in range(0, GROUP, step):
        rows = slice(t, t + step)
        mix(weights_ref, 0, feats, t, blocks1, befores[rows], into(near, dests[rows]))
    for put, jb in enumerate(blocks2):
        conv(near, tables_ref[1], 0, GROUP + 2 * SPAN, feats, 0, GROUP, jb, put)
    for t in range(0, GROUP, step):
        befores = [near.at[SPAN + t + m] for m in range(step)]
        rows = [GROUP * (1 - lat) + t + m for m in range(step)]
        mix(weights_ref, 1, feats, t, blocks2, befores, into_turned(turned, rows, lat_rows))


def near1_kernel(
    half,
    ext_ref,
    next_ref,
    lat_ref,
    tables_ref,
    weights_ref,
    order_ref,
    turned_in,
    fields_ref,
    near_ref,
    table_ref,
    turned_ref,
    keep_ref,
    send_ref,
    feats,
):
    lon_total = ext_ref.shape[1]

    def body(lat, core):
        halo = (HALO + SPAN) * (1 - lat)
        own = HALO * lat
        for t in range(HALO + SPAN):
            fields_ref[own + t] = ext_ref[SPAN + SPAN * (1 - lat) + t]
        add_lat_halo([fields_ref.at[halo + t] for t in range(HALO)], lat_ref, half + WIDE, core)
        table = halo_table(lat_ref, order_ref[...])
        table_ref[...] = table
        for t in range(GROUP):
            near_ref[GROUP * lat + t] = next_ref[GROUP * (1 - lat) + t]
        near_rows(
            lat,
            fields_ref,
            near_ref,
            table,
            tables_ref,
            weights_ref,
            feats,
            turned_ref,
            early_blocks(core, lon_total // BLOCK - 1),
            early_blocks(core, half // BLOCK),
            4,
        )
        hand_out(turned_ref, keep_ref, send_ref, core, early_start(core))

    for_each_core(lambda core: for_each_lat(functools.partial(body, core=core)))


def near2_kernel(
    half,
    cols,
    corner_ref,
    table_ref,
    tables_ref,
    weights_ref,
    fields_in,
    near_in,
    turned_in,
    fields_ref,
    near_ref,
    turned_ref,
    keep_ref,
    send_ref,
    feats,
):
    def body(lat, core):
        halo = (HALO + SPAN) * (1 - lat)
        add_lon_halo(
            cols,
            half,
            [fields_ref.at[halo + t] for t in range(HALO)],
            [corner_ref.at[t] for t in range(HALO)],
            core,
        )
        near_rows(
            lat,
            fields_ref,
            near_ref,
            table_ref[...],
            tables_ref,
            weights_ref,
            feats,
            turned_ref,
            late_blocks(core, fields_ref.shape[1] // BLOCK - 1),
            late_blocks(core, half // BLOCK),
            1,
        )
        hand_out(turned_ref, keep_ref, send_ref, core, late_start(core, half))

    for_each_core(lambda core: for_each_lat(functools.partial(body, core=core)))


def all_kernel(half, cols, own_ref, lon_ref, *rest):
    lat_refs, corner_refs = rest[:2], rest[2:4]
    (tables_ref, weights_ref, order_ref), rest = rest[4:7], rest[7:]
    (late_keep_ref, late_send_ref, keep_ref, send_ref), rest = rest[:4], rest[4:]
    fields, feats, after, turned = rest
    lat_rows, lon_total, chans = own_ref.shape
    groups = lat_rows // GROUP
    lon1 = lon_total - BLOCK
    halo_base = [0, lat_rows + HALO]
    win_base = [0, lat_rows + HALO - SPAN]
    out_base = [0, lat_rows + SPAN]
    rows6 = PAIR + 2 * SPAN

    fields[HALO : HALO + lat_rows] = own_ref[...]

    @for_each_core
    def _(core):
        rows = [fields.at[HALO + r] for r in range(lat_rows)]
        halos = [lon_ref.at[r] for r in range(lat_rows)]
        for n in range(2):
            halo_rows = [fields.at[halo_base[n] + t] for t in range(HALO)]
            add_lat_halo(halo_rows, lat_refs[n], half + WIDE, core)
            rows += halo_rows
            halos += [corner_refs[n].at[t] for t in range(HALO)]
        add_lon_halo(cols, half, rows, halos, core)

    halo_tables = [
        halo_table(lat_refs[n], order_ref[...])[:, 0 : rows6 * WINDOW] for n in range(2)
    ]
    blocks = range(lon1 // BLOCK)
    for jb in blocks:
        for g in range(groups):
            base = HALO - SPAN + g * GROUP
            conv(
                fields, tables_ref[g], base, GROUP + 2 * SPAN, feats, g * GROUP, GROUP, jb, jb
            )
        for n in range(2):
            first = lat_rows + n * PAIR
            conv(fields, halo_tables[n], win_base[n], rows6, feats, first, PAIR, jb, jb)
    dests = [SPAN + i for i in range(lat_rows)]
    dests += [out_base[n] + m for n in range(2) for m in range(PAIR)]
    for i in range(0, len(dests), PAIR):
        befores = [fields.at[dest + SPAN] for dest in dests[i : i + PAIR]]
        mix(weights_ref, 0, feats, i, blocks, befores, into(after, dests[i : i + PAIR]))
    blocks = range(half // BLOCK)
    for jb in blocks:
        for g in range(groups):
            base = g * GROUP
            conv(after, tables_ref[g], base, GROUP + 2 * SPAN, feats, base, GROUP, jb, jb)
    for i in range(0, lat_rows, PAIR):
        befores = [after.at[SPAN + i + m] for m in range(PAIR)]
        rows = [i + m for m in range(PAIR)]
        mix(weights_ref, 1, feats, i, blocks, befores, into_turned(turned, rows, lat_rows))

    @for_each_core
    def _(core):
        hand_out(turned, late_keep_ref, late_send_ref, core, late_start(core, half))
        hand_out(turned, keep_ref, send_ref, core, early_start(core))


def write(copies, sems):
    copies = [
        pltpu.make_async_copy(source, dest, sems.at[n])
        for n, (source, dest) in enumerate(copies)
    ]
    for copy in copies:
        copy.start()
    for copy in copies:
        copy.wait()


def early_kernel(half, keep_ref, got_ref, out_hbm, sems):
    @for_each_core
    def _(core):
        copies = []
        for which, ref in ((core, keep_ref), (1 - core, got_ref)):
            at = which * half + early_start(which)
            copies.append((ref, out_hbm.at[at : at + ref.shape[0]]))
        write(copies, sems)


def late_kernel(half, keep_ref, got_ref, out_in, out_hbm, sems):
    cols = out_hbm.shape[0]

    @for_each_core
    def _(core):
        copies = []
        for which, ref in ((core, keep_ref), (1 - core, got_ref)):
            at = which * half + late_start(which, half)
            count = min(LATE, cols - at)
            copies.append((ref.at[0:count], out_hbm.at[at : at + count]))
        write(copies, sems)


def per_device(state, sup_rows, sup_count, lon_reach, psi, weights):
    lat_rows, cols, width = state.shape
    basis = psi.shape[2]
    chans = weights.shape[2]
    lats, lons = lax.axis_size("lat"), lax.axis_size("lon")
    sides = 1 if lats == 2 else 2
    groups = lat_rows // GROUP
    lanes = (GROUP + 2 * SPAN) * WINDOW
    half = -(-cols // (2 * BLOCK)) * BLOCK
    part = half + WIDE
    lon_total = half + 2 * WIDE
    lon1 = lon_total - BLOCK
    swap = [(0, 1), (1, 0)]
    params = pltpu.CompilerParams(vmem_limit_bytes=VMEM_LIMIT)

    def shape(*dims):
        return jax.ShapeDtypeStruct(dims, BF16)

    def to_lat(step):
        if lats == 2:
            return [(a, 1 - a) for a in range(lats)]
        return [(a, a + step) for a in range(lats) if 0 <= a + step < lats]

    forth = [((z, 1), ((z + 1) % lons, 0)) for z in range(lons)]
    back = [((z, 0), ((z - 1) % lons, 1)) for z in range(lons)]
    to_lon = forth + back

    own = jnp.transpose(state, (1, 0, 2))
    other = lax.ppermute(own, "chan", swap)

    def scratch(*dims):
        return pltpu.VMEM(dims, F32)

    wide = scratch((half + part) * lat_rows, width)
    smalls = [sup_rows, sup_count, lon_reach]
    part_own, edge_own, bands = pl.pallas_call(
        functools.partial(own_kernel, sides, half),
        out_shape=[
            shape(lat_rows, part, width),
            shape(lat_rows, WIDE, width),
            shape(sides, PAIR * basis, lanes),
        ],
        in_specs=[hbm()] * 5,
        out_specs=[vmem()] * 3,
        scratch_shapes=[pltpu.SMEM(x.shape, x.dtype) for x in smalls]
        + [
            scratch(*psi.shape),
            pltpu.VMEM(own.shape, BF16),
            scratch(sides * PAIR, 2 * SPAN + 1, basis, lanes),
            scratch(PAIR * basis, lanes),
            wide,
            pltpu.SemaphoreType.DMA((5,)),
        ],
        compiler_params=params,
        name="own",
    )(*[in_hbm(x) for x in smalls + [psi, own]])

    fields, lon_edge, *sends = pl.pallas_call(
        functools.partial(edges_kernel, sides, half),
        out_shape=[shape(lat_rows, lon_total, chans), shape(lat_rows, WIDE, chans)]
        + [shape(HALO * part + PAIR * basis, chans)] * sides
        + [shape(HALO, WIDE, chans)] * sides,
        in_specs=[vmem()] * 4,
        out_specs=[vmem()] * (2 + 2 * sides),
        scratch_shapes=[wide],
        compiler_params=params,
        name="edges",
    )(part_own, edge_own, other, bands)

    steps = [1, -1][:sides]
    lat_halos = [lax.ppermute(x, "lat", to_lat(step)) for x, step in zip(sends, steps)]
    lon_halo = lax.ppermute(
        lon_edge, ("lon", "chan"), [(z * 2 + c, y * 2 + d) for (z, c), (y, d) in to_lon]
    )

    corners = [
        lax.ppermute(
            x,
            ("lon", "lat", "chan"),
            [
                ((z * lats + a) * 2 + c, (y * lats + b) * 2 + d)
                for a, b in to_lat(step)
                for (z, c), (y, d) in to_lon
            ],
        )
        for x, step in zip(sends[sides:], steps)
    ]

    weights_in, tables, order = pl.pallas_call(
        functools.partial(tables_kernel, sides),
        out_shape=[
            shape(*weights.shape),
            shape(groups, GROUP * basis * BLOCK, lanes),
            shape(PAIR * basis * BLOCK, PAIR * basis * BLOCK),
        ],
        in_specs=[hbm()] * 5 + [vmem()],
        out_specs=[vmem()] * 3,
        scratch_shapes=[pltpu.SMEM(x.shape, x.dtype) for x in smalls]
        + [
            scratch(*psi.shape),
            scratch(lat_rows, 2 * SPAN + 1, basis, lanes),
            scratch(lat_rows // PAIR, PAIR * basis, lanes),
            pltpu.SemaphoreType.DMA((5,)),
        ],
        compiler_params=params,
        name="tables",
    )(*[in_hbm(x) for x in smalls + [psi, weights]], lon_edge)

    late_shapes = [shape(LATE, lat_rows, width)] * 2
    early_shapes = [shape(half - LATE, lat_rows, width)] * 2
    turned = (2, half * lat_rows, width)
    if sides == 1:
        far_shapes = [
            shape(lat_rows + 2 * SPAN, lon_total, chans),
            shape(lat_rows, lon1, chans),
            jax.ShapeDtypeStruct(turned, F32),
        ]
        far_feats = pltpu.VMEM((GROUP + PAIR, lon1, basis * chans), BF16)
        far = pl.pallas_call(
            functools.partial(far1_kernel, half),
            out_shape=far_shapes,
            in_specs=[vmem()] * 3,
            out_specs=[vmem()] * 3,
            scratch_shapes=[far_feats],
            compiler_params=params,
            name="far_rows_1",
        )(fields, tables, weights_in)
        ext, after, done = pl.pallas_call(
            functools.partial(far2_kernel, half, cols),
            out_shape=far_shapes,
            in_specs=[vmem()] * 6,
            out_specs=[vmem()] * 3,
            scratch_shapes=[far_feats],
            input_output_aliases={3: 0, 4: 1, 5: 2},
            compiler_params=params,
            name="far_rows_2",
        )(lon_halo, tables, weights_in, *far)
        near_shapes = [shape(2 * HALO + SPAN, lon_total, chans), shape(GROUP + 2 * SPAN, lon1, chans)]
        near_feats = pltpu.VMEM((GROUP, lon1, basis * chans), BF16)
        ext, near, halo_tab, done, keep, send = pl.pallas_call(
            functools.partial(near1_kernel, half),
            out_shape=near_shapes
            + [shape(PAIR * basis * BLOCK, lanes), jax.ShapeDtypeStruct(turned, F32)]
            + early_shapes,
            in_specs=[vmem()] * 7,
            out_specs=[vmem()] * 6,
            scratch_shapes=[near_feats],
            input_output_aliases={6: 3},
            compiler_params=params,
            name="near_rows_1",
        )(ext, after, lat_halos[0], tables, weights_in, order, done)
        *_, late_keep, late_send = pl.pallas_call(
            functools.partial(near2_kernel, half, cols),
            out_shape=near_shapes + [jax.ShapeDtypeStruct(turned, F32)] + late_shapes,
            in_specs=[vmem()] * 7,
            out_specs=[vmem()] * 5,
            scratch_shapes=[near_feats],
            input_output_aliases={4: 0, 5: 1, 6: 2},
            compiler_params=params,
            name="near_rows_2",
        )(corners[0], halo_tab, tables, weights_in, ext, near, done)
    else:
        late_keep, late_send, keep, send = pl.pallas_call(
            functools.partial(all_kernel, half, cols),
            out_shape=late_shapes + early_shapes,
            in_specs=[vmem()] * (5 + 2 * sides),
            out_specs=[vmem()] * 4,
            scratch_shapes=[
                pltpu.VMEM((lat_rows + 2 * HALO, lon_total, chans), BF16),
                pltpu.VMEM((lat_rows + 2 * PAIR, lon1, basis * chans), BF16),
                pltpu.VMEM((lat_rows + 2 * SPAN, lon1, chans), BF16),
                scratch(*turned),
            ],
            compiler_params=params,
            name="all_rows",
        )(fields, lon_halo, *lat_halos, *corners, tables, weights_in, order)
    got = lax.ppermute(send, "chan", swap)
    late_got = lax.ppermute(late_send, "chan", swap)

    out_type = shape(cols, lat_rows, width)
    out = pl.pallas_call(
        functools.partial(early_kernel, half),
        out_shape=out_type,
        in_specs=[vmem()] * 2,
        out_specs=hbm(),
        scratch_shapes=[pltpu.SemaphoreType.DMA((2,))],
        compiler_params=params,
        name="write_early",
    )(keep, got)
    out = pl.pallas_call(
        functools.partial(late_kernel, half),
        out_shape=out_type,
        in_specs=[vmem()] * 2 + [hbm()],
        out_specs=hbm(),
        scratch_shapes=[pltpu.SemaphoreType.DMA((2,))],
        input_output_aliases={2: 0},
        compiler_params=params,
        name="write_late",
    )(late_keep, late_got, out)
    return jnp.transpose(out, (1, 0, 2))


def solution(mesh):
    return jax.shard_map(
        per_device,
        mesh=mesh,
        in_specs=(
            P(("groups", "lat"), "lon", "chan"),
            P("lat", None),
            P("lat"),
            P("lat"),
            P("lat", None, None, None),
            P(),
        ),
        out_specs=P(("groups", "lat"), "lon", "chan"),
        check_vma=False,
    )
```
